32 devices in a mesh: ctx: 16 (over z, x, core), ch: 2 (over y).
Axes of the slice: x: 2, y: 2, z: 4, core: 2. Of those that a mesh axis runs over, the one named last changes fastest.
Arguments:
- q_in: bfloat16 [2048, 8192], P('ctx', 'ch'), may hold values from -6 to 6
- k_in: bfloat16 [2048, 8192], P('ctx', 'ch'), may hold values from -6 to 6
- v_in: bfloat16 [2048, 8192], P('ctx', 'ch'), may hold values from -6 to 6
- stretch_of_slot: int32 [32], replicated, may hold values from 0 to 31, each once
- short_weight: float32 [3, 7, 8192], P(None, None, 'ch'), may hold values from -2 to 2
- rates: float32 [16, 8192], P(None, 'ch'), may hold values from 4.8828124e-06 to 0.03
- residues: float32 [16, 8192], P(None, 'ch'), may hold values from -12 to 12
- skip: float32 [8192], P('ch'), may hold values from -4 to 4
- gain: float32 [8192], P('ch'), may hold values from 0.5 to 1.5
Outputs:
- operator_out: bfloat16 [2048, 8192], P('ctx', 'ch')
The draws below stay inside these ranges and needn't reach their ends.
Inputs may be any that keep to these rules, and one draw needn't show every extreme that they name: stretch_of_slot names every sequence stretch exactly once.
All inputs are finite; a program needn't handle non-finite values.
Results may differ from the reference program's by a relative error of at most 0.001.
Values may be sent and summed in bfloat16 or wider, within the bound.
No kernel may reach another device: no remote copies, remote signals or barrier semaphores. Data moves between devices by JAX's collectives and lax.ppermute only.
A program may use at most 64 MiB of HBM per device.

```python
import math
import jax
import jax.numpy as jnp
from jax import lax

D = 8192
ORDER = 16
SHORT = 7
STRETCH = 64
NCHUNK = 32
SEQ = 2048


def draw_residues(key, part):
    ramp = jnp.exp(jnp.log(3.0) * jnp.arange(D, dtype=jnp.float32) / D)
    base = jnp.clip(jax.random.normal(key, (ORDER, D), jnp.float32), -4.0, 4.0)
    return base * ramp[None, :]


def level_of(own_key, shape, cuts, smallest, largest):
    level, own = 1.0, jax.random.fold_in(own_key, 6)
    for axis_at, shards_of in cuts:
        heights = jnp.exp(jax.random.uniform(jax.random.fold_in(own, axis_at), (shards_of,), jnp.float32, smallest / len(cuts), largest / len(cuts)))
        level = level * jnp.repeat(heights, shape[axis_at] // shards_of).reshape([-1 if axis == axis_at else 1 for axis in range(len(shape))])
    return level


def scatter_about(stream_key, dims, scale, limit, shards=(), held_as=jnp.bfloat16):
    factor_of = level_of(stream_key, dims, shards, -0.22, 0.18) if shards else 1.0
    drawn = jax.random.normal(stream_key, dims, jnp.float32) * scale * factor_of
    return jnp.minimum(jnp.maximum(drawn, -limit), limit).astype(held_as)


def setup_inputs(seed: int = 0) -> dict:
    streams_of = jax.random.split(jax.random.key(seed), 10)
    return {
        "q_in": scatter_about(streams_of[0], (SEQ, D), 1.0, 6.0, ((0, 16), (1, 2))),
        "k_in": scatter_about(streams_of[1], (SEQ, D), 1.0, 6.0, ((0, 16), (1, 2))),
        "v_in": scatter_about(streams_of[2], (SEQ, D), 1.0, 6.0, ((0, 16), (1, 2))),
        "stretch_of_slot": jax.random.permutation(streams_of[3], NCHUNK).astype(jnp.int32),
        "short_weight": scatter_about(streams_of[4], (3, SHORT, D), SHORT ** -0.5, 2.0, ((2, 2),), jnp.float32),
        "rates": jnp.clip(jnp.exp(math.log(0.03) - 8.723231 * jax.random.uniform(streams_of[5], (ORDER, D), jnp.float32) ** level_of(streams_of[5], (ORDER, D), ((1, 2),), -0.2, 0.2)), 4.882812390860636e-06, 0.03),
        "residues": draw_residues(jax.random.fold_in(streams_of[9], 71), 0),
        "skip": scatter_about(streams_of[7], (D,), 1.0, 4.0, ((0, 2),), jnp.float32),
        "gain": jnp.clip(1.0 + 0.1 * jax.random.normal(streams_of[8], (D,), jnp.float32), 0.5, 1.5),
    }


def reference(q_in, k_in, v_in, stretch_of_slot, short_weight, rates, residues, skip, gain):
    inverse = jnp.zeros((NCHUNK,), jnp.int32).at[stretch_of_slot].set(jnp.arange(NCHUNK, dtype=jnp.int32))

    def ordered(values):
        return values.reshape(NCHUNK, STRETCH, D)[inverse].reshape(SEQ, D)
    q_seq = ordered(q_in)
    k_seq = ordered(k_in)
    v_seq = ordered(v_in)
    width = min(D, 512)
    groups = D // width

    def columns(values, group):
        return lax.dynamic_slice_in_dim(values, group * width, width, values.ndim - 1)

    def short_conv(values, taps):
        padded = jnp.pad(values.astype(jnp.float32), ((SHORT - 1, 0), (0, 0)))
        total = jnp.zeros((SEQ, width), jnp.float32)
        for shift_by in range(SHORT):
            total = total + taps[shift_by][None, :] * padded[SHORT - 1 - shift_by:SHORT - 1 - shift_by + SEQ]
        return total

    def one_group(group):
        taps = columns(short_weight, group)
        query = short_conv(columns(q_seq, group), taps[0])
        keys = short_conv(columns(k_seq, group), taps[1])
        values = short_conv(columns(v_seq, group), taps[2])
        mixed_in = keys * values
        rate = columns(rates, group)
        scaled = columns(residues, group) * jnp.sqrt(-jnp.expm1(-2.0 * rate))
        times = jnp.arange(SEQ, dtype=jnp.float32)
        filt = jnp.zeros((SEQ, width), jnp.float32)
        for mode in range(ORDER):
            filt = filt + scaled[mode][None, :] * jnp.exp(-rate[mode][None, :] * times[:, None])
        length = 2 * SEQ
        spectrum = jnp.fft.rfft(mixed_in, length, axis=0) * jnp.fft.rfft(filt, length, axis=0)
        conv = jnp.fft.irfft(spectrum, length, axis=0)[:SEQ]
        output = conv + columns(skip, group)[None, :] * mixed_in
        return query * output
    blocks = lax.map(one_group, jnp.arange(groups, dtype=jnp.int32))
    zvalues = blocks.transpose(1, 0, 2).reshape(SEQ, D)
    scale = lax.rsqrt(lax.optimization_barrier(jnp.mean(zvalues * zvalues, axis=1, keepdims=True)) + 1e-05)
    normed = (zvalues * scale * gain[None, :]).astype(jnp.bfloat16)
    return normed.reshape(NCHUNK, STRETCH, D)[stretch_of_slot].reshape(SEQ, D)
```

```python
from decimal import Decimal, getcontext

import jax
import jax.numpy as jnp
import ml_dtypes
import numpy as np
from jax import lax
from jax.experimental import pallas as pl
from jax.experimental.pallas import tpu as pltpu
from jax.sharding import PartitionSpec as P

F32, BF16 = jnp.float32, jnp.bfloat16
LANES = 128
STRETCH = 64
REACH = 6
INNER = STRETCH - REACH
NODES = (1, 8, 21, 36, 49, 56)
ANCHORS = ("0.000511", "0.004393", "0.011118", "0.018882", "0.025607", "0.029489")
RANK = len(NODES)
PIECE = 6 * REACH + 2 * RANK
BACK = 2 * REACH + 2 * RANK


def cardinal_table():
    getcontext().prec = 50
    anchors = [Decimal(a) for a in ANCHORS]
    table = [[(-a * n).exp() for n in NODES] for a in anchors]
    right = [[(-a * d).exp() for d in range(INNER)] for a in anchors]
    for col in range(RANK):
        pivot = max(range(col, RANK), key=lambda row: abs(table[row][col]))
        table[col], table[pivot] = table[pivot], table[col]
        right[col], right[pivot] = right[pivot], right[col]
        for row in range(RANK):
            if row != col:
                factor = table[row][col] / table[col][col]
                table[row] = [x - factor * y for x, y in zip(table[row], table[col])]
                right[row] = [x - factor * y for x, y in zip(right[row], right[col])]
    return np.array([[float(x / table[j][j]) for x in right[j]] for j in range(RANK)], np.float32)


def halves(values):
    high = values.astype(ml_dtypes.bfloat16)
    low = (values - high.astype(np.float32)).astype(ml_dtypes.bfloat16)
    return high, low


def constant_matrices():
    cardinal = cardinal_table()
    ends = np.zeros((16, STRETCH), np.float32)
    local = np.zeros((RANK, STRETCH, STRETCH), np.float32)
    lift = np.zeros((2, 2 * STRETCH, 2 * BACK), np.float32)
    high, low = (h.astype(np.float32) for h in halves(cardinal))
    for j in range(RANK):
        for s in range(REACH, STRETCH):
            ends[j, s] = cardinal[j, STRETCH - 1 - s]
            local[j, s:, s] = cardinal[j, : STRETCH - s]
        for half in range(2):
            rows = slice(half * STRETCH + REACH, (half + 1) * STRETCH)
            at = half * BACK + 2 * REACH
            lift[0, rows, at + j] = high[j]
            lift[0, rows, at + RANK + j] = high[j]
            lift[1, rows, at + j] = low[j]
    for half in range(2):
        for t in range(REACH):
            lift[0, half * STRETCH + t, half * BACK + t] = 1.0
            lift[0, half * STRETCH + t, half * BACK + REACH + t] = 1.0
    local = local.reshape(RANK * STRETCH, STRETCH)

    def triple(m):
        h, l = halves(m)
        return np.concatenate([h, h, l], axis=1)

    lifted = np.concatenate([lift[0], lift[1]], axis=1).astype(ml_dtypes.bfloat16)
    return triple(ends), triple(local), lifted


def split(values):
    high = values.astype(BF16)
    return high, (values - high.astype(F32)).astype(BF16)


def amplitude(rate, residue):
    x = 2.0 * rate
    series = 1.0 - x * (0.5 - x * (1 / 6 - x * (1 / 24 - x * (1 / 120 - x * (1 / 720)))))
    return residue * jnp.sqrt(x * series)


def gather_kernel(q_ref, k_ref, v_ref, taps_ref, ends_ref, pay_ref, u_ref, xs, pay):
    tile = k_ref.shape[1]
    for g in range(tile // LANES):
        cols = slice(g * LANES, (g + 1) * LANES)
        for i in range(2):
            rows = slice(i * STRETCH, (i + 1) * STRETCH)
            for a, ref in enumerate((q_ref, k_ref, v_ref)):
                base = i * (STRETCH + 8) + 8
                if a == 0:
                    xs[a, g, base : base + 16, :] = ref[i * STRETCH : i * STRETCH + 16, cols].astype(F32)
                    xs[a, g, base + STRETCH - 16 : base + STRETCH, :] = ref[
                        (i + 1) * STRETCH - 16 : (i + 1) * STRETCH, cols
                    ].astype(F32)
                else:
                    xs[a, g, base - 8 : base, :] = jnp.zeros((8, LANES), F32)
                    xs[a, g, base : base + STRETCH, :] = ref[rows, cols].astype(F32)
                pay[g, i * PIECE + a * REACH : i * PIECE + (a + 1) * REACH, :] = xs[
                    a, g, base + STRETCH - REACH : base + STRETCH, :
                ]
                pay[g, i * PIECE + (3 + a) * REACH : i * PIECE + (4 + a) * REACH, :] = xs[
                    a, g, base : base + REACH, :
                ]
        taps = [[taps_ref[a, j : j + 1, cols] for j in range(REACH + 1)] for a in (1, 2)]
        for i in range(2):
            for b in range(STRETCH // 16):
                base = i * (STRETCH + 8) + 8 + 16 * b
                both = []
                for a in range(2):
                    total = taps[a][0] * xs[1 + a, g, base : base + 16, :]
                    for j in range(1, REACH + 1):
                        total = total + taps[a][j] * xs[1 + a, g, base - j : base - j + 16, :]
                    both.append(total)
                mixed = both[0] * both[1]
                if b == 0:
                    row = lax.broadcasted_iota(jnp.int32, (16, LANES), 0)
                    mixed = jnp.where(row >= REACH, mixed, 0.0)
                high, low = split(mixed)
                rows = slice(i * STRETCH + 16 * b, i * STRETCH + 16 * b + 16)
                u_ref[0, rows, cols] = high
                u_ref[1, rows, cols] = low
    for i in range(2):
        rows = slice(i * STRETCH, (i + 1) * STRETCH)
        high, low = u_ref[0, rows, :], u_ref[1, rows, :]
        moments = jnp.dot(
            ends_ref[...], jnp.concatenate([high, low, high], axis=0), preferred_element_type=F32
        )
        top, rest = split(moments)
        for g in range(tile // LANES):
            cols = slice(g * LANES, (g + 1) * LANES)
            at = i * PIECE + 6 * REACH
            pay[g, at : at + RANK, :] = top.astype(F32)[:RANK, cols]
            pay[g, at + RANK : at + 2 * RANK, :] = rest.astype(F32)[:RANK, cols]
    for g in range(tile // LANES):
        cols = slice(g * LANES, (g + 1) * LANES)
        pay_ref[:, cols] = pay[g].astype(BF16)


def local_kernel(q_ref, u_ref, taps_ref, rates_ref, res_ref, skip_ref, local_ref, qc_ref, y_ref, xs):
    tile = q_ref.shape[1]
    for g in range(tile // LANES):
        cols = slice(g * LANES, (g + 1) * LANES)
        taps = [taps_ref[0, j : j + 1, cols] for j in range(REACH + 1)]
        for i in range(2):
            base = i * (STRETCH + 8) + 8
            xs[g, base - 8 : base, :] = jnp.zeros((8, LANES), F32)
            xs[g, base : base + STRETCH, :] = q_ref[i * STRETCH : (i + 1) * STRETCH, cols].astype(F32)
            for b in range(STRETCH // 8):
                at = base + 8 * b
                total = taps[0] * xs[g, at : at + 8, :]
                for j in range(1, REACH + 1):
                    total = total + taps[j] * xs[g, at - j : at - j + 8, :]
                if b == 0:
                    row = lax.broadcasted_iota(jnp.int32, (8, LANES), 0)
                    total = jnp.where(row >= REACH, total, 1.0)
                qc_ref[i * STRETCH + 8 * b : i * STRETCH + 8 * b + 8, cols] = total
    rate = rates_ref[...]
    amount = amplitude(rate, res_ref[...])
    weights = [jnp.sum(amount * jnp.exp(-rate * float(n)), axis=0, keepdims=True) for n in NODES]
    for i in range(2):
        rows = slice(i * STRETCH, (i + 1) * STRETCH)
        high, low = u_ref[0, rows, :], u_ref[1, rows, :]
        parts = jnp.dot(
            local_ref[...], jnp.concatenate([high, low, high], axis=0), preferred_element_type=F32
        )
        total = skip_ref[...] * (high.astype(F32) + low.astype(F32))
        for j in range(RANK):
            total = total + weights[j] * parts[j * STRETCH : (j + 1) * STRETCH, :]
        y_ref[rows, :] = total


def middle_kernel(
    me_ref, perm_ref, x_ref, taps_ref, rates_ref, res_ref, skip_ref, out_ref,
    raw, ext, moments, heads, inject, states, mids, carried, result,
):
    slots = perm_ref.shape[0]
    width = x_ref.shape[2]
    groups = width // LANES

    ext[:, :, 0, :, :] = jnp.zeros((3, groups, 16, LANES), F32)
    ext[:, :, :, 8:16, :] = jnp.zeros((3, groups, slots + 1, 8, LANES), F32)
    heads[:, :, 0:8, :] = jnp.zeros((groups, slots, 8, LANES), F32)

    def unpack(src, carry):
        for g in range(groups):
            raw[g] = x_ref[src, :, g * LANES : (g + 1) * LANES].astype(F32)
        for i in range(2):
            n = perm_ref[2 * src + i]
            for g in range(groups):
                for a in range(3):
                    at = i * PIECE + a * REACH
                    ext[a, g, n + 1, 0:REACH, :] = raw[g, at : at + REACH, :]
                    at = i * PIECE + (3 + a) * REACH
                    ext[a, g, n, REACH : 2 * REACH, :] = raw[g, at : at + REACH, :]
                at = i * PIECE + 6 * REACH
                moments[g, n, 0:RANK, :] = raw[g, at : at + RANK, :] + raw[g, at + RANK : at + 2 * RANK, :]
        return carry

    lax.fori_loop(0, slots // 2, unpack, 0)

    row = lax.broadcasted_iota(jnp.int32, (8, LANES), 0)
    rate = [rates_ref[:, g * LANES : (g + 1) * LANES] for g in range(groups)]
    amount = [amplitude(rate[g], res_ref[:, g * LANES : (g + 1) * LANES]) for g in range(groups)]

    for g in range(groups):
        cols = slice(g * LANES, (g + 1) * LANES)
        enter = [jnp.exp(-rate[g] * float(REACH - 1 - s)) for s in range(REACH)]
        gather = [jnp.exp(-rate[g] * float(n)) for n in NODES]
        taps = [[taps_ref[a, j : j + 1, cols] for j in range(REACH + 1)] for a in range(3)]

        def head_pass(n, carry, g=g, taps=taps, enter=enter, gather=gather):
            feats = []
            for a in range(3):
                total = taps[a][0] * ext[a, g, n, REACH : REACH + 8, :]
                for j in range(1, REACH + 1):
                    total = total + taps[a][j] * ext[a, g, n, REACH - j : REACH - j + 8, :]
                feats.append(jnp.where(row < REACH, total, 0.0))
            mixed = feats[1] * feats[2]
            heads[g, n, 8:16, :] = mixed
            carried[g, n, 0:8, :] = feats[0]
            first = enter[0] * mixed[0:1, :]
            for s in range(1, REACH):
                first = first + enter[s] * mixed[s : s + 1, :]
            second = gather[0] * moments[g, n, 0:1, :]
            for j in range(1, RANK):
                second = second + gather[j] * moments[g, n, j : j + 1, :]
            inject[g, n, 0:16, :] = first
            inject[g, n, 16:32, :] = second
            return carry

        lax.fori_loop(0, slots, head_pass, 0, unroll=2)

    fade_head = [jnp.exp(-rate[g] * float(REACH)) for g in range(groups)]
    fade_rest = [jnp.exp(-rate[g] * float(INNER)) for g in range(groups)]

    def scan_pass(n, state):
        after = []
        for g in range(groups):
            states[g, n] = state[g]
            mid = fade_head[g] * state[g] + inject[g, n, 0:16, :]
            mids[g, n] = mid
            after.append(fade_rest[g] * mid + inject[g, n, 16:32, :])
        return tuple(after)

    lax.fori_loop(0, slots, scan_pass, tuple(jnp.zeros((16, LANES), F32) for _ in range(groups)), unroll=4)

    for g in range(groups):
        cols = slice(g * LANES, (g + 1) * LANES)
        taps = [jnp.sum(amount[g] * jnp.exp(-rate[g] * float(d)), axis=0, keepdims=True) for d in range(REACH)]
        taps[0] = taps[0] + skip_ref[:, cols]
        lifts = [amount[g] * jnp.exp(-rate[g] * float(t + 1)) for t in range(REACH)]
        spread = [amount[g] * jnp.exp(-rate[g] * float(n + 1)) for n in NODES]

        def out_pass(n, carry, g=g, taps=taps, lifts=lifts, spread=spread):
            state, mid = states[g, n], mids[g, n]
            total = taps[0] * heads[g, n, 8:16, :]
            for d in range(1, REACH):
                total = total + taps[d] * heads[g, n, 8 - d : 16 - d, :]
            for t in range(REACH):
                carried[g, n, 8 + t : 9 + t, :] = jnp.sum(lifts[t] * state, axis=0, keepdims=True)
                carried[g, n, 16 + t : 17 + t, :] = jnp.sum(spread[t] * mid, axis=0, keepdims=True)
            z = carried[g, n, 0:8, :] * (total + carried[g, n, 8:16, :])
            high, low = split(z)
            result[g, n, 0:REACH, :] = high.astype(F32)[:REACH]
            result[g, n, REACH : 2 * REACH, :] = low.astype(F32)[:REACH]
            high, low = split(carried[g, n, 16:24, :])
            result[g, n, 2 * REACH : 2 * REACH + RANK, :] = high.astype(F32)[:RANK]
            result[g, n, 2 * REACH + RANK : BACK, :] = low.astype(F32)[:RANK]
            return carry

        lax.fori_loop(0, slots, out_pass, 0, unroll=2)

    def pack(src, carry):
        for g in range(groups):
            both = [result[g, perm_ref[2 * src + i], :, :] for i in range(2)]
            out_ref[src, :, g * LANES : (g + 1) * LANES] = jnp.concatenate(both, axis=0).astype(BF16)
        return carry

    lax.fori_loop(0, slots // 2, pack, 0)


def join_kernel(back_ref, lift_ref, qc_ref, y_ref, z_ref, sq_ref, total):
    step = pl.program_id(0)
    back = back_ref[...]
    carry = jnp.dot(lift_ref[...], jnp.concatenate([back, back], axis=0), preferred_element_type=F32)
    z = qc_ref[...] * (y_ref[...] + carry)
    z_ref[...] = z
    squares = z * z
    part = squares[:, :LANES]
    for g in range(1, z.shape[1] // LANES):
        part = part + squares[:, g * LANES : (g + 1) * LANES]

    @pl.when(step == 0)
    def _():
        total[...] = part

    @pl.when(step > 0)
    def _():
        total[...] += part

    @pl.when(step == pl.num_programs(0) - 1)
    def _():
        sq_ref[...] = jnp.sum(total[...], axis=1, keepdims=True)


PARAMS = pltpu.CompilerParams(vmem_limit_bytes=48 * 1024 * 1024)


def on_device(sizes, q_in, k_in, v_in, stretch_of_slot, short_weight, rates, residues, skip, gain):
    n_ctx, n_ch = sizes
    tokens, width = q_in.shape
    slots = stretch_of_slot.shape[0]
    order = rates.shape[0]
    share = width // n_ctx
    direct = share % LANES == 0
    tile = share if direct else 2 * LANES
    steps = width // tile
    ends_np, local_np, lift_np = constant_matrices()
    ends, local, lift = jnp.asarray(ends_np), jnp.asarray(local_np), jnp.asarray(lift_np)
    skip, gain = skip.reshape(1, width), gain.reshape(1, width)
    me = lax.axis_index("ctx").astype(jnp.int32).reshape(1)

    def whole(array):
        return pl.BlockSpec(array.shape, lambda c: (0,) * array.ndim)

    def columns(*lead):
        return pl.BlockSpec((*lead, tile), lambda c: (0,) * len(lead) + (c,))

    def payload(rows):
        if direct:
            return (
                jax.ShapeDtypeStruct((n_ctx, rows, share), BF16),
                pl.BlockSpec((None, rows, share), lambda c: (c, 0, 0)),
            )
        return jax.ShapeDtypeStruct((rows, width), BF16), columns(rows)

    groups = tile // LANES
    pay_shape, pay_spec = payload(2 * PIECE)
    pay, mixed = pl.pallas_call(
        gather_kernel,
        grid=(steps,),
        in_specs=[columns(tokens)] * 3 + [columns(3, REACH + 1), whole(ends)],
        out_specs=[pay_spec, columns(2, tokens)],
        out_shape=[pay_shape, jax.ShapeDtypeStruct((2, tokens, width), BF16)],
        scratch_shapes=[
            pltpu.VMEM((3, groups, 2 * (STRETCH + 8), LANES), F32),
            pltpu.VMEM((groups, 2 * PIECE, LANES), F32),
        ],
        compiler_params=PARAMS,
        name="gather_pieces",
    )(q_in, k_in, v_in, short_weight, ends)
    if not direct:
        pay = pay.reshape(2 * PIECE, n_ctx, share).transpose(1, 0, 2)
    arrived = lax.all_to_all(pay, "ctx", 0, 0, tiled=True)

    query, inner = pl.pallas_call(
        local_kernel,
        grid=(steps,),
        in_specs=[
            columns(tokens),
            columns(2, tokens),
            columns(3, REACH + 1),
            columns(order),
            columns(order),
            columns(1),
            whole(local),
        ],
        out_specs=[columns(tokens)] * 2,
        out_shape=[jax.ShapeDtypeStruct((tokens, width), F32)] * 2,
        scratch_shapes=[pltpu.VMEM((groups, 2 * (STRETCH + 8), LANES), F32)],
        compiler_params=PARAMS,
        name="local_filter",
        cost_estimate=pl.CostEstimate(flops=10**10, bytes_accessed=8 * 10**6, transcendentals=0),
    )(q_in, mixed, short_weight, rates, residues, skip, local)

    if direct:
        mine = (short_weight, rates, residues, skip)
        lanes = share

        def own(*lead):
            return pl.BlockSpec((*lead, share), lambda c, me_ref, perm_ref: (0,) * len(lead) + (me_ref[0],))

    else:
        lanes = -(-share // LANES) * LANES

        def widen(array, fill=0.0):
            pad = [(0, 0)] * (array.ndim - 1) + [(0, lanes - share)]
            return jnp.pad(array, pad, constant_values=fill)

        def cut(array, fill=0.0):
            return widen(
                lax.dynamic_slice_in_dim(array, lax.axis_index("ctx") * share, share, array.ndim - 1), fill
            )

        mine = (cut(short_weight), cut(rates, 0.01), cut(residues), cut(skip))
        arrived = widen(arrived)

        def own(*lead):
            return pl.BlockSpec((*lead, lanes), lambda c, me_ref, perm_ref: (0,) * (len(lead) + 1))

    groups = lanes // LANES
    back = pl.pallas_call(
        middle_kernel,
        grid_spec=pltpu.PrefetchScalarGridSpec(
            num_scalar_prefetch=2,
            grid=(1,),
            in_specs=[
                pl.BlockSpec((n_ctx, 2 * PIECE, lanes), lambda c, me_ref, perm_ref: (0, 0, 0)),
                own(3, REACH + 1),
                own(order),
                own(order),
                own(1),
            ],
            out_specs=pl.BlockSpec((n_ctx, 2 * BACK, lanes), lambda c, me_ref, perm_ref: (0, 0, 0)),
            scratch_shapes=[
                pltpu.VMEM((groups, 2 * PIECE, LANES), F32),
                pltpu.VMEM((3, groups, slots + 1, 16, LANES), F32),
                pltpu.VMEM((groups, slots, 8, LANES), F32),
                pltpu.VMEM((groups, slots, 16, LANES), F32),
                pltpu.VMEM((groups, slots, 2 * order, LANES), F32),
                pltpu.VMEM((groups, slots, order, LANES), F32),
                pltpu.VMEM((groups, slots, order, LANES), F32),
                pltpu.VMEM((groups, slots, 24, LANES), F32),
                pltpu.VMEM((groups, slots, BACK, LANES), F32),
            ],
        ),
        out_shape=jax.ShapeDtypeStruct((n_ctx, 2 * BACK, lanes), BF16),
        compiler_params=PARAMS,
        name="carry_states",
    )(me, stretch_of_slot, arrived, *mine)
    if not direct:
        back = back[:, :, :share]
    back = lax.all_to_all(back, "ctx", 0, 0, tiled=True)
    if not direct:
        back = back.transpose(1, 0, 2).reshape(2 * BACK, width)

    _, back_spec = payload(2 * BACK)
    zvalues, squares = pl.pallas_call(
        join_kernel,
        grid=(steps,),
        in_specs=[back_spec, whole(lift), columns(tokens), columns(tokens)],
        out_specs=[columns(tokens), pl.BlockSpec((tokens, 1), lambda c: (0, 0))],
        out_shape=[
            jax.ShapeDtypeStruct((tokens, width), F32),
            jax.ShapeDtypeStruct((tokens, 1), F32),
        ],
        scratch_shapes=[pltpu.VMEM((tokens, LANES), F32)],
        compiler_params=PARAMS,
        name="join_carry",
    )(back, lift, query, inner)
    total = squares
    for shift in range(1, n_ch):
        total = total + lax.ppermute(squares, "ch", [(i, (i + shift) % n_ch) for i in range(n_ch)])
    scale = lax.rsqrt(total / (width * n_ch) + 1e-05)
    return (zvalues * scale * gain).astype(BF16)


def solution(mesh):
    sizes = (mesh.shape["ctx"], mesh.shape["ch"])
    in_specs = (
        P("ctx", "ch"),
        P("ctx", "ch"),
        P("ctx", "ch"),
        P(),
        P(None, None, "ch"),
        P(None, "ch"),
        P(None, "ch"),
        P("ch"),
        P("ch"),
    )

    def run(*arrays):
        return on_device(sizes, *arrays)

    return jax.shard_map(run, mesh=mesh, in_specs=in_specs, out_specs=P("ctx", "ch"), check_vma=False)
```

```python
from decimal import Decimal, getcontext

import jax
import jax.numpy as jnp
import ml_dtypes
import numpy as np
from jax import lax
from jax.experimental import pallas as pl
from jax.experimental.pallas import tpu as pltpu
from jax.sharding import PartitionSpec as P

F32, BF16 = jnp.float32, jnp.bfloat16
LANES = 128
STRETCH = 64
REACH = 6
INNER = STRETCH - REACH
NODES = (1, 8, 21, 36, 49, 56)
ANCHORS = ("0.000511", "0.004393", "0.011118", "0.018882", "0.025607", "0.029489")
RANK = len(NODES)
RAW = 6 * REACH
BACK = 2 * REACH + 2 * RANK


def cardinal_table():
    getcontext().prec = 50
    anchors = [Decimal(a) for a in ANCHORS]
    table = [[(-a * n).exp() for n in NODES] for a in anchors]
    right = [[(-a * d).exp() for d in range(INNER)] for a in anchors]
    for col in range(RANK):
        pivot = max(range(col, RANK), key=lambda row: abs(table[row][col]))
        table[col], table[pivot] = table[pivot], table[col]
        right[col], right[pivot] = right[pivot], right[col]
        for row in range(RANK):
            if row != col:
                factor = table[row][col] / table[col][col]
                table[row] = [x - factor * y for x, y in zip(table[row], table[col])]
                right[row] = [x - factor * y for x, y in zip(right[row], right[col])]
    return np.array([[float(x / table[j][j]) for x in right[j]] for j in range(RANK)], np.float32)


def halves(values):
    high = values.astype(ml_dtypes.bfloat16)
    low = (values - high.astype(np.float32)).astype(ml_dtypes.bfloat16)
    return high, low


def constant_matrices():
    cardinal = cardinal_table()
    ends = np.zeros((16, STRETCH), np.float32)
    local = np.zeros((RANK, STRETCH, STRETCH), np.float32)
    lift = np.zeros((2, 2 * STRETCH, 2 * BACK), np.float32)
    high, low = (h.astype(np.float32) for h in halves(cardinal))
    for j in range(RANK):
        for s in range(REACH, STRETCH):
            ends[j, s] = cardinal[j, STRETCH - 1 - s]
            local[j, s:, s] = cardinal[j, : STRETCH - s]
        for half in range(2):
            rows = slice(half * STRETCH + REACH, (half + 1) * STRETCH)
            at = half * BACK + 2 * REACH
            lift[0, rows, at + j] = high[j]
            lift[0, rows, at + RANK + j] = high[j]
            lift[1, rows, at + j] = low[j]
    for half in range(2):
        for t in range(REACH):
            lift[0, half * STRETCH + t, half * BACK + t] = 1.0
            lift[0, half * STRETCH + t, half * BACK + REACH + t] = 1.0
    local = local.reshape(RANK * STRETCH, STRETCH)

    def triple(m):
        h, l = halves(m)
        return np.concatenate([h, h, l], axis=1)

    lifted = np.concatenate([lift[0], lift[1]], axis=1).astype(ml_dtypes.bfloat16)
    return triple(ends), triple(local), lifted


def split(values):
    high = values.astype(BF16)
    return high, (values - high.astype(F32)).astype(BF16)


def amplitude(rate, residue):
    x = 2.0 * rate
    series = 1.0 - x * (0.5 - x * (1 / 6 - x * (1 / 24 - x * (1 / 120 - x * (1 / 720)))))
    return residue * jnp.sqrt(x * series)


def put(ref, group, values):
    if len(ref.shape) == 3:
        share = ref.shape[2]
        dest, at = divmod(group * LANES, share)
        ref[dest, :, at : at + LANES] = values
    else:
        ref[:, group * LANES : (group + 1) * LANES] = values


def raw_kernel(*refs):
    ins, out_ref, rows, pay = refs[:12], refs[12], refs[13], refs[14]
    for g in range(ins[0].shape[1] // LANES):
        cols = slice(g * LANES, (g + 1) * LANES)
        for a in range(3):
            for i in range(2):
                first, last = ins[4 * a + 2 * i], ins[4 * a + 2 * i + 1]
                rows[g, 2 * a + i, 0:16, :] = first[:, cols].astype(F32)
                rows[g, 2 * a + i, 16:32, :] = last[:, cols].astype(F32)
                at = i * RAW + a * REACH
                pay[g, at : at + REACH, :] = rows[g, 2 * a + i, 32 - REACH : 32, :]
                at = at + 3 * REACH
                pay[g, at : at + REACH, :] = rows[g, 2 * a + i, 0:REACH, :]
        put(out_ref, g, pay[g].astype(BF16))


def gather_kernel(k_ref, v_ref, taps_ref, ends_ref, pay_ref, u_ref, xs, pay):
    tile = k_ref.shape[1]
    groups = tile // LANES
    for g in range(groups):
        cols = slice(g * LANES, (g + 1) * LANES)
        for i in range(2):
            rows = slice(i * STRETCH, (i + 1) * STRETCH)
            for a, ref in enumerate((k_ref, v_ref)):
                base = i * (STRETCH + 8) + 8
                xs[a, g, base - 8 : base, :] = jnp.zeros((8, LANES), F32)
                xs[a, g, base : base + STRETCH, :] = ref[rows, cols].astype(F32)
        taps = [[taps_ref[a, j : j + 1, cols] for j in range(REACH + 1)] for a in (1, 2)]
        for i in range(2):
            for b in range(STRETCH // 16):
                base = i * (STRETCH + 8) + 8 + 16 * b
                both = []
                for a in range(2):
                    total = taps[a][0] * xs[a, g, base : base + 16, :]
                    for j in range(1, REACH + 1):
                        total = total + taps[a][j] * xs[a, g, base - j : base - j + 16, :]
                    both.append(total)
                mixed = both[0] * both[1]
                if b == 0:
                    row = lax.broadcasted_iota(jnp.int32, (16, LANES), 0)
                    mixed = jnp.where(row >= REACH, mixed, 0.0)
                high, low = split(mixed)
                rows = slice(i * STRETCH + 16 * b, i * STRETCH + 16 * b + 16)
                u_ref[0, rows, cols] = high
                u_ref[1, rows, cols] = low
    span = min(tile, 2 * LANES)
    for c in range(tile // span):
        cols = slice(c * span, (c + 1) * span)
        for i in range(2):
            rows = slice(i * STRETCH, (i + 1) * STRETCH)
            high, low = u_ref[0, rows, cols], u_ref[1, rows, cols]
            moments = jnp.dot(
                ends_ref[...], jnp.concatenate([high, low, high], axis=0), preferred_element_type=F32
            )
            top, rest = split(moments)
            for h in range(span // LANES):
                g = c * (span // LANES) + h
                lanes = slice(h * LANES, (h + 1) * LANES)
                at = 2 * RANK * i
                pay[g, at : at + RANK, :] = top.astype(F32)[:RANK, lanes]
                pay[g, at + RANK : at + 2 * RANK, :] = rest.astype(F32)[:RANK, lanes]
    for g in range(groups):
        put(pay_ref, g, pay[g].astype(BF16))


def local_kernel(q_ref, u_ref, taps_ref, rates_ref, res_ref, skip_ref, local_ref, qc_ref, y_ref, xs):
    tile = q_ref.shape[1]
    for g in range(tile // LANES):
        cols = slice(g * LANES, (g + 1) * LANES)
        taps = [taps_ref[0, j : j + 1, cols] for j in range(REACH + 1)]
        for i in range(2):
            base = i * (STRETCH + 8) + 8
            xs[g, base - 8 : base, :] = jnp.zeros((8, LANES), F32)
            xs[g, base : base + STRETCH, :] = q_ref[i * STRETCH : (i + 1) * STRETCH, cols].astype(F32)
            for b in range(STRETCH // 8):
                at = base + 8 * b
                total = taps[0] * xs[g, at : at + 8, :]
                for j in range(1, REACH + 1):
                    total = total + taps[j] * xs[g, at - j : at - j + 8, :]
                if b == 0:
                    row = lax.broadcasted_iota(jnp.int32, (8, LANES), 0)
                    total = jnp.where(row >= REACH, total, 1.0)
                qc_ref[i * STRETCH + 8 * b : i * STRETCH + 8 * b + 8, cols] = total
    span = min(tile, 2 * LANES)
    for c in range(tile // span):
        cols = slice(c * span, (c + 1) * span)
        rate = rates_ref[:, cols]
        amount = amplitude(rate, res_ref[:, cols])
        weights = [jnp.sum(amount * jnp.exp(-rate * float(n)), axis=0, keepdims=True) for n in NODES]
        for i in range(2):
            rows = slice(i * STRETCH, (i + 1) * STRETCH)
            high, low = u_ref[0, rows, cols], u_ref[1, rows, cols]
            parts = jnp.dot(
                local_ref[...], jnp.concatenate([high, low, high], axis=0), preferred_element_type=F32
            )
            total = skip_ref[:, cols] * (high.astype(F32) + low.astype(F32))
            for j in range(RANK):
                total = total + weights[j] * parts[j * STRETCH : (j + 1) * STRETCH, :]
            y_ref[rows, cols] = total


def heads_kernel(
    me_ref, perm_ref, x_ref, taps_ref, rates_ref, res_ref, skip_ref, heads_ref, first_ref, raw, ext, past
):
    slots = perm_ref.shape[0]
    groups = x_ref.shape[2] // LANES
    ext[:, :, 0, :, :] = jnp.zeros((3, groups, 16, LANES), F32)
    ext[:, :, :, 8:16, :] = jnp.zeros((3, groups, slots + 1, 8, LANES), F32)
    past[:, :, 0:8, :] = jnp.zeros((groups, slots, 8, LANES), F32)

    def unpack(src, carry):
        for g in range(groups):
            raw[g] = x_ref[src, :, g * LANES : (g + 1) * LANES].astype(F32)
        for i in range(2):
            n = perm_ref[2 * src + i]
            for g in range(groups):
                for a in range(3):
                    at = i * RAW + a * REACH
                    ext[a, g, n + 1, 0:REACH, :] = raw[g, at : at + REACH, :]
                    at = at + 3 * REACH
                    ext[a, g, n, REACH : 2 * REACH, :] = raw[g, at : at + REACH, :]
        return carry

    lax.fori_loop(0, slots // 2, unpack, 0)
    row = lax.broadcasted_iota(jnp.int32, (8, LANES), 0)

    for g in range(groups):
        cols = slice(g * LANES, (g + 1) * LANES)
        rate = rates_ref[:, cols]
        amount = amplitude(rate, res_ref[:, cols])
        enter = [jnp.exp(-rate * float(REACH - 1 - s)) for s in range(REACH)]
        taps = [[taps_ref[a, j : j + 1, cols] for j in range(REACH + 1)] for a in range(3)]
        near = [jnp.sum(amount * jnp.exp(-rate * float(d)), axis=0, keepdims=True) for d in range(REACH)]
        near[0] = near[0] + skip_ref[:, cols]

        def head_pass(n, carry, g=g, taps=taps, enter=enter, near=near):
            feats = []
            for a in range(3):
                total = taps[a][0] * ext[a, g, n, REACH : REACH + 8, :]
                for j in range(1, REACH + 1):
                    total = total + taps[a][j] * ext[a, g, n, REACH - j : REACH - j + 8, :]
                feats.append(jnp.where(row < REACH, total, 0.0))
            mixed = feats[1] * feats[2]
            past[g, n, 8:16, :] = mixed
            total = near[0] * mixed
            for d in range(1, REACH):
                total = total + near[d] * past[g, n, 8 - d : 16 - d, :]
            heads_ref[g, n, 0:8, :] = feats[0]
            heads_ref[g, n, 8:16, :] = total
            first = enter[0] * mixed[0:1, :]
            for s in range(1, REACH):
                first = first + enter[s] * mixed[s : s + 1, :]
            first_ref[g, n] = first
            return carry

        lax.fori_loop(0, slots, head_pass, 0, unroll=2)


def states_kernel(
    me_ref, perm_ref, x_ref, heads_ref, first_ref, rates_ref, res_ref, out_ref,
    raw, moments, second, states, mids, carried, result,
):
    slots = perm_ref.shape[0]
    groups = x_ref.shape[2] // LANES

    def unpack(src, carry):
        for g in range(groups):
            raw[g] = x_ref[src, :, g * LANES : (g + 1) * LANES].astype(F32)
        for i in range(2):
            n = perm_ref[2 * src + i]
            for g in range(groups):
                at = 2 * RANK * i
                moments[g, n, 0:RANK, :] = raw[g, at : at + RANK, :] + raw[g, at + RANK : at + 2 * RANK, :]
        return carry

    lax.fori_loop(0, slots // 2, unpack, 0)

    rate = [rates_ref[:, g * LANES : (g + 1) * LANES] for g in range(groups)]
    amount = [amplitude(rate[g], res_ref[:, g * LANES : (g + 1) * LANES]) for g in range(groups)]
    for g in range(groups):
        gather = [jnp.exp(-rate[g] * float(n)) for n in NODES]

        def rest_pass(n, carry, g=g, gather=gather):
            total = gather[0] * moments[g, n, 0:1, :]
            for j in range(1, RANK):
                total = total + gather[j] * moments[g, n, j : j + 1, :]
            second[g, n] = total
            return carry

        lax.fori_loop(0, slots, rest_pass, 0, unroll=4)

    fade_head = [jnp.exp(-rate[g] * float(REACH)) for g in range(groups)]
    fade_rest = [jnp.exp(-rate[g] * float(INNER)) for g in range(groups)]

    def scan_pass(n, state):
        after = []
        for g in range(groups):
            states[g, n] = state[g]
            mid = fade_head[g] * state[g] + first_ref[g, n]
            mids[g, n] = mid
            after.append(fade_rest[g] * mid + second[g, n])
        return tuple(after)

    lax.fori_loop(0, slots, scan_pass, tuple(jnp.zeros((16, LANES), F32) for _ in range(groups)), unroll=4)

    for g in range(groups):
        lifts = [amount[g] * jnp.exp(-rate[g] * float(t + 1)) for t in range(REACH)]
        spread = [amount[g] * jnp.exp(-rate[g] * float(n + 1)) for n in NODES]

        def out_pass(n, carry, g=g, lifts=lifts, spread=spread):
            state, mid = states[g, n], mids[g, n]
            for t in range(REACH):
                carried[g, n, t : 1 + t, :] = jnp.sum(lifts[t] * state, axis=0, keepdims=True)
                carried[g, n, 8 + t : 9 + t, :] = jnp.sum(spread[t] * mid, axis=0, keepdims=True)
            z = heads_ref[g, n, 0:8, :] * (heads_ref[g, n, 8:16, :] + carried[g, n, 0:8, :])
            high, low = split(z)
            result[g, n, 0:REACH, :] = high.astype(F32)[:REACH]
            result[g, n, REACH : 2 * REACH, :] = low.astype(F32)[:REACH]
            high, low = split(carried[g, n, 8:16, :])
            result[g, n, 2 * REACH : 2 * REACH + RANK, :] = high.astype(F32)[:RANK]
            result[g, n, 2 * REACH + RANK : BACK, :] = low.astype(F32)[:RANK]
            return carry

        lax.fori_loop(0, slots, out_pass, 0, unroll=2)

    def pack(src, carry):
        for g in range(groups):
            both = [result[g, perm_ref[2 * src + i], :, :] for i in range(2)]
            out_ref[src, :, g * LANES : (g + 1) * LANES] = jnp.concatenate(both, axis=0).astype(BF16)
        return carry

    lax.fori_loop(0, slots // 2, pack, 0)


def join_kernel(back_ref, lift_ref, qc_ref, y_ref, z_ref, sq_ref, total):
    step = pl.program_id(0)
    part = jnp.zeros(total.shape, F32)
    by_dest = len(back_ref.shape) == 3
    span = back_ref.shape[-1] if by_dest else 2 * LANES
    for c in range(qc_ref.shape[1] // span):
        cols = slice(c * span, (c + 1) * span)
        back = back_ref[c] if by_dest else back_ref[:, cols]
        carry = jnp.dot(lift_ref[...], jnp.concatenate([back, back], axis=0), preferred_element_type=F32)
        z = qc_ref[:, cols] * (y_ref[:, cols] + carry)
        z_ref[:, cols] = z
        squares = z * z
        for g in range(span // LANES):
            part = part + squares[:, g * LANES : (g + 1) * LANES]

    @pl.when(step == 0)
    def _():
        total[...] = part

    @pl.when(step > 0)
    def _():
        total[...] += part

    @pl.when(step == pl.num_programs(0) - 1)
    def _():
        sq_ref[...] = jnp.sum(total[...].T, axis=0, keepdims=True)


def limit(mib):
    return pltpu.CompilerParams(vmem_limit_bytes=mib * 1024 * 1024)


def on_device(sizes, q_in, k_in, v_in, stretch_of_slot, short_weight, rates, residues, skip, gain):
    n_ctx, n_ch = sizes
    tokens, width = q_in.shape
    slots = stretch_of_slot.shape[0]
    order = rates.shape[0]
    share = width // n_ctx
    direct = share % LANES == 0
    tile = min(width, 1024)
    steps = width // tile
    groups = tile // LANES
    ends_np, local_np, lift_np = constant_matrices()
    ends, local, lift = jnp.asarray(ends_np), jnp.asarray(local_np), jnp.asarray(lift_np)
    skip, gain = skip.reshape(1, width), gain.reshape(1, width)
    me = lax.axis_index("ctx").astype(jnp.int32).reshape(1)

    def whole(array):
        return pl.BlockSpec(array.shape, lambda c: (0,) * array.ndim)

    def columns(*lead):
        return pl.BlockSpec((*lead, tile), lambda c: (0,) * len(lead) + (c,))

    def payload(rows):
        if direct:
            return (
                jax.ShapeDtypeStruct((n_ctx, rows, share), BF16),
                pl.BlockSpec((tile // share, rows, share), lambda c: (c, 0, 0)),
            )
        return jax.ShapeDtypeStruct((rows, width), BF16), columns(rows)

    def exchange(array):
        if direct:
            return lax.all_to_all(array, "ctx", 0, 0, tiled=True)
        array = array.reshape(array.shape[0], n_ctx, share).transpose(1, 0, 2)
        return widen(lax.all_to_all(array, "ctx", 0, 0, tiled=True))

    lanes = -(-share // LANES) * LANES

    def widen(array, fill=0.0):
        pad = [(0, 0)] * (array.ndim - 1) + [(0, lanes - share)]
        return jnp.pad(array, pad, constant_values=fill)

    if direct:
        mine = (short_weight, rates, residues, skip)

        def own(*lead):
            return pl.BlockSpec((*lead, share), lambda c, me_ref, perm_ref: (0,) * len(lead) + (me_ref[0],))

    else:

        def cut(array, fill=0.0):
            return widen(
                lax.dynamic_slice_in_dim(array, lax.axis_index("ctx") * share, share, array.ndim - 1), fill
            )

        mine = (cut(short_weight), cut(rates, 0.01), cut(residues), cut(skip))

        def own(*lead):
            return pl.BlockSpec((*lead, lanes), lambda c, me_ref, perm_ref: (0,) * (len(lead) + 1))

    def full(*shape):
        return pl.BlockSpec(shape, lambda c, me_ref, perm_ref: (0,) * len(shape))

    raw_shape, raw_spec = payload(2 * RAW)
    edges = [0, STRETCH // 16 - 1, STRETCH // 16, 2 * STRETCH // 16 - 1]
    raw = pl.pallas_call(
        raw_kernel,
        grid=(steps,),
        in_specs=[pl.BlockSpec((16, tile), lambda c, r=r: (r, c)) for _ in range(3) for r in edges],
        out_specs=raw_spec,
        out_shape=raw_shape,
        scratch_shapes=[pltpu.VMEM((groups, 6, 32, LANES), F32), pltpu.VMEM((groups, 2 * RAW, LANES), F32)],
        compiler_params=limit(60),
        name="edge_rows",
    )(*[array for array in (q_in, k_in, v_in) for _ in edges])
    raw = exchange(raw)

    pay_shape, pay_spec = payload(4 * RANK)
    pay, mixed = pl.pallas_call(
        gather_kernel,
        grid=(steps,),
        in_specs=[columns(tokens)] * 2 + [columns(3, REACH + 1), whole(ends)],
        out_specs=[pay_spec, columns(2, tokens)],
        out_shape=[pay_shape, jax.ShapeDtypeStruct((2, tokens, width), BF16)],
        scratch_shapes=[
            pltpu.VMEM((2, groups, 2 * (STRETCH + 8), LANES), F32),
            pltpu.VMEM((groups, 4 * RANK, LANES), F32),
        ],
        compiler_params=limit(60),
        name="gather_moments",
        cost_estimate=pl.CostEstimate(flops=10**9, bytes_accessed=10 * 10**6, transcendentals=0),
    )(k_in, v_in, short_weight, ends)
    pay = exchange(pay)

    query, inner = pl.pallas_call(
        local_kernel,
        grid=(steps,),
        in_specs=[
            columns(tokens),
            columns(2, tokens),
            columns(3, REACH + 1),
            columns(order),
            columns(order),
            columns(1),
            whole(local),
        ],
        out_specs=[columns(tokens)] * 2,
        out_shape=[jax.ShapeDtypeStruct((tokens, width), F32)] * 2,
        scratch_shapes=[pltpu.VMEM((groups, 2 * (STRETCH + 8), LANES), F32)],
        compiler_params=limit(40),
        name="local_filter",
        cost_estimate=pl.CostEstimate(flops=10**9, bytes_accessed=20 * 10**6, transcendentals=0),
    )(q_in, mixed, short_weight, rates, residues, skip, local)
    raw, query, inner = lax.optimization_barrier((raw, query, inner))

    groups = lanes // LANES
    heads, first = pl.pallas_call(
        heads_kernel,
        grid_spec=pltpu.PrefetchScalarGridSpec(
            num_scalar_prefetch=2,
            grid=(1,),
            in_specs=[full(n_ctx, 2 * RAW, lanes), own(3, REACH + 1), own(order), own(order), own(1)],
            out_specs=[full(groups, slots, 16, LANES), full(groups, slots, order, LANES)],
            scratch_shapes=[
                pltpu.VMEM((groups, 2 * RAW, LANES), F32),
                pltpu.VMEM((3, groups, slots + 1, 16, LANES), F32),
                pltpu.VMEM((groups, slots, 16, LANES), F32),
            ],
        ),
        out_shape=[
            jax.ShapeDtypeStruct((groups, slots, 16, LANES), F32),
            jax.ShapeDtypeStruct((groups, slots, order, LANES), F32),
        ],
        compiler_params=limit(32),
        name="head_tokens",
    )(me, stretch_of_slot, raw, *mine)

    back = pl.pallas_call(
        states_kernel,
        grid_spec=pltpu.PrefetchScalarGridSpec(
            num_scalar_prefetch=2,
            grid=(1,),
            in_specs=[
                full(n_ctx, 4 * RANK, lanes),
                full(groups, slots, 16, LANES),
                full(groups, slots, order, LANES),
                own(order),
                own(order),
            ],
            out_specs=full(n_ctx, 2 * BACK, lanes),
            scratch_shapes=[
                pltpu.VMEM((groups, 4 * RANK, LANES), F32),
                pltpu.VMEM((groups, slots, 8, LANES), F32),
                pltpu.VMEM((groups, slots, order, LANES), F32),
                pltpu.VMEM((groups, slots, order, LANES), F32),
                pltpu.VMEM((groups, slots, order, LANES), F32),
                pltpu.VMEM((groups, slots, 16, LANES), F32),
                pltpu.VMEM((groups, slots, BACK, LANES), F32),
            ],
        ),
        out_shape=jax.ShapeDtypeStruct((n_ctx, 2 * BACK, lanes), BF16),
        compiler_params=limit(32),
        name="carry_states",
    )(me, stretch_of_slot, pay, heads, first, mine[1], mine[2])
    if not direct:
        back = back[:, :, :share]
    back = lax.all_to_all(back, "ctx", 0, 0, tiled=True)
    if not direct:
        back = back.transpose(1, 0, 2).reshape(2 * BACK, width)

    _, back_spec = payload(2 * BACK)
    zvalues, squares = pl.pallas_call(
        join_kernel,
        grid=(steps,),
        in_specs=[back_spec, whole(lift), columns(tokens), columns(tokens)],
        out_specs=[columns(tokens), pl.BlockSpec((1, tokens), lambda c: (0, 0))],
        out_shape=[
            jax.ShapeDtypeStruct((tokens, width), F32),
            jax.ShapeDtypeStruct((1, tokens), F32),
        ],
        scratch_shapes=[pltpu.VMEM((tokens, LANES), F32)],
        compiler_params=limit(32),
        name="join_carry",
    )(back, lift, query, inner)
    total = squares
    for shift in range(1, n_ch):
        total = total + lax.ppermute(squares, "ch", [(i, (i + shift) % n_ch) for i in range(n_ch)])
    scale = lax.rsqrt(total / (width * n_ch) + 1e-05)
    return (zvalues * scale.reshape(tokens, 1) * gain).astype(BF16)


def solution(mesh):
    sizes = (mesh.shape["ctx"], mesh.shape["ch"])
    in_specs = (
        P("ctx", "ch"),
        P("ctx", "ch"),
        P("ctx", "ch"),
        P(),
        P(None, None, "ch"),
        P(None, "ch"),
        P(None, "ch"),
        P("ch"),
        P("ch"),
    )

    def run(*arrays):
        return on_device(sizes, *arrays)

    return jax.shard_map(run, mesh=mesh, in_specs=in_specs, out_specs=P("ctx", "ch"), check_vma=False)
```

```python
import functools
from decimal import Decimal, getcontext

import jax
import jax.numpy as jnp
import ml_dtypes
import numpy as np
from jax import lax
from jax.experimental import pallas as pl
from jax.experimental.pallas import tpu as pltpu
from jax.sharding import PartitionSpec as P

F32, BF16 = jnp.float32, jnp.bfloat16
LANES = 128
STRETCH = 64
REACH = 6
INNER = STRETCH - REACH
NODES = (1, 8, 21, 36, 49, 56)
ANCHORS = ("0.000511", "0.004393", "0.011118", "0.018882", "0.025607", "0.029489")
RANK = len(NODES)
RAW = 6 * REACH
BACK = 2 * REACH + 2 * RANK


def cardinal_table():
    getcontext().prec = 50
    anchors = [Decimal(a) for a in ANCHORS]
    table = [[(-a * n).exp() for n in NODES] for a in anchors]
    right = [[(-a * d).exp() for d in range(INNER)] for a in anchors]
    for col in range(RANK):
        pivot = max(range(col, RANK), key=lambda row: abs(table[row][col]))
        table[col], table[pivot] = table[pivot], table[col]
        right[col], right[pivot] = right[pivot], right[col]
        for row in range(RANK):
            if row != col:
                factor = table[row][col] / table[col][col]
                table[row] = [x - factor * y for x, y in zip(table[row], table[col])]
                right[row] = [x - factor * y for x, y in zip(right[row], right[col])]
    return np.array([[float(x / table[j][j]) for x in right[j]] for j in range(RANK)], np.float32)


def halves(values):
    high = values.astype(ml_dtypes.bfloat16)
    low = (values - high.astype(np.float32)).astype(ml_dtypes.bfloat16)
    return high, low


def constant_matrices():
    cardinal = cardinal_table()
    ends = np.zeros((16, STRETCH), np.float32)
    local = np.zeros((RANK, STRETCH, STRETCH), np.float32)
    lift = np.zeros((2, 2 * STRETCH, 2 * BACK), np.float32)
    high, low = (h.astype(np.float32) for h in halves(cardinal))
    for j in range(RANK):
        for s in range(REACH, STRETCH):
            ends[j, s] = cardinal[j, STRETCH - 1 - s]
            local[j, s:, s] = cardinal[j, : STRETCH - s]
        for half in range(2):
            rows = slice(half * STRETCH + REACH, (half + 1) * STRETCH)
            at = half * BACK + 2 * REACH
            lift[0, rows, at + j] = high[j]
            lift[0, rows, at + RANK + j] = high[j]
            lift[1, rows, at + j] = low[j]
    for half in range(2):
        for t in range(REACH):
            lift[0, half * STRETCH + t, half * BACK + t] = 1.0
            lift[0, half * STRETCH + t, half * BACK + REACH + t] = 1.0
    local = local.reshape(RANK * STRETCH, STRETCH)

    def triple(m):
        h, l = halves(m)
        return np.concatenate([h, h, l], axis=1)

    lifted = np.concatenate([lift[0], lift[1]], axis=1).astype(ml_dtypes.bfloat16)
    return triple(ends), triple(local), lifted


def split(values):
    high = values.astype(BF16)
    return high, (values - high.astype(F32)).astype(BF16)


def amplitude(rate, residue):
    x = 2.0 * rate
    series = 1.0 - x * (0.5 - x * (1 / 6 - x * (1 / 24 - x * (1 / 120 - x * (1 / 720)))))
    return residue * jnp.sqrt(x * series)


def put(ref, group, values):
    if len(ref.shape) == 3:
        share = ref.shape[2]
        dest, at = divmod(group * LANES, share)
        ref[dest, :, at : at + LANES] = values
    else:
        ref[:, group * LANES : (group + 1) * LANES] = values


EDGES = (0, STRETCH - 16, STRETCH, 2 * STRETCH - 16)


def raw_kernel(q_ref, k_ref, v_ref, out_ref, held, rows, pay, sems):
    chunks = sems.shape[0]
    wide = q_ref.shape[1] // chunks

    def copies(c):
        cols = pl.ds(c * wide, wide)
        return [
            pltpu.make_async_copy(ref.at[pl.ds(at, 16), cols], held.at[4 * a + e, :, cols], sems.at[c, 4 * a + e])
            for a, ref in enumerate((q_ref, k_ref, v_ref))
            for e, at in enumerate(EDGES)
        ]

    for c in range(chunks):
        for copy in copies(c):
            copy.start()
    for c in range(chunks):
        for copy in copies(c):
            copy.wait()
        for g in range(c * wide // LANES, (c + 1) * wide // LANES):
            cols = slice(g * LANES, (g + 1) * LANES)
            for a in range(3):
                for i in range(2):
                    for e in range(2):
                        rows[g, 2 * a + i, 16 * e : 16 * e + 16, :] = held[4 * a + 2 * i + e, :, cols].astype(F32)
                    at = i * RAW + a * REACH
                    pay[g, at : at + REACH, :] = rows[g, 2 * a + i, 32 - REACH : 32, :]
                    at = at + 3 * REACH
                    pay[g, at : at + REACH, :] = rows[g, 2 * a + i, 0:REACH, :]
            put(out_ref, g, pay[g].astype(BF16))


def gather_kernel(*refs, pieces, direct):
    me_ref, k_ref, v_ref, taps_ref, ends_ref = refs[:5]
    refs = refs[5:]
    weights, refs = (refs[:4], refs[4:]) if direct else ((), refs)
    u_ref, pay_refs, refs = refs[0], refs[1 : 1 + pieces], refs[1 + pieces :]
    kept, refs = (refs[:4], refs[4:]) if direct else ((), refs)
    held, taps_vm, xs, pay, sems, tap_sem, own_sems = refs
    width = k_ref.shape[1]
    span = 2 * LANES
    blocks = width // span

    def copies(c):
        cols = pl.ds(pl.multiple_of(c * span, span), span)
        return [
            pltpu.make_async_copy(ref.at[:, cols], held.at[a, :, cols], sems.at[a, c])
            for a, ref in enumerate((k_ref, v_ref))
        ]

    def own_copies():
        share = kept[0].shape[-1]
        cols = pl.ds(pl.multiple_of(me_ref[0] * share, share), share)
        views = (weights[0].at[:, :, cols], weights[1].at[:, cols], weights[2].at[:, cols], weights[3].at[:, cols])
        return [pltpu.make_async_copy(view, ref, own_sems.at[n]) for n, (view, ref) in enumerate(zip(views, kept))]

    tap_copy = pltpu.make_async_copy(taps_ref, taps_vm, tap_sem.at[0])
    tap_copy.start()

    def begin(c, carry):
        for copy in copies(c):
            copy.start()
        return carry

    lax.fori_loop(0, blocks, begin, 0)
    if direct:
        for copy in own_copies():
            copy.start()
    for a in range(2):
        for h in range(2):
            for i in range(2):
                at = i * (STRETCH + 8)
                xs[a, h, at : at + 8, :] = jnp.zeros((8, LANES), F32)
    tap_copy.wait()

    def features(c, carry):
        for copy in copies(c):
            copy.wait()
        for h in range(2):
            cols = pl.ds(pl.multiple_of(c * span + h * LANES, LANES), LANES)
            for a in range(2):
                for i in range(2):
                    base = i * (STRETCH + 8) + 8
                    xs[a, h, base : base + STRETCH, :] = held[a, i * STRETCH : (i + 1) * STRETCH, cols].astype(F32)
            taps = [[taps_vm[a, j : j + 1, cols] for j in range(REACH + 1)] for a in (1, 2)]
            for i in range(2):
                for b in range(STRETCH // 16):
                    base = i * (STRETCH + 8) + 8 + 16 * b
                    both = []
                    for a in range(2):
                        total = taps[a][0] * xs[a, h, base : base + 16, :]
                        for j in range(1, REACH + 1):
                            total = total + taps[a][j] * xs[a, h, base - j : base - j + 16, :]
                        both.append(total)
                    mixed = both[0] * both[1]
                    if b == 0:
                        row = lax.broadcasted_iota(jnp.int32, (16, LANES), 0)
                        mixed = jnp.where(row >= REACH, mixed, 0.0)
                    high, low = split(mixed)
                    rows = slice(i * STRETCH + 16 * b, i * STRETCH + 16 * b + 16)
                    u_ref[0, rows, cols] = high
                    u_ref[1, rows, cols] = low
        return carry

    lax.fori_loop(0, blocks, features, 0)
    for c in range(blocks):
        cols = slice(c * span, (c + 1) * span)
        for i in range(2):
            rows = slice(i * STRETCH, (i + 1) * STRETCH)
            high, low = u_ref[0, rows, cols], u_ref[1, rows, cols]
            moments = jnp.dot(
                ends_ref[...], jnp.concatenate([high, low, high], axis=0), preferred_element_type=F32
            )
            top, rest = split(moments)
            at = 2 * RANK * i
            for h in range(2):
                lanes = slice(h * LANES, (h + 1) * LANES)
                pay[2 * c + h, at : at + RANK, :] = top.astype(F32)[:RANK, lanes]
                pay[2 * c + h, at + RANK : at + 2 * RANK, :] = rest.astype(F32)[:RANK, lanes]
    if direct:
        share = kept[0].shape[-1]
        per = share // LANES
        for s in range(pieces):
            dest = lax.rem(me_ref[0] + s, pieces)
            for h in range(per):
                pay_refs[s][:, h * LANES : (h + 1) * LANES] = pay[per * dest + h].astype(BF16)
        for copy in own_copies():
            copy.wait()
    else:
        for g in range(width // LANES):
            pay_refs[0][:, g * LANES : (g + 1) * LANES] = pay[g].astype(BF16)


def local_kernel(q_ref, u_ref, taps_ref, rates_ref, res_ref, skip_ref, local_ref, qc_ref, y_ref, xs):
    tile = q_ref.shape[1]
    for g in range(tile // LANES):
        cols = slice(g * LANES, (g + 1) * LANES)
        taps = [taps_ref[0, j : j + 1, cols] for j in range(REACH + 1)]
        for i in range(2):
            base = i * (STRETCH + 8) + 8
            xs[g, base - 8 : base, :] = jnp.zeros((8, LANES), F32)
            xs[g, base : base + STRETCH, :] = q_ref[i * STRETCH : (i + 1) * STRETCH, cols].astype(F32)
            for b in range(STRETCH // 8):
                at = base + 8 * b
                total = taps[0] * xs[g, at : at + 8, :]
                for j in range(1, REACH + 1):
                    total = total + taps[j] * xs[g, at - j : at - j + 8, :]
                if b == 0:
                    row = lax.broadcasted_iota(jnp.int32, (8, LANES), 0)
                    total = jnp.where(row >= REACH, total, 1.0)
                qc_ref[i * STRETCH + 8 * b : i * STRETCH + 8 * b + 8, cols] = total
    span = min(tile, 2 * LANES)
    for c in range(tile // span):
        cols = slice(c * span, (c + 1) * span)
        rate = rates_ref[:, cols]
        amount = amplitude(rate, res_ref[:, cols])
        weights = [jnp.sum(amount * jnp.exp(-rate * float(n)), axis=0, keepdims=True) for n in NODES]
        for i in range(2):
            rows = slice(i * STRETCH, (i + 1) * STRETCH)
            high, low = u_ref[0, rows, cols], u_ref[1, rows, cols]
            parts = jnp.dot(
                local_ref[...], jnp.concatenate([high, low, high], axis=0), preferred_element_type=F32
            )
            total = skip_ref[:, cols] * (high.astype(F32) + low.astype(F32))
            for j in range(RANK):
                total = total + weights[j] * parts[j * STRETCH : (j + 1) * STRETCH, :]
            y_ref[rows, cols] = total


def heads_kernel(
    perm_ref, x_ref, taps_ref, rates_ref, res_ref, skip_ref, heads_ref, first_ref, raw, ext, past
):
    slots = perm_ref.shape[0]
    groups = x_ref.shape[2] // LANES
    ext[:, :, 0, :, :] = jnp.zeros((3, groups, 16, LANES), F32)
    ext[:, :, :, 8:16, :] = jnp.zeros((3, groups, slots + 1, 8, LANES), F32)
    past[:, :, 0:8, :] = jnp.zeros((groups, slots, 8, LANES), F32)

    def unpack(src, carry):
        for g in range(groups):
            raw[g] = x_ref[src, :, g * LANES : (g + 1) * LANES].astype(F32)
        for i in range(2):
            n = perm_ref[2 * src + i]
            for g in range(groups):
                for a in range(3):
                    at = i * RAW + a * REACH
                    ext[a, g, n + 1, 0:REACH, :] = raw[g, at : at + REACH, :]
                    at = at + 3 * REACH
                    ext[a, g, n, REACH : 2 * REACH, :] = raw[g, at : at + REACH, :]
        return carry

    lax.fori_loop(0, slots // 2, unpack, 0)
    row = lax.broadcasted_iota(jnp.int32, (8, LANES), 0)

    for g in range(groups):
        cols = slice(g * LANES, (g + 1) * LANES)
        rate = rates_ref[:, cols]
        amount = amplitude(rate, res_ref[:, cols])
        enter = [jnp.exp(-rate * float(REACH - 1 - s)) for s in range(REACH)]
        taps = [[taps_ref[a, j : j + 1, cols] for j in range(REACH + 1)] for a in range(3)]
        near = [jnp.sum(amount * jnp.exp(-rate * float(d)), axis=0, keepdims=True) for d in range(REACH)]
        near[0] = near[0] + skip_ref[:, cols]

        def head_pass(n, carry, g=g, taps=taps, enter=enter, near=near):
            feats = []
            for a in range(3):
                total = taps[a][0] * ext[a, g, n, REACH : REACH + 8, :]
                for j in range(1, REACH + 1):
                    total = total + taps[a][j] * ext[a, g, n, REACH - j : REACH - j + 8, :]
                feats.append(jnp.where(row < REACH, total, 0.0))
            mixed = feats[1] * feats[2]
            past[g, n, 8:16, :] = mixed
            total = near[0] * mixed
            for d in range(1, REACH):
                total = total + near[d] * past[g, n, 8 - d : 16 - d, :]
            heads_ref[g, n, 0:8, :] = feats[0]
            heads_ref[g, n, 8:16, :] = total
            first = enter[0] * mixed[0:1, :]
            for s in range(1, REACH):
                first = first + enter[s] * mixed[s : s + 1, :]
            first_ref[g, n] = first
            return carry

        lax.fori_loop(0, slots, head_pass, 0, unroll=2)


def states_kernel(me_ref, perm_ref, *refs, pieces):
    xs, refs = refs[:pieces], refs[pieces:]
    heads_ref, first_ref, rates_ref, res_ref, out_ref = refs[:5]
    raw, moments, second, states, mids, carried, result = refs[5:]
    slots = perm_ref.shape[0]
    groups = rates_ref.shape[1] // LANES

    def place(src, values):
        for g in range(groups):
            raw[g] = values(g).astype(F32)
        for i in range(2):
            n = perm_ref[2 * src + i]
            for g in range(groups):
                at = 2 * RANK * i
                moments[g, n, 0:RANK, :] = raw[g, at : at + RANK, :] + raw[g, at + RANK : at + 2 * RANK, :]

    if pieces > 1:
        for s in range(pieces):
            src = lax.rem(me_ref[0] + (pieces - s), pieces)
            place(src, lambda g, s=s: xs[s][:, g * LANES : (g + 1) * LANES])
    else:

        def unpack(src, carry):
            place(src, lambda g: xs[0][src, :, g * LANES : (g + 1) * LANES])
            return carry

        lax.fori_loop(0, slots // 2, unpack, 0)

    rate = [rates_ref[:, g * LANES : (g + 1) * LANES] for g in range(groups)]
    amount = [amplitude(rate[g], res_ref[:, g * LANES : (g + 1) * LANES]) for g in range(groups)]
    for g in range(groups):
        gather = [jnp.exp(-rate[g] * float(n)) for n in NODES]

        def rest_pass(n, carry, g=g, gather=gather):
            total = gather[0] * moments[g, n, 0:1, :]
            for j in range(1, RANK):
                total = total + gather[j] * moments[g, n, j : j + 1, :]
            second[g, n] = total
            return carry

        lax.fori_loop(0, slots, rest_pass, 0, unroll=4)

    fade_head = [jnp.exp(-rate[g] * float(REACH)) for g in range(groups)]
    fade_rest = [jnp.exp(-rate[g] * float(INNER)) for g in range(groups)]

    def scan_pass(n, state):
        after = []
        for g in range(groups):
            states[g, n] = state[g]
            mid = fade_head[g] * state[g] + first_ref[g, n]
            mids[g, n] = mid
            after.append(fade_rest[g] * mid + second[g, n])
        return tuple(after)

    lax.fori_loop(0, slots, scan_pass, tuple(jnp.zeros((16, LANES), F32) for _ in range(groups)), unroll=4)

    for g in range(groups):
        lifts = [amount[g] * jnp.exp(-rate[g] * float(t + 1)) for t in range(REACH)]
        spread = [amount[g] * jnp.exp(-rate[g] * float(n + 1)) for n in NODES]

        def out_pass(n, carry, g=g, lifts=lifts, spread=spread):
            state, mid = states[g, n], mids[g, n]
            for t in range(REACH):
                carried[g, n, t : 1 + t, :] = jnp.sum(lifts[t] * state, axis=0, keepdims=True)
                carried[g, n, 8 + t : 9 + t, :] = jnp.sum(spread[t] * mid, axis=0, keepdims=True)
            z = heads_ref[g, n, 0:8, :] * (heads_ref[g, n, 8:16, :] + carried[g, n, 0:8, :])
            high, low = split(z)
            result[g, n, 0:REACH, :] = high.astype(F32)[:REACH]
            result[g, n, REACH : 2 * REACH, :] = low.astype(F32)[:REACH]
            high, low = split(carried[g, n, 8:16, :])
            result[g, n, 2 * REACH : 2 * REACH + RANK, :] = high.astype(F32)[:RANK]
            result[g, n, 2 * REACH + RANK : BACK, :] = low.astype(F32)[:RANK]
            return carry

        lax.fori_loop(0, slots, out_pass, 0, unroll=2)

    def pack(src, carry):
        for g in range(groups):
            both = [result[g, perm_ref[2 * src + i], :, :] for i in range(2)]
            out_ref[src, :, g * LANES : (g + 1) * LANES] = jnp.concatenate(both, axis=0).astype(BF16)
        return carry

    lax.fori_loop(0, slots // 2, pack, 0)


def join_kernel(back_ref, lift_ref, qc_ref, y_ref, z_ref, sq_ref, total):
    step = pl.program_id(0)
    part = jnp.zeros(total.shape, F32)
    by_dest = len(back_ref.shape) == 3
    span = back_ref.shape[-1] if by_dest else 2 * LANES
    for c in range(qc_ref.shape[1] // span):
        cols = slice(c * span, (c + 1) * span)
        back = back_ref[c] if by_dest else back_ref[:, cols]
        carry = jnp.dot(lift_ref[...], jnp.concatenate([back, back], axis=0), preferred_element_type=F32)
        z = qc_ref[:, cols] * (y_ref[:, cols] + carry)
        z_ref[:, cols] = z
        squares = z * z
        for g in range(span // LANES):
            part = part + squares[:, g * LANES : (g + 1) * LANES]

    @pl.when(step == 0)
    def _():
        total[...] = part

    @pl.when(step > 0)
    def _():
        total[...] += part

    @pl.when(step == pl.num_programs(0) - 1)
    def _():
        sq_ref[...] = jnp.sum(total[...].T, axis=0, keepdims=True)


def limit(mib):
    return pltpu.CompilerParams(vmem_limit_bytes=mib * 1024 * 1024)


def on_device(sizes, q_in, k_in, v_in, stretch_of_slot, short_weight, rates, residues, skip, gain):
    n_ctx, n_ch = sizes
    tokens, width = q_in.shape
    slots = stretch_of_slot.shape[0]
    order = rates.shape[0]
    share = width // n_ctx
    direct = share % LANES == 0
    tile = min(width, 1024)
    steps = width // tile
    groups = tile // LANES
    ends_np, local_np, lift_np = constant_matrices()
    ends, local, lift = jnp.asarray(ends_np), jnp.asarray(local_np), jnp.asarray(lift_np)
    skip, gain = skip.reshape(1, width), gain.reshape(1, width)
    me = lax.axis_index("ctx").astype(jnp.int32).reshape(1)

    def whole(array):
        return pl.BlockSpec(array.shape, lambda c: (0,) * array.ndim)

    def columns(*lead):
        return pl.BlockSpec((*lead, tile), lambda c: (0,) * len(lead) + (c,))

    def payload(rows):
        if direct:
            return (
                jax.ShapeDtypeStruct((n_ctx, rows, share), BF16),
                pl.BlockSpec((tile // share, rows, share), lambda c: (c, 0, 0)),
            )
        return jax.ShapeDtypeStruct((rows, width), BF16), columns(rows)

    def exchange(array):
        if direct:
            return lax.all_to_all(array, "ctx", 0, 0, tiled=True)
        array = array.reshape(array.shape[0], n_ctx, share).transpose(1, 0, 2)
        return widen(lax.all_to_all(array, "ctx", 0, 0, tiled=True))

    lanes = -(-share // LANES) * LANES

    def widen(array, fill=0.0):
        pad = [(0, 0)] * (array.ndim - 1) + [(0, lanes - share)]
        return jnp.pad(array, pad, constant_values=fill)

    def cut(array, fill=0.0):
        return widen(lax.dynamic_slice_in_dim(array, lax.axis_index("ctx") * share, share, array.ndim - 1), fill)

    smem = pl.BlockSpec(memory_space=pltpu.SMEM)
    vmem = pl.BlockSpec(memory_space=pltpu.VMEM)
    hbm = pl.BlockSpec(memory_space=pltpu.HBM)
    f32 = lambda *shape: jax.ShapeDtypeStruct(shape, F32)

    pin = lambda array: pltpu.with_memory_space_constraint(array, pltpu.HBM)
    raw_shape, _ = payload(2 * RAW)
    all_groups = width // LANES
    chunks = 2
    raw = pl.pallas_call(
        raw_kernel,
        in_specs=[hbm] * 3,
        out_specs=vmem,
        out_shape=raw_shape,
        scratch_shapes=[
            pltpu.VMEM((12, 16, width), BF16),
            pltpu.VMEM((all_groups, 6, 32, LANES), F32),
            pltpu.VMEM((all_groups, 2 * RAW, LANES), F32),
            pltpu.SemaphoreType.DMA((chunks, 12)),
        ],
        compiler_params=limit(24),
        name="edge_rows",
    )(pin(q_in), pin(k_in), pin(v_in))
    raw, after_raw = lax.optimization_barrier((raw, me))
    raw = exchange(raw)

    pieces = n_ctx if direct else 1
    pay_shape = jax.ShapeDtypeStruct((4 * RANK, share if direct else width), BF16)
    weights = (short_weight, rates, residues, skip)
    own = [f32(*w.shape[:-1], share) for w in weights] if direct else []
    blocks = width // (2 * LANES)
    outs = pl.pallas_call(
        functools.partial(gather_kernel, pieces=pieces, direct=direct),
        in_specs=[smem] + [hbm] * 3 + [vmem] + [hbm] * len(own),
        out_specs=[vmem] * (1 + pieces + len(own)),
        out_shape=[jax.ShapeDtypeStruct((2, tokens, width), BF16)] + [pay_shape] * pieces + own,
        scratch_shapes=[
            pltpu.VMEM((2, tokens, width), BF16),
            pltpu.VMEM(short_weight.shape, F32),
            pltpu.VMEM((2, 2, 2 * (STRETCH + 8), LANES), F32),
            pltpu.VMEM((all_groups, 4 * RANK, LANES), F32),
            pltpu.SemaphoreType.DMA((2, blocks)),
            pltpu.SemaphoreType.DMA((1,)),
            pltpu.SemaphoreType.DMA((4,)),
        ],
        compiler_params=limit(24),
        name="gather_moments",
        cost_estimate=pl.CostEstimate(flops=10**9, bytes_accessed=10 * 10**6, transcendentals=0),
    )(after_raw, pin(k_in), pin(v_in), pin(short_weight), ends, *(map(pin, weights) if direct else ()))
    mixed = outs[0]
    if direct:
        mine = outs[1 + pieces :]
        pays = [outs[1]]
        for shift in range(1, n_ctx):
            pays.append(lax.ppermute(outs[1 + shift], "ctx", [(i, (i + shift) % n_ctx) for i in range(n_ctx)]))
    else:
        mine = (cut(short_weight), cut(rates, 0.01), cut(residues), cut(skip))
        pays = [exchange(outs[1])]

    query, inner = pl.pallas_call(
        local_kernel,
        grid=(steps,),
        in_specs=[
            columns(tokens),
            columns(2, tokens),
            columns(3, REACH + 1),
            columns(order),
            columns(order),
            columns(1),
            whole(local),
        ],
        out_specs=[columns(tokens)] * 2,
        out_shape=[f32(tokens, width)] * 2,
        scratch_shapes=[pltpu.VMEM((groups, 2 * (STRETCH + 8), LANES), F32)],
        compiler_params=limit(24),
        name="local_filter",
        cost_estimate=pl.CostEstimate(flops=10**9, bytes_accessed=20 * 10**6, transcendentals=0),
    )(q_in, mixed, short_weight, rates, residues, skip, local)

    groups = lanes // LANES
    heads, first = pl.pallas_call(
        heads_kernel,
        in_specs=[smem] + [vmem] * 5,
        out_specs=[vmem] * 2,
        scratch_shapes=[
            pltpu.VMEM((groups, 2 * RAW, LANES), F32),
            pltpu.VMEM((3, groups, slots + 1, 16, LANES), F32),
            pltpu.VMEM((groups, slots, 16, LANES), F32),
        ],
        out_shape=[f32(groups, slots, 16, LANES), f32(groups, slots, order, LANES)],
        compiler_params=limit(24),
        name="head_tokens",
    )(stretch_of_slot, raw, *mine)

    back = pl.pallas_call(
        functools.partial(states_kernel, pieces=pieces),
        in_specs=[smem] * 2 + [vmem] * (pieces + 4),
        out_specs=vmem,
        scratch_shapes=[
            pltpu.VMEM((groups, 4 * RANK, LANES), F32),
            pltpu.VMEM((groups, slots, 8, LANES), F32),
            pltpu.VMEM((groups, slots, order, LANES), F32),
            pltpu.VMEM((groups, slots, order, LANES), F32),
            pltpu.VMEM((groups, slots, order, LANES), F32),
            pltpu.VMEM((groups, slots, 16, LANES), F32),
            pltpu.VMEM((groups, slots, BACK, LANES), F32),
        ],
        out_shape=jax.ShapeDtypeStruct((n_ctx, 2 * BACK, lanes), BF16),
        compiler_params=limit(24),
        name="carry_states",
    )(me, stretch_of_slot, *pays, heads, first, mine[1], mine[2])
    if not direct:
        back = back[:, :, :share]
    back = lax.all_to_all(back, "ctx", 0, 0, tiled=True)
    if not direct:
        back = back.transpose(1, 0, 2).reshape(2 * BACK, width)

    _, back_spec = payload(2 * BACK)
    zvalues, squares = pl.pallas_call(
        join_kernel,
        grid=(steps,),
        in_specs=[back_spec, whole(lift), columns(tokens), columns(tokens)],
        out_specs=[columns(tokens), pl.BlockSpec((1, tokens), lambda c: (0, 0))],
        out_shape=[
            jax.ShapeDtypeStruct((tokens, width), F32),
            jax.ShapeDtypeStruct((1, tokens), F32),
        ],
        scratch_shapes=[pltpu.VMEM((tokens, LANES), F32)],
        compiler_params=limit(24),
        name="join_carry",
    )(back, lift, query, inner)
    total = squares
    for shift in range(1, n_ch):
        total = total + lax.ppermute(squares, "ch", [(i, (i + shift) % n_ch) for i in range(n_ch)])
    scale = lax.rsqrt(total / (width * n_ch) + 1e-05)
    return (zvalues * scale.reshape(tokens, 1) * gain).astype(BF16)


def solution(mesh):
    sizes = (mesh.shape["ctx"], mesh.shape["ch"])
    in_specs = (
        P("ctx", "ch"),
        P("ctx", "ch"),
        P("ctx", "ch"),
        P(),
        P(None, None, "ch"),
        P(None, "ch"),
        P(None, "ch"),
        P("ch"),
        P("ch"),
    )

    def run(*arrays):
        return on_device(sizes, *arrays)

    return jax.shard_map(run, mesh=mesh, in_specs=in_specs, out_specs=P("ctx", "ch"), check_vma=False)
```

```python
import functools
from decimal import Decimal, getcontext

import jax
import jax.numpy as jnp
import ml_dtypes
import numpy as np
from jax import lax
from jax.experimental import pallas as pl
from jax.experimental.pallas import tpu as pltpu
from jax.sharding import PartitionSpec as P

F32, BF16 = jnp.float32, jnp.bfloat16
LANES = 128
SPAN = 256
STRETCH = 64
REACH = 6
INNER = STRETCH - REACH
PIVOTS = (8, 49, 21, 56, 36, 1)
ANCHORS = ("0.0020", "0.0235", "0.0110", "0.0295", "0.0185", "0.0004")
RANK = len(PIVOTS)
FINE = 2
COEFS = RANK + FINE
RAW = 6 * REACH
PIECE = RAW + COEFS
BACK = 2 * REACH + COEFS


def shape_table():
    getcontext().prec = 50
    rest = [[(-Decimal(a) * d).exp() for d in range(INNER)] for a in ANCHORS]
    table = []
    for p in range(RANK):
        shape = [x / rest[p][PIVOTS[p]] for x in rest[p]]
        rest = [[x - row[PIVOTS[p]] * y for x, y in zip(row, shape)] for row in rest]
        table.append([float(x) for x in shape])
    return table


SHAPE = shape_table()


def halves(values):
    high = values.astype(ml_dtypes.bfloat16)
    low = (values - high.astype(np.float32)).astype(ml_dtypes.bfloat16)
    return high, low


def constant_matrices():
    shape = np.array(SHAPE, np.float32)
    ends = np.zeros((16, STRETCH), np.float32)
    local = np.zeros((RANK, STRETCH, STRETCH), np.float32)
    lift = np.zeros((2, 2 * STRETCH, 2 * BACK), np.float32)
    parts = [h.astype(np.float32) for h in halves(shape)]
    for p in range(RANK):
        for s in range(REACH, STRETCH):
            ends[p, s] = shape[p, STRETCH - 1 - s]
            local[p, s:, s] = shape[p, : STRETCH - s]
        for half in range(2):
            rows = slice(half * STRETCH + REACH, (half + 1) * STRETCH)
            at = half * BACK + 2 * REACH
            for k in range(2):
                lift[k, rows, at + p] = parts[k][p]
                if p < FINE:
                    lift[k, rows, at + RANK + p] = parts[k][p]
    for half in range(2):
        for t in range(REACH):
            lift[0, half * STRETCH + t, half * BACK + t] = 1.0
            lift[0, half * STRETCH + t, half * BACK + REACH + t] = 1.0
    local = local.reshape(RANK * STRETCH, STRETCH)

    def triple(m):
        h, l = halves(m)
        return np.concatenate([h, h, l], axis=1)

    return triple(ends), triple(local), lift.astype(ml_dtypes.bfloat16)


def strengths(rate):
    found = []
    for p in range(RANK):
        value = jnp.exp(-rate * float(PIVOTS[p]))
        for q in range(p):
            value = value - found[q] * SHAPE[q][PIVOTS[p]]
        found.append(value)
    return found


def split(values):
    high = values.astype(BF16)
    return high, (values - high.astype(F32)).astype(BF16)


def amplitude(rate, residue):
    x = 2.0 * rate
    series = 1.0 - x * (0.5 - x * (1 / 6 - x * (1 / 24 - x * (1 / 120 - x * (1 / 720)))))
    return residue * jnp.sqrt(x * series)


EDGES = (0, STRETCH - 16, STRETCH, 2 * STRETCH - 16)


def front_kernel(*refs, direct):
    me_ref, q_ref, k_ref, v_ref, taps_ref, ends_ref = refs[:6]
    refs = refs[6:]
    weights, refs = (refs[:4], refs[4:]) if direct else ((), refs)
    pay_ref, u_ref, refs = refs[0], refs[1], refs[2:]
    kept, refs = (refs[:4], refs[4:]) if direct else ((), refs)
    held, edge, taps_vm, xs, qs, pay, packed, u_vm, in_sems, edge_sems, tap_sem, own_sems, out_sems = refs
    blocks = k_ref.shape[1] // SPAN

    def lanes(c):
        return pl.ds(pl.multiple_of(c * SPAN, SPAN), SPAN)

    def loads(c):
        return [
            pltpu.make_async_copy(ref.at[:, lanes(c)], held.at[a, :, lanes(c)], in_sems.at[a, c])
            for a, ref in enumerate((k_ref, v_ref))
        ]

    def edge_loads():
        return [
            pltpu.make_async_copy(q_ref.at[pl.ds(at, 16), :], edge.at[e], edge_sems.at[e])
            for e, at in enumerate(EDGES)
        ]

    def stores(c):
        target = pay_ref.at[c] if direct else pay_ref.at[:, lanes(c)]
        return [
            pltpu.make_async_copy(packed.at[c], target, out_sems.at[0, c]),
            pltpu.make_async_copy(u_vm.at[:, :, lanes(c)], u_ref.at[:, :, lanes(c)], out_sems.at[1, c]),
        ]

    def own_loads():
        share = kept[0].shape[-1]
        cols = pl.ds(pl.multiple_of(me_ref[0] * share, share), share)
        views = (weights[0].at[:, :, cols], weights[1].at[:, cols], weights[2].at[:, cols], weights[3].at[:, cols])
        return [pltpu.make_async_copy(view, ref, own_sems.at[n]) for n, (view, ref) in enumerate(zip(views, kept))]

    tap_copy = pltpu.make_async_copy(taps_ref, taps_vm, tap_sem.at[0])
    tap_copy.start()
    for copy in loads(0) + edge_loads():
        copy.start()

    def begin(c, carry):
        for copy in loads(c):
            copy.start()
        return carry

    lax.fori_loop(1, blocks, begin, 0)
    if direct:
        for copy in own_loads():
            copy.start()
    for parity in range(2):
        for a in range(2):
            for h in range(2):
                for i in range(2):
                    at = i * (STRETCH + 8)
                    xs[parity, a, h, at : at + 8, :] = jnp.zeros((8, LANES), F32)
    tap_copy.wait()

    def features(c):
        for copy in loads(c):
            copy.wait()
        parity = lax.rem(c, 2)
        for h in range(2):
            cols = pl.ds(pl.multiple_of(c * SPAN + h * LANES, LANES), LANES)
            for a in range(2):
                for i in range(2):
                    base = i * (STRETCH + 8) + 8
                    xs[parity, a, h, base : base + STRETCH, :] = held[
                        a, i * STRETCH : (i + 1) * STRETCH, cols
                    ].astype(F32)
            taps = [[taps_vm[a, j : j + 1, cols] for j in range(REACH + 1)] for a in (1, 2)]
            for i in range(2):
                for b in range(STRETCH // 16):
                    base = i * (STRETCH + 8) + 8 + 16 * b
                    both = []
                    for a in range(2):
                        total = taps[a][0] * xs[parity, a, h, base : base + 16, :]
                        for j in range(1, REACH + 1):
                            total = total + taps[a][j] * xs[parity, a, h, base - j : base - j + 16, :]
                        both.append(total)
                    mixed = both[0] * both[1]
                    if b == 0:
                        row = lax.broadcasted_iota(jnp.int32, (16, LANES), 0)
                        mixed = jnp.where(row >= REACH, mixed, 0.0)
                    high, low = split(mixed)
                    rows = slice(i * STRETCH + 16 * b, i * STRETCH + 16 * b + 16)
                    u_vm[0, rows, cols] = high
                    u_vm[1, rows, cols] = low

    def finish(c):
        parity = lax.rem(c, 2)
        for i in range(2):
            rows = slice(i * STRETCH, (i + 1) * STRETCH)
            high, low = u_vm[0, rows, lanes(c)], u_vm[1, rows, lanes(c)]
            moments = jnp.dot(
                ends_ref[...], jnp.concatenate([high, low, high], axis=0), preferred_element_type=F32
            )[:8]
            rest = (moments - moments.astype(BF16).astype(F32))[:FINE]
            at = PIECE * i + RAW
            for h in range(2):
                part = slice(h * LANES, (h + 1) * LANES)
                pay[h, at : at + RANK, :] = moments[:RANK, part]
                pay[h, at + RANK : at + COEFS, :] = rest[:, part]
        for h in range(2):
            cols = pl.ds(pl.multiple_of(c * SPAN + h * LANES, LANES), LANES)
            for i in range(2):
                base = i * (STRETCH + 8) + 8
                qs[h, i, 0:16, :] = edge[2 * i, :, cols].astype(F32)
                qs[h, i, 16:32, :] = edge[2 * i + 1, :, cols].astype(F32)
                at = i * PIECE
                pay[h, at : at + REACH, :] = qs[h, i, 32 - REACH : 32, :]
                pay[h, at + 3 * REACH : at + 4 * REACH, :] = qs[h, i, 0:REACH, :]
                for a in range(2):
                    at = i * PIECE + (1 + a) * REACH
                    pay[h, at : at + REACH, :] = xs[parity, a, h, base + STRETCH - REACH : base + STRETCH, :]
                    at = at + 3 * REACH
                    pay[h, at : at + REACH, :] = xs[parity, a, h, base : base + REACH, :]
            packed[c, :, h * LANES : (h + 1) * LANES] = pay[h].astype(BF16)
        for copy in stores(c):
            copy.start()

    features(0)
    for copy in edge_loads():
        copy.wait()

    def both(c, carry):
        finish(c - 1)
        features(c)
        return carry

    lax.fori_loop(1, blocks, both, 0)
    finish(blocks - 1)

    def end(c, carry):
        for copy in stores(c):
            copy.wait()
        return carry

    lax.fori_loop(0, blocks, end, 0)
    if direct:
        for copy in own_loads():
            copy.wait()


def local_kernel(q_ref, u_ref, taps_ref, rates_ref, res_ref, skip_ref, local_ref, qc_ref, y_ref, xs):
    tile = q_ref.shape[1]
    for g in range(tile // LANES):
        cols = slice(g * LANES, (g + 1) * LANES)
        taps = [taps_ref[0, j : j + 1, cols] for j in range(REACH + 1)]
        for i in range(2):
            base = i * (STRETCH + 8) + 8
            xs[g, base - 8 : base, :] = jnp.zeros((8, LANES), F32)
            xs[g, base : base + STRETCH, :] = q_ref[i * STRETCH : (i + 1) * STRETCH, cols].astype(F32)
            for b in range(STRETCH // 8):
                at = base + 8 * b
                total = taps[0] * xs[g, at : at + 8, :]
                for j in range(1, REACH + 1):
                    total = total + taps[j] * xs[g, at - j : at - j + 8, :]
                if b == 0:
                    row = lax.broadcasted_iota(jnp.int32, (8, LANES), 0)
                    total = jnp.where(row >= REACH, total, 1.0)
                qc_ref[i * STRETCH + 8 * b : i * STRETCH + 8 * b + 8, cols] = total
    span = min(tile, 2 * LANES)
    for c in range(tile // span):
        cols = slice(c * span, (c + 1) * span)
        rate = rates_ref[:, cols]
        amount = amplitude(rate, res_ref[:, cols])
        weights = [jnp.sum(amount * value, axis=0, keepdims=True) for value in strengths(rate)]
        for i in range(2):
            rows = slice(i * STRETCH, (i + 1) * STRETCH)
            high, low = u_ref[0, rows, cols], u_ref[1, rows, cols]
            parts = jnp.dot(
                local_ref[...], jnp.concatenate([high, low, high], axis=0), preferred_element_type=F32
            )
            total = skip_ref[:, cols] * (high.astype(F32) + low.astype(F32))
            for p in range(RANK):
                total = total + weights[p] * parts[p * STRETCH : (p + 1) * STRETCH, :]
            y_ref[rows, cols] = total


def middle_kernel(
    perm_ref, x_ref, taps_ref, rates_ref, res_ref, skip_ref, out_ref,
    raw, ext, moments, past, heads, first, second, states, mids, carried, result, packed, out_sems,
):
    slots = perm_ref.shape[0]
    groups = x_ref.shape[2] // LANES
    ext[:, :, 0, :, :] = jnp.zeros((3, groups, 16, LANES), F32)
    ext[:, :, :, 8:16, :] = jnp.zeros((3, groups, slots + 1, 8, LANES), F32)
    past[:, :, 0:8, :] = jnp.zeros((groups, slots, 8, LANES), F32)

    def unpack(src, carry):
        for g in range(groups):
            raw[g] = x_ref[src, :, g * LANES : (g + 1) * LANES].astype(F32)
        for i in range(2):
            n = perm_ref[2 * src + i]
            for g in range(groups):
                for a in range(3):
                    at = i * PIECE + a * REACH
                    ext[a, g, n + 1, 0:REACH, :] = raw[g, at : at + REACH, :]
                    at = at + 3 * REACH
                    ext[a, g, n, REACH : 2 * REACH, :] = raw[g, at : at + REACH, :]
                at = i * PIECE + RAW
                moments[g, n, 0:RANK, :] = raw[g, at : at + RANK, :]
                moments[g, n, 0:FINE, :] = moments[g, n, 0:FINE, :] + raw[g, at + RANK : at + COEFS, :]
        return carry

    lax.fori_loop(0, slots // 2, unpack, 0)
    row = lax.broadcasted_iota(jnp.int32, (8, LANES), 0)
    rate = [rates_ref[:, g * LANES : (g + 1) * LANES] for g in range(groups)]
    amount = [amplitude(rate[g], res_ref[:, g * LANES : (g + 1) * LANES]) for g in range(groups)]
    basis = [strengths(rate[g]) for g in range(groups)]

    for g in range(groups):
        cols = slice(g * LANES, (g + 1) * LANES)
        enter = [jnp.exp(-rate[g] * float(REACH - 1 - s)) for s in range(REACH)]
        taps = [[taps_ref[a, j : j + 1, cols] for j in range(REACH + 1)] for a in range(3)]
        near = [jnp.sum(amount[g] * jnp.exp(-rate[g] * float(d)), axis=0, keepdims=True) for d in range(REACH)]
        near[0] = near[0] + skip_ref[:, cols]

        def head_pass(n, carry, g=g, taps=taps, enter=enter, near=near):
            feats = []
            for a in range(3):
                total = taps[a][0] * ext[a, g, n, REACH : REACH + 8, :]
                for j in range(1, REACH + 1):
                    total = total + taps[a][j] * ext[a, g, n, REACH - j : REACH - j + 8, :]
                feats.append(jnp.where(row < REACH, total, 0.0))
            mixed = feats[1] * feats[2]
            past[g, n, 8:16, :] = mixed
            total = near[0] * mixed
            for d in range(1, REACH):
                total = total + near[d] * past[g, n, 8 - d : 16 - d, :]
            heads[g, n, 0:8, :] = feats[0]
            heads[g, n, 8:16, :] = total
            value = enter[0] * mixed[0:1, :]
            for s in range(1, REACH):
                value = value + enter[s] * mixed[s : s + 1, :]
            first[g, n] = value
            return carry

        lax.fori_loop(0, slots, head_pass, 0, unroll=2)

        def rest_pass(n, carry, g=g):
            value = basis[g][0] * moments[g, n, 0:1, :]
            for p in range(1, RANK):
                value = value + basis[g][p] * moments[g, n, p : p + 1, :]
            second[g, n] = value
            return carry

        lax.fori_loop(0, slots, rest_pass, 0, unroll=4)

    fade_head = [jnp.exp(-rate[g] * float(REACH)) for g in range(groups)]
    fade_rest = [jnp.exp(-rate[g] * float(INNER)) for g in range(groups)]

    def scan_pass(n, state):
        after = []
        for g in range(groups):
            states[g, n] = state[g]
            mid = fade_head[g] * state[g] + first[g, n]
            mids[g, n] = mid
            after.append(fade_rest[g] * mid + second[g, n])
        return tuple(after)

    lax.fori_loop(0, slots, scan_pass, tuple(jnp.zeros((16, LANES), F32) for _ in range(groups)), unroll=4)

    for g in range(groups):
        lifts = [amount[g] * jnp.exp(-rate[g] * float(t + 1)) for t in range(REACH)]
        next_amount = amount[g] * jnp.exp(-rate[g])
        spread = [next_amount * value for value in basis[g]]

        def out_pass(n, carry, g=g, lifts=lifts, spread=spread):
            state, mid = states[g, n], mids[g, n]
            for t in range(REACH):
                carried[g, n, t : 1 + t, :] = jnp.sum(lifts[t] * state, axis=0, keepdims=True)
                carried[g, n, 8 + t : 9 + t, :] = jnp.sum(spread[t] * mid, axis=0, keepdims=True)
            z = heads[g, n, 0:8, :] * (heads[g, n, 8:16, :] + carried[g, n, 0:8, :])
            high, low = split(z)
            result[g, n, 0:REACH, :] = high.astype(F32)[:REACH]
            result[g, n, REACH : 2 * REACH, :] = low.astype(F32)[:REACH]
            coefs = carried[g, n, 8:16, :]
            result[g, n, 2 * REACH : 2 * REACH + RANK, :] = coefs[:RANK]
            result[g, n, 2 * REACH + RANK : BACK, :] = (coefs - coefs.astype(BF16).astype(F32))[:FINE]
            return carry

        lax.fori_loop(0, slots, out_pass, 0, unroll=2)

    def store(src):
        return pltpu.make_async_copy(packed.at[src], out_ref.at[src], out_sems.at[src])

    def pack(src, carry):
        for g in range(groups):
            for i in range(2):
                raw[g, i * BACK : (i + 1) * BACK, :] = result[g, perm_ref[2 * src + i], 0:BACK, :]
            packed[src, :, g * LANES : (g + 1) * LANES] = raw[g, 0 : 2 * BACK, :].astype(BF16)
        store(src).start()
        return carry

    lax.fori_loop(0, slots // 2, pack, 0)

    def end(src, carry):
        store(src).wait()
        return carry

    lax.fori_loop(0, slots // 2, end, 0)


def join_kernel(back_ref, lift_ref, qc_ref, y_ref, z_ref, sq_ref, total):
    step = pl.program_id(0)
    part = jnp.zeros(total.shape, F32)
    by_dest = len(back_ref.shape) == 3
    span = back_ref.shape[-1] if by_dest else 2 * LANES
    for c in range(qc_ref.shape[1] // span):
        cols = slice(c * span, (c + 1) * span)
        back = back_ref[c] if by_dest else back_ref[:, cols]
        carry = jnp.dot(lift_ref[0], back, preferred_element_type=F32)
        carry = carry + jnp.dot(lift_ref[1], back, preferred_element_type=F32)
        z = qc_ref[:, cols] * (y_ref[:, cols] + carry)
        z_ref[:, cols] = z
        squares = z * z
        for g in range(span // LANES):
            part = part + squares[:, g * LANES : (g + 1) * LANES]

    @pl.when(step == 0)
    def _():
        total[...] = part

    @pl.when(step > 0)
    def _():
        total[...] += part

    @pl.when(step == pl.num_programs(0) - 1)
    def _():
        sq_ref[...] = jnp.sum(total[...].T, axis=0, keepdims=True)


def limit(mib):
    return pltpu.CompilerParams(vmem_limit_bytes=mib * 1024 * 1024)


def on_device(sizes, q_in, k_in, v_in, stretch_of_slot, short_weight, rates, residues, skip, gain):
    n_ctx, n_ch = sizes
    tokens, width = q_in.shape
    slots = stretch_of_slot.shape[0]
    order = rates.shape[0]
    share = width // n_ctx
    direct = share == SPAN
    tile = min(width, 1024)
    steps = width // tile
    groups = tile // LANES
    ends_np, local_np, lift_np = constant_matrices()
    ends, local, lift = jnp.asarray(ends_np), jnp.asarray(local_np), jnp.asarray(lift_np)
    skip, gain = skip.reshape(1, width), gain.reshape(1, width)
    me = lax.axis_index("ctx").astype(jnp.int32).reshape(1)

    def whole(array):
        return pl.BlockSpec(array.shape, lambda c: (0,) * array.ndim)

    def columns(*lead):
        return pl.BlockSpec((*lead, tile), lambda c: (0,) * len(lead) + (c,))

    def payload(rows):
        if direct:
            return (
                jax.ShapeDtypeStruct((n_ctx, rows, share), BF16),
                pl.BlockSpec((tile // share, rows, share), lambda c: (c, 0, 0)),
            )
        return jax.ShapeDtypeStruct((rows, width), BF16), columns(rows)

    def exchange(array):
        if direct:
            return lax.all_to_all(array, "ctx", 0, 0, tiled=True)
        array = array.reshape(array.shape[0], n_ctx, share).transpose(1, 0, 2)
        return widen(lax.all_to_all(array, "ctx", 0, 0, tiled=True))

    lanes = -(-share // LANES) * LANES

    def widen(array, fill=0.0):
        pad = [(0, 0)] * (array.ndim - 1) + [(0, lanes - share)]
        return jnp.pad(array, pad, constant_values=fill)

    def cut(array, fill=0.0):
        return widen(lax.dynamic_slice_in_dim(array, lax.axis_index("ctx") * share, share, array.ndim - 1), fill)

    smem = pl.BlockSpec(memory_space=pltpu.SMEM)
    vmem = pl.BlockSpec(memory_space=pltpu.VMEM)
    hbm = pl.BlockSpec(memory_space=pltpu.HBM)
    f32 = lambda *shape: jax.ShapeDtypeStruct(shape, F32)
    pin = lambda array: pltpu.with_memory_space_constraint(array, pltpu.HBM)

    weights = (short_weight, rates, residues, skip)
    own = [f32(*w.shape[:-1], share) for w in weights] if direct else []
    blocks = width // SPAN
    pay, mixed, *mine = pl.pallas_call(
        functools.partial(front_kernel, direct=direct),
        in_specs=[smem] + [hbm] * 4 + [vmem] + [hbm] * len(own),
        out_specs=[hbm] * 2 + [vmem] * len(own),
        out_shape=[
            pltpu.HBM((n_ctx, 2 * PIECE, share) if direct else (2 * PIECE, width), BF16),
            pltpu.HBM((2, tokens, width), BF16),
        ]
        + own,
        scratch_shapes=[
            pltpu.VMEM((2, tokens, width), BF16),
            pltpu.VMEM((4, 16, width), BF16),
            pltpu.VMEM(short_weight.shape, F32),
            pltpu.VMEM((2, 2, 2, 2 * (STRETCH + 8), LANES), F32),
            pltpu.VMEM((2, 2, 32, LANES), F32),
            pltpu.VMEM((2, 2 * PIECE, LANES), F32),
            pltpu.VMEM((blocks, 2 * PIECE, SPAN), BF16),
            pltpu.VMEM((2, tokens, width), BF16),
            pltpu.SemaphoreType.DMA((2, blocks)),
            pltpu.SemaphoreType.DMA((4,)),
            pltpu.SemaphoreType.DMA((1,)),
            pltpu.SemaphoreType.DMA((4,)),
            pltpu.SemaphoreType.DMA((2, blocks)),
        ],
        compiler_params=limit(24),
        name="front_pieces",
    )(me, *map(pin, (q_in, k_in, v_in, short_weight)), ends, *(map(pin, weights) if direct else ()))
    arrived = exchange(pay)
    if not direct:
        mine = (cut(short_weight), cut(rates, 0.01), cut(residues), cut(skip))

    query, inner = pl.pallas_call(
        local_kernel,
        grid=(steps,),
        in_specs=[
            columns(tokens),
            columns(2, tokens),
            columns(3, REACH + 1),
            columns(order),
            columns(order),
            columns(1),
            whole(local),
        ],
        out_specs=[columns(tokens)] * 2,
        out_shape=[pltpu.HBM((tokens, width), F32)] * 2,
        scratch_shapes=[pltpu.VMEM((groups, 2 * (STRETCH + 8), LANES), F32)],
        compiler_params=limit(24),
        name="local_filter",
        cost_estimate=pl.CostEstimate(flops=10**9, bytes_accessed=20 * 10**6, transcendentals=0),
    )(*map(pin, (q_in, mixed, short_weight, rates, residues)), skip, local)
    arrived, query, inner = lax.optimization_barrier((arrived, query, inner))

    groups = lanes // LANES
    back = pl.pallas_call(
        middle_kernel,
        in_specs=[smem] + [vmem] * 5,
        out_specs=hbm,
        scratch_shapes=[
            pltpu.VMEM((groups, 2 * PIECE, LANES), F32),
            pltpu.VMEM((3, groups, slots + 1, 16, LANES), F32),
            pltpu.VMEM((groups, slots, 8, LANES), F32),
            pltpu.VMEM((groups, slots, 16, LANES), F32),
            pltpu.VMEM((groups, slots, 16, LANES), F32),
            pltpu.VMEM((groups, slots, order, LANES), F32),
            pltpu.VMEM((groups, slots, order, LANES), F32),
            pltpu.VMEM((groups, slots, order, LANES), F32),
            pltpu.VMEM((groups, slots, order, LANES), F32),
            pltpu.VMEM((groups, slots, 16, LANES), F32),
            pltpu.VMEM((groups, slots, 24, LANES), F32),
            pltpu.VMEM((n_ctx, 2 * BACK, lanes), BF16),
            pltpu.SemaphoreType.DMA((n_ctx,)),
        ],
        out_shape=pltpu.HBM((n_ctx, 2 * BACK, lanes), BF16),
        compiler_params=limit(24),
        name="middle_states",
    )(stretch_of_slot, arrived, *mine)
    if not direct:
        back = back[:, :, :share]
    back = lax.all_to_all(back, "ctx", 0, 0, tiled=True)
    if not direct:
        back = back.transpose(1, 0, 2).reshape(2 * BACK, width)

    _, back_spec = payload(2 * BACK)
    zvalues, squares = pl.pallas_call(
        join_kernel,
        grid=(steps,),
        in_specs=[back_spec, whole(lift), columns(tokens), columns(tokens)],
        out_specs=[columns(tokens), pl.BlockSpec((1, tokens), lambda c: (0, 0))],
        out_shape=[
            jax.ShapeDtypeStruct((tokens, width), F32),
            jax.ShapeDtypeStruct((1, tokens), F32),
        ],
        scratch_shapes=[pltpu.VMEM((tokens, LANES), F32)],
        compiler_params=limit(24),
        name="join_carry",
    )(back, lift, pin(query), pin(inner))
    total = squares
    for shift in range(1, n_ch):
        total = total + lax.ppermute(squares, "ch", [(i, (i + shift) % n_ch) for i in range(n_ch)])
    scale = lax.rsqrt(total / (width * n_ch) + 1e-05)
    return (zvalues * scale.reshape(tokens, 1) * gain).astype(BF16)


def solution(mesh):
    sizes = (mesh.shape["ctx"], mesh.shape["ch"])
    in_specs = (
        P("ctx", "ch"),
        P("ctx", "ch"),
        P("ctx", "ch"),
        P(),
        P(None, None, "ch"),
        P(None, "ch"),
        P(None, "ch"),
        P("ch"),
        P("ch"),
    )

    def run(*arrays):
        return on_device(sizes, *arrays)

    return jax.shard_map(run, mesh=mesh, in_specs=in_specs, out_specs=P("ctx", "ch"), check_vma=False)
```

```python
import functools
from decimal import Decimal, getcontext

import jax
import jax.numpy as jnp
import ml_dtypes
import numpy as np
from jax import lax
from jax.experimental import pallas as pl
from jax.experimental.pallas import tpu as pltpu
from jax.sharding import PartitionSpec as P

F32, BF16 = jnp.float32, jnp.bfloat16
LANES = 128
SPAN = 256
STRETCH = 64
REACH = 6
INNER = STRETCH - REACH
PIVOTS = (8, 49, 21, 56, 36, 1)
ANCHORS = ("0.0020", "0.0235", "0.0110", "0.0295", "0.0185", "0.0004")
RANK = len(PIVOTS)
FINE = 2
COEFS = RANK + FINE
RAW = 6 * REACH
PIECE = RAW + COEFS
BACK = 2 * REACH + COEFS


def shape_table():
    getcontext().prec = 50
    rest = [[(-Decimal(a) * d).exp() for d in range(INNER)] for a in ANCHORS]
    table = []
    for p in range(RANK):
        shape = [x / rest[p][PIVOTS[p]] for x in rest[p]]
        rest = [[x - row[PIVOTS[p]] * y for x, y in zip(row, shape)] for row in rest]
        table.append([float(x) for x in shape])
    return table


SHAPE = shape_table()


def halves(values):
    high = values.astype(ml_dtypes.bfloat16)
    low = (values - high.astype(np.float32)).astype(ml_dtypes.bfloat16)
    return high, low


def constant_matrices():
    shape = np.array(SHAPE, np.float32)
    ends = np.zeros((16, STRETCH), np.float32)
    local = np.zeros((RANK, STRETCH, STRETCH), np.float32)
    lift = np.zeros((2, 2 * STRETCH, 2 * BACK), np.float32)
    parts = [h.astype(np.float32) for h in halves(shape)]
    for p in range(RANK):
        for s in range(REACH, STRETCH):
            ends[p, s] = shape[p, STRETCH - 1 - s]
            local[p, s:, s] = shape[p, : STRETCH - s]
        for half in range(2):
            rows = slice(half * STRETCH + REACH, (half + 1) * STRETCH)
            at = half * BACK + 2 * REACH
            for k in range(2):
                lift[k, rows, at + p] = parts[k][p]
                if p < FINE:
                    lift[k, rows, at + RANK + p] = parts[k][p]
    for half in range(2):
        for t in range(REACH):
            lift[0, half * STRETCH + t, half * BACK + t] = 1.0
            lift[0, half * STRETCH + t, half * BACK + REACH + t] = 1.0
    local = local.reshape(RANK * STRETCH, STRETCH)

    def triple(m):
        h, l = halves(m)
        return np.concatenate([h, h, l], axis=1)

    return triple(ends), triple(local), lift.astype(ml_dtypes.bfloat16)


def strengths(rate):
    found = []
    for p in range(RANK):
        value = jnp.exp(-rate * float(PIVOTS[p]))
        for q in range(p):
            value = value - found[q] * SHAPE[q][PIVOTS[p]]
        found.append(value)
    return found


def split(values):
    high = values.astype(BF16)
    return high, (values - high.astype(F32)).astype(BF16)


def amplitude(rate, residue):
    x = 2.0 * rate
    series = 1.0 - x * (0.5 - x * (1 / 6 - x * (1 / 24 - x * (1 / 120 - x * (1 / 720)))))
    return residue * jnp.sqrt(x * series)


EDGES = (0, STRETCH - 16, STRETCH, 2 * STRETCH - 16)


def front_kernel(*refs, direct):
    me_ref, q_ref, k_ref, v_ref, taps_ref, ends_ref = refs[:6]
    refs = refs[6:]
    weights, refs = (refs[:4], refs[4:]) if direct else ((), refs)
    pay_ref, u_ref, refs = refs[0], refs[1], refs[2:]
    kept, refs = (refs[:4], refs[4:]) if direct else ((), refs)
    held, edge, taps_vm, ends_vm, xs, qs, pay, packed, u_vm, in_sems, edge_sems, tap_sem, own_sems, out_sems = refs
    blocks = k_ref.shape[1] // SPAN

    def lanes(c):
        return pl.ds(pl.multiple_of(c * SPAN, SPAN), SPAN)

    def loads(c):
        return [
            pltpu.make_async_copy(ref.at[:, lanes(c)], held.at[a, :, lanes(c)], in_sems.at[a, c])
            for a, ref in enumerate((k_ref, v_ref))
        ]

    def edge_loads():
        return [
            pltpu.make_async_copy(q_ref.at[pl.ds(at, 16), :], edge.at[e], edge_sems.at[e])
            for e, at in enumerate(EDGES)
        ]

    def stores(c):
        target = pay_ref.at[c] if direct else pay_ref.at[:, lanes(c)]
        return [
            pltpu.make_async_copy(packed.at[c], target, out_sems.at[0, c]),
            pltpu.make_async_copy(u_vm.at[c], u_ref.at[c], out_sems.at[1, c]),
        ]

    def own_loads():
        share = kept[0].shape[-1]
        cols = pl.ds(pl.multiple_of(me_ref[0] * share, share), share)
        views = (weights[0].at[:, :, cols], weights[1].at[:, cols], weights[2].at[:, cols], weights[3].at[:, cols])
        return [pltpu.make_async_copy(view, ref, own_sems.at[n]) for n, (view, ref) in enumerate(zip(views, kept))]

    tap_copy = pltpu.make_async_copy(taps_ref, taps_vm, tap_sem.at[0])
    ends_copy = pltpu.make_async_copy(ends_ref, ends_vm, tap_sem.at[1])
    tap_copy.start()
    ends_copy.start()
    for copy in loads(0) + edge_loads():
        copy.start()

    def begin(c, carry):
        for copy in loads(c):
            copy.start()
        return carry

    lax.fori_loop(1, blocks, begin, 0)
    if direct:
        for copy in own_loads():
            copy.start()
    for parity in range(2):
        for a in range(2):
            for h in range(2):
                for i in range(2):
                    at = i * (STRETCH + 8)
                    xs[parity, a, h, at : at + 8, :] = jnp.zeros((8, LANES), F32)
    tap_copy.wait()
    ends_copy.wait()

    def arrive(c):
        for copy in loads(c):
            copy.wait()

    def features(c):
        parity = lax.rem(c, 2)
        for h in range(2):
            part = slice(h * LANES, (h + 1) * LANES)
            cols = pl.ds(pl.multiple_of(c * SPAN + h * LANES, LANES), LANES)
            for a in range(2):
                for i in range(2):
                    base = i * (STRETCH + 8) + 8
                    xs[parity, a, h, base : base + STRETCH, :] = held[
                        a, i * STRETCH : (i + 1) * STRETCH, cols
                    ].astype(F32)
            taps = [[taps_vm[a, j : j + 1, cols] for j in range(REACH + 1)] for a in (1, 2)]
            for i in range(2):
                for b in range(STRETCH // 16):
                    base = i * (STRETCH + 8) + 8 + 16 * b
                    both = []
                    for a in range(2):
                        total = taps[a][0] * xs[parity, a, h, base : base + 16, :]
                        for j in range(1, REACH + 1):
                            total = total + taps[a][j] * xs[parity, a, h, base - j : base - j + 16, :]
                        both.append(total)
                    mixed = both[0] * both[1]
                    if b == 0:
                        row = lax.broadcasted_iota(jnp.int32, (16, LANES), 0)
                        mixed = jnp.where(row >= REACH, mixed, 0.0)
                    high, low = split(mixed)
                    rows = slice(i * STRETCH + 16 * b, i * STRETCH + 16 * b + 16)
                    u_vm[c, 0, rows, part] = high
                    u_vm[c, 1, rows, part] = low

    def products(c):
        found = []
        for i in range(2):
            rows = slice(i * STRETCH, (i + 1) * STRETCH)
            high, low = u_vm[c, 0, rows, :], u_vm[c, 1, rows, :]
            stacked = jnp.concatenate([high, low, high], axis=0)
            found.append(jnp.dot(ends_vm[...], stacked, preferred_element_type=F32)[:8])
        return found

    def finish(c, found):
        parity = lax.rem(c, 2)
        for i in range(2):
            moments = found[i]
            rest = (moments - moments.astype(BF16).astype(F32))[:FINE]
            at = PIECE * i + RAW
            for h in range(2):
                part = slice(h * LANES, (h + 1) * LANES)
                pay[h, at : at + RANK, :] = moments[:RANK, part]
                pay[h, at + RANK : at + COEFS, :] = rest[:, part]
        for h in range(2):
            cols = pl.ds(pl.multiple_of(c * SPAN + h * LANES, LANES), LANES)
            for i in range(2):
                base = i * (STRETCH + 8) + 8
                qs[h, i, 0:16, :] = edge[2 * i, :, cols].astype(F32)
                qs[h, i, 16:32, :] = edge[2 * i + 1, :, cols].astype(F32)
                at = i * PIECE
                pay[h, at : at + REACH, :] = qs[h, i, 32 - REACH : 32, :]
                pay[h, at + 3 * REACH : at + 4 * REACH, :] = qs[h, i, 0:REACH, :]
                for a in range(2):
                    at = i * PIECE + (1 + a) * REACH
                    pay[h, at : at + REACH, :] = xs[parity, a, h, base + STRETCH - REACH : base + STRETCH, :]
                    at = at + 3 * REACH
                    pay[h, at : at + REACH, :] = xs[parity, a, h, base : base + REACH, :]
            packed[c, :, h * LANES : (h + 1) * LANES] = pay[h].astype(BF16)

    def send(c):
        for copy in stores(c):
            copy.start()

    arrive(0)
    for copy in edge_loads():
        copy.wait()
    features(0)

    def both(c, carry):
        arrive(c)
        found = products(c - 1)
        features(c)
        finish(c - 1, found)
        send(c - 1)
        return carry

    lax.fori_loop(1, blocks, both, 0)
    finish(blocks - 1, products(blocks - 1))
    send(blocks - 1)

    def end(c, carry):
        for copy in stores(c):
            copy.wait()
        return carry

    lax.fori_loop(0, blocks, end, 0)
    if direct:
        for copy in own_loads():
            copy.wait()


def local_kernel(q_ref, u_ref, taps_ref, rates_ref, res_ref, skip_ref, local_ref, qc_ref, y_ref, xs):
    tile = q_ref.shape[1]
    per = SPAN // LANES
    for g in range(tile // LANES):
        cols = slice(g * LANES, (g + 1) * LANES)
        part = slice(g % per * LANES, (g % per + 1) * LANES)
        taps = [taps_ref[0, j : j + 1, cols] for j in range(REACH + 1)]
        for i in range(2):
            base = i * (STRETCH + 8) + 8
            xs[g, base - 8 : base, :] = jnp.zeros((8, LANES), F32)
            xs[g, base : base + STRETCH, :] = q_ref[i * STRETCH : (i + 1) * STRETCH, cols].astype(F32)
            for b in range(STRETCH // 8):
                at = base + 8 * b
                total = taps[0] * xs[g, at : at + 8, :]
                for j in range(1, REACH + 1):
                    total = total + taps[j] * xs[g, at - j : at - j + 8, :]
                if b == 0:
                    row = lax.broadcasted_iota(jnp.int32, (8, LANES), 0)
                    total = jnp.where(row >= REACH, total, 1.0)
                qc_ref[g // per, i * STRETCH + 8 * b : i * STRETCH + 8 * b + 8, part] = total
    for c in range(tile // SPAN):
        cols = slice(c * SPAN, (c + 1) * SPAN)
        rate = rates_ref[:, cols]
        amount = amplitude(rate, res_ref[:, cols])
        weights = [jnp.sum(amount * value, axis=0, keepdims=True) for value in strengths(rate)]
        for i in range(2):
            rows = slice(i * STRETCH, (i + 1) * STRETCH)
            high, low = u_ref[c, 0, rows, :], u_ref[c, 1, rows, :]
            parts = jnp.dot(
                local_ref[...], jnp.concatenate([high, low, high], axis=0), preferred_element_type=F32
            )
            total = skip_ref[:, cols] * (high.astype(F32) + low.astype(F32))
            for p in range(RANK):
                total = total + weights[p] * parts[p * STRETCH : (p + 1) * STRETCH, :]
            y_ref[c, rows, :] = total


def middle_kernel(
    perm_ref, x_ref, taps_ref, rates_ref, res_ref, skip_ref, out_ref,
    raw, ext, moments, past, heads, first, second, states, mids, coefs, result, slab, packed, out_sems,
):
    slots = perm_ref.shape[0]
    groups = x_ref.shape[2] // LANES
    order = rates_ref.shape[0]
    span = 2 * PIECE
    row = lax.broadcasted_iota(jnp.int32, (8, LANES), 0)
    ext[:, :, 0, 0:8, :] = jnp.zeros((3, groups, 8, LANES), F32)
    past[:, :, 0:8, :] = jnp.zeros((groups, slots, 8, LANES), F32)

    def unpack(src, carry):
        for g in range(groups):
            raw[src, g, 8 : 8 + span, :] = x_ref[src, :, g * LANES : (g + 1) * LANES].astype(F32)
        for i in range(2):
            n = perm_ref[2 * src + i]
            for g in range(groups):
                for a in range(3):
                    at = 8 + i * PIECE + a * REACH
                    ext[a, g, n + 1, 0:8, :] = raw[src, g, at + REACH - 8 : at + REACH, :]
                    at = at + 3 * REACH
                    ext[a, g, n, 8:16, :] = raw[src, g, at : at + 8, :]
                at = 8 + i * PIECE + RAW
                fine = jnp.where(row < FINE, raw[src, g, at + RANK : at + RANK + 8, :], 0.0)
                moments[g, n] = raw[src, g, at : at + 8, :] + fine
        return carry

    lax.fori_loop(0, slots // 2, unpack, 0, unroll=2)

    fades = []
    for g in range(groups):
        cols = slice(g * LANES, (g + 1) * LANES)
        rate = rates_ref[:, cols]
        amount = amplitude(rate, res_ref[:, cols])
        basis = strengths(rate)
        powers = [jnp.ones_like(rate), jnp.exp(-rate)]
        for d in range(2, REACH + 1):
            powers.append(powers[-1] * powers[1])
        for t in range(REACH):
            coefs[g, 0, t * order : (t + 1) * order, :] = amount * powers[t + 1]
        for p in range(RANK):
            coefs[g, 1, p * order : (p + 1) * order, :] = amount * powers[1] * basis[p]
        fade_rest = jnp.exp(-rate * float(INNER))
        fades.append((powers[REACH], fade_rest, fade_rest * powers[REACH]))
        taps = [[taps_ref[a, j : j + 1, cols] for j in range(REACH + 1)] for a in range(3)]
        near = [jnp.sum(amount * powers[d], axis=0, keepdims=True) for d in range(REACH)]
        near[0] = near[0] + skip_ref[:, cols]

        def head_pass(n, carry, g=g, taps=taps, powers=powers, near=near):
            feats = []
            for a in range(3):
                total = taps[a][0] * ext[a, g, n, 8:16, :]
                for j in range(1, REACH + 1):
                    total = total + taps[a][j] * ext[a, g, n, 8 - j : 16 - j, :]
                feats.append(jnp.where(row < REACH, total, 0.0))
            mixed = feats[1] * feats[2]
            past[g, n, 8:16, :] = mixed
            total = near[0] * mixed
            for d in range(1, REACH):
                total = total + near[d] * past[g, n, 8 - d : 16 - d, :]
            at = pl.multiple_of(n * 16, 16)
            heads[g, pl.ds(at, 8), :] = feats[0]
            heads[g, pl.ds(at + 8, 8), :] = total
            value = powers[REACH - 1] * past[g, n, 8:9, :]
            for s in range(1, REACH):
                value = value + powers[REACH - 1 - s] * past[g, n, 8 + s : 9 + s, :]
            first[g, n] = value
            return carry

        lax.fori_loop(0, slots, head_pass, 0, unroll=4)

        def rest_pass(n, carry, g=g, basis=basis, fade_rest=fade_rest):
            value = fade_rest * first[g, n]
            for p in range(RANK):
                value = value + basis[p] * moments[g, n, p : p + 1, :]
            second[g, n] = value
            return carry

        lax.fori_loop(0, slots, rest_pass, 0, unroll=4)

    def scan_pass(n, state):
        after = []
        at = pl.multiple_of(n * order, order)
        for g in range(groups):
            states[g, pl.ds(at, order), :] = state[g]
            mids[g, pl.ds(at, order), :] = fades[g][0] * state[g] + first[g, n]
            after.append(fades[g][2] * state[g] + second[g, n])
        return tuple(after)

    lax.fori_loop(0, slots, scan_pass, tuple(jnp.zeros((order, LANES), F32) for _ in range(groups)), unroll=4)

    quad = 4

    def sums(g, kind, held, first_tile):
        totals = [[None] * quad for _ in range(RANK)]
        for r in range(order):
            values = [held[g, pl.ds((first_tile + k) * 8 * order + r, 8, stride=order), :] for k in range(quad)]
            for p in range(RANK):
                weight = coefs[g, kind, p * order + r : p * order + r + 1, :]
                for k in range(quad):
                    term = weight * values[k]
                    totals[p][k] = term if r == 0 else totals[p][k] + term
        return totals

    def out_pass(q, carry):
        for g in range(groups):
            totals = sums(g, 0, states, q * quad)
            for t in range(REACH):
                for k in range(quad):
                    tile = q * quad + k
                    query = heads[g, pl.ds(tile * 128 + t, 8, stride=16), :]
                    local = heads[g, pl.ds(tile * 128 + 8 + t, 8, stride=16), :]
                    z = query * (local + totals[t][k])
                    result[g, pl.ds(tile * 192 + t, 8, stride=24), :] = z
                    result[g, pl.ds(tile * 192 + REACH + t, 8, stride=24), :] = z - z.astype(BF16).astype(F32)
            totals = sums(g, 1, mids, q * quad)
            for p in range(RANK):
                for k in range(quad):
                    tile = q * quad + k
                    value = totals[p][k]
                    result[g, pl.ds(tile * 192 + 2 * REACH + p, 8, stride=24), :] = value
                    if p < FINE:
                        rest = value - value.astype(BF16).astype(F32)
                        result[g, pl.ds(tile * 192 + 2 * REACH + RANK + p, 8, stride=24), :] = rest
        return carry

    lax.fori_loop(0, slots // (8 * quad), out_pass, 0)

    def store(src):
        return pltpu.make_async_copy(packed.at[src], out_ref.at[src], out_sems.at[src])

    def pack(src, carry):
        for g in range(groups):
            for i in range(2):
                at = pl.multiple_of(perm_ref[2 * src + i] * 24, 8)
                slab[src, g, i * BACK : i * BACK + 24, :] = result[g, pl.ds(at, 24), :]
            packed[src, :, g * LANES : (g + 1) * LANES] = slab[src, g, 0 : 2 * BACK, :].astype(BF16)
        return carry

    lax.fori_loop(0, slots // 2, pack, 0, unroll=2)

    def send(src, carry):
        store(src).start()
        return carry

    def end(src, carry):
        store(src).wait()
        return carry

    lax.fori_loop(0, slots // 2, send, 0)
    lax.fori_loop(0, slots // 2, end, 0)


def join_kernel(back_ref, lift_ref, qc_ref, y_ref, z_ref, sq_ref, qc_vm, y_vm, carry, sems):
    blocks, tokens, _ = qc_vm.shape
    by_dest = len(back_ref.shape) == 3
    chunk = 4

    def loads(c):
        rows = pl.ds(c * chunk, chunk)
        return [
            pltpu.make_async_copy(ref.at[rows], held.at[rows], sems.at[n, c])
            for n, (ref, held) in enumerate(((qc_ref, qc_vm), (y_ref, y_vm)))
        ]

    for c in range(blocks // chunk):
        for copy in loads(c):
            copy.start()
    for b in range(blocks):
        back = back_ref[b] if by_dest else back_ref[:, b * SPAN : (b + 1) * SPAN]
        carry[b] = jnp.dot(lift_ref[0], back, preferred_element_type=F32) + jnp.dot(
            lift_ref[1], back, preferred_element_type=F32
        )
    total = jnp.zeros((tokens, LANES), F32)
    for c in range(blocks // chunk):
        for copy in loads(c):
            copy.wait()
        for b in range(c * chunk, (c + 1) * chunk):
            z = qc_vm[b] * (y_vm[b] + carry[b])
            z_ref[:, b * SPAN : (b + 1) * SPAN] = z
            squares = z * z
            for h in range(SPAN // LANES):
                total = total + squares[:, h * LANES : (h + 1) * LANES]
    sq_ref[...] = jnp.sum(total.T, axis=0, keepdims=True)


def limit(mib):
    return pltpu.CompilerParams(vmem_limit_bytes=mib * 1024 * 1024)


def on_device(sizes, q_in, k_in, v_in, stretch_of_slot, short_weight, rates, residues, skip, gain):
    n_ctx, n_ch = sizes
    tokens, width = q_in.shape
    slots = stretch_of_slot.shape[0]
    order = rates.shape[0]
    share = width // n_ctx
    direct = share == SPAN
    tile = min(width, 1024)
    steps = width // tile
    groups = tile // LANES
    ends_np, local_np, lift_np = constant_matrices()
    ends, local, lift = jnp.asarray(ends_np), jnp.asarray(local_np), jnp.asarray(lift_np)
    skip, gain = skip.reshape(1, width), gain.reshape(1, width)
    me = lax.axis_index("ctx").astype(jnp.int32).reshape(1)

    def whole(array):
        return pl.BlockSpec(array.shape, lambda c: (0,) * array.ndim)

    def columns(*lead):
        return pl.BlockSpec((*lead, tile), lambda c: (0,) * len(lead) + (c,))

    def exchange(array):
        if direct:
            return lax.all_to_all(array, "ctx", 0, 0, tiled=True)
        array = array.reshape(array.shape[0], n_ctx, share).transpose(1, 0, 2)
        return widen(lax.all_to_all(array, "ctx", 0, 0, tiled=True))

    lanes = -(-share // LANES) * LANES

    def widen(array, fill=0.0):
        pad = [(0, 0)] * (array.ndim - 1) + [(0, lanes - share)]
        return jnp.pad(array, pad, constant_values=fill)

    def cut(array, fill=0.0):
        return widen(lax.dynamic_slice_in_dim(array, lax.axis_index("ctx") * share, share, array.ndim - 1), fill)

    smem = pl.BlockSpec(memory_space=pltpu.SMEM)
    vmem = pl.BlockSpec(memory_space=pltpu.VMEM)
    hbm = pl.BlockSpec(memory_space=pltpu.HBM)
    f32 = lambda *shape: jax.ShapeDtypeStruct(shape, F32)
    pin = lambda array: pltpu.with_memory_space_constraint(array, pltpu.HBM)

    weights = (short_weight, rates, residues, skip)
    own = [f32(*w.shape[:-1], share) for w in weights] if direct else []
    blocks = width // SPAN
    pay, mixed, *mine = pl.pallas_call(
        functools.partial(front_kernel, direct=direct),
        in_specs=[smem] + [hbm] * (5 + len(own)),
        out_specs=[hbm] * 2 + [vmem] * len(own),
        out_shape=[
            pltpu.HBM((n_ctx, 2 * PIECE, share) if direct else (2 * PIECE, width), BF16),
            pltpu.HBM((blocks, 2, tokens, SPAN), BF16),
        ]
        + own,
        scratch_shapes=[
            pltpu.VMEM((2, tokens, width), BF16),
            pltpu.VMEM((4, 16, width), BF16),
            pltpu.VMEM(short_weight.shape, F32),
            pltpu.VMEM(ends.shape, BF16),
            pltpu.VMEM((2, 2, 2, 2 * (STRETCH + 8), LANES), F32),
            pltpu.VMEM((2, 2, 32, LANES), F32),
            pltpu.VMEM((2, 2 * PIECE, LANES), F32),
            pltpu.VMEM((blocks, 2 * PIECE, SPAN), BF16),
            pltpu.VMEM((blocks, 2, tokens, SPAN), BF16),
            pltpu.SemaphoreType.DMA((2, blocks)),
            pltpu.SemaphoreType.DMA((4,)),
            pltpu.SemaphoreType.DMA((2,)),
            pltpu.SemaphoreType.DMA((4,)),
            pltpu.SemaphoreType.DMA((2, blocks)),
        ],
        compiler_params=limit(24),
        name="front_pieces",
    )(me, *map(pin, (q_in, k_in, v_in, short_weight, ends)), *(map(pin, weights) if direct else ()))
    arrived = exchange(pay)
    if not direct:
        mine = (cut(short_weight), cut(rates, 0.01), cut(residues), cut(skip))

    query, inner = pl.pallas_call(
        local_kernel,
        grid=(steps,),
        in_specs=[
            columns(tokens),
            pl.BlockSpec((tile // SPAN, 2, tokens, SPAN), lambda c: (c, 0, 0, 0)),
            columns(3, REACH + 1),
            columns(order),
            columns(order),
            columns(1),
            whole(local),
        ],
        out_specs=[pl.BlockSpec((tile // SPAN, tokens, SPAN), lambda c: (c, 0, 0))] * 2,
        out_shape=[pltpu.HBM((blocks, tokens, SPAN), F32)] * 2,
        scratch_shapes=[pltpu.VMEM((groups, 2 * (STRETCH + 8), LANES), F32)],
        compiler_params=limit(24),
        name="local_filter",
        cost_estimate=pl.CostEstimate(flops=10**9, bytes_accessed=20 * 10**6, transcendentals=0),
    )(*map(pin, (q_in, mixed, short_weight, rates, residues)), skip, local)
    arrived, query, inner = lax.optimization_barrier((arrived, query, inner))

    groups = lanes // LANES
    back = pl.pallas_call(
        middle_kernel,
        in_specs=[smem] + [vmem] * 5,
        out_specs=hbm,
        scratch_shapes=[
            pltpu.VMEM((n_ctx, groups, 8 + 2 * PIECE + 8, LANES), F32),
            pltpu.VMEM((3, groups, slots + 1, 16, LANES), F32),
            pltpu.VMEM((groups, slots, 8, LANES), F32),
            pltpu.VMEM((groups, slots, 16, LANES), F32),
            pltpu.VMEM((groups, slots * 16, LANES), F32),
            pltpu.VMEM((groups, slots, order, LANES), F32),
            pltpu.VMEM((groups, slots, order, LANES), F32),
            pltpu.VMEM((groups, slots * order, LANES), F32),
            pltpu.VMEM((groups, slots * order, LANES), F32),
            pltpu.VMEM((groups, 2, RANK * order, LANES), F32),
            pltpu.VMEM((groups, slots * 24, LANES), F32),
            pltpu.VMEM((n_ctx, groups, BACK + 28, LANES), F32),
            pltpu.VMEM((n_ctx, 2 * BACK, lanes), BF16),
            pltpu.SemaphoreType.DMA((n_ctx,)),
        ],
        out_shape=pltpu.HBM((n_ctx, 2 * BACK, lanes), BF16),
        compiler_params=limit(24),
        name="middle_states",
    )(stretch_of_slot, arrived, *mine)
    if not direct:
        back = back[:, :, :share]
    back = lax.all_to_all(back, "ctx", 0, 0, tiled=True)
    if not direct:
        back = back.transpose(1, 0, 2).reshape(2 * BACK, width)

    zvalues, squares = pl.pallas_call(
        join_kernel,
        in_specs=[vmem] * 2 + [hbm] * 2,
        out_specs=[vmem] * 2,
        out_shape=[f32(tokens, width), f32(1, tokens)],
        scratch_shapes=[pltpu.VMEM((blocks, tokens, SPAN), F32)] * 3 + [pltpu.SemaphoreType.DMA((2, blocks // 4))],
        compiler_params=limit(24),
        name="join_carry",
    )(back, lift, pin(query), pin(inner))
    total = squares
    for shift in range(1, n_ch):
        total = total + lax.ppermute(squares, "ch", [(i, (i + shift) % n_ch) for i in range(n_ch)])
    scale = lax.rsqrt(total / (width * n_ch) + 1e-05)
    return (zvalues * scale.reshape(tokens, 1) * gain).astype(BF16)


def solution(mesh):
    sizes = (mesh.shape["ctx"], mesh.shape["ch"])
    in_specs = (
        P("ctx", "ch"),
        P("ctx", "ch"),
        P("ctx", "ch"),
        P(),
        P(None, None, "ch"),
        P(None, "ch"),
        P(None, "ch"),
        P("ch"),
        P("ch"),
    )

    def run(*arrays):
        return on_device(sizes, *arrays)

    return jax.shard_map(run, mesh=mesh, in_specs=in_specs, out_specs=P("ctx", "ch"), check_vma=False)
```

```python
import functools
from decimal import Decimal, getcontext

import jax
import jax.numpy as jnp
import ml_dtypes
import numpy as np
from jax import lax
from jax.experimental import pallas as pl
from jax.experimental.pallas import tpu as pltpu
from jax.sharding import PartitionSpec as P

F32, BF16 = jnp.float32, jnp.bfloat16
LANES = 128
SPAN = 256
STRETCH = 64
REACH = 6
INNER = STRETCH - REACH
PIVOTS = (8, 49, 21, 56, 36, 1)
ANCHORS = ("0.0020", "0.0235", "0.0110", "0.0295", "0.0185", "0.0004")
RANK = len(PIVOTS)
FINE = 2
COEFS = RANK + FINE
ROLLED = 3
RAW = 6 * REACH
PIECE = RAW + COEFS
BACK = 2 * REACH + COEFS


def shape_table():
    getcontext().prec = 50
    rest = [[(-Decimal(a) * d).exp() for d in range(INNER)] for a in ANCHORS]
    table = []
    for p in range(RANK):
        shape = [x / rest[p][PIVOTS[p]] for x in rest[p]]
        rest = [[x - row[PIVOTS[p]] * y for x, y in zip(row, shape)] for row in rest]
        table.append([float(x) for x in shape])
    return table


SHAPE = shape_table()


def halves(values):
    high = values.astype(ml_dtypes.bfloat16)
    low = (values - high.astype(np.float32)).astype(ml_dtypes.bfloat16)
    return high, low


def constant_matrices():
    shape = np.array(SHAPE, np.float32)
    ends = np.zeros((16, STRETCH), np.float32)
    local = np.zeros((RANK, STRETCH, STRETCH), np.float32)
    lift = np.zeros((2, 2 * STRETCH, 2 * BACK), np.float32)
    parts = [h.astype(np.float32) for h in halves(shape)]
    for p in range(RANK):
        for s in range(REACH, STRETCH):
            ends[p, s] = shape[p, STRETCH - 1 - s]
            local[p, s:, s] = shape[p, : STRETCH - s]
        for half in range(2):
            rows = slice(half * STRETCH + REACH, (half + 1) * STRETCH)
            at = half * BACK + 2 * REACH
            for k in range(2):
                lift[k, rows, at + p] = parts[k][p]
                if p < FINE:
                    lift[k, rows, at + RANK + p] = parts[k][p]
    for half in range(2):
        for t in range(REACH):
            lift[0, half * STRETCH + t, half * BACK + t] = 1.0
            lift[0, half * STRETCH + t, half * BACK + REACH + t] = 1.0
    local = local.reshape(RANK * STRETCH, STRETCH)

    def triple(m):
        h, l = halves(m)
        return np.concatenate([h, h, l], axis=1)

    return triple(ends), triple(local), lift.astype(ml_dtypes.bfloat16)


def strengths(rate):
    found = []
    for p in range(RANK):
        value = jnp.exp(-rate * float(PIVOTS[p]))
        for q in range(p):
            value = value - found[q] * SHAPE[q][PIVOTS[p]]
        found.append(value)
    return found


def split(values):
    high = values.astype(BF16)
    return high, (values - high.astype(F32)).astype(BF16)


def amplitude(rate, residue):
    x = 2.0 * rate
    series = 1.0 - x * (0.5 - x * (1 / 6 - x * (1 / 24 - x * (1 / 120 - x * (1 / 720)))))
    return residue * jnp.sqrt(x * series)


EDGES = (0, STRETCH - 16, STRETCH, 2 * STRETCH - 16)


def front_kernel(*refs, direct):
    me_ref, q_ref, k_ref, v_ref, taps_ref, ends_ref = refs[:6]
    refs = refs[6:]
    weights, refs = (refs[:4], refs[4:]) if direct else ((), refs)
    pay_ref, u_ref, refs = refs[0], refs[1], refs[2:]
    kept, refs = (refs[:4], refs[4:]) if direct else ((), refs)
    held, edge, taps_vm, ends_vm, xs, qs, pay, packed, u_vm, in_sems, edge_sems, tap_sem, own_sems, out_sems = refs
    blocks = k_ref.shape[1] // SPAN

    def lanes(c):
        return pl.ds(pl.multiple_of(c * SPAN, SPAN), SPAN)

    def loads(c):
        return [
            pltpu.make_async_copy(ref.at[:, lanes(c)], held.at[a, :, lanes(c)], in_sems.at[a, c])
            for a, ref in enumerate((k_ref, v_ref))
        ]

    def edge_loads():
        return [
            pltpu.make_async_copy(q_ref.at[pl.ds(at, 16), :], edge.at[e], edge_sems.at[e])
            for e, at in enumerate(EDGES)
        ]

    def stores(c):
        target = pay_ref.at[c] if direct else pay_ref.at[:, lanes(c)]
        return [
            pltpu.make_async_copy(packed.at[c], target, out_sems.at[0, c]),
            pltpu.make_async_copy(u_vm.at[c], u_ref.at[c], out_sems.at[1, c]),
        ]

    def own_loads():
        share = kept[0].shape[-1]
        cols = pl.ds(pl.multiple_of(me_ref[0] * share, share), share)
        views = (weights[0].at[:, :, cols], weights[1].at[:, cols], weights[2].at[:, cols], weights[3].at[:, cols])
        return [pltpu.make_async_copy(view, ref, own_sems.at[n]) for n, (view, ref) in enumerate(zip(views, kept))]

    tap_copy = pltpu.make_async_copy(taps_ref, taps_vm, tap_sem.at[0])
    ends_copy = pltpu.make_async_copy(ends_ref, ends_vm, tap_sem.at[1])
    tap_copy.start()
    ends_copy.start()
    for copy in loads(0) + edge_loads():
        copy.start()

    def begin(c, carry):
        for copy in loads(c):
            copy.start()
        return carry

    lax.fori_loop(1, blocks, begin, 0)
    if direct:
        for copy in own_loads():
            copy.start()
    for parity in range(2):
        for a in range(2):
            for h in range(2):
                for i in range(2):
                    at = i * (STRETCH + 8)
                    xs[parity, a, h, at : at + 8, :] = jnp.zeros((8, LANES), F32)
    tap_copy.wait()
    ends_copy.wait()

    def arrive(c):
        for copy in loads(c):
            copy.wait()

    def features(c):
        parity = lax.rem(c, 2)
        for h in range(2):
            part = slice(h * LANES, (h + 1) * LANES)
            cols = pl.ds(pl.multiple_of(c * SPAN + h * LANES, LANES), LANES)
            for a in range(2):
                for i in range(2):
                    base = i * (STRETCH + 8) + 8
                    xs[parity, a, h, base : base + STRETCH, :] = held[
                        a, i * STRETCH : (i + 1) * STRETCH, cols
                    ].astype(F32)
            taps = [[taps_vm[a, j : j + 1, cols] for j in range(REACH + 1)] for a in (1, 2)]
            for i in range(2):
                for b in range(STRETCH // 16):
                    base = i * (STRETCH + 8) + 8 + 16 * b
                    both = []
                    for a in range(2):
                        near = xs[parity, a, h, base - 8 : base + 16, :]
                        total = taps[a][0] * near[8:]
                        for j in range(1, REACH + 1):
                            if j <= ROLLED:
                                shifted = pltpu.roll(near, j, 0)[8:]
                            else:
                                shifted = xs[parity, a, h, base - j : base - j + 16, :]
                            total = total + taps[a][j] * shifted
                        both.append(total)
                    mixed = both[0] * both[1]
                    if b == 0:
                        row = lax.broadcasted_iota(jnp.int32, (16, LANES), 0)
                        mixed = jnp.where(row >= REACH, mixed, 0.0)
                    high, low = split(mixed)
                    rows = slice(i * STRETCH + 16 * b, i * STRETCH + 16 * b + 16)
                    u_vm[c, 0, rows, part] = high
                    u_vm[c, 1, rows, part] = low

    def products(c):
        found = []
        for i in range(2):
            rows = slice(i * STRETCH, (i + 1) * STRETCH)
            high, low = u_vm[c, 0, rows, :], u_vm[c, 1, rows, :]
            stacked = jnp.concatenate([high, low, high], axis=0)
            found.append(jnp.dot(ends_vm[...], stacked, preferred_element_type=F32)[:8])
        return found

    def finish(c, found):
        parity = lax.rem(c, 2)
        for i in range(2):
            moments = found[i]
            rest = (moments - moments.astype(BF16).astype(F32))[:FINE]
            at = PIECE * i + RAW
            for h in range(2):
                part = slice(h * LANES, (h + 1) * LANES)
                pay[h, at : at + RANK, :] = moments[:RANK, part]
                pay[h, at + RANK : at + COEFS, :] = rest[:, part]
        for h in range(2):
            cols = pl.ds(pl.multiple_of(c * SPAN + h * LANES, LANES), LANES)
            for i in range(2):
                base = i * (STRETCH + 8) + 8
                qs[h, i, 0:16, :] = edge[2 * i, :, cols].astype(F32)
                qs[h, i, 16:32, :] = edge[2 * i + 1, :, cols].astype(F32)
                at = i * PIECE
                pay[h, at : at + REACH, :] = qs[h, i, 32 - REACH : 32, :]
                pay[h, at + 3 * REACH : at + 4 * REACH, :] = qs[h, i, 0:REACH, :]
                for a in range(2):
                    at = i * PIECE + (1 + a) * REACH
                    pay[h, at : at + REACH, :] = xs[parity, a, h, base + STRETCH - REACH : base + STRETCH, :]
                    at = at + 3 * REACH
                    pay[h, at : at + REACH, :] = xs[parity, a, h, base : base + REACH, :]
            packed[c, :, h * LANES : (h + 1) * LANES] = pay[h].astype(BF16)

    def send(c):
        for copy in stores(c):
            copy.start()

    arrive(0)
    for copy in edge_loads():
        copy.wait()
    features(0)

    def both(c, carry):
        arrive(c)
        found = products(c - 1)
        features(c)
        finish(c - 1, found)
        send(c - 1)
        return carry

    lax.fori_loop(1, blocks, both, 0)
    finish(blocks - 1, products(blocks - 1))
    send(blocks - 1)

    def end(c, carry):
        for copy in stores(c):
            copy.wait()
        return carry

    lax.fori_loop(0, blocks, end, 0)
    if direct:
        for copy in own_loads():
            copy.wait()


def local_kernel(q_ref, u_ref, taps_ref, rates_ref, res_ref, skip_ref, local_ref, qc_ref, y_ref, xs):
    tile = q_ref.shape[1]
    per = SPAN // LANES
    for g in range(tile // LANES):
        cols = slice(g * LANES, (g + 1) * LANES)
        part = slice(g % per * LANES, (g % per + 1) * LANES)
        taps = [taps_ref[0, j : j + 1, cols] for j in range(REACH + 1)]
        for i in range(2):
            base = i * (STRETCH + 8) + 8
            xs[g, base - 8 : base, :] = jnp.zeros((8, LANES), F32)
            xs[g, base : base + STRETCH, :] = q_ref[i * STRETCH : (i + 1) * STRETCH, cols].astype(F32)
            for b in range(STRETCH // 8):
                at = base + 8 * b
                total = taps[0] * xs[g, at : at + 8, :]
                for j in range(1, REACH + 1):
                    total = total + taps[j] * xs[g, at - j : at - j + 8, :]
                if b == 0:
                    row = lax.broadcasted_iota(jnp.int32, (8, LANES), 0)
                    total = jnp.where(row >= REACH, total, 1.0)
                qc_ref[g // per, i * STRETCH + 8 * b : i * STRETCH + 8 * b + 8, part] = total
    for c in range(tile // SPAN):
        cols = slice(c * SPAN, (c + 1) * SPAN)
        rate = rates_ref[:, cols]
        amount = amplitude(rate, res_ref[:, cols])
        weights = [jnp.sum(amount * value, axis=0, keepdims=True) for value in strengths(rate)]
        for i in range(2):
            rows = slice(i * STRETCH, (i + 1) * STRETCH)
            high, low = u_ref[c, 0, rows, :], u_ref[c, 1, rows, :]
            parts = jnp.dot(
                local_ref[...], jnp.concatenate([high, low, high], axis=0), preferred_element_type=F32
            )
            total = skip_ref[:, cols] * (high.astype(F32) + low.astype(F32))
            for p in range(RANK):
                total = total + weights[p] * parts[p * STRETCH : (p + 1) * STRETCH, :]
            y_ref[c, rows, :] = total


def middle_kernel(
    perm_ref, x_ref, taps_ref, rates_ref, res_ref, skip_ref, out_ref,
    raw, ext, moments, past, heads, first, second, states, mids, coefs, result, slab, packed, out_sems,
):
    slots = perm_ref.shape[0]
    groups = x_ref.shape[2] // LANES
    order = rates_ref.shape[0]
    span = 2 * PIECE
    row = lax.broadcasted_iota(jnp.int32, (8, LANES), 0)
    ext[:, :, 0, 0:8, :] = jnp.zeros((3, groups, 8, LANES), F32)
    past[:, :, 0:8, :] = jnp.zeros((groups, slots, 8, LANES), F32)

    def unpack(src, carry):
        for g in range(groups):
            raw[src, g, 8 : 8 + span, :] = x_ref[src, :, g * LANES : (g + 1) * LANES].astype(F32)
        for i in range(2):
            n = perm_ref[2 * src + i]
            for g in range(groups):
                for a in range(3):
                    at = 8 + i * PIECE + a * REACH
                    ext[a, g, n + 1, 0:8, :] = raw[src, g, at + REACH - 8 : at + REACH, :]
                    at = at + 3 * REACH
                    ext[a, g, n, 8:16, :] = raw[src, g, at : at + 8, :]
                at = 8 + i * PIECE + RAW
                fine = jnp.where(row < FINE, raw[src, g, at + RANK : at + RANK + 8, :], 0.0)
                moments[g, n] = raw[src, g, at : at + 8, :] + fine
        return carry

    lax.fori_loop(0, slots // 2, unpack, 0, unroll=2)

    fades = []
    for g in range(groups):
        cols = slice(g * LANES, (g + 1) * LANES)
        rate = rates_ref[:, cols]
        amount = amplitude(rate, res_ref[:, cols])
        basis = strengths(rate)
        powers = [jnp.ones_like(rate), jnp.exp(-rate)]
        for d in range(2, REACH + 1):
            powers.append(powers[-1] * powers[1])
        for t in range(REACH):
            coefs[g, 0, t * order : (t + 1) * order, :] = amount * powers[t + 1]
        for p in range(RANK):
            coefs[g, 1, p * order : (p + 1) * order, :] = amount * powers[1] * basis[p]
        fade_rest = jnp.exp(-rate * float(INNER))
        fades.append((powers[REACH], fade_rest, fade_rest * powers[REACH]))
        taps = [[taps_ref[a, j : j + 1, cols] for j in range(REACH + 1)] for a in range(3)]
        near = [jnp.sum(amount * powers[d], axis=0, keepdims=True) for d in range(REACH)]
        near[0] = near[0] + skip_ref[:, cols]

        def head_pass(n, carry, g=g, taps=taps, powers=powers, near=near):
            feats = []
            for a in range(3):
                total = taps[a][0] * ext[a, g, n, 8:16, :]
                for j in range(1, REACH + 1):
                    total = total + taps[a][j] * ext[a, g, n, 8 - j : 16 - j, :]
                feats.append(jnp.where(row < REACH, total, 0.0))
            mixed = feats[1] * feats[2]
            past[g, n, 8:16, :] = mixed
            total = near[0] * mixed
            for d in range(1, REACH):
                total = total + near[d] * past[g, n, 8 - d : 16 - d, :]
            at = pl.multiple_of(n * 16, 16)
            heads[g, pl.ds(at, 8), :] = feats[0]
            heads[g, pl.ds(at + 8, 8), :] = total
            value = powers[REACH - 1] * past[g, n, 8:9, :]
            for s in range(1, REACH):
                value = value + powers[REACH - 1 - s] * past[g, n, 8 + s : 9 + s, :]
            first[g, n] = value
            return carry

        lax.fori_loop(0, slots, head_pass, 0, unroll=4)

        def rest_pass(n, carry, g=g, basis=basis, fade_rest=fade_rest):
            value = fade_rest * first[g, n]
            for p in range(RANK):
                value = value + basis[p] * moments[g, n, p : p + 1, :]
            second[g, n] = value
            return carry

        lax.fori_loop(0, slots, rest_pass, 0, unroll=4)

    def scan_pass(n, state):
        after = []
        at = pl.multiple_of(n * order, order)
        for g in range(groups):
            states[g, pl.ds(at, order), :] = state[g]
            mids[g, pl.ds(at, order), :] = fades[g][0] * state[g] + first[g, n]
            after.append(fades[g][2] * state[g] + second[g, n])
        return tuple(after)

    lax.fori_loop(0, slots, scan_pass, tuple(jnp.zeros((order, LANES), F32) for _ in range(groups)), unroll=4)

    quad = 4

    def sums(g, kind, held, first_tile):
        totals = [[None] * quad for _ in range(RANK)]
        for r in range(order):
            values = [held[g, pl.ds((first_tile + k) * 8 * order + r, 8, stride=order), :] for k in range(quad)]
            for p in range(RANK):
                weight = coefs[g, kind, p * order + r : p * order + r + 1, :]
                for k in range(quad):
                    term = weight * values[k]
                    totals[p][k] = term if r == 0 else totals[p][k] + term
        return totals

    def out_pass(q, carry):
        for g in range(groups):
            totals = sums(g, 0, states, q * quad)
            for t in range(REACH):
                for k in range(quad):
                    tile = q * quad + k
                    query = heads[g, pl.ds(tile * 128 + t, 8, stride=16), :]
                    local = heads[g, pl.ds(tile * 128 + 8 + t, 8, stride=16), :]
                    z = query * (local + totals[t][k])
                    result[g, pl.ds(tile * 192 + t, 8, stride=24), :] = z
                    result[g, pl.ds(tile * 192 + REACH + t, 8, stride=24), :] = z - z.astype(BF16).astype(F32)
            totals = sums(g, 1, mids, q * quad)
            for p in range(RANK):
                for k in range(quad):
                    tile = q * quad + k
                    value = totals[p][k]
                    result[g, pl.ds(tile * 192 + 2 * REACH + p, 8, stride=24), :] = value
                    if p < FINE:
                        rest = value - value.astype(BF16).astype(F32)
                        result[g, pl.ds(tile * 192 + 2 * REACH + RANK + p, 8, stride=24), :] = rest
        return carry

    lax.fori_loop(0, slots // (8 * quad), out_pass, 0)

    def store(src):
        return pltpu.make_async_copy(packed.at[src], out_ref.at[src], out_sems.at[src])

    def pack(src, carry):
        for g in range(groups):
            for i in range(2):
                at = pl.multiple_of(perm_ref[2 * src + i] * 24, 8)
                slab[src, g, i * BACK : i * BACK + 24, :] = result[g, pl.ds(at, 24), :]
            packed[src, :, g * LANES : (g + 1) * LANES] = slab[src, g, 0 : 2 * BACK, :].astype(BF16)
        return carry

    lax.fori_loop(0, slots // 2, pack, 0, unroll=2)

    def send(src, carry):
        store(src).start()
        return carry

    def end(src, carry):
        store(src).wait()
        return carry

    lax.fori_loop(0, slots // 2, send, 0)
    lax.fori_loop(0, slots // 2, end, 0)


def join_kernel(back_ref, lift_ref, qc_ref, y_ref, z_ref, sq_ref):
    blocks, tokens, _ = qc_ref.shape
    by_dest = len(back_ref.shape) == 3
    total = jnp.zeros((tokens, LANES), F32)
    for b in range(blocks):
        back = back_ref[b] if by_dest else back_ref[:, b * SPAN : (b + 1) * SPAN]
        carry = jnp.dot(lift_ref[0], back, preferred_element_type=F32)
        carry = carry + jnp.dot(lift_ref[1], back, preferred_element_type=F32)
        z = qc_ref[b] * (y_ref[b] + carry)
        z_ref[:, b * SPAN : (b + 1) * SPAN] = z
        squares = z * z
        for h in range(SPAN // LANES):
            total = total + squares[:, h * LANES : (h + 1) * LANES]
    sq_ref[...] = jnp.sum(total.T, axis=0, keepdims=True)


def scale_kernel(*refs, channels):
    z_ref, gain_ref, refs, (out_ref, held, sems) = refs[0], refs[1], refs[2:-3], refs[-3:]
    tokens, width = z_ref.shape
    chunks = sems.shape[0]
    wide = width // chunks
    total = refs[0][...]
    for ref in refs[1:]:
        total = total + ref[...]
    scale = lax.rsqrt(total / channels + 1e-05)
    scale = jnp.broadcast_to(scale, (LANES, tokens)).T
    copies = []
    for c in range(chunks):
        for g in range(c * wide // LANES, (c + 1) * wide // LANES):
            cols = slice(g * LANES, (g + 1) * LANES)
            held[:, cols] = (z_ref[:, cols] * scale * gain_ref[:, cols]).astype(BF16)
        cols = pl.ds(c * wide, wide)
        copy = pltpu.make_async_copy(held.at[:, cols], out_ref.at[:, cols], sems.at[c])
        copy.start()
        copies.append(copy)
    for copy in copies:
        copy.wait()


def limit(mib):
    return pltpu.CompilerParams(vmem_limit_bytes=mib * 1024 * 1024)


def on_device(sizes, q_in, k_in, v_in, stretch_of_slot, short_weight, rates, residues, skip, gain):
    n_ctx, n_ch = sizes
    tokens, width = q_in.shape
    slots = stretch_of_slot.shape[0]
    order = rates.shape[0]
    share = width // n_ctx
    direct = share == SPAN
    tile = min(width, 1024)
    steps = width // tile
    groups = tile // LANES
    ends_np, local_np, lift_np = constant_matrices()
    ends, local, lift = jnp.asarray(ends_np), jnp.asarray(local_np), jnp.asarray(lift_np)
    skip, gain = skip.reshape(1, width), gain.reshape(1, width)
    me = lax.axis_index("ctx").astype(jnp.int32).reshape(1)

    def whole(array):
        return pl.BlockSpec(array.shape, lambda c: (0,) * array.ndim)

    def columns(*lead):
        return pl.BlockSpec((*lead, tile), lambda c: (0,) * len(lead) + (c,))

    def exchange(array):
        if direct:
            return lax.all_to_all(array, "ctx", 0, 0, tiled=True)
        array = array.reshape(array.shape[0], n_ctx, share).transpose(1, 0, 2)
        return widen(lax.all_to_all(array, "ctx", 0, 0, tiled=True))

    lanes = -(-share // LANES) * LANES

    def widen(array, fill=0.0):
        pad = [(0, 0)] * (array.ndim - 1) + [(0, lanes - share)]
        return jnp.pad(array, pad, constant_values=fill)

    def cut(array, fill=0.0):
        return widen(lax.dynamic_slice_in_dim(array, lax.axis_index("ctx") * share, share, array.ndim - 1), fill)

    smem = pl.BlockSpec(memory_space=pltpu.SMEM)
    vmem = pl.BlockSpec(memory_space=pltpu.VMEM)
    hbm = pl.BlockSpec(memory_space=pltpu.HBM)
    f32 = lambda *shape: jax.ShapeDtypeStruct(shape, F32)
    pin = lambda array: pltpu.with_memory_space_constraint(array, pltpu.HBM)

    weights = (short_weight, rates, residues, skip)
    own = [f32(*w.shape[:-1], share) for w in weights] if direct else []
    blocks = width // SPAN
    pay, mixed, *mine = pl.pallas_call(
        functools.partial(front_kernel, direct=direct),
        in_specs=[smem] + [hbm] * (5 + len(own)),
        out_specs=[hbm] * 2 + [vmem] * len(own),
        out_shape=[
            pltpu.HBM((n_ctx, 2 * PIECE, share) if direct else (2 * PIECE, width), BF16),
            pltpu.HBM((blocks, 2, tokens, SPAN), BF16),
        ]
        + own,
        scratch_shapes=[
            pltpu.VMEM((2, tokens, width), BF16),
            pltpu.VMEM((4, 16, width), BF16),
            pltpu.VMEM(short_weight.shape, F32),
            pltpu.VMEM(ends.shape, BF16),
            pltpu.VMEM((2, 2, 2, 2 * (STRETCH + 8), LANES), F32),
            pltpu.VMEM((2, 2, 32, LANES), F32),
            pltpu.VMEM((2, 2 * PIECE, LANES), F32),
            pltpu.VMEM((blocks, 2 * PIECE, SPAN), BF16),
            pltpu.VMEM((blocks, 2, tokens, SPAN), BF16),
            pltpu.SemaphoreType.DMA((2, blocks)),
            pltpu.SemaphoreType.DMA((4,)),
            pltpu.SemaphoreType.DMA((2,)),
            pltpu.SemaphoreType.DMA((4,)),
            pltpu.SemaphoreType.DMA((2, blocks)),
        ],
        compiler_params=limit(24),
        name="front_pieces",
    )(me, *map(pin, (q_in, k_in, v_in, short_weight, ends)), *(map(pin, weights) if direct else ()))
    arrived = exchange(pay)
    if not direct:
        mine = (cut(short_weight), cut(rates, 0.01), cut(residues), cut(skip))

    query, inner = pl.pallas_call(
        local_kernel,
        grid=(steps,),
        in_specs=[
            columns(tokens),
            pl.BlockSpec((tile // SPAN, 2, tokens, SPAN), lambda c: (c, 0, 0, 0)),
            columns(3, REACH + 1),
            columns(order),
            columns(order),
            columns(1),
            whole(local),
        ],
        out_specs=[pl.BlockSpec((tile // SPAN, tokens, SPAN), lambda c: (c, 0, 0))] * 2,
        out_shape=[pltpu.VMEM((blocks, tokens, SPAN), F32)] * 2,
        scratch_shapes=[pltpu.VMEM((groups, 2 * (STRETCH + 8), LANES), F32)],
        compiler_params=limit(24),
        name="local_filter",
        cost_estimate=pl.CostEstimate(flops=10**9, bytes_accessed=20 * 10**6, transcendentals=0),
    )(*map(pin, (q_in, mixed, short_weight, rates, residues)), skip, local)
    arrived, query, inner = lax.optimization_barrier((arrived, query, inner))

    groups = lanes // LANES
    back = pl.pallas_call(
        middle_kernel,
        in_specs=[smem] + [vmem] * 5,
        out_specs=hbm,
        scratch_shapes=[
            pltpu.VMEM((n_ctx, groups, 8 + 2 * PIECE + 8, LANES), F32),
            pltpu.VMEM((3, groups, slots + 1, 16, LANES), F32),
            pltpu.VMEM((groups, slots, 8, LANES), F32),
            pltpu.VMEM((groups, slots, 16, LANES), F32),
            pltpu.VMEM((groups, slots * 16, LANES), F32),
            pltpu.VMEM((groups, slots, order, LANES), F32),
            pltpu.VMEM((groups, slots, order, LANES), F32),
            pltpu.VMEM((groups, slots * order, LANES), F32),
            pltpu.VMEM((groups, slots * order, LANES), F32),
            pltpu.VMEM((groups, 2, RANK * order, LANES), F32),
            pltpu.VMEM((groups, slots * 24, LANES), F32),
            pltpu.VMEM((n_ctx, groups, BACK + 28, LANES), F32),
            pltpu.VMEM((n_ctx, 2 * BACK, lanes), BF16),
            pltpu.SemaphoreType.DMA((n_ctx,)),
        ],
        out_shape=pltpu.HBM((n_ctx, 2 * BACK, lanes), BF16),
        compiler_params=limit(24),
        name="middle_states",
    )(stretch_of_slot, arrived, *mine)
    if not direct:
        back = back[:, :, :share]
    back = lax.all_to_all(back, "ctx", 0, 0, tiled=True)
    if not direct:
        back = back.transpose(1, 0, 2).reshape(2 * BACK, width)

    keep = lambda array: pltpu.with_memory_space_constraint(array, pltpu.VMEM)
    zvalues, squares = pl.pallas_call(
        join_kernel,
        in_specs=[vmem] * 4,
        out_specs=[vmem] * 2,
        out_shape=[f32(tokens, width), f32(1, tokens)],
        compiler_params=limit(24),
        name="join_carry",
    )(back, lift, keep(query), keep(inner))
    sums = [squares]
    for shift in range(1, n_ch):
        sums.append(lax.ppermute(squares, "ch", [(i, (i + shift) % n_ch) for i in range(n_ch)]))
    return pl.pallas_call(
        functools.partial(scale_kernel, channels=width * n_ch),
        in_specs=[vmem] * (2 + n_ch),
        out_specs=hbm,
        out_shape=pltpu.HBM((tokens, width), BF16),
        scratch_shapes=[pltpu.VMEM((tokens, width), BF16), pltpu.SemaphoreType.DMA((8 if width % 1024 == 0 else 1,))],
        compiler_params=limit(24),
        name="scale_rows",
    )(zvalues, gain, *sums)


def solution(mesh):
    sizes = (mesh.shape["ctx"], mesh.shape["ch"])
    in_specs = (
        P("ctx", "ch"),
        P("ctx", "ch"),
        P("ctx", "ch"),
        P(),
        P(None, None, "ch"),
        P(None, "ch"),
        P(None, "ch"),
        P("ch"),
        P("ch"),
    )

    def run(*arrays):
        return on_device(sizes, *arrays)

    return jax.shard_map(run, mesh=mesh, in_specs=in_specs, out_specs=P("ctx", "ch"), check_vma=False)
```

```python
import functools
from decimal import Decimal, getcontext

import jax
import jax.numpy as jnp
import ml_dtypes
import numpy as np
from jax import lax
from jax.experimental import pallas as pl
from jax.experimental.pallas import tpu as pltpu
from jax.sharding import PartitionSpec as P

F32, BF16 = jnp.float32, jnp.bfloat16
LANES = 128
SPAN = 256
STRETCH = 64
REACH = 6
INNER = STRETCH - REACH
PIVOTS = (8, 49, 21, 56, 36, 1)
ANCHORS = ("0.0020", "0.0235", "0.0110", "0.0295", "0.0185", "0.0004")
RANK = len(PIVOTS)
FINE = 2
COEFS = RANK + FINE
RAW = 6 * REACH
PIECE = RAW + COEFS
BACK = 2 * REACH + COEFS


def shape_table():
    getcontext().prec = 50
    rest = [[(-Decimal(a) * d).exp() for d in range(INNER)] for a in ANCHORS]
    table = []
    for p in range(RANK):
        shape = [x / rest[p][PIVOTS[p]] for x in rest[p]]
        rest = [[x - row[PIVOTS[p]] * y for x, y in zip(row, shape)] for row in rest]
        table.append([float(x) for x in shape])
    return table


SHAPE = shape_table()


def halves(values):
    high = values.astype(ml_dtypes.bfloat16)
    low = (values - high.astype(np.float32)).astype(ml_dtypes.bfloat16)
    return high, low


def constant_matrices():
    shape = np.array(SHAPE, np.float32)
    ends = np.zeros((16, STRETCH), np.float32)
    local = np.zeros((RANK, STRETCH, STRETCH), np.float32)
    lift = np.zeros((2, 2 * STRETCH, 2 * BACK), np.float32)
    parts = [h.astype(np.float32) for h in halves(shape)]
    for p in range(RANK):
        for s in range(REACH, STRETCH):
            ends[p, s] = shape[p, STRETCH - 1 - s]
            local[p, s:, s] = shape[p, : STRETCH - s]
        for half in range(2):
            rows = slice(half * STRETCH + REACH, (half + 1) * STRETCH)
            at = half * BACK + 2 * REACH
            for k in range(2):
                lift[k, rows, at + p] = parts[k][p]
                if p < FINE:
                    lift[k, rows, at + RANK + p] = parts[k][p]
    for half in range(2):
        for t in range(REACH):
            lift[0, half * STRETCH + t, half * BACK + t] = 1.0
            lift[0, half * STRETCH + t, half * BACK + REACH + t] = 1.0
    local = local.reshape(RANK * STRETCH, STRETCH)

    def triple(m):
        h, l = halves(m)
        return np.concatenate([h, h, l], axis=1)

    return triple(ends), triple(local), lift.astype(ml_dtypes.bfloat16)


def strengths(rate):
    found = []
    for p in range(RANK):
        value = jnp.exp(-rate * float(PIVOTS[p]))
        for q in range(p):
            value = value - found[q] * SHAPE[q][PIVOTS[p]]
        found.append(value)
    return found


def split(values):
    high = values.astype(BF16)
    return high, (values - high.astype(F32)).astype(BF16)


def amplitude(rate, residue):
    x = 2.0 * rate
    series = 1.0 - x * (0.5 - x * (1 / 6 - x * (1 / 24 - x * (1 / 120 - x * (1 / 720)))))
    return residue * jnp.sqrt(x * series)


EDGES = (0, STRETCH - 16, STRETCH, 2 * STRETCH - 16)


def front_kernel(*refs, direct):
    me_ref, q_ref, k_ref, v_ref, taps_ref, ends_ref = refs[:6]
    refs = refs[6:]
    weights, refs = (refs[:4], refs[4:]) if direct else ((), refs)
    pay_ref, refs = refs[0], refs[1:]
    kept, refs = (refs[:4], refs[4:]) if direct else ((), refs)
    held, edge, taps_vm, ends_vm, xs, qs, pay, packed, u_vm, in_sems, edge_sems, tap_sem, own_sems, out_sems = refs
    blocks = k_ref.shape[1] // SPAN

    def lanes(c):
        return pl.ds(pl.multiple_of(c * SPAN, SPAN), SPAN)

    def loads(c):
        return [
            pltpu.make_async_copy(ref.at[:, lanes(c)], held.at[a, :, lanes(c)], in_sems.at[a, c])
            for a, ref in enumerate((k_ref, v_ref))
        ] + [pltpu.make_async_copy(taps_ref.at[pl.ds(1, 2), :, lanes(c)], taps_vm.at[c], in_sems.at[2, c])]

    def edge_loads():
        return [
            pltpu.make_async_copy(q_ref.at[pl.ds(at, 16), :], edge.at[e], edge_sems.at[e])
            for e, at in enumerate(EDGES)
        ]

    def stores(c):
        target = pay_ref.at[c] if direct else pay_ref.at[:, lanes(c)]
        return [pltpu.make_async_copy(packed.at[c], target, out_sems.at[c])]

    def own_loads():
        share = kept[0].shape[-1]
        cols = pl.ds(pl.multiple_of(me_ref[0] * share, share), share)
        views = (weights[0].at[:, :, cols], weights[1].at[:, cols], weights[2].at[:, cols], weights[3].at[:, cols])
        return [pltpu.make_async_copy(view, ref, own_sems.at[n]) for n, (view, ref) in enumerate(zip(views, kept))]

    ends_copy = pltpu.make_async_copy(ends_ref, ends_vm, tap_sem.at[0])
    for copy in loads(0) + edge_loads():
        copy.start()
    ends_copy.start()

    def begin(c, carry):
        for copy in loads(c):
            copy.start()
        return carry

    lax.fori_loop(1, blocks, begin, 0)
    if direct:
        for copy in own_loads():
            copy.start()
    for parity in range(2):
        for a in range(2):
            for h in range(2):
                for i in range(2):
                    at = i * (STRETCH + 8)
                    xs[parity, a, h, at : at + 8, :] = jnp.zeros((8, LANES), F32)

    def arrive(c):
        for copy in loads(c):
            copy.wait()

    def features(c):
        parity = lax.rem(c, 2)
        for h in range(2):
            part = slice(h * LANES, (h + 1) * LANES)
            cols = pl.ds(pl.multiple_of(c * SPAN + h * LANES, LANES), LANES)
            for a in range(2):
                for i in range(2):
                    base = i * (STRETCH + 8) + 8
                    xs[parity, a, h, base : base + STRETCH, :] = held[
                        a, i * STRETCH : (i + 1) * STRETCH, cols
                    ].astype(F32)
            taps = [[taps_vm[c, a, j : j + 1, part] for j in range(REACH + 1)] for a in range(2)]
            for i in range(2):
                for b in range(STRETCH // 16):
                    base = i * (STRETCH + 8) + 8 + 16 * b
                    both = []
                    for a in range(2):
                        total = taps[a][0] * xs[parity, a, h, base : base + 16, :]
                        for j in range(1, REACH + 1):
                            total = total + taps[a][j] * xs[parity, a, h, base - j : base - j + 16, :]
                        both.append(total)
                    mixed = both[0] * both[1]
                    if b == 0:
                        row = lax.broadcasted_iota(jnp.int32, (16, LANES), 0)
                        mixed = jnp.where(row >= REACH, mixed, 0.0)
                    high, low = split(mixed)
                    rows = slice(i * STRETCH + 16 * b, i * STRETCH + 16 * b + 16)
                    u_vm[parity, 0, rows, part] = high
                    u_vm[parity, 1, rows, part] = low

    def products(c):
        found = []
        parity = lax.rem(c, 2)
        for i in range(2):
            rows = slice(i * STRETCH, (i + 1) * STRETCH)
            high, low = u_vm[parity, 0, rows, :], u_vm[parity, 1, rows, :]
            stacked = jnp.concatenate([high, low, high], axis=0)
            found.append(jnp.dot(ends_vm[...], stacked, preferred_element_type=F32)[:8])
        return found

    def finish(c, found):
        parity = lax.rem(c, 2)
        for i in range(2):
            moments = found[i]
            rest = (moments - moments.astype(BF16).astype(F32))[:FINE]
            at = PIECE * i + RAW
            for h in range(2):
                part = slice(h * LANES, (h + 1) * LANES)
                pay[h, at : at + RANK, :] = moments[:RANK, part]
                pay[h, at + RANK : at + COEFS, :] = rest[:, part]
        for h in range(2):
            cols = pl.ds(pl.multiple_of(c * SPAN + h * LANES, LANES), LANES)
            for i in range(2):
                base = i * (STRETCH + 8) + 8
                qs[h, i, 0:16, :] = edge[2 * i, :, cols].astype(F32)
                qs[h, i, 16:32, :] = edge[2 * i + 1, :, cols].astype(F32)
                at = i * PIECE
                pay[h, at : at + REACH, :] = qs[h, i, 32 - REACH : 32, :]
                pay[h, at + 3 * REACH : at + 4 * REACH, :] = qs[h, i, 0:REACH, :]
                for a in range(2):
                    at = i * PIECE + (1 + a) * REACH
                    pay[h, at : at + REACH, :] = xs[parity, a, h, base + STRETCH - REACH : base + STRETCH, :]
                    at = at + 3 * REACH
                    pay[h, at : at + REACH, :] = xs[parity, a, h, base : base + REACH, :]
            packed[c, :, h * LANES : (h + 1) * LANES] = pay[h].astype(BF16)

    def send(c):
        for copy in stores(c):
            copy.start()

    arrive(0)
    for copy in edge_loads():
        copy.wait()
    ends_copy.wait()
    features(0)

    def both(c, carry):
        arrive(c)
        found = products(c - 1)
        features(c)
        finish(c - 1, found)
        send(c - 1)
        return carry

    lax.fori_loop(1, blocks, both, 0)
    finish(blocks - 1, products(blocks - 1))
    send(blocks - 1)

    def end(c, carry):
        for copy in stores(c):
            copy.wait()
        return carry

    lax.fori_loop(0, blocks, end, 0)
    if direct:
        for copy in own_loads():
            copy.wait()


def local_kernel(
    q_ref, k_ref, v_ref, taps_ref, rates_ref, res_ref, skip_ref, local_ref, qc_ref, y_ref, xs, u_vm
):
    tile = q_ref.shape[1]
    per = SPAN // LANES
    first_row = lax.broadcasted_iota(jnp.int32, (8, LANES), 0)
    for g in range(tile // LANES):
        cols = slice(g * LANES, (g + 1) * LANES)
        part = slice(g % per * LANES, (g % per + 1) * LANES)
        taps = [[taps_ref[a, j : j + 1, cols] for j in range(REACH + 1)] for a in range(3)]
        for i in range(2):
            base = i * (STRETCH + 8) + 8
            for a, ref in enumerate((q_ref, k_ref, v_ref)):
                xs[a, g, base - 8 : base, :] = jnp.zeros((8, LANES), F32)
                xs[a, g, base : base + STRETCH, :] = ref[i * STRETCH : (i + 1) * STRETCH, cols].astype(F32)
            for b in range(STRETCH // 8):
                at = base + 8 * b
                totals = []
                for a in range(3):
                    total = taps[a][0] * xs[a, g, at : at + 8, :]
                    for j in range(1, REACH + 1):
                        total = total + taps[a][j] * xs[a, g, at - j : at - j + 8, :]
                    totals.append(total)
                query, mixed = totals[0], totals[1] * totals[2]
                if b == 0:
                    query = jnp.where(first_row >= REACH, query, 1.0)
                    mixed = jnp.where(first_row >= REACH, mixed, 0.0)
                rows = slice(i * STRETCH + 8 * b, i * STRETCH + 8 * b + 8)
                qc_ref[g // per, rows, part] = query
                u_vm[g // per, rows, part] = mixed
    for c in range(tile // SPAN):
        cols = slice(c * SPAN, (c + 1) * SPAN)
        rate = rates_ref[:, cols]
        amount = amplitude(rate, res_ref[:, cols])
        weights = [jnp.sum(amount * value, axis=0, keepdims=True) for value in strengths(rate)]
        for i in range(2):
            rows = slice(i * STRETCH, (i + 1) * STRETCH)
            mixed = u_vm[c, rows, :]
            high, low = split(mixed)
            parts = jnp.dot(
                local_ref[...], jnp.concatenate([high, low, high], axis=0), preferred_element_type=F32
            )
            total = skip_ref[:, cols] * mixed
            for p in range(RANK):
                total = total + weights[p] * parts[p * STRETCH : (p + 1) * STRETCH, :]
            y_ref[c, rows, :] = total


def middle_kernel(
    perm_ref, x_ref, taps_ref, rates_ref, res_ref, skip_ref, out_ref,
    raw, ext, moments, past, heads, first, second, states, mids, coefs, result, slab, packed, out_sems,
):
    slots = perm_ref.shape[0]
    groups = x_ref.shape[2] // LANES
    order = rates_ref.shape[0]
    span = 2 * PIECE
    row = lax.broadcasted_iota(jnp.int32, (8, LANES), 0)
    ext[:, :, 0, 0:8, :] = jnp.zeros((3, groups, 8, LANES), F32)
    past[:, :, 0:8, :] = jnp.zeros((groups, slots, 8, LANES), F32)

    def unpack(src, carry):
        for g in range(groups):
            raw[src, g, 8 : 8 + span, :] = x_ref[src, :, g * LANES : (g + 1) * LANES].astype(F32)
        for i in range(2):
            n = perm_ref[2 * src + i]
            for g in range(groups):
                for a in range(3):
                    at = 8 + i * PIECE + a * REACH
                    ext[a, g, n + 1, 0:8, :] = raw[src, g, at + REACH - 8 : at + REACH, :]
                    at = at + 3 * REACH
                    ext[a, g, n, 8:16, :] = raw[src, g, at : at + 8, :]
                at = 8 + i * PIECE + RAW
                fine = jnp.where(row < FINE, raw[src, g, at + RANK : at + RANK + 8, :], 0.0)
                moments[g, n] = raw[src, g, at : at + 8, :] + fine
        return carry

    lax.fori_loop(0, slots // 2, unpack, 0, unroll=2)

    fades = []
    for g in range(groups):
        cols = slice(g * LANES, (g + 1) * LANES)
        rate = rates_ref[:, cols]
        amount = amplitude(rate, res_ref[:, cols])
        basis = strengths(rate)
        powers = [jnp.ones_like(rate), jnp.exp(-rate)]
        for d in range(2, REACH + 1):
            powers.append(powers[-1] * powers[1])
        for t in range(REACH):
            coefs[g, 0, t * order : (t + 1) * order, :] = amount * powers[t + 1]
        for p in range(RANK):
            coefs[g, 1, p * order : (p + 1) * order, :] = amount * powers[1] * basis[p]
        fade_rest = jnp.exp(-rate * float(INNER))
        fades.append((powers[REACH], fade_rest, fade_rest * powers[REACH]))
        taps = [[taps_ref[a, j : j + 1, cols] for j in range(REACH + 1)] for a in range(3)]
        near = [jnp.sum(amount * powers[d], axis=0, keepdims=True) for d in range(REACH)]
        near[0] = near[0] + skip_ref[:, cols]

        def head_pass(n, carry, g=g, taps=taps, powers=powers, near=near):
            feats = []
            for a in range(3):
                total = taps[a][0] * ext[a, g, n, 8:16, :]
                for j in range(1, REACH + 1):
                    total = total + taps[a][j] * ext[a, g, n, 8 - j : 16 - j, :]
                feats.append(jnp.where(row < REACH, total, 0.0))
            mixed = feats[1] * feats[2]
            past[g, n, 8:16, :] = mixed
            total = near[0] * mixed
            for d in range(1, REACH):
                total = total + near[d] * past[g, n, 8 - d : 16 - d, :]
            at = pl.multiple_of(n * 16, 16)
            heads[g, pl.ds(at, 8), :] = feats[0]
            heads[g, pl.ds(at + 8, 8), :] = total
            value = powers[REACH - 1] * past[g, n, 8:9, :]
            for s in range(1, REACH):
                value = value + powers[REACH - 1 - s] * past[g, n, 8 + s : 9 + s, :]
            first[g, n] = value
            return carry

        lax.fori_loop(0, slots, head_pass, 0, unroll=4)

        def rest_pass(n, carry, g=g, basis=basis, fade_rest=fade_rest):
            value = fade_rest * first[g, n]
            for p in range(RANK):
                value = value + basis[p] * moments[g, n, p : p + 1, :]
            second[g, n] = value
            return carry

        lax.fori_loop(0, slots, rest_pass, 0, unroll=4)

    def scan_pass(n, state):
        after = []
        at = pl.multiple_of(n * order, order)
        for g in range(groups):
            states[g, pl.ds(at, order), :] = state[g]
            mids[g, pl.ds(at, order), :] = fades[g][0] * state[g] + first[g, n]
            after.append(fades[g][2] * state[g] + second[g, n])
        return tuple(after)

    lax.fori_loop(0, slots, scan_pass, tuple(jnp.zeros((order, LANES), F32) for _ in range(groups)), unroll=4)

    quad = 4

    def sums(g, kind, held, first_tile):
        totals = [[None] * quad for _ in range(RANK)]
        for r in range(order):
            values = [held[g, pl.ds((first_tile + k) * 8 * order + r, 8, stride=order), :] for k in range(quad)]
            for p in range(RANK):
                weight = coefs[g, kind, p * order + r : p * order + r + 1, :]
                for k in range(quad):
                    term = weight * values[k]
                    totals[p][k] = term if r == 0 else totals[p][k] + term
        return totals

    def out_pass(q, carry):
        for g in range(groups):
            totals = sums(g, 0, states, q * quad)
            for t in range(REACH):
                for k in range(quad):
                    tile = q * quad + k
                    query = heads[g, pl.ds(tile * 128 + t, 8, stride=16), :]
                    local = heads[g, pl.ds(tile * 128 + 8 + t, 8, stride=16), :]
                    z = query * (local + totals[t][k])
                    result[g, pl.ds(tile * 192 + t, 8, stride=24), :] = z
                    result[g, pl.ds(tile * 192 + REACH + t, 8, stride=24), :] = z - z.astype(BF16).astype(F32)
            totals = sums(g, 1, mids, q * quad)
            for p in range(RANK):
                for k in range(quad):
                    tile = q * quad + k
                    value = totals[p][k]
                    result[g, pl.ds(tile * 192 + 2 * REACH + p, 8, stride=24), :] = value
                    if p < FINE:
                        rest = value - value.astype(BF16).astype(F32)
                        result[g, pl.ds(tile * 192 + 2 * REACH + RANK + p, 8, stride=24), :] = rest
        return carry

    lax.fori_loop(0, slots // (8 * quad), out_pass, 0)

    def store(src):
        return pltpu.make_async_copy(packed.at[src], out_ref.at[src], out_sems.at[src])

    def pack(src, carry):
        for g in range(groups):
            for i in range(2):
                at = pl.multiple_of(perm_ref[2 * src + i] * 24, 8)
                slab[src, g, i * BACK : i * BACK + 24, :] = result[g, pl.ds(at, 24), :]
            packed[src, :, g * LANES : (g + 1) * LANES] = slab[src, g, 0 : 2 * BACK, :].astype(BF16)
        return carry

    lax.fori_loop(0, slots // 2, pack, 0, unroll=2)

    def send(src, carry):
        store(src).start()
        return carry

    def end(src, carry):
        store(src).wait()
        return carry

    lax.fori_loop(0, slots // 2, send, 0)
    lax.fori_loop(0, slots // 2, end, 0)


def join_kernel(back_ref, lift_ref, qc_ref, y_ref, z_ref, sq_ref, qc_vm, carry, sems):
    blocks, tokens, _ = qc_vm.shape
    by_dest = len(back_ref.shape) == 3
    chunk = 4
    copies = []
    for c in range(blocks // chunk):
        rows = pl.ds(c * chunk, chunk)
        copies.append(pltpu.make_async_copy(qc_ref.at[rows], qc_vm.at[rows], sems.at[c]))
        copies[-1].start()
    for b in range(blocks):
        back = back_ref[b] if by_dest else back_ref[:, b * SPAN : (b + 1) * SPAN]
        product = jnp.dot(lift_ref[0], back, preferred_element_type=F32)
        carry[b] = y_ref[b] + product + jnp.dot(lift_ref[1], back, preferred_element_type=F32)
    total = jnp.zeros((tokens, LANES), F32)
    for c in range(blocks // chunk):
        copies[c].wait()
        for b in range(c * chunk, (c + 1) * chunk):
            z = qc_vm[b] * carry[b]
            z_ref[:, b * SPAN : (b + 1) * SPAN] = z
            squares = z * z
            for h in range(SPAN // LANES):
                total = total + squares[:, h * LANES : (h + 1) * LANES]
    sq_ref[...] = jnp.sum(total.T, axis=0, keepdims=True)


def scale_kernel(*refs, channels):
    z_ref, gain_ref, refs, (out_ref, held, sems) = refs[0], refs[1], refs[2:-3], refs[-3:]
    tokens, width = z_ref.shape
    chunks = sems.shape[0]
    wide = width // chunks
    total = refs[0][...]
    for ref in refs[1:]:
        total = total + ref[...]
    scale = lax.rsqrt(total / channels + 1e-05)
    scale = jnp.broadcast_to(scale, (LANES, tokens)).T
    copies = []
    for c in range(chunks):
        for g in range(c * wide // LANES, (c + 1) * wide // LANES):
            cols = slice(g * LANES, (g + 1) * LANES)
            held[:, cols] = (z_ref[:, cols] * scale * gain_ref[:, cols]).astype(BF16)
        cols = pl.ds(c * wide, wide)
        copy = pltpu.make_async_copy(held.at[:, cols], out_ref.at[:, cols], sems.at[c])
        copy.start()
        copies.append(copy)
    for copy in copies:
        copy.wait()


def limit(mib):
    return pltpu.CompilerParams(vmem_limit_bytes=mib * 1024 * 1024)


def on_device(sizes, q_in, k_in, v_in, stretch_of_slot, short_weight, rates, residues, skip, gain):
    n_ctx, n_ch = sizes
    tokens, width = q_in.shape
    slots = stretch_of_slot.shape[0]
    order = rates.shape[0]
    share = width // n_ctx
    direct = share == SPAN
    tile = min(width, 1024)
    steps = width // tile
    groups = tile // LANES
    ends_np, local_np, lift_np = constant_matrices()
    ends, local, lift = jnp.asarray(ends_np), jnp.asarray(local_np), jnp.asarray(lift_np)
    skip, gain = skip.reshape(1, width), gain.reshape(1, width)
    me = lax.axis_index("ctx").astype(jnp.int32).reshape(1)

    def whole(array):
        return pl.BlockSpec(array.shape, lambda c: (0,) * array.ndim)

    def columns(*lead):
        return pl.BlockSpec((*lead, tile), lambda c: (0,) * len(lead) + (c,))

    def exchange(array):
        if direct:
            return lax.all_to_all(array, "ctx", 0, 0, tiled=True)
        array = array.reshape(array.shape[0], n_ctx, share).transpose(1, 0, 2)
        return widen(lax.all_to_all(array, "ctx", 0, 0, tiled=True))

    lanes = -(-share // LANES) * LANES

    def widen(array, fill=0.0):
        pad = [(0, 0)] * (array.ndim - 1) + [(0, lanes - share)]
        return jnp.pad(array, pad, constant_values=fill)

    def cut(array, fill=0.0):
        return widen(lax.dynamic_slice_in_dim(array, lax.axis_index("ctx") * share, share, array.ndim - 1), fill)

    smem = pl.BlockSpec(memory_space=pltpu.SMEM)
    vmem = pl.BlockSpec(memory_space=pltpu.VMEM)
    hbm = pl.BlockSpec(memory_space=pltpu.HBM)
    f32 = lambda *shape: jax.ShapeDtypeStruct(shape, F32)
    pin = lambda array: pltpu.with_memory_space_constraint(array, pltpu.HBM)

    weights = (short_weight, rates, residues, skip)
    own = [f32(*w.shape[:-1], share) for w in weights] if direct else []
    blocks = width // SPAN
    pay, *mine = pl.pallas_call(
        functools.partial(front_kernel, direct=direct),
        in_specs=[smem] + [hbm] * (5 + len(own)),
        out_specs=[hbm] + [vmem] * len(own),
        out_shape=[
            pltpu.HBM((n_ctx, 2 * PIECE, share) if direct else (2 * PIECE, width), BF16),
        ]
        + own,
        scratch_shapes=[
            pltpu.VMEM((2, tokens, width), BF16),
            pltpu.VMEM((4, 16, width), BF16),
            pltpu.VMEM((blocks, 2, REACH + 1, SPAN), F32),
            pltpu.VMEM(ends.shape, BF16),
            pltpu.VMEM((2, 2, 2, 2 * (STRETCH + 8), LANES), F32),
            pltpu.VMEM((2, 2, 32, LANES), F32),
            pltpu.VMEM((2, 2 * PIECE, LANES), F32),
            pltpu.VMEM((blocks, 2 * PIECE, SPAN), BF16),
            pltpu.VMEM((2, 2, tokens, SPAN), BF16),
            pltpu.SemaphoreType.DMA((3, blocks)),
            pltpu.SemaphoreType.DMA((4,)),
            pltpu.SemaphoreType.DMA((1,)),
            pltpu.SemaphoreType.DMA((4,)),
            pltpu.SemaphoreType.DMA((blocks,)),
        ],
        compiler_params=limit(24),
        name="front_pieces",
    )(me, *map(pin, (q_in, k_in, v_in, short_weight, ends)), *(map(pin, weights) if direct else ()))
    arrived = exchange(pay)
    if not direct:
        mine = (cut(short_weight), cut(rates, 0.01), cut(residues), cut(skip))

    query, inner = pl.pallas_call(
        local_kernel,
        grid=(steps,),
        in_specs=[columns(tokens)] * 3
        + [columns(3, REACH + 1), columns(order), columns(order), columns(1), whole(local)],
        out_specs=[pl.BlockSpec((tile // SPAN, tokens, SPAN), lambda c: (c, 0, 0))] * 2,
        out_shape=[pltpu.HBM((blocks, tokens, SPAN), F32), pltpu.VMEM((blocks, tokens, SPAN), F32)],
        scratch_shapes=[
            pltpu.VMEM((3, groups, 2 * (STRETCH + 8), LANES), F32),
            pltpu.VMEM((tile // SPAN, tokens, SPAN), F32),
        ],
        compiler_params=limit(24),
        name="local_filter",
        cost_estimate=pl.CostEstimate(flops=10**9, bytes_accessed=20 * 10**6, transcendentals=0),
    )(*map(pin, (q_in, k_in, v_in, short_weight, rates, residues)), skip, local)
    arrived, query, inner = lax.optimization_barrier((arrived, query, inner))

    groups = lanes // LANES
    back = pl.pallas_call(
        middle_kernel,
        in_specs=[smem] + [vmem] * 5,
        out_specs=hbm,
        scratch_shapes=[
            pltpu.VMEM((n_ctx, groups, 8 + 2 * PIECE + 8, LANES), F32),
            pltpu.VMEM((3, groups, slots + 1, 16, LANES), F32),
            pltpu.VMEM((groups, slots, 8, LANES), F32),
            pltpu.VMEM((groups, slots, 16, LANES), F32),
            pltpu.VMEM((groups, slots * 16, LANES), F32),
            pltpu.VMEM((groups, slots, order, LANES), F32),
            pltpu.VMEM((groups, slots, order, LANES), F32),
            pltpu.VMEM((groups, slots * order, LANES), F32),
            pltpu.VMEM((groups, slots * order, LANES), F32),
            pltpu.VMEM((groups, 2, RANK * order, LANES), F32),
            pltpu.VMEM((groups, slots * 24, LANES), F32),
            pltpu.VMEM((n_ctx, groups, BACK + 28, LANES), F32),
            pltpu.VMEM((n_ctx, 2 * BACK, lanes), BF16),
            pltpu.SemaphoreType.DMA((n_ctx,)),
        ],
        out_shape=pltpu.HBM((n_ctx, 2 * BACK, lanes), BF16),
        compiler_params=limit(24),
        name="middle_states",
    )(stretch_of_slot, arrived, *mine)
    if not direct:
        back = back[:, :, :share]
    back = lax.all_to_all(back, "ctx", 0, 0, tiled=True)
    if not direct:
        back = back.transpose(1, 0, 2).reshape(2 * BACK, width)

    keep = lambda array: pltpu.with_memory_space_constraint(array, pltpu.VMEM)
    zvalues, squares = pl.pallas_call(
        join_kernel,
        in_specs=[vmem] * 2 + [hbm, vmem],
        out_specs=[vmem] * 2,
        out_shape=[f32(tokens, width), f32(1, tokens)],
        scratch_shapes=[pltpu.VMEM((blocks, tokens, SPAN), F32)] * 2 + [pltpu.SemaphoreType.DMA((blocks // 4,))],
        compiler_params=limit(24),
        name="join_carry",
    )(back, lift, pin(query), keep(inner))
    sums = [squares]
    for shift in range(1, n_ch):
        sums.append(lax.ppermute(squares, "ch", [(i, (i + shift) % n_ch) for i in range(n_ch)]))
    return pl.pallas_call(
        functools.partial(scale_kernel, channels=width * n_ch),
        in_specs=[vmem] * (2 + n_ch),
        out_specs=hbm,
        out_shape=pltpu.HBM((tokens, width), BF16),
        scratch_shapes=[pltpu.VMEM((tokens, width), BF16), pltpu.SemaphoreType.DMA((8 if width % 1024 == 0 else 1,))],
        compiler_params=limit(24),
        name="scale_rows",
    )(zvalues, gain, *sums)


def solution(mesh):
    sizes = (mesh.shape["ctx"], mesh.shape["ch"])
    in_specs = (
        P("ctx", "ch"),
        P("ctx", "ch"),
        P("ctx", "ch"),
        P(),
        P(None, None, "ch"),
        P(None, "ch"),
        P(None, "ch"),
        P("ch"),
        P("ch"),
    )

    def run(*arrays):
        return on_device(sizes, *arrays)

    return jax.shard_map(run, mesh=mesh, in_specs=in_specs, out_specs=P("ctx", "ch"), check_vma=False)
```

```python
import functools
from decimal import Decimal, getcontext

import jax
import jax.numpy as jnp
import ml_dtypes
import numpy as np
from jax import lax
from jax.experimental import pallas as pl
from jax.experimental.pallas import tpu as pltpu
from jax.sharding import PartitionSpec as P

F32, BF16 = jnp.float32, jnp.bfloat16
LANES = 128
SPAN = 256
STRETCH = 64
REACH = 6
INNER = STRETCH - REACH
PIVOTS = (8, 49, 21, 56, 36, 1)
ANCHORS = ("0.0020", "0.0235", "0.0110", "0.0295", "0.0185", "0.0004")
RANK = len(PIVOTS)
FINE = 2
COEFS = RANK + FINE
RAW = 6 * REACH
PIECE = RAW + COEFS
BACK = 2 * REACH + COEFS


def shape_table():
    getcontext().prec = 50
    rest = [[(-Decimal(a) * d).exp() for d in range(INNER)] for a in ANCHORS]
    table = []
    for p in range(RANK):
        shape = [x / rest[p][PIVOTS[p]] for x in rest[p]]
        rest = [[x - row[PIVOTS[p]] * y for x, y in zip(row, shape)] for row in rest]
        table.append([float(x) for x in shape])
    return table


SHAPE = shape_table()


def halves(values):
    high = values.astype(ml_dtypes.bfloat16)
    low = (values - high.astype(np.float32)).astype(ml_dtypes.bfloat16)
    return high, low


def constant_matrices():
    shape = np.array(SHAPE, np.float32)
    ends = np.zeros((16, STRETCH), np.float32)
    local = np.zeros((RANK, STRETCH, STRETCH), np.float32)
    lift = np.zeros((2, 2 * STRETCH, 2 * BACK), np.float32)
    parts = [h.astype(np.float32) for h in halves(shape)]
    for p in range(RANK):
        for s in range(REACH, STRETCH):
            ends[p, s] = shape[p, STRETCH - 1 - s]
            local[p, s:, s] = shape[p, : STRETCH - s]
        for half in range(2):
            rows = slice(half * STRETCH + REACH, (half + 1) * STRETCH)
            at = half * BACK + 2 * REACH
            for k in range(2):
                lift[k, rows, at + p] = parts[k][p]
                if p < FINE:
                    lift[k, rows, at + RANK + p] = parts[k][p]
    for half in range(2):
        for t in range(REACH):
            lift[0, half * STRETCH + t, half * BACK + t] = 1.0
            lift[0, half * STRETCH + t, half * BACK + REACH + t] = 1.0
    local = local.reshape(RANK * STRETCH, STRETCH)

    def triple(m):
        h, l = halves(m)
        return np.concatenate([h, h, l], axis=1)

    return triple(ends), triple(local), lift.astype(ml_dtypes.bfloat16)


def strengths(rate):
    found = []
    for p in range(RANK):
        value = jnp.exp(-rate * float(PIVOTS[p]))
        for q in range(p):
            value = value - found[q] * SHAPE[q][PIVOTS[p]]
        found.append(value)
    return found


def split(values):
    high = values.astype(BF16)
    return high, (values - high.astype(F32)).astype(BF16)


def amplitude(rate, residue):
    x = 2.0 * rate
    series = 1.0 - x * (0.5 - x * (1 / 6 - x * (1 / 24 - x * (1 / 120 - x * (1 / 720)))))
    return residue * jnp.sqrt(x * series)


EDGES = (0, STRETCH - 16, STRETCH, 2 * STRETCH - 16)


def front_kernel(*refs, direct):
    me_ref, q_ref, k_ref, v_ref, taps_ref, ends_ref = refs[:6]
    refs = refs[6:]
    weights, refs = (refs[:4], refs[4:]) if direct else ((), refs)
    pay_ref, refs = refs[0], refs[1:]
    kept, refs = (refs[:4], refs[4:]) if direct else ((), refs)
    held, edge, taps_vm, ends_vm, xs, qs, pay, packed, u_vm, in_sems, edge_sems, tap_sem, own_sems, out_sems = refs
    blocks = k_ref.shape[1] // SPAN

    def lanes(c):
        return pl.ds(pl.multiple_of(c * SPAN, SPAN), SPAN)

    def loads(c):
        return [
            pltpu.make_async_copy(ref.at[:, lanes(c)], held.at[a, :, lanes(c)], in_sems.at[a, c])
            for a, ref in enumerate((k_ref, v_ref))
        ] + [pltpu.make_async_copy(taps_ref.at[pl.ds(1, 2), :, lanes(c)], taps_vm.at[c], in_sems.at[2, c])]

    def edge_loads():
        return [
            pltpu.make_async_copy(q_ref.at[pl.ds(at, 16), :], edge.at[e], edge_sems.at[e])
            for e, at in enumerate(EDGES)
        ]

    def stores(c):
        target = pay_ref.at[c] if direct else pay_ref.at[:, lanes(c)]
        return [pltpu.make_async_copy(packed.at[c], target, out_sems.at[c])]

    def own_loads():
        share = kept[0].shape[-1]
        cols = pl.ds(pl.multiple_of(me_ref[0] * share, share), share)
        views = (weights[0].at[:, :, cols], weights[1].at[:, cols], weights[2].at[:, cols], weights[3].at[:, cols])
        return [pltpu.make_async_copy(view, ref, own_sems.at[n]) for n, (view, ref) in enumerate(zip(views, kept))]

    ends_copy = pltpu.make_async_copy(ends_ref, ends_vm, tap_sem.at[0])
    for copy in edge_loads() + loads(0) + loads(1):
        copy.start()
    ends_copy.start()

    def begin(c, carry):
        for copy in loads(c):
            copy.start()
        return carry

    lax.fori_loop(2, blocks, begin, 0)
    if direct:
        for copy in own_loads():
            copy.start()
    for parity in range(4):
        for a in range(2):
            for h in range(2):
                for i in range(2):
                    at = i * (STRETCH + 8)
                    xs[parity, a, h, at : at + 8, :] = jnp.zeros((8, LANES), F32)

    def arrive(c):
        for copy in loads(c):
            copy.wait()

    def features(c):
        parity = lax.rem(c, 4)
        for h in range(2):
            part = slice(h * LANES, (h + 1) * LANES)
            cols = pl.ds(pl.multiple_of(c * SPAN + h * LANES, LANES), LANES)
            for a in range(2):
                for i in range(2):
                    base = i * (STRETCH + 8) + 8
                    xs[parity, a, h, base : base + STRETCH, :] = held[
                        a, i * STRETCH : (i + 1) * STRETCH, cols
                    ].astype(F32)
            taps = [[taps_vm[c, a, j : j + 1, part] for j in range(REACH + 1)] for a in range(2)]
            for i in range(2):
                for b in range(STRETCH // 16):
                    base = i * (STRETCH + 8) + 8 + 16 * b
                    both = []
                    for a in range(2):
                        total = taps[a][0] * xs[parity, a, h, base : base + 16, :]
                        for j in range(1, REACH + 1):
                            total = total + taps[a][j] * xs[parity, a, h, base - j : base - j + 16, :]
                        both.append(total)
                    mixed = both[0] * both[1]
                    if b == 0:
                        row = lax.broadcasted_iota(jnp.int32, (16, LANES), 0)
                        mixed = jnp.where(row >= REACH, mixed, 0.0)
                    high, low = split(mixed)
                    rows = slice(i * STRETCH + 16 * b, i * STRETCH + 16 * b + 16)
                    u_vm[parity, 0, rows, part] = high
                    u_vm[parity, 1, rows, part] = low

    def products(c):
        found = []
        parity = lax.rem(c, 4)
        for i in range(2):
            rows = slice(i * STRETCH, (i + 1) * STRETCH)
            high, low = u_vm[parity, 0, rows, :], u_vm[parity, 1, rows, :]
            stacked = jnp.concatenate([high, low, high], axis=0)
            found.append(jnp.dot(ends_vm[...], stacked, preferred_element_type=F32)[:8])
        return found

    def query_rows(c, carry):
        for h in range(2):
            cols = pl.ds(pl.multiple_of(c * SPAN + h * LANES, LANES), LANES)
            for i in range(2):
                qs[h, i, 0:16, :] = edge[2 * i, :, cols].astype(F32)
                qs[h, i, 16:32, :] = edge[2 * i + 1, :, cols].astype(F32)
                at = i * PIECE
                pay[c, h, at : at + REACH, :] = qs[h, i, 32 - REACH : 32, :]
                pay[c, h, at + 3 * REACH : at + 4 * REACH, :] = qs[h, i, 0:REACH, :]
        return carry

    def finish(c, found):
        parity = lax.rem(c, 4)
        for i in range(2):
            moments = found[i]
            rest = (moments - moments.astype(BF16).astype(F32))[:FINE]
            at = PIECE * i + RAW
            for h in range(2):
                part = slice(h * LANES, (h + 1) * LANES)
                pay[c, h, at : at + RANK, :] = moments[:RANK, part]
                pay[c, h, at + RANK : at + COEFS, :] = rest[:, part]
        for h in range(2):
            for i in range(2):
                base = i * (STRETCH + 8) + 8
                for a in range(2):
                    at = i * PIECE + (1 + a) * REACH
                    pay[c, h, at : at + REACH, :] = xs[parity, a, h, base + STRETCH - REACH : base + STRETCH, :]
                    at = at + 3 * REACH
                    pay[c, h, at : at + REACH, :] = xs[parity, a, h, base : base + REACH, :]
            packed[c, :, h * LANES : (h + 1) * LANES] = pay[c, h].astype(BF16)

    def send(c):
        for copy in stores(c):
            copy.start()

    for copy in edge_loads():
        copy.wait()
    lax.fori_loop(0, blocks, query_rows, 0, unroll=2)
    ends_copy.wait()
    arrive(0)
    arrive(1)
    features(0)
    features(1)

    def both(step, carry):
        c = 2 * step
        arrive(c)
        arrive(c + 1)
        before = [products(c - 2), products(c - 1)]
        features(c)
        finish(c - 2, before[0])
        features(c + 1)
        finish(c - 1, before[1])
        send(c - 2)
        send(c - 1)
        return carry

    lax.fori_loop(1, blocks // 2, both, 0)
    for c in (blocks - 2, blocks - 1):
        finish(c, products(c))
    send(blocks - 2)
    send(blocks - 1)

    def end(c, carry):
        for copy in stores(c):
            copy.wait()
        return carry

    lax.fori_loop(0, blocks, end, 0)
    if direct:
        for copy in own_loads():
            copy.wait()


def local_kernel(
    q_ref, k_ref, v_ref, taps_ref, rates_ref, res_ref, skip_ref, local_ref, qc_ref, y_ref, xs, u_vm
):
    tile = q_ref.shape[1]
    per = SPAN // LANES
    first_row = lax.broadcasted_iota(jnp.int32, (8, LANES), 0)
    for g in range(tile // LANES):
        cols = slice(g * LANES, (g + 1) * LANES)
        part = slice(g % per * LANES, (g % per + 1) * LANES)
        taps = [[taps_ref[a, j : j + 1, cols] for j in range(REACH + 1)] for a in range(3)]
        for i in range(2):
            base = i * (STRETCH + 8) + 8
            for a, ref in enumerate((q_ref, k_ref, v_ref)):
                xs[a, g, base - 8 : base, :] = jnp.zeros((8, LANES), F32)
                xs[a, g, base : base + STRETCH, :] = ref[i * STRETCH : (i + 1) * STRETCH, cols].astype(F32)
            for b in range(STRETCH // 8):
                at = base + 8 * b
                totals = []
                for a in range(3):
                    total = taps[a][0] * xs[a, g, at : at + 8, :]
                    for j in range(1, REACH + 1):
                        total = total + taps[a][j] * xs[a, g, at - j : at - j + 8, :]
                    totals.append(total)
                query, mixed = totals[0], totals[1] * totals[2]
                if b == 0:
                    query = jnp.where(first_row >= REACH, query, 1.0)
                    mixed = jnp.where(first_row >= REACH, mixed, 0.0)
                rows = slice(i * STRETCH + 8 * b, i * STRETCH + 8 * b + 8)
                qc_ref[g // per, rows, part] = query
                u_vm[g // per, rows, part] = mixed
    for c in range(tile // SPAN):
        cols = slice(c * SPAN, (c + 1) * SPAN)
        rate = rates_ref[:, cols]
        amount = amplitude(rate, res_ref[:, cols])
        weights = [jnp.sum(amount * value, axis=0, keepdims=True) for value in strengths(rate)]
        for i in range(2):
            rows = slice(i * STRETCH, (i + 1) * STRETCH)
            mixed = u_vm[c, rows, :]
            high, low = split(mixed)
            parts = jnp.dot(
                local_ref[...], jnp.concatenate([high, low, high], axis=0), preferred_element_type=F32
            )
            total = skip_ref[:, cols] * mixed
            for p in range(RANK):
                total = total + weights[p] * parts[p * STRETCH : (p + 1) * STRETCH, :]
            y_ref[c, rows, :] = total


def middle_kernel(
    perm_ref, x_ref, taps_ref, rates_ref, res_ref, skip_ref, out_ref,
    raw, ext, moments, past, heads, first, second, states, mids, coefs, result, slab, packed, out_sems,
):
    slots = perm_ref.shape[0]
    groups = x_ref.shape[2] // LANES
    order = rates_ref.shape[0]
    span = 2 * PIECE
    row = lax.broadcasted_iota(jnp.int32, (8, LANES), 0)
    ext[:, :, 0, 0:8, :] = jnp.zeros((3, groups, 8, LANES), F32)
    past[:, :, 0:8, :] = jnp.zeros((groups, slots, 8, LANES), F32)

    def unpack(src, carry):
        for g in range(groups):
            raw[src, g, 8 : 8 + span, :] = x_ref[src, :, g * LANES : (g + 1) * LANES].astype(F32)
        for i in range(2):
            n = perm_ref[2 * src + i]
            for g in range(groups):
                for a in range(3):
                    at = 8 + i * PIECE + a * REACH
                    ext[a, g, n + 1, 0:8, :] = raw[src, g, at + REACH - 8 : at + REACH, :]
                    at = at + 3 * REACH
                    ext[a, g, n, 8:16, :] = raw[src, g, at : at + 8, :]
                at = 8 + i * PIECE + RAW
                fine = jnp.where(row < FINE, raw[src, g, at + RANK : at + RANK + 8, :], 0.0)
                moments[g, n] = raw[src, g, at : at + 8, :] + fine
        return carry

    lax.fori_loop(0, slots // 2, unpack, 0, unroll=2)

    fades = []
    for g in range(groups):
        cols = slice(g * LANES, (g + 1) * LANES)
        rate = rates_ref[:, cols]
        amount = amplitude(rate, res_ref[:, cols])
        basis = strengths(rate)
        powers = [jnp.ones_like(rate), jnp.exp(-rate)]
        for d in range(2, REACH + 1):
            powers.append(powers[-1] * powers[1])
        for t in range(REACH):
            coefs[g, 0, t * order : (t + 1) * order, :] = amount * powers[t + 1]
        for p in range(RANK):
            coefs[g, 1, p * order : (p + 1) * order, :] = amount * powers[1] * basis[p]
        fade_rest = jnp.exp(-rate * float(INNER))
        fades.append((powers[REACH], fade_rest, fade_rest * powers[REACH]))
        taps = [[taps_ref[a, j : j + 1, cols] for j in range(REACH + 1)] for a in range(3)]
        near = [jnp.sum(amount * powers[d], axis=0, keepdims=True) for d in range(REACH)]
        near[0] = near[0] + skip_ref[:, cols]

        def head_pass(n, carry, g=g, taps=taps, powers=powers, near=near):
            feats = []
            for a in range(3):
                total = taps[a][0] * ext[a, g, n, 8:16, :]
                for j in range(1, REACH + 1):
                    total = total + taps[a][j] * ext[a, g, n, 8 - j : 16 - j, :]
                feats.append(jnp.where(row < REACH, total, 0.0))
            mixed = feats[1] * feats[2]
            past[g, n, 8:16, :] = mixed
            total = near[0] * mixed
            for d in range(1, REACH):
                total = total + near[d] * past[g, n, 8 - d : 16 - d, :]
            at = pl.multiple_of(n * 16, 16)
            heads[g, pl.ds(at, 8), :] = feats[0]
            heads[g, pl.ds(at + 8, 8), :] = total
            value = powers[REACH - 1] * past[g, n, 8:9, :]
            for s in range(1, REACH):
                value = value + powers[REACH - 1 - s] * past[g, n, 8 + s : 9 + s, :]
            first[g, n] = value
            return carry

        lax.fori_loop(0, slots, head_pass, 0, unroll=4)

        def rest_pass(n, carry, g=g, basis=basis, fade_rest=fade_rest):
            value = fade_rest * first[g, n]
            for p in range(RANK):
                value = value + basis[p] * moments[g, n, p : p + 1, :]
            second[g, n] = value
            return carry

        lax.fori_loop(0, slots, rest_pass, 0, unroll=4)

    def scan_pass(n, state):
        after = []
        at = pl.multiple_of(n * order, order)
        for g in range(groups):
            states[g, pl.ds(at, order), :] = state[g]
            mids[g, pl.ds(at, order), :] = fades[g][0] * state[g] + first[g, n]
            after.append(fades[g][2] * state[g] + second[g, n])
        return tuple(after)

    lax.fori_loop(0, slots, scan_pass, tuple(jnp.zeros((order, LANES), F32) for _ in range(groups)), unroll=4)

    quad = 4

    def sums(g, kind, held, first_tile):
        totals = [[None] * quad for _ in range(RANK)]
        for r in range(order):
            values = [held[g, pl.ds((first_tile + k) * 8 * order + r, 8, stride=order), :] for k in range(quad)]
            for p in range(RANK):
                weight = coefs[g, kind, p * order + r : p * order + r + 1, :]
                for k in range(quad):
                    term = weight * values[k]
                    totals[p][k] = term if r == 0 else totals[p][k] + term
        return totals

    def out_pass(q, carry):
        for g in range(groups):
            totals = sums(g, 0, states, q * quad)
            for t in range(REACH):
                for k in range(quad):
                    tile = q * quad + k
                    query = heads[g, pl.ds(tile * 128 + t, 8, stride=16), :]
                    local = heads[g, pl.ds(tile * 128 + 8 + t, 8, stride=16), :]
                    z = query * (local + totals[t][k])
                    result[g, pl.ds(tile * 192 + t, 8, stride=24), :] = z
                    result[g, pl.ds(tile * 192 + REACH + t, 8, stride=24), :] = z - z.astype(BF16).astype(F32)
            totals = sums(g, 1, mids, q * quad)
            for p in range(RANK):
                for k in range(quad):
                    tile = q * quad + k
                    value = totals[p][k]
                    result[g, pl.ds(tile * 192 + 2 * REACH + p, 8, stride=24), :] = value
                    if p < FINE:
                        rest = value - value.astype(BF16).astype(F32)
                        result[g, pl.ds(tile * 192 + 2 * REACH + RANK + p, 8, stride=24), :] = rest
        return carry

    lax.fori_loop(0, slots // (8 * quad), out_pass, 0)

    def store(src):
        return pltpu.make_async_copy(packed.at[src], out_ref.at[src], out_sems.at[src])

    def pack(src, carry):
        for g in range(groups):
            for i in range(2):
                at = pl.multiple_of(perm_ref[2 * src + i] * 24, 8)
                slab[src, g, i * BACK : i * BACK + 24, :] = result[g, pl.ds(at, 24), :]
            packed[src, :, g * LANES : (g + 1) * LANES] = slab[src, g, 0 : 2 * BACK, :].astype(BF16)
        return carry

    lax.fori_loop(0, slots // 2, pack, 0, unroll=2)

    def send(src, carry):
        store(src).start()
        return carry

    def end(src, carry):
        store(src).wait()
        return carry

    lax.fori_loop(0, slots // 2, send, 0)
    lax.fori_loop(0, slots // 2, end, 0)


def join_kernel(back_ref, lift_ref, qc_ref, y_ref, z_ref, sq_ref, qc_vm, carry, sems):
    blocks, tokens, _ = qc_vm.shape
    by_dest = len(back_ref.shape) == 3
    chunk = 4
    copies = []
    for c in range(blocks // chunk):
        rows = pl.ds(c * chunk, chunk)
        copies.append(pltpu.make_async_copy(qc_ref.at[rows], qc_vm.at[rows], sems.at[c]))
        copies[-1].start()
    for b in range(blocks):
        back = back_ref[b] if by_dest else back_ref[:, b * SPAN : (b + 1) * SPAN]
        product = jnp.dot(lift_ref[0], back, preferred_element_type=F32)
        carry[b] = y_ref[b] + product + jnp.dot(lift_ref[1], back, preferred_element_type=F32)
    total = jnp.zeros((tokens, LANES), F32)
    for c in range(blocks // chunk):
        copies[c].wait()
        for b in range(c * chunk, (c + 1) * chunk):
            z = qc_vm[b] * carry[b]
            z_ref[:, b * SPAN : (b + 1) * SPAN] = z
            squares = z * z
            for h in range(SPAN // LANES):
                total = total + squares[:, h * LANES : (h + 1) * LANES]
    sq_ref[...] = jnp.sum(total.T, axis=0, keepdims=True)


def scale_kernel(*refs, channels):
    z_ref, gain_ref, refs, (out_ref, held, sems) = refs[0], refs[1], refs[2:-3], refs[-3:]
    tokens, width = z_ref.shape
    chunks = sems.shape[0]
    wide = width // chunks
    total = refs[0][...]
    for ref in refs[1:]:
        total = total + ref[...]
    scale = lax.rsqrt(total / channels + 1e-05)
    scale = jnp.broadcast_to(scale, (LANES, tokens)).T
    copies = []
    for c in range(chunks):
        for g in range(c * wide // LANES, (c + 1) * wide // LANES):
            cols = slice(g * LANES, (g + 1) * LANES)
            held[:, cols] = (z_ref[:, cols] * scale * gain_ref[:, cols]).astype(BF16)
        cols = pl.ds(c * wide, wide)
        copy = pltpu.make_async_copy(held.at[:, cols], out_ref.at[:, cols], sems.at[c])
        copy.start()
        copies.append(copy)
    for copy in copies:
        copy.wait()


def limit(mib):
    return pltpu.CompilerParams(vmem_limit_bytes=mib * 1024 * 1024)


def on_device(sizes, q_in, k_in, v_in, stretch_of_slot, short_weight, rates, residues, skip, gain):
    n_ctx, n_ch = sizes
    tokens, width = q_in.shape
    slots = stretch_of_slot.shape[0]
    order = rates.shape[0]
    share = width // n_ctx
    direct = share == SPAN
    tile = min(width, 1024)
    steps = width // tile
    groups = tile // LANES
    ends_np, local_np, lift_np = constant_matrices()
    ends, local, lift = jnp.asarray(ends_np), jnp.asarray(local_np), jnp.asarray(lift_np)
    skip, gain = skip.reshape(1, width), gain.reshape(1, width)
    me = lax.axis_index("ctx").astype(jnp.int32).reshape(1)

    def whole(array):
        return pl.BlockSpec(array.shape, lambda c: (0,) * array.ndim)

    def columns(*lead):
        return pl.BlockSpec((*lead, tile), lambda c: (0,) * len(lead) + (c,))

    def exchange(array):
        if direct:
            return lax.all_to_all(array, "ctx", 0, 0, tiled=True)
        array = array.reshape(array.shape[0], n_ctx, share).transpose(1, 0, 2)
        return widen(lax.all_to_all(array, "ctx", 0, 0, tiled=True))

    lanes = -(-share // LANES) * LANES

    def widen(array, fill=0.0):
        pad = [(0, 0)] * (array.ndim - 1) + [(0, lanes - share)]
        return jnp.pad(array, pad, constant_values=fill)

    def cut(array, fill=0.0):
        return widen(lax.dynamic_slice_in_dim(array, lax.axis_index("ctx") * share, share, array.ndim - 1), fill)

    smem = pl.BlockSpec(memory_space=pltpu.SMEM)
    vmem = pl.BlockSpec(memory_space=pltpu.VMEM)
    hbm = pl.BlockSpec(memory_space=pltpu.HBM)
    f32 = lambda *shape: jax.ShapeDtypeStruct(shape, F32)
    pin = lambda array: pltpu.with_memory_space_constraint(array, pltpu.HBM)

    weights = (short_weight, rates, residues, skip)
    own = [f32(*w.shape[:-1], share) for w in weights] if direct else []
    blocks = width // SPAN
    pay, *mine = pl.pallas_call(
        functools.partial(front_kernel, direct=direct),
        in_specs=[smem] + [hbm] * (5 + len(own)),
        out_specs=[hbm] + [vmem] * len(own),
        out_shape=[
            pltpu.HBM((n_ctx, 2 * PIECE, share) if direct else (2 * PIECE, width), BF16),
        ]
        + own,
        scratch_shapes=[
            pltpu.VMEM((2, tokens, width), BF16),
            pltpu.VMEM((4, 16, width), BF16),
            pltpu.VMEM((blocks, 2, REACH + 1, SPAN), F32),
            pltpu.VMEM(ends.shape, BF16),
            pltpu.VMEM((4, 2, 2, 2 * (STRETCH + 8), LANES), F32),
            pltpu.VMEM((2, 2, 32, LANES), F32),
            pltpu.VMEM((blocks, 2, 2 * PIECE, LANES), F32),
            pltpu.VMEM((blocks, 2 * PIECE, SPAN), BF16),
            pltpu.VMEM((4, 2, tokens, SPAN), BF16),
            pltpu.SemaphoreType.DMA((3, blocks)),
            pltpu.SemaphoreType.DMA((4,)),
            pltpu.SemaphoreType.DMA((1,)),
            pltpu.SemaphoreType.DMA((4,)),
            pltpu.SemaphoreType.DMA((blocks,)),
        ],
        compiler_params=limit(24),
        name="front_pieces",
    )(me, *map(pin, (q_in, k_in, v_in, short_weight, ends)), *(map(pin, weights) if direct else ()))
    arrived = exchange(pay)
    if not direct:
        mine = (cut(short_weight), cut(rates, 0.01), cut(residues), cut(skip))

    query, inner = pl.pallas_call(
        local_kernel,
        grid=(steps,),
        in_specs=[columns(tokens)] * 3
        + [columns(3, REACH + 1), columns(order), columns(order), columns(1), whole(local)],
        out_specs=[pl.BlockSpec((tile // SPAN, tokens, SPAN), lambda c: (c, 0, 0))] * 2,
        out_shape=[pltpu.HBM((blocks, tokens, SPAN), F32), pltpu.VMEM((blocks, tokens, SPAN), F32)],
        scratch_shapes=[
            pltpu.VMEM((3, groups, 2 * (STRETCH + 8), LANES), F32),
            pltpu.VMEM((tile // SPAN, tokens, SPAN), F32),
        ],
        compiler_params=limit(24),
        name="local_filter",
        cost_estimate=pl.CostEstimate(flops=10**9, bytes_accessed=20 * 10**6, transcendentals=0),
    )(*map(pin, (q_in, k_in, v_in, short_weight, rates, residues)), skip, local)
    arrived, query, inner = lax.optimization_barrier((arrived, query, inner))

    groups = lanes // LANES
    back = pl.pallas_call(
        middle_kernel,
        in_specs=[smem] + [vmem] * 5,
        out_specs=hbm,
        scratch_shapes=[
            pltpu.VMEM((n_ctx, groups, 8 + 2 * PIECE + 8, LANES), F32),
            pltpu.VMEM((3, groups, slots + 1, 16, LANES), F32),
            pltpu.VMEM((groups, slots, 8, LANES), F32),
            pltpu.VMEM((groups, slots, 16, LANES), F32),
            pltpu.VMEM((groups, slots * 16, LANES), F32),
            pltpu.VMEM((groups, slots, order, LANES), F32),
            pltpu.VMEM((groups, slots, order, LANES), F32),
            pltpu.VMEM((groups, slots * order, LANES), F32),
            pltpu.VMEM((groups, slots * order, LANES), F32),
            pltpu.VMEM((groups, 2, RANK * order, LANES), F32),
            pltpu.VMEM((groups, slots * 24, LANES), F32),
            pltpu.VMEM((n_ctx, groups, BACK + 28, LANES), F32),
            pltpu.VMEM((n_ctx, 2 * BACK, lanes), BF16),
            pltpu.SemaphoreType.DMA((n_ctx,)),
        ],
        out_shape=pltpu.HBM((n_ctx, 2 * BACK, lanes), BF16),
        compiler_params=limit(24),
        name="middle_states",
    )(stretch_of_slot, arrived, *mine)
    if not direct:
        back = back[:, :, :share]
    back = lax.all_to_all(back, "ctx", 0, 0, tiled=True)
    if not direct:
        back = back.transpose(1, 0, 2).reshape(2 * BACK, width)

    keep = lambda array: pltpu.with_memory_space_constraint(array, pltpu.VMEM)
    zvalues, squares = pl.pallas_call(
        join_kernel,
        in_specs=[vmem] * 2 + [hbm, vmem],
        out_specs=[vmem] * 2,
        out_shape=[f32(tokens, width), f32(1, tokens)],
        scratch_shapes=[pltpu.VMEM((blocks, tokens, SPAN), F32)] * 2 + [pltpu.SemaphoreType.DMA((blocks // 4,))],
        compiler_params=limit(24),
        name="join_carry",
    )(back, lift, pin(query), keep(inner))
    sums = [squares]
    for shift in range(1, n_ch):
        sums.append(lax.ppermute(squares, "ch", [(i, (i + shift) % n_ch) for i in range(n_ch)]))
    return pl.pallas_call(
        functools.partial(scale_kernel, channels=width * n_ch),
        in_specs=[vmem] * (2 + n_ch),
        out_specs=hbm,
        out_shape=pltpu.HBM((tokens, width), BF16),
        scratch_shapes=[pltpu.VMEM((tokens, width), BF16), pltpu.SemaphoreType.DMA((8 if width % 1024 == 0 else 1,))],
        compiler_params=limit(24),
        name="scale_rows",
    )(zvalues, gain, *sums)


def solution(mesh):
    sizes = (mesh.shape["ctx"], mesh.shape["ch"])
    in_specs = (
        P("ctx", "ch"),
        P("ctx", "ch"),
        P("ctx", "ch"),
        P(),
        P(None, None, "ch"),
        P(None, "ch"),
        P(None, "ch"),
        P("ch"),
        P("ch"),
    )

    def run(*arrays):
        return on_device(sizes, *arrays)

    return jax.shard_map(run, mesh=mesh, in_specs=in_specs, out_specs=P("ctx", "ch"), check_vma=False)
```

```python
import functools
from decimal import Decimal, getcontext

import jax
import jax.numpy as jnp
import ml_dtypes
import numpy as np
from jax import lax
from jax.experimental import pallas as pl
from jax.experimental.pallas import tpu as pltpu
from jax.sharding import PartitionSpec as P

F32, BF16 = jnp.float32, jnp.bfloat16
LANES = 128
SPAN = 256
STRETCH = 64
REACH = 6
INNER = STRETCH - REACH
PIVOTS = (8, 49, 21, 56, 36, 1)
ANCHORS = ("0.0020", "0.0235", "0.0110", "0.0295", "0.0185", "0.0004")
RANK = len(PIVOTS)
FINE = 2
COEFS = RANK + FINE
RAW = 6 * REACH
PIECE = RAW + COEFS
BACK = 2 * REACH + COEFS


def shape_table():
    getcontext().prec = 50
    rest = [[(-Decimal(a) * d).exp() for d in range(INNER)] for a in ANCHORS]
    table = []
    for p in range(RANK):
        shape = [x / rest[p][PIVOTS[p]] for x in rest[p]]
        rest = [[x - row[PIVOTS[p]] * y for x, y in zip(row, shape)] for row in rest]
        table.append([float(x) for x in shape])
    return table


SHAPE = shape_table()


def halves(values):
    high = values.astype(ml_dtypes.bfloat16)
    low = (values - high.astype(np.float32)).astype(ml_dtypes.bfloat16)
    return high, low


def constant_matrices():
    shape = np.array(SHAPE, np.float32)
    ends = np.zeros((16, STRETCH), np.float32)
    local = np.zeros((RANK, STRETCH, STRETCH), np.float32)
    lift = np.zeros((2, 2 * STRETCH, 2 * BACK), np.float32)
    parts = [h.astype(np.float32) for h in halves(shape)]
    for p in range(RANK):
        for s in range(REACH, STRETCH):
            ends[p, s] = shape[p, STRETCH - 1 - s]
            local[p, s:, s] = shape[p, : STRETCH - s]
        for half in range(2):
            rows = slice(half * STRETCH + REACH, (half + 1) * STRETCH)
            at = half * BACK + 2 * REACH
            for k in range(2):
                lift[k, rows, at + p] = parts[k][p]
                if p < FINE:
                    lift[k, rows, at + RANK + p] = parts[k][p]
    for half in range(2):
        for t in range(REACH):
            lift[0, half * STRETCH + t, half * BACK + t] = 1.0
            lift[0, half * STRETCH + t, half * BACK + REACH + t] = 1.0
    local = local.reshape(RANK * STRETCH, STRETCH)

    def triple(m):
        h, l = halves(m)
        return np.concatenate([h, h, l], axis=1)

    return triple(ends), triple(local), lift.astype(ml_dtypes.bfloat16)


def strengths(rate):
    found = []
    for p in range(RANK):
        value = jnp.exp(-rate * float(PIVOTS[p]))
        for q in range(p):
            value = value - found[q] * SHAPE[q][PIVOTS[p]]
        found.append(value)
    return found


def split(values):
    high = values.astype(BF16)
    return high, (values - high.astype(F32)).astype(BF16)


def amplitude(rate, residue):
    x = 2.0 * rate
    series = 1.0 - x * (0.5 - x * (1 / 6 - x * (1 / 24 - x * (1 / 120 - x * (1 / 720)))))
    return residue * jnp.sqrt(x * series)


EDGES = (0, STRETCH - 16, STRETCH, 2 * STRETCH - 16)


def front_kernel(*refs, direct):
    me_ref, q_ref, k_ref, v_ref, taps_ref, ends_ref = refs[:6]
    refs = refs[6:]
    weights, refs = (refs[:4], refs[4:]) if direct else ((), refs)
    pay_ref, refs = refs[0], refs[1:]
    kept, refs = (refs[:4], refs[4:]) if direct else ((), refs)
    held, edge, taps_vm, ends_vm, xs, qs, pay, packed, u_vm, in_sems, edge_sems, tap_sem, own_sems, out_sems = refs
    blocks = k_ref.shape[1] // SPAN

    def lanes(c):
        return pl.ds(pl.multiple_of(c * SPAN, SPAN), SPAN)

    def loads(c):
        return [
            pltpu.make_async_copy(ref.at[:, lanes(c)], held.at[a, :, lanes(c)], in_sems.at[a, c])
            for a, ref in enumerate((k_ref, v_ref))
        ] + [pltpu.make_async_copy(taps_ref.at[pl.ds(1, 2), :, lanes(c)], taps_vm.at[c], in_sems.at[2, c])]

    def edge_loads():
        return [
            pltpu.make_async_copy(q_ref.at[pl.ds(at, 16), :], edge.at[e], edge_sems.at[e])
            for e, at in enumerate(EDGES)
        ]

    def stores(c):
        target = pay_ref.at[c] if direct else pay_ref.at[:, lanes(c)]
        return [pltpu.make_async_copy(packed.at[c], target, out_sems.at[c])]

    def own_loads():
        share = kept[0].shape[-1]
        cols = pl.ds(pl.multiple_of(me_ref[0] * share, share), share)
        views = (weights[0].at[:, :, cols], weights[1].at[:, cols], weights[2].at[:, cols], weights[3].at[:, cols])
        return [pltpu.make_async_copy(view, ref, own_sems.at[n]) for n, (view, ref) in enumerate(zip(views, kept))]

    ends_copy = pltpu.make_async_copy(ends_ref, ends_vm, tap_sem.at[0])
    for copy in loads(0) + edge_loads():
        copy.start()
    ends_copy.start()

    def begin(c, carry):
        for copy in loads(c):
            copy.start()
        return carry

    lax.fori_loop(1, blocks, begin, 0)
    if direct:
        for copy in own_loads():
            copy.start()
    for parity in range(2):
        for a in range(2):
            for i in range(2):
                at = i * (STRETCH + 8)
                xs[parity, a, at : at + 8, :] = jnp.zeros((8, LANES), F32)
    for copy in edge_loads():
        copy.wait()
    ends_copy.wait()
    halves_of = SPAN // LANES
    groups = blocks * halves_of

    def features(g):
        parity = lax.rem(g, 2)
        block, part = g // halves_of, pl.ds(pl.multiple_of(lax.rem(g, halves_of) * LANES, LANES), LANES)
        cols = pl.ds(pl.multiple_of(g * LANES, LANES), LANES)
        for a in range(2):
            for i in range(2):
                base = i * (STRETCH + 8) + 8
                xs[parity, a, base : base + STRETCH, :] = held[a, i * STRETCH : (i + 1) * STRETCH, cols].astype(F32)
        taps = [[taps_vm[block, a, j : j + 1, part] for j in range(REACH + 1)] for a in range(2)]
        for i in range(2):
            for b in range(STRETCH // 16):
                base = i * (STRETCH + 8) + 8 + 16 * b
                both = []
                for a in range(2):
                    total = taps[a][0] * xs[parity, a, base : base + 16, :]
                    for j in range(1, REACH + 1):
                        total = total + taps[a][j] * xs[parity, a, base - j : base - j + 16, :]
                    both.append(total)
                mixed = both[0] * both[1]
                if b == 0:
                    row = lax.broadcasted_iota(jnp.int32, (16, LANES), 0)
                    mixed = jnp.where(row >= REACH, mixed, 0.0)
                high, low = split(mixed)
                rows = slice(i * STRETCH + 16 * b, i * STRETCH + 16 * b + 16)
                u_vm[parity, 0, rows, :] = high
                u_vm[parity, 1, rows, :] = low

    def products(g):
        parity = lax.rem(g, 2)
        found = []
        for i in range(2):
            rows = slice(i * STRETCH, (i + 1) * STRETCH)
            high, low = u_vm[parity, 0, rows, :], u_vm[parity, 1, rows, :]
            stacked = jnp.concatenate([high, low, high], axis=0)
            found.append(jnp.dot(ends_vm[...], stacked, preferred_element_type=F32)[:8])
        return found

    def finish(g, found):
        parity = lax.rem(g, 2)
        block, part = g // halves_of, pl.ds(pl.multiple_of(lax.rem(g, halves_of) * LANES, LANES), LANES)
        cols = pl.ds(pl.multiple_of(g * LANES, LANES), LANES)
        for i in range(2):
            at = PIECE * i + RAW
            pay[parity, at : at + RANK, :] = found[i][:RANK]
            pay[parity, at + RANK : at + COEFS, :] = (found[i] - found[i].astype(BF16).astype(F32))[:FINE]
            base = i * (STRETCH + 8) + 8
            qs[parity, i, 0:16, :] = edge[2 * i, :, cols].astype(F32)
            qs[parity, i, 16:32, :] = edge[2 * i + 1, :, cols].astype(F32)
            at = i * PIECE
            pay[parity, at : at + REACH, :] = qs[parity, i, 32 - REACH : 32, :]
            pay[parity, at + 3 * REACH : at + 4 * REACH, :] = qs[parity, i, 0:REACH, :]
            for a in range(2):
                at = i * PIECE + (1 + a) * REACH
                pay[parity, at : at + REACH, :] = xs[parity, a, base + STRETCH - REACH : base + STRETCH, :]
                at = at + 3 * REACH
                pay[parity, at : at + REACH, :] = xs[parity, a, base : base + REACH, :]
        packed[block, :, part] = pay[parity].astype(BF16)

    def step(g, carry):
        now, before = jnp.minimum(g, groups - 1), jnp.maximum(g - 1, 0)

        @pl.when((lax.rem(g, halves_of) == 0) & (g < groups))
        def _():
            for copy in loads(g // halves_of):
                copy.wait()

        found = products(before)
        features(now)
        finish(before, found)

        @pl.when((lax.rem(g, halves_of) == 0) & (g > 0))
        def _():
            for copy in stores(g // halves_of - 1):
                copy.start()

        return carry

    lax.fori_loop(0, groups + 1, step, 0)

    def end(c, carry):
        for copy in stores(c):
            copy.wait()
        return carry

    lax.fori_loop(0, blocks, end, 0)
    if direct:
        for copy in own_loads():
            copy.wait()


def local_kernel(
    q_ref, k_ref, v_ref, taps_ref, rates_ref, res_ref, skip_ref, local_ref, qc_ref, y_ref, xs, u_vm
):
    tile = q_ref.shape[1]
    per = SPAN // LANES
    first_row = lax.broadcasted_iota(jnp.int32, (8, LANES), 0)
    for g in range(tile // LANES):
        cols = slice(g * LANES, (g + 1) * LANES)
        part = slice(g % per * LANES, (g % per + 1) * LANES)
        taps = [[taps_ref[a, j : j + 1, cols] for j in range(REACH + 1)] for a in range(3)]
        for i in range(2):
            base = i * (STRETCH + 8) + 8
            for a, ref in enumerate((q_ref, k_ref, v_ref)):
                xs[a, g, base - 8 : base, :] = jnp.zeros((8, LANES), F32)
                xs[a, g, base : base + STRETCH, :] = ref[i * STRETCH : (i + 1) * STRETCH, cols].astype(F32)
            for b in range(STRETCH // 8):
                at = base + 8 * b
                totals = []
                for a in range(3):
                    total = taps[a][0] * xs[a, g, at : at + 8, :]
                    for j in range(1, REACH + 1):
                        total = total + taps[a][j] * xs[a, g, at - j : at - j + 8, :]
                    totals.append(total)
                query, mixed = totals[0], totals[1] * totals[2]
                if b == 0:
                    query = jnp.where(first_row >= REACH, query, 1.0)
                    mixed = jnp.where(first_row >= REACH, mixed, 0.0)
                rows = slice(i * STRETCH + 8 * b, i * STRETCH + 8 * b + 8)
                qc_ref[g // per, rows, part] = query
                u_vm[g // per, rows, part] = mixed
    for c in range(tile // SPAN):
        cols = slice(c * SPAN, (c + 1) * SPAN)
        rate = rates_ref[:, cols]
        amount = amplitude(rate, res_ref[:, cols])
        weights = [jnp.sum(amount * value, axis=0, keepdims=True) for value in strengths(rate)]
        for i in range(2):
            rows = slice(i * STRETCH, (i + 1) * STRETCH)
            mixed = u_vm[c, rows, :]
            high, low = split(mixed)
            parts = jnp.dot(
                local_ref[...], jnp.concatenate([high, low, high], axis=0), preferred_element_type=F32
            )
            total = skip_ref[:, cols] * mixed
            for p in range(RANK):
                total = total + weights[p] * parts[p * STRETCH : (p + 1) * STRETCH, :]
            y_ref[c, rows, :] = total


def middle_kernel(
    perm_ref, x_ref, taps_ref, rates_ref, res_ref, skip_ref, out_ref,
    raw, ext, moments, past, heads, first, second, states, mids, coefs, fades, result, slab, packed, out_sems,
):
    slots = perm_ref.shape[0]
    groups = x_ref.shape[2] // LANES
    order = rates_ref.shape[0]
    span = 2 * PIECE
    row = lax.broadcasted_iota(jnp.int32, (8, LANES), 0)
    ext[:, :, 0, 0:8, :] = jnp.zeros((3, groups, 8, LANES), F32)
    past[:, :, 0:8, :] = jnp.zeros((groups, slots, 8, LANES), F32)

    def unpack(src, carry):
        for g in range(groups):
            raw[src, g, 8 : 8 + span, :] = x_ref[src, :, g * LANES : (g + 1) * LANES].astype(F32)
        for i in range(2):
            n = perm_ref[2 * src + i]
            for g in range(groups):
                for a in range(3):
                    at = 8 + i * PIECE + a * REACH
                    ext[a, g, n + 1, 0:8, :] = raw[src, g, at + REACH - 8 : at + REACH, :]
                    at = at + 3 * REACH
                    ext[a, g, n, 8:16, :] = raw[src, g, at : at + 8, :]
                at = 8 + i * PIECE + RAW
                fine = jnp.where(row < FINE, raw[src, g, at + RANK : at + RANK + 8, :], 0.0)
                moments[g, n] = raw[src, g, at : at + 8, :] + fine
        return carry

    lax.fori_loop(0, slots // 2, unpack, 0, unroll=2)

    def group_pass(g, carry):
        cols = pl.ds(pl.multiple_of(g * LANES, LANES), LANES)
        rate = rates_ref[:, cols]
        amount = amplitude(rate, res_ref[:, cols])
        basis = strengths(rate)
        powers = [jnp.ones_like(rate), jnp.exp(-rate)]
        for d in range(2, REACH + 1):
            powers.append(powers[-1] * powers[1])
        for t in range(REACH):
            coefs[g, 0, t * order : (t + 1) * order, :] = amount * powers[t + 1]
        for p in range(RANK):
            coefs[g, 1, p * order : (p + 1) * order, :] = amount * powers[1] * basis[p]
        fade_rest = jnp.exp(-rate * float(INNER))
        fades[g, 0] = powers[REACH]
        fades[g, 1] = fade_rest * powers[REACH]
        taps = [[taps_ref[a, j : j + 1, cols] for j in range(REACH + 1)] for a in range(3)]
        near = [jnp.sum(amount * powers[d], axis=0, keepdims=True) for d in range(REACH)]
        near[0] = near[0] + skip_ref[:, cols]

        def head_pass(n, carry):
            feats = []
            for a in range(3):
                total = taps[a][0] * ext[a, g, n, 8:16, :]
                for j in range(1, REACH + 1):
                    total = total + taps[a][j] * ext[a, g, n, 8 - j : 16 - j, :]
                feats.append(jnp.where(row < REACH, total, 0.0))
            mixed = feats[1] * feats[2]
            past[g, n, 8:16, :] = mixed
            total = near[0] * mixed
            for d in range(1, REACH):
                total = total + near[d] * past[g, n, 8 - d : 16 - d, :]
            at = pl.multiple_of(n * 16, 16)
            heads[g, pl.ds(at, 8), :] = feats[0]
            heads[g, pl.ds(at + 8, 8), :] = total
            value = powers[REACH - 1] * past[g, n, 8:9, :]
            for s in range(1, REACH):
                value = value + powers[REACH - 1 - s] * past[g, n, 8 + s : 9 + s, :]
            first[g, n] = value
            return carry

        lax.fori_loop(0, slots, head_pass, 0, unroll=4)

        def rest_pass(n, carry):
            value = fade_rest * first[g, n]
            for p in range(RANK):
                value = value + basis[p] * moments[g, n, p : p + 1, :]
            second[g, n] = value
            return carry

        lax.fori_loop(0, slots, rest_pass, 0, unroll=4)
        return carry

    lax.fori_loop(0, groups, group_pass, 0)

    def scan_pass(n, state):
        after = []
        at = pl.multiple_of(n * order, order)
        for g in range(groups):
            states[g, pl.ds(at, order), :] = state[g]
            mids[g, pl.ds(at, order), :] = fades[g, 0] * state[g] + first[g, n]
            after.append(fades[g, 1] * state[g] + second[g, n])
        return tuple(after)

    lax.fori_loop(0, slots, scan_pass, tuple(jnp.zeros((order, LANES), F32) for _ in range(groups)), unroll=4)

    quad = 4

    def sums(g, kind, held, first_tile):
        totals = [[None] * quad for _ in range(RANK)]
        for r in range(order):
            values = [held[g, pl.ds((first_tile + k) * 8 * order + r, 8, stride=order), :] for k in range(quad)]
            for p in range(RANK):
                weight = coefs[g, kind, p * order + r : p * order + r + 1, :]
                for k in range(quad):
                    term = weight * values[k]
                    totals[p][k] = term if r == 0 else totals[p][k] + term
        return totals

    quads = slots // (8 * quad)

    def out_pass(step, carry):
        g, q = step // quads, lax.rem(step, quads)
        totals = sums(g, 0, states, q * quad)
        for t in range(REACH):
            for k in range(quad):
                tile = q * quad + k
                query = heads[g, pl.ds(tile * 128 + t, 8, stride=16), :]
                local = heads[g, pl.ds(tile * 128 + 8 + t, 8, stride=16), :]
                z = query * (local + totals[t][k])
                result[g, pl.ds(tile * 192 + t, 8, stride=24), :] = z
                result[g, pl.ds(tile * 192 + REACH + t, 8, stride=24), :] = z - z.astype(BF16).astype(F32)
        totals = sums(g, 1, mids, q * quad)
        for p in range(RANK):
            for k in range(quad):
                tile = q * quad + k
                value = totals[p][k]
                result[g, pl.ds(tile * 192 + 2 * REACH + p, 8, stride=24), :] = value
                if p < FINE:
                    rest = value - value.astype(BF16).astype(F32)
                    result[g, pl.ds(tile * 192 + 2 * REACH + RANK + p, 8, stride=24), :] = rest
        return carry

    lax.fori_loop(0, groups * quads, out_pass, 0)

    def store(src):
        return pltpu.make_async_copy(packed.at[src], out_ref.at[src], out_sems.at[src])

    def pack(src, carry):
        for g in range(groups):
            for i in range(2):
                at = pl.multiple_of(perm_ref[2 * src + i] * 24, 8)
                slab[src, g, i * BACK : i * BACK + 24, :] = result[g, pl.ds(at, 24), :]
            packed[src, :, g * LANES : (g + 1) * LANES] = slab[src, g, 0 : 2 * BACK, :].astype(BF16)
        return carry

    lax.fori_loop(0, slots // 2, pack, 0, unroll=2)

    def send(src, carry):
        store(src).start()
        return carry

    def end(src, carry):
        store(src).wait()
        return carry

    lax.fori_loop(0, slots // 2, send, 0)
    lax.fori_loop(0, slots // 2, end, 0)


def join_kernel(back_ref, lift_ref, qc_ref, y_ref, z_ref, sq_ref, qc_vm, carry, total, sems):
    blocks, tokens, _ = qc_vm.shape
    by_dest = len(back_ref.shape) == 3
    chunk = 4

    def load(c):
        rows = pl.ds(c * chunk, chunk)
        return pltpu.make_async_copy(qc_ref.at[rows], qc_vm.at[rows], sems.at[c])

    def lanes(b):
        return pl.ds(pl.multiple_of(b * SPAN, SPAN), SPAN)

    for c in range(blocks // chunk):
        load(c).start()

    def products(c, unused):
        for k in range(chunk):
            b = c * chunk + k
            back = back_ref[b] if by_dest else back_ref[:, lanes(b)]
            product = jnp.dot(lift_ref[0], back, preferred_element_type=F32)
            carry[b] = y_ref[b] + product + jnp.dot(lift_ref[1], back, preferred_element_type=F32)
        return unused

    lax.fori_loop(0, blocks // chunk, products, 0)
    total[...] = jnp.zeros((tokens, LANES), F32)

    def square(c, unused):
        load(c).wait()
        part = total[...]
        for k in range(chunk):
            b = c * chunk + k
            z = qc_vm[b] * carry[b]
            z_ref[:, lanes(b)] = z
            squares = z * z
            for h in range(SPAN // LANES):
                part = part + squares[:, h * LANES : (h + 1) * LANES]
        total[...] = part
        return unused

    lax.fori_loop(0, blocks // chunk, square, 0)
    sq_ref[...] = jnp.sum(total[...].T, axis=0, keepdims=True)


def scale_kernel(*refs, channels):
    z_ref, gain_ref, refs, (out_ref, held, sems) = refs[0], refs[1], refs[2:-3], refs[-3:]
    tokens, width = z_ref.shape
    chunks = sems.shape[0]
    wide = width // chunks
    total = refs[0][...]
    for ref in refs[1:]:
        total = total + ref[...]
    scale = lax.rsqrt(total / channels + 1e-05)
    scale = jnp.broadcast_to(scale, (LANES, tokens)).T

    def store(c):
        cols = pl.ds(pl.multiple_of(c * wide, LANES), wide)
        return pltpu.make_async_copy(held.at[:, cols], out_ref.at[:, cols], sems.at[c])

    def run(c, unused):
        for g in range(wide // LANES):
            cols = pl.ds(pl.multiple_of(c * wide + g * LANES, LANES), LANES)
            held[:, cols] = (z_ref[:, cols] * scale * gain_ref[:, cols]).astype(BF16)
        store(c).start()
        return unused

    def end(c, unused):
        store(c).wait()
        return unused

    lax.fori_loop(0, chunks, run, 0)
    lax.fori_loop(0, chunks, end, 0)


def limit(mib):
    return pltpu.CompilerParams(vmem_limit_bytes=mib * 1024 * 1024)


def on_device(sizes, q_in, k_in, v_in, stretch_of_slot, short_weight, rates, residues, skip, gain):
    n_ctx, n_ch = sizes
    tokens, width = q_in.shape
    slots = stretch_of_slot.shape[0]
    order = rates.shape[0]
    share = width // n_ctx
    direct = share == SPAN
    tile = min(width, 1024)
    steps = width // tile
    groups = tile // LANES
    ends_np, local_np, lift_np = constant_matrices()
    ends, local, lift = jnp.asarray(ends_np), jnp.asarray(local_np), jnp.asarray(lift_np)
    skip, gain = skip.reshape(1, width), gain.reshape(1, width)
    me = lax.axis_index("ctx").astype(jnp.int32).reshape(1)

    def whole(array):
        return pl.BlockSpec(array.shape, lambda c: (0,) * array.ndim)

    def columns(*lead):
        return pl.BlockSpec((*lead, tile), lambda c: (0,) * len(lead) + (c,))

    def exchange(array):
        if direct:
            return lax.all_to_all(array, "ctx", 0, 0, tiled=True)
        array = array.reshape(array.shape[0], n_ctx, share).transpose(1, 0, 2)
        return widen(lax.all_to_all(array, "ctx", 0, 0, tiled=True))

    lanes = -(-share // LANES) * LANES

    def widen(array, fill=0.0):
        pad = [(0, 0)] * (array.ndim - 1) + [(0, lanes - share)]
        return jnp.pad(array, pad, constant_values=fill)

    def cut(array, fill=0.0):
        return widen(lax.dynamic_slice_in_dim(array, lax.axis_index("ctx") * share, share, array.ndim - 1), fill)

    smem = pl.BlockSpec(memory_space=pltpu.SMEM)
    vmem = pl.BlockSpec(memory_space=pltpu.VMEM)
    hbm = pl.BlockSpec(memory_space=pltpu.HBM)
    f32 = lambda *shape: jax.ShapeDtypeStruct(shape, F32)
    pin = lambda array: pltpu.with_memory_space_constraint(array, pltpu.HBM)

    weights = (short_weight, rates, residues, skip)
    own = [f32(*w.shape[:-1], share) for w in weights] if direct else []
    blocks = width // SPAN
    pay, *mine = pl.pallas_call(
        functools.partial(front_kernel, direct=direct),
        in_specs=[smem] + [hbm] * (5 + len(own)),
        out_specs=[hbm] + [vmem] * len(own),
        out_shape=[
            pltpu.HBM((n_ctx, 2 * PIECE, share) if direct else (2 * PIECE, width), BF16),
        ]
        + own,
        scratch_shapes=[
            pltpu.VMEM((2, tokens, width), BF16),
            pltpu.VMEM((4, 16, width), BF16),
            pltpu.VMEM((blocks, 2, REACH + 1, SPAN), F32),
            pltpu.VMEM(ends.shape, BF16),
            pltpu.VMEM((2, 2, 2 * (STRETCH + 8), LANES), F32),
            pltpu.VMEM((2, 2, 32, LANES), F32),
            pltpu.VMEM((2, 2 * PIECE, LANES), F32),
            pltpu.VMEM((blocks, 2 * PIECE, SPAN), BF16),
            pltpu.VMEM((2, 2, tokens, LANES), BF16),
            pltpu.SemaphoreType.DMA((3, blocks)),
            pltpu.SemaphoreType.DMA((4,)),
            pltpu.SemaphoreType.DMA((1,)),
            pltpu.SemaphoreType.DMA((4,)),
            pltpu.SemaphoreType.DMA((blocks,)),
        ],
        compiler_params=limit(24),
        name="front_pieces",
    )(me, *map(pin, (q_in, k_in, v_in, short_weight, ends)), *(map(pin, weights) if direct else ()))
    arrived = exchange(pay)
    if not direct:
        mine = (cut(short_weight), cut(rates, 0.01), cut(residues), cut(skip))

    query, inner = pl.pallas_call(
        local_kernel,
        grid=(steps,),
        in_specs=[columns(tokens)] * 3
        + [columns(3, REACH + 1), columns(order), columns(order), columns(1), whole(local)],
        out_specs=[pl.BlockSpec((tile // SPAN, tokens, SPAN), lambda c: (c, 0, 0))] * 2,
        out_shape=[pltpu.HBM((blocks, tokens, SPAN), F32), pltpu.VMEM((blocks, tokens, SPAN), F32)],
        scratch_shapes=[
            pltpu.VMEM((3, groups, 2 * (STRETCH + 8), LANES), F32),
            pltpu.VMEM((tile // SPAN, tokens, SPAN), F32),
        ],
        compiler_params=limit(24),
        name="local_filter",
        cost_estimate=pl.CostEstimate(flops=10**9, bytes_accessed=20 * 10**6, transcendentals=0),
    )(*map(pin, (q_in, k_in, v_in, short_weight, rates, residues)), skip, local)
    arrived, query, inner = lax.optimization_barrier((arrived, query, inner))

    groups = lanes // LANES
    back = pl.pallas_call(
        middle_kernel,
        in_specs=[smem] + [vmem] * 5,
        out_specs=hbm,
        scratch_shapes=[
            pltpu.VMEM((n_ctx, groups, 8 + 2 * PIECE + 8, LANES), F32),
            pltpu.VMEM((3, groups, slots + 1, 16, LANES), F32),
            pltpu.VMEM((groups, slots, 8, LANES), F32),
            pltpu.VMEM((groups, slots, 16, LANES), F32),
            pltpu.VMEM((groups, slots * 16, LANES), F32),
            pltpu.VMEM((groups, slots, order, LANES), F32),
            pltpu.VMEM((groups, slots, order, LANES), F32),
            pltpu.VMEM((groups, slots * order, LANES), F32),
            pltpu.VMEM((groups, slots * order, LANES), F32),
            pltpu.VMEM((groups, 2, RANK * order, LANES), F32),
            pltpu.VMEM((groups, 2, order, LANES), F32),
            pltpu.VMEM((groups, slots * 24, LANES), F32),
            pltpu.VMEM((n_ctx, groups, BACK + 28, LANES), F32),
            pltpu.VMEM((n_ctx, 2 * BACK, lanes), BF16),
            pltpu.SemaphoreType.DMA((n_ctx,)),
        ],
        out_shape=pltpu.HBM((n_ctx, 2 * BACK, lanes), BF16),
        compiler_params=limit(24),
        name="middle_states",
    )(stretch_of_slot, arrived, *mine)
    if not direct:
        back = back[:, :, :share]
    back = lax.all_to_all(back, "ctx", 0, 0, tiled=True)
    if not direct:
        back = back.transpose(1, 0, 2).reshape(2 * BACK, width)

    keep = lambda array: pltpu.with_memory_space_constraint(array, pltpu.VMEM)
    zvalues, squares = pl.pallas_call(
        join_kernel,
        in_specs=[vmem] * 2 + [hbm, vmem],
        out_specs=[vmem] * 2,
        out_shape=[f32(tokens, width), f32(1, tokens)],
        scratch_shapes=[pltpu.VMEM((blocks, tokens, SPAN), F32)] * 2
        + [pltpu.VMEM((tokens, LANES), F32), pltpu.SemaphoreType.DMA((blocks // 4,))],
        compiler_params=limit(24),
        name="join_carry",
    )(back, lift, pin(query), keep(inner))
    sums = [squares]
    for shift in range(1, n_ch):
        sums.append(lax.ppermute(squares, "ch", [(i, (i + shift) % n_ch) for i in range(n_ch)]))
    return pl.pallas_call(
        functools.partial(scale_kernel, channels=width * n_ch),
        in_specs=[vmem] * (2 + n_ch),
        out_specs=hbm,
        out_shape=pltpu.HBM((tokens, width), BF16),
        scratch_shapes=[pltpu.VMEM((tokens, width), BF16), pltpu.SemaphoreType.DMA((8 if width % 1024 == 0 else 1,))],
        compiler_params=limit(24),
        name="scale_rows",
    )(zvalues, gain, *sums)


def solution(mesh):
    sizes = (mesh.shape["ctx"], mesh.shape["ch"])
    in_specs = (
        P("ctx", "ch"),
        P("ctx", "ch"),
        P("ctx", "ch"),
        P(),
        P(None, None, "ch"),
        P(None, "ch"),
        P(None, "ch"),
        P("ch"),
        P("ch"),
    )

    def run(*arrays):
        return on_device(sizes, *arrays)

    return jax.shard_map(run, mesh=mesh, in_specs=in_specs, out_specs=P("ctx", "ch"), check_vma=False)
```

```python
import functools
from decimal import Decimal, getcontext

import jax
import jax.numpy as jnp
import ml_dtypes
import numpy as np
from jax import lax
from jax.experimental import pallas as pl
from jax.experimental.pallas import tpu as pltpu
from jax.sharding import PartitionSpec as P

F32, BF16 = jnp.float32, jnp.bfloat16
LANES = 128
SPAN = 256
STRETCH = 64
REACH = 6
INNER = STRETCH - REACH
PIVOTS = (8, 49, 21, 56, 36, 1)
ANCHORS = ("0.0020", "0.0235", "0.0110", "0.0295", "0.0185", "0.0004")
RANK = len(PIVOTS)
FINE = 2
COEFS = RANK + FINE
RAW = 6 * REACH
PIECE = RAW + COEFS
BACK = 2 * REACH + COEFS


def shape_table():
    getcontext().prec = 50
    rest = [[(-Decimal(a) * d).exp() for d in range(INNER)] for a in ANCHORS]
    table = []
    for p in range(RANK):
        shape = [x / rest[p][PIVOTS[p]] for x in rest[p]]
        rest = [[x - row[PIVOTS[p]] * y for x, y in zip(row, shape)] for row in rest]
        table.append([float(x) for x in shape])
    return table


SHAPE = shape_table()


def halves(values):
    high = values.astype(ml_dtypes.bfloat16)
    low = (values - high.astype(np.float32)).astype(ml_dtypes.bfloat16)
    return high, low


def constant_matrices():
    shape = np.array(SHAPE, np.float32)
    ends = np.zeros((16, STRETCH), np.float32)
    local = np.zeros((RANK, STRETCH, STRETCH), np.float32)
    lift = np.zeros((2, 2 * STRETCH, 2 * BACK), np.float32)
    parts = [h.astype(np.float32) for h in halves(shape)]
    for p in range(RANK):
        for s in range(REACH, STRETCH):
            ends[p, s] = shape[p, STRETCH - 1 - s]
            local[p, s:, s] = shape[p, : STRETCH - s]
        for half in range(2):
            rows = slice(half * STRETCH + REACH, (half + 1) * STRETCH)
            at = half * BACK + 2 * REACH
            for k in range(2):
                lift[k, rows, at + p] = parts[k][p]
                if p < FINE:
                    lift[k, rows, at + RANK + p] = parts[k][p]
    for half in range(2):
        for t in range(REACH):
            lift[0, half * STRETCH + t, half * BACK + t] = 1.0
            lift[0, half * STRETCH + t, half * BACK + REACH + t] = 1.0
    local = local.reshape(RANK * STRETCH, STRETCH)

    def triple(m):
        h, l = halves(m)
        return np.concatenate([h, h, l], axis=1)

    return triple(ends), triple(local), lift.astype(ml_dtypes.bfloat16)


def strengths(rate):
    found = []
    for p in range(RANK):
        value = jnp.exp(-rate * float(PIVOTS[p]))
        for q in range(p):
            value = value - found[q] * SHAPE[q][PIVOTS[p]]
        found.append(value)
    return found


def split(values):
    high = values.astype(BF16)
    return high, (values - high.astype(F32)).astype(BF16)


def amplitude(rate, residue):
    x = 2.0 * rate
    series = 1.0 - x * (0.5 - x * (1 / 6 - x * (1 / 24 - x * (1 / 120 - x * (1 / 720)))))
    return residue * jnp.sqrt(x * series)


EDGES = (0, STRETCH - 16, STRETCH, 2 * STRETCH - 16)


def front_kernel(*refs, direct):
    me_ref, q_ref, k_ref, v_ref, taps_ref, ends_ref = refs[:6]
    refs = refs[6:]
    weights, refs = (refs[:4], refs[4:]) if direct else ((), refs)
    pay_ref, refs = refs[0], refs[1:]
    kept, refs = (refs[:4], refs[4:]) if direct else ((), refs)
    held, edge, taps_vm, ends_vm, xs, qs, pay, packed, u_vm, in_sems, edge_sems, tap_sem, own_sems, out_sems = refs
    blocks = k_ref.shape[1] // SPAN

    def lanes(c):
        return pl.ds(pl.multiple_of(c * SPAN, SPAN), SPAN)

    def loads(c):
        return [
            pltpu.make_async_copy(ref.at[:, lanes(c)], held.at[a, :, lanes(c)], in_sems.at[a, c])
            for a, ref in enumerate((k_ref, v_ref))
        ] + [pltpu.make_async_copy(taps_ref.at[pl.ds(1, 2), :, lanes(c)], taps_vm.at[c], in_sems.at[2, c])]

    def edge_loads():
        return [
            pltpu.make_async_copy(q_ref.at[pl.ds(at, 16), :], edge.at[e], edge_sems.at[e])
            for e, at in enumerate(EDGES)
        ]

    def stores(c):
        target = pay_ref.at[c] if direct else pay_ref.at[:, lanes(c)]
        return [pltpu.make_async_copy(packed.at[c], target, out_sems.at[c])]

    def own_loads():
        share = kept[0].shape[-1]
        cols = pl.ds(pl.multiple_of(me_ref[0] * share, share), share)
        views = (weights[0].at[:, :, cols], weights[1].at[:, cols], weights[2].at[:, cols], weights[3].at[:, cols])
        return [pltpu.make_async_copy(view, ref, own_sems.at[n]) for n, (view, ref) in enumerate(zip(views, kept))]

    ends_copy = pltpu.make_async_copy(ends_ref, ends_vm, tap_sem.at[0])
    for copy in loads(0) + edge_loads():
        copy.start()
    ends_copy.start()

    def begin(c, carry):
        for copy in loads(c):
            copy.start()
        return carry

    lax.fori_loop(1, blocks, begin, 0)
    if direct:
        for copy in own_loads():
            copy.start()
    for parity in range(2):
        for a in range(2):
            for h in range(2):
                for i in range(2):
                    at = i * (STRETCH + 8)
                    xs[parity, a, h, at : at + 8, :] = jnp.zeros((8, LANES), F32)
    for copy in edge_loads():
        copy.wait()
    ends_copy.wait()

    def features(c, carry):
        for copy in loads(c):
            copy.wait()
        parity = lax.rem(c, 2)
        for h in range(2):
            part = slice(h * LANES, (h + 1) * LANES)
            cols = pl.ds(pl.multiple_of(c * SPAN + h * LANES, LANES), LANES)
            for i in range(2):
                base = i * (STRETCH + 8) + 8
                for a in range(2):
                    xs[parity, a, h, base : base + STRETCH, :] = held[
                        a, i * STRETCH : (i + 1) * STRETCH, cols
                    ].astype(F32)
                    at = i * PIECE + (1 + a) * REACH
                    pay[c, h, at : at + REACH, :] = xs[parity, a, h, base + STRETCH - REACH : base + STRETCH, :]
                    at = at + 3 * REACH
                    pay[c, h, at : at + REACH, :] = xs[parity, a, h, base : base + REACH, :]
                qs[parity, h, i, 0:16, :] = edge[2 * i, :, cols].astype(F32)
                qs[parity, h, i, 16:32, :] = edge[2 * i + 1, :, cols].astype(F32)
                at = i * PIECE
                pay[c, h, at : at + REACH, :] = qs[parity, h, i, 32 - REACH : 32, :]
                pay[c, h, at + 3 * REACH : at + 4 * REACH, :] = qs[parity, h, i, 0:REACH, :]
            taps = [[taps_vm[c, a, j : j + 1, part] for j in range(REACH + 1)] for a in range(2)]
            for i in range(2):
                for b in range(STRETCH // 16):
                    base = i * (STRETCH + 8) + 8 + 16 * b
                    both = []
                    for a in range(2):
                        total = taps[a][0] * xs[parity, a, h, base : base + 16, :]
                        for j in range(1, REACH + 1):
                            total = total + taps[a][j] * xs[parity, a, h, base - j : base - j + 16, :]
                        both.append(total)
                    mixed = both[0] * both[1]
                    if b == 0:
                        row = lax.broadcasted_iota(jnp.int32, (16, LANES), 0)
                        mixed = jnp.where(row >= REACH, mixed, 0.0)
                    high, low = split(mixed)
                    rows = slice(i * STRETCH + 16 * b, i * STRETCH + 16 * b + 16)
                    u_vm[c, 0, rows, part] = high
                    u_vm[c, 1, rows, part] = low
        return carry

    lax.fori_loop(0, blocks, features, 0)
    chunk = 4

    def finish(step, carry):
        for k in range(chunk):
            c = step * chunk + k
            for i in range(2):
                rows = slice(i * STRETCH, (i + 1) * STRETCH)
                high, low = u_vm[c, 0, rows, :], u_vm[c, 1, rows, :]
                stacked = jnp.concatenate([high, low, high], axis=0)
                moments = jnp.dot(ends_vm[...], stacked, preferred_element_type=F32)[:8]
                rest = (moments - moments.astype(BF16).astype(F32))[:FINE]
                at = PIECE * i + RAW
                for h in range(2):
                    part = slice(h * LANES, (h + 1) * LANES)
                    pay[c, h, at : at + RANK, :] = moments[:RANK, part]
                    pay[c, h, at + RANK : at + COEFS, :] = rest[:, part]
            for h in range(2):
                packed[c, :, h * LANES : (h + 1) * LANES] = pay[c, h].astype(BF16)
        for k in range(chunk):
            for copy in stores(step * chunk + k):
                copy.start()
        return carry

    lax.fori_loop(0, blocks // chunk, finish, 0)

    def end(c, carry):
        for copy in stores(c):
            copy.wait()
        return carry

    lax.fori_loop(0, blocks, end, 0)
    if direct:
        for copy in own_loads():
            copy.wait()


def local_kernel(
    q_ref, k_ref, v_ref, taps_ref, rates_ref, res_ref, skip_ref, local_ref, qc_ref, y_ref, xs, u_vm
):
    tile = q_ref.shape[1]
    per = SPAN // LANES
    first_row = lax.broadcasted_iota(jnp.int32, (8, LANES), 0)
    for g in range(tile // LANES):
        cols = slice(g * LANES, (g + 1) * LANES)
        part = slice(g % per * LANES, (g % per + 1) * LANES)
        taps = [[taps_ref[a, j : j + 1, cols] for j in range(REACH + 1)] for a in range(3)]
        for i in range(2):
            base = i * (STRETCH + 8) + 8
            for a, ref in enumerate((q_ref, k_ref, v_ref)):
                xs[a, g, base - 8 : base, :] = jnp.zeros((8, LANES), F32)
                xs[a, g, base : base + STRETCH, :] = ref[i * STRETCH : (i + 1) * STRETCH, cols].astype(F32)
            for b in range(STRETCH // 8):
                at = base + 8 * b
                totals = []
                for a in range(3):
                    total = taps[a][0] * xs[a, g, at : at + 8, :]
                    for j in range(1, REACH + 1):
                        total = total + taps[a][j] * xs[a, g, at - j : at - j + 8, :]
                    totals.append(total)
                query, mixed = totals[0], totals[1] * totals[2]
                if b == 0:
                    query = jnp.where(first_row >= REACH, query, 1.0)
                    mixed = jnp.where(first_row >= REACH, mixed, 0.0)
                rows = slice(i * STRETCH + 8 * b, i * STRETCH + 8 * b + 8)
                qc_ref[g // per, rows, part] = query
                u_vm[g // per, rows, part] = mixed
    for c in range(tile // SPAN):
        cols = slice(c * SPAN, (c + 1) * SPAN)
        rate = rates_ref[:, cols]
        amount = amplitude(rate, res_ref[:, cols])
        weights = [jnp.sum(amount * value, axis=0, keepdims=True) for value in strengths(rate)]
        for i in range(2):
            rows = slice(i * STRETCH, (i + 1) * STRETCH)
            mixed = u_vm[c, rows, :]
            high, low = split(mixed)
            parts = jnp.dot(
                local_ref[...], jnp.concatenate([high, low, high], axis=0), preferred_element_type=F32
            )
            total = skip_ref[:, cols] * mixed
            for p in range(RANK):
                total = total + weights[p] * parts[p * STRETCH : (p + 1) * STRETCH, :]
            y_ref[c, rows, :] = total


def middle_kernel(
    perm_ref, x_ref, taps_ref, rates_ref, res_ref, skip_ref, out_ref,
    raw, ext, moments, past, heads, first, second, states, mids, coefs, fades, result, slab, packed, out_sems,
):
    slots = perm_ref.shape[0]
    groups = x_ref.shape[2] // LANES
    order = rates_ref.shape[0]
    span = 2 * PIECE
    row = lax.broadcasted_iota(jnp.int32, (8, LANES), 0)
    ext[:, :, 0, 0:8, :] = jnp.zeros((3, groups, 8, LANES), F32)
    past[:, :, 0:8, :] = jnp.zeros((groups, slots, 8, LANES), F32)

    def unpack(src, carry):
        for g in range(groups):
            raw[src, g, 8 : 8 + span, :] = x_ref[src, :, g * LANES : (g + 1) * LANES].astype(F32)
        for i in range(2):
            n = perm_ref[2 * src + i]
            for g in range(groups):
                for a in range(3):
                    at = 8 + i * PIECE + a * REACH
                    ext[a, g, n + 1, 0:8, :] = raw[src, g, at + REACH - 8 : at + REACH, :]
                    at = at + 3 * REACH
                    ext[a, g, n, 8:16, :] = raw[src, g, at : at + 8, :]
                at = 8 + i * PIECE + RAW
                fine = jnp.where(row < FINE, raw[src, g, at + RANK : at + RANK + 8, :], 0.0)
                moments[g, n] = raw[src, g, at : at + 8, :] + fine
        return carry

    lax.fori_loop(0, slots // 2, unpack, 0, unroll=2)

    def group_pass(g, carry):
        cols = pl.ds(pl.multiple_of(g * LANES, LANES), LANES)
        rate = rates_ref[:, cols]
        amount = amplitude(rate, res_ref[:, cols])
        basis = strengths(rate)
        powers = [jnp.ones_like(rate), jnp.exp(-rate)]
        for d in range(2, REACH + 1):
            powers.append(powers[-1] * powers[1])
        for t in range(REACH):
            coefs[g, 0, t * order : (t + 1) * order, :] = amount * powers[t + 1]
        for p in range(RANK):
            coefs[g, 1, p * order : (p + 1) * order, :] = amount * powers[1] * basis[p]
        fade_rest = jnp.exp(-rate * float(INNER))
        fades[g, 0] = powers[REACH]
        fades[g, 1] = fade_rest * powers[REACH]
        taps = [[taps_ref[a, j : j + 1, cols] for j in range(REACH + 1)] for a in range(3)]
        near = [jnp.sum(amount * powers[d], axis=0, keepdims=True) for d in range(REACH)]
        near[0] = near[0] + skip_ref[:, cols]

        def head_pass(n, carry):
            feats = []
            for a in range(3):
                total = taps[a][0] * ext[a, g, n, 8:16, :]
                for j in range(1, REACH + 1):
                    total = total + taps[a][j] * ext[a, g, n, 8 - j : 16 - j, :]
                feats.append(jnp.where(row < REACH, total, 0.0))
            mixed = feats[1] * feats[2]
            past[g, n, 8:16, :] = mixed
            total = near[0] * mixed
            for d in range(1, REACH):
                total = total + near[d] * past[g, n, 8 - d : 16 - d, :]
            at = pl.multiple_of(n * 16, 16)
            heads[g, pl.ds(at, 8), :] = feats[0]
            heads[g, pl.ds(at + 8, 8), :] = total
            value = powers[REACH - 1] * past[g, n, 8:9, :]
            for s in range(1, REACH):
                value = value + powers[REACH - 1 - s] * past[g, n, 8 + s : 9 + s, :]
            first[g, n] = value
            return carry

        lax.fori_loop(0, slots, head_pass, 0, unroll=4)

        def rest_pass(n, carry):
            value = fade_rest * first[g, n]
            for p in range(RANK):
                value = value + basis[p] * moments[g, n, p : p + 1, :]
            second[g, n] = value
            return carry

        lax.fori_loop(0, slots, rest_pass, 0, unroll=4)
        return carry

    lax.fori_loop(0, groups, group_pass, 0)

    def scan_pass(n, state):
        after = []
        at = pl.multiple_of(n * order, order)
        for g in range(groups):
            states[g, pl.ds(at, order), :] = state[g]
            mids[g, pl.ds(at, order), :] = fades[g, 0] * state[g] + first[g, n]
            after.append(fades[g, 1] * state[g] + second[g, n])
        return tuple(after)

    lax.fori_loop(0, slots, scan_pass, tuple(jnp.zeros((order, LANES), F32) for _ in range(groups)), unroll=4)

    quad = 4

    def sums(g, kind, held, first_tile):
        totals = [[None] * quad for _ in range(RANK)]
        for r in range(order):
            values = [held[g, pl.ds((first_tile + k) * 8 * order + r, 8, stride=order), :] for k in range(quad)]
            for p in range(RANK):
                weight = coefs[g, kind, p * order + r : p * order + r + 1, :]
                for k in range(quad):
                    term = weight * values[k]
                    totals[p][k] = term if r == 0 else totals[p][k] + term
        return totals

    quads = slots // (8 * quad)

    def out_pass(step, carry):
        g, q = step // quads, lax.rem(step, quads)
        totals = sums(g, 0, states, q * quad)
        for t in range(REACH):
            for k in range(quad):
                tile = q * quad + k
                query = heads[g, pl.ds(tile * 128 + t, 8, stride=16), :]
                local = heads[g, pl.ds(tile * 128 + 8 + t, 8, stride=16), :]
                z = query * (local + totals[t][k])
                result[g, pl.ds(tile * 192 + t, 8, stride=24), :] = z
                result[g, pl.ds(tile * 192 + REACH + t, 8, stride=24), :] = z - z.astype(BF16).astype(F32)
        totals = sums(g, 1, mids, q * quad)
        for p in range(RANK):
            for k in range(quad):
                tile = q * quad + k
                value = totals[p][k]
                result[g, pl.ds(tile * 192 + 2 * REACH + p, 8, stride=24), :] = value
                if p < FINE:
                    rest = value - value.astype(BF16).astype(F32)
                    result[g, pl.ds(tile * 192 + 2 * REACH + RANK + p, 8, stride=24), :] = rest
        return carry

    lax.fori_loop(0, groups * quads, out_pass, 0)

    def store(src):
        return pltpu.make_async_copy(packed.at[src], out_ref.at[src], out_sems.at[src])

    def pack(src, carry):
        for g in range(groups):
            for i in range(2):
                at = pl.multiple_of(perm_ref[2 * src + i] * 24, 8)
                slab[src, g, i * BACK : i * BACK + 24, :] = result[g, pl.ds(at, 24), :]
            packed[src, :, g * LANES : (g + 1) * LANES] = slab[src, g, 0 : 2 * BACK, :].astype(BF16)
        return carry

    lax.fori_loop(0, slots // 2, pack, 0, unroll=2)

    def send(src, carry):
        store(src).start()
        return carry

    def end(src, carry):
        store(src).wait()
        return carry

    lax.fori_loop(0, slots // 2, send, 0)
    lax.fori_loop(0, slots // 2, end, 0)


def join_kernel(back_ref, lift_ref, qc_ref, y_ref, z_ref, sq_ref, qc_vm, carry, total, sems):
    blocks, tokens, _ = qc_vm.shape
    by_dest = len(back_ref.shape) == 3
    chunk = 4

    def load(c):
        rows = pl.ds(c * chunk, chunk)
        return pltpu.make_async_copy(qc_ref.at[rows], qc_vm.at[rows], sems.at[c])

    def lanes(b):
        return pl.ds(pl.multiple_of(b * SPAN, SPAN), SPAN)

    for c in range(blocks // chunk):
        load(c).start()

    def products(c, unused):
        for k in range(chunk):
            b = c * chunk + k
            back = back_ref[b] if by_dest else back_ref[:, lanes(b)]
            product = jnp.dot(lift_ref[0], back, preferred_element_type=F32)
            carry[b] = y_ref[b] + product + jnp.dot(lift_ref[1], back, preferred_element_type=F32)
        return unused

    lax.fori_loop(0, blocks // chunk, products, 0)
    total[...] = jnp.zeros((tokens, LANES), F32)

    def square(c, unused):
        load(c).wait()
        part = total[...]
        for k in range(chunk):
            b = c * chunk + k
            z = qc_vm[b] * carry[b]
            z_ref[:, lanes(b)] = z
            squares = z * z
            for h in range(SPAN // LANES):
                part = part + squares[:, h * LANES : (h + 1) * LANES]
        total[...] = part
        return unused

    lax.fori_loop(0, blocks // chunk, square, 0)
    sq_ref[...] = jnp.sum(total[...].T, axis=0, keepdims=True)


def scale_kernel(*refs, channels):
    z_ref, gain_ref, refs, (out_ref, held, sems) = refs[0], refs[1], refs[2:-3], refs[-3:]
    tokens, width = z_ref.shape
    chunks = sems.shape[0]
    wide = width // chunks
    total = refs[0][...]
    for ref in refs[1:]:
        total = total + ref[...]
    scale = lax.rsqrt(total / channels + 1e-05)
    scale = jnp.broadcast_to(scale, (LANES, tokens)).T
    copies = []
    for c in range(chunks):
        for g in range(c * wide // LANES, (c + 1) * wide // LANES):
            cols = slice(g * LANES, (g + 1) * LANES)
            held[:, cols] = (z_ref[:, cols] * scale * gain_ref[:, cols]).astype(BF16)
        cols = pl.ds(c * wide, wide)
        copy = pltpu.make_async_copy(held.at[:, cols], out_ref.at[:, cols], sems.at[c])
        copy.start()
        copies.append(copy)
    for copy in copies:
        copy.wait()


def limit(mib):
    return pltpu.CompilerParams(vmem_limit_bytes=mib * 1024 * 1024)


def on_device(sizes, q_in, k_in, v_in, stretch_of_slot, short_weight, rates, residues, skip, gain):
    n_ctx, n_ch = sizes
    tokens, width = q_in.shape
    slots = stretch_of_slot.shape[0]
    order = rates.shape[0]
    share = width // n_ctx
    direct = share == SPAN
    tile = min(width, 1024)
    steps = width // tile
    groups = tile // LANES
    ends_np, local_np, lift_np = constant_matrices()
    ends, local, lift = jnp.asarray(ends_np), jnp.asarray(local_np), jnp.asarray(lift_np)
    skip, gain = skip.reshape(1, width), gain.reshape(1, width)
    me = lax.axis_index("ctx").astype(jnp.int32).reshape(1)

    def whole(array):
        return pl.BlockSpec(array.shape, lambda c: (0,) * array.ndim)

    def columns(*lead):
        return pl.BlockSpec((*lead, tile), lambda c: (0,) * len(lead) + (c,))

    def exchange(array):
        if direct:
            return lax.all_to_all(array, "ctx", 0, 0, tiled=True)
        array = array.reshape(array.shape[0], n_ctx, share).transpose(1, 0, 2)
        return widen(lax.all_to_all(array, "ctx", 0, 0, tiled=True))

    lanes = -(-share // LANES) * LANES

    def widen(array, fill=0.0):
        pad = [(0, 0)] * (array.ndim - 1) + [(0, lanes - share)]
        return jnp.pad(array, pad, constant_values=fill)

    def cut(array, fill=0.0):
        return widen(lax.dynamic_slice_in_dim(array, lax.axis_index("ctx") * share, share, array.ndim - 1), fill)

    smem = pl.BlockSpec(memory_space=pltpu.SMEM)
    vmem = pl.BlockSpec(memory_space=pltpu.VMEM)
    hbm = pl.BlockSpec(memory_space=pltpu.HBM)
    f32 = lambda *shape: jax.ShapeDtypeStruct(shape, F32)
    pin = lambda array: pltpu.with_memory_space_constraint(array, pltpu.HBM)

    weights = (short_weight, rates, residues, skip)
    own = [f32(*w.shape[:-1], share) for w in weights] if direct else []
    blocks = width // SPAN
    pay, *mine = pl.pallas_call(
        functools.partial(front_kernel, direct=direct),
        in_specs=[smem] + [hbm] * (5 + len(own)),
        out_specs=[hbm] + [vmem] * len(own),
        out_shape=[
            pltpu.HBM((n_ctx, 2 * PIECE, share) if direct else (2 * PIECE, width), BF16),
        ]
        + own,
        scratch_shapes=[
            pltpu.VMEM((2, tokens, width), BF16),
            pltpu.VMEM((4, 16, width), BF16),
            pltpu.VMEM((blocks, 2, REACH + 1, SPAN), F32),
            pltpu.VMEM(ends.shape, BF16),
            pltpu.VMEM((2, 2, 2, 2 * (STRETCH + 8), LANES), F32),
            pltpu.VMEM((2, 2, 2, 32, LANES), F32),
            pltpu.VMEM((blocks, 2, 2 * PIECE, LANES), F32),
            pltpu.VMEM((blocks, 2 * PIECE, SPAN), BF16),
            pltpu.VMEM((blocks, 2, tokens, SPAN), BF16),
            pltpu.SemaphoreType.DMA((3, blocks)),
            pltpu.SemaphoreType.DMA((4,)),
            pltpu.SemaphoreType.DMA((1,)),
            pltpu.SemaphoreType.DMA((4,)),
            pltpu.SemaphoreType.DMA((blocks,)),
        ],
        compiler_params=limit(24),
        name="front_pieces",
    )(me, *map(pin, (q_in, k_in, v_in, short_weight, ends)), *(map(pin, weights) if direct else ()))
    arrived = exchange(pay)
    if not direct:
        mine = (cut(short_weight), cut(rates, 0.01), cut(residues), cut(skip))

    query, inner = pl.pallas_call(
        local_kernel,
        grid=(steps,),
        in_specs=[columns(tokens)] * 3
        + [columns(3, REACH + 1), columns(order), columns(order), columns(1), whole(local)],
        out_specs=[pl.BlockSpec((tile // SPAN, tokens, SPAN), lambda c: (c, 0, 0))] * 2,
        out_shape=[pltpu.HBM((blocks, tokens, SPAN), F32), pltpu.VMEM((blocks, tokens, SPAN), F32)],
        scratch_shapes=[
            pltpu.VMEM((3, groups, 2 * (STRETCH + 8), LANES), F32),
            pltpu.VMEM((tile // SPAN, tokens, SPAN), F32),
        ],
        compiler_params=limit(24),
        name="local_filter",
        cost_estimate=pl.CostEstimate(flops=10**9, bytes_accessed=20 * 10**6, transcendentals=0),
    )(*map(pin, (q_in, k_in, v_in, short_weight, rates, residues)), skip, local)
    arrived, query, inner = lax.optimization_barrier((arrived, query, inner))

    groups = lanes // LANES
    back = pl.pallas_call(
        middle_kernel,
        in_specs=[smem] + [vmem] * 5,
        out_specs=hbm,
        scratch_shapes=[
            pltpu.VMEM((n_ctx, groups, 8 + 2 * PIECE + 8, LANES), F32),
            pltpu.VMEM((3, groups, slots + 1, 16, LANES), F32),
            pltpu.VMEM((groups, slots, 8, LANES), F32),
            pltpu.VMEM((groups, slots, 16, LANES), F32),
            pltpu.VMEM((groups, slots * 16, LANES), F32),
            pltpu.VMEM((groups, slots, order, LANES), F32),
            pltpu.VMEM((groups, slots, order, LANES), F32),
            pltpu.VMEM((groups, slots * order, LANES), F32),
            pltpu.VMEM((groups, slots * order, LANES), F32),
            pltpu.VMEM((groups, 2, RANK * order, LANES), F32),
            pltpu.VMEM((groups, 2, order, LANES), F32),
            pltpu.VMEM((groups, slots * 24, LANES), F32),
            pltpu.VMEM((n_ctx, groups, BACK + 28, LANES), F32),
            pltpu.VMEM((n_ctx, 2 * BACK, lanes), BF16),
            pltpu.SemaphoreType.DMA((n_ctx,)),
        ],
        out_shape=pltpu.HBM((n_ctx, 2 * BACK, lanes), BF16),
        compiler_params=limit(24),
        name="middle_states",
    )(stretch_of_slot, arrived, *mine)
    if not direct:
        back = back[:, :, :share]
    back = lax.all_to_all(back, "ctx", 0, 0, tiled=True)
    if not direct:
        back = back.transpose(1, 0, 2).reshape(2 * BACK, width)

    keep = lambda array: pltpu.with_memory_space_constraint(array, pltpu.VMEM)
    zvalues, squares = pl.pallas_call(
        join_kernel,
        in_specs=[vmem] * 2 + [hbm, vmem],
        out_specs=[vmem] * 2,
        out_shape=[f32(tokens, width), f32(1, tokens)],
        scratch_shapes=[pltpu.VMEM((blocks, tokens, SPAN), F32)] * 2
        + [pltpu.VMEM((tokens, LANES), F32), pltpu.SemaphoreType.DMA((blocks // 4,))],
        compiler_params=limit(24),
        name="join_carry",
    )(back, lift, pin(query), keep(inner))
    sums = [squares]
    for shift in range(1, n_ch):
        sums.append(lax.ppermute(squares, "ch", [(i, (i + shift) % n_ch) for i in range(n_ch)]))
    return pl.pallas_call(
        functools.partial(scale_kernel, channels=width * n_ch),
        in_specs=[vmem] * (2 + n_ch),
        out_specs=hbm,
        out_shape=pltpu.HBM((tokens, width), BF16),
        scratch_shapes=[pltpu.VMEM((tokens, width), BF16), pltpu.SemaphoreType.DMA((8 if width % 1024 == 0 else 1,))],
        compiler_params=limit(24),
        name="scale_rows",
    )(zvalues, gain, *sums)


def solution(mesh):
    sizes = (mesh.shape["ctx"], mesh.shape["ch"])
    in_specs = (
        P("ctx", "ch"),
        P("ctx", "ch"),
        P("ctx", "ch"),
        P(),
        P(None, None, "ch"),
        P(None, "ch"),
        P(None, "ch"),
        P("ch"),
        P("ch"),
    )

    def run(*arrays):
        return on_device(sizes, *arrays)

    return jax.shard_map(run, mesh=mesh, in_specs=in_specs, out_specs=P("ctx", "ch"), check_vma=False)
```

```python
import functools
from decimal import Decimal, getcontext

import jax
import jax.numpy as jnp
import ml_dtypes
import numpy as np
from jax import lax
from jax.experimental import pallas as pl
from jax.experimental.pallas import tpu as pltpu
from jax.sharding import PartitionSpec as P

F32, BF16 = jnp.float32, jnp.bfloat16
LANES = 128
SPAN = 256
WIDE = 4
STRETCH = 64
REACH = 6
INNER = STRETCH - REACH
PIVOTS = (8, 49, 21, 56, 36, 1)
ANCHORS = ("0.0020", "0.0235", "0.0110", "0.0295", "0.0185", "0.0004")
RANK = len(PIVOTS)
FINE = 2
COEFS = RANK + FINE
RAW = 6 * REACH
PIECE = RAW + COEFS
BACK = 2 * REACH + COEFS


def shape_table():
    getcontext().prec = 50
    rest = [[(-Decimal(a) * d).exp() for d in range(INNER)] for a in ANCHORS]
    table = []
    for p in range(RANK):
        shape = [x / rest[p][PIVOTS[p]] for x in rest[p]]
        rest = [[x - row[PIVOTS[p]] * y for x, y in zip(row, shape)] for row in rest]
        table.append([float(x) for x in shape])
    return table


SHAPE = shape_table()


def halves(values):
    high = values.astype(ml_dtypes.bfloat16)
    low = (values - high.astype(np.float32)).astype(ml_dtypes.bfloat16)
    return high, low


def constant_matrices():
    shape = np.array(SHAPE, np.float32)
    ends = np.zeros((16, STRETCH), np.float32)
    local = np.zeros((RANK, STRETCH, STRETCH), np.float32)
    lift = np.zeros((2, 2 * STRETCH, 2 * BACK), np.float32)
    parts = [h.astype(np.float32) for h in halves(shape)]
    for p in range(RANK):
        for s in range(REACH, STRETCH):
            ends[p, s] = shape[p, STRETCH - 1 - s]
            local[p, s:, s] = shape[p, : STRETCH - s]
        for half in range(2):
            rows = slice(half * STRETCH + REACH, (half + 1) * STRETCH)
            at = half * BACK + 2 * REACH
            for k in range(2):
                lift[k, rows, at + p] = parts[k][p]
                if p < FINE:
                    lift[k, rows, at + RANK + p] = parts[k][p]
    for half in range(2):
        for t in range(REACH):
            lift[0, half * STRETCH + t, half * BACK + t] = 1.0
            lift[0, half * STRETCH + t, half * BACK + REACH + t] = 1.0
    local = local.reshape(RANK * STRETCH, STRETCH)

    def triple(m):
        h, l = halves(m)
        return np.concatenate([h, h, l], axis=1)

    return triple(ends), triple(local), lift.astype(ml_dtypes.bfloat16)


def strengths(rate):
    found = []
    for p in range(RANK):
        value = jnp.exp(-rate * float(PIVOTS[p]))
        for q in range(p):
            value = value - found[q] * SHAPE[q][PIVOTS[p]]
        found.append(value)
    return found


def split(values):
    high = values.astype(BF16)
    return high, (values - high.astype(F32)).astype(BF16)


def amplitude(rate, residue):
    x = 2.0 * rate
    series = 1.0 - x * (0.5 - x * (1 / 6 - x * (1 / 24 - x * (1 / 120 - x * (1 / 720)))))
    return residue * jnp.sqrt(x * series)


EDGES = (0, STRETCH - 16, STRETCH, 2 * STRETCH - 16)


def front_kernel(*refs, direct):
    me_ref, q_ref, k_ref, v_ref, taps_ref, ends_ref = refs[:6]
    refs = refs[6:]
    weights, refs = (refs[:4], refs[4:]) if direct else ((), refs)
    pay_ref, refs = refs[0], refs[1:]
    kept, refs = (refs[:4], refs[4:]) if direct else ((), refs)
    held, edge, taps_vm, ends_vm, xs, qs, pay, packed, u_vm, in_sems, edge_sems, tap_sem, own_sems, out_sems = refs
    blocks = k_ref.shape[1] // SPAN

    def lanes(c):
        return pl.ds(pl.multiple_of(c * SPAN, SPAN), SPAN)

    def loads(w):
        cols = pl.ds(pl.multiple_of(w * WIDE * SPAN, SPAN), WIDE * SPAN)
        return [
            pltpu.make_async_copy(ref.at[:, cols], held.at[a, :, cols], in_sems.at[a, w])
            for a, ref in enumerate((k_ref, v_ref))
        ] + [pltpu.make_async_copy(taps_ref.at[pl.ds(1, 2), :, cols], taps_vm.at[:, :, cols], in_sems.at[2, w])]

    def edge_loads():
        return [
            pltpu.make_async_copy(q_ref.at[pl.ds(at, 16), :], edge.at[e], edge_sems.at[e])
            for e, at in enumerate(EDGES)
        ]

    def stores(c):
        target = pay_ref.at[c] if direct else pay_ref.at[:, lanes(c)]
        return [pltpu.make_async_copy(packed.at[c], target, out_sems.at[c])]

    def own_loads():
        share = kept[0].shape[-1]
        cols = pl.ds(pl.multiple_of(me_ref[0] * share, share), share)
        views = (weights[0].at[:, :, cols], weights[1].at[:, cols], weights[2].at[:, cols], weights[3].at[:, cols])
        return [pltpu.make_async_copy(view, ref, own_sems.at[n]) for n, (view, ref) in enumerate(zip(views, kept))]

    ends_copy = pltpu.make_async_copy(ends_ref, ends_vm, tap_sem.at[0])
    for copy in loads(0) + edge_loads():
        copy.start()
    ends_copy.start()
    waves = blocks // WIDE

    def begin(c, carry):
        for copy in loads(c):
            copy.start()
        return carry

    lax.fori_loop(1, waves, begin, 0)
    if direct:
        for copy in own_loads():
            copy.start()
    for parity in range(2):
        for a in range(2):
            for h in range(2):
                for i in range(2):
                    at = i * (STRETCH + 8)
                    xs[parity, a, h, at : at + 8, :] = jnp.zeros((8, LANES), F32)
    for copy in edge_loads():
        copy.wait()
    ends_copy.wait()

    def features(c, carry):
        @pl.when(lax.rem(c, WIDE) == 0)
        def _():
            for copy in loads(c // WIDE):
                copy.wait()

        parity = lax.rem(c, 2)
        for h in range(2):
            part = slice(h * LANES, (h + 1) * LANES)
            cols = pl.ds(pl.multiple_of(c * SPAN + h * LANES, LANES), LANES)
            for i in range(2):
                base = i * (STRETCH + 8) + 8
                for a in range(2):
                    xs[parity, a, h, base : base + STRETCH, :] = held[
                        a, i * STRETCH : (i + 1) * STRETCH, cols
                    ].astype(F32)
                    at = i * PIECE + (1 + a) * REACH
                    pay[c, h, at : at + REACH, :] = xs[parity, a, h, base + STRETCH - REACH : base + STRETCH, :]
                    at = at + 3 * REACH
                    pay[c, h, at : at + REACH, :] = xs[parity, a, h, base : base + REACH, :]
                qs[parity, h, i, 0:16, :] = edge[2 * i, :, cols].astype(F32)
                qs[parity, h, i, 16:32, :] = edge[2 * i + 1, :, cols].astype(F32)
                at = i * PIECE
                pay[c, h, at : at + REACH, :] = qs[parity, h, i, 32 - REACH : 32, :]
                pay[c, h, at + 3 * REACH : at + 4 * REACH, :] = qs[parity, h, i, 0:REACH, :]
            taps = [[taps_vm[a, j : j + 1, cols] for j in range(REACH + 1)] for a in range(2)]
            for i in range(2):
                for b in range(STRETCH // 16):
                    base = i * (STRETCH + 8) + 8 + 16 * b
                    both = []
                    for a in range(2):
                        total = taps[a][0] * xs[parity, a, h, base : base + 16, :]
                        for j in range(1, REACH + 1):
                            total = total + taps[a][j] * xs[parity, a, h, base - j : base - j + 16, :]
                        both.append(total)
                    mixed = both[0] * both[1]
                    if b == 0:
                        row = lax.broadcasted_iota(jnp.int32, (16, LANES), 0)
                        mixed = jnp.where(row >= REACH, mixed, 0.0)
                    high, low = split(mixed)
                    rows = slice(i * STRETCH + 16 * b, i * STRETCH + 16 * b + 16)
                    u_vm[c, 0, rows, part] = high
                    u_vm[c, 1, rows, part] = low
        return carry

    lax.fori_loop(0, blocks, features, 0)
    chunk = 4

    def finish(step, carry):
        for k in range(chunk):
            c = step * chunk + k
            for i in range(2):
                rows = slice(i * STRETCH, (i + 1) * STRETCH)
                high, low = u_vm[c, 0, rows, :], u_vm[c, 1, rows, :]
                stacked = jnp.concatenate([high, low, high], axis=0)
                moments = jnp.dot(ends_vm[...], stacked, preferred_element_type=F32)[:8]
                rest = (moments - moments.astype(BF16).astype(F32))[:FINE]
                at = PIECE * i + RAW
                for h in range(2):
                    part = slice(h * LANES, (h + 1) * LANES)
                    pay[c, h, at : at + RANK, :] = moments[:RANK, part]
                    pay[c, h, at + RANK : at + COEFS, :] = rest[:, part]
            for h in range(2):
                packed[c, :, h * LANES : (h + 1) * LANES] = pay[c, h].astype(BF16)
        for k in range(chunk):
            for copy in stores(step * chunk + k):
                copy.start()
        return carry

    lax.fori_loop(0, blocks // chunk, finish, 0)

    def end(c, carry):
        for copy in stores(c):
            copy.wait()
        return carry

    lax.fori_loop(0, blocks, end, 0)
    if direct:
        for copy in own_loads():
            copy.wait()


def local_kernel(
    q_ref, k_ref, v_ref, taps_ref, rates_ref, res_ref, skip_ref, local_ref, qc_ref, y_ref, xs, u_vm
):
    tile = q_ref.shape[1]
    per = SPAN // LANES
    first_row = lax.broadcasted_iota(jnp.int32, (8, LANES), 0)
    for g in range(tile // LANES):
        cols = slice(g * LANES, (g + 1) * LANES)
        part = slice(g % per * LANES, (g % per + 1) * LANES)
        taps = [[taps_ref[a, j : j + 1, cols] for j in range(REACH + 1)] for a in range(3)]
        for i in range(2):
            base = i * (STRETCH + 8) + 8
            for a, ref in enumerate((q_ref, k_ref, v_ref)):
                xs[a, g, base - 8 : base, :] = jnp.zeros((8, LANES), F32)
                xs[a, g, base : base + STRETCH, :] = ref[i * STRETCH : (i + 1) * STRETCH, cols].astype(F32)
            for b in range(STRETCH // 8):
                at = base + 8 * b
                totals = []
                for a in range(3):
                    total = taps[a][0] * xs[a, g, at : at + 8, :]
                    for j in range(1, REACH + 1):
                        total = total + taps[a][j] * xs[a, g, at - j : at - j + 8, :]
                    totals.append(total)
                query, mixed = totals[0], totals[1] * totals[2]
                if b == 0:
                    query = jnp.where(first_row >= REACH, query, 1.0)
                    mixed = jnp.where(first_row >= REACH, mixed, 0.0)
                rows = slice(i * STRETCH + 8 * b, i * STRETCH + 8 * b + 8)
                qc_ref[g // per, rows, part] = query
                u_vm[g // per, rows, part] = mixed
    for c in range(tile // SPAN):
        cols = slice(c * SPAN, (c + 1) * SPAN)
        rate = rates_ref[:, cols]
        amount = amplitude(rate, res_ref[:, cols])
        weights = [jnp.sum(amount * value, axis=0, keepdims=True) for value in strengths(rate)]
        for i in range(2):
            rows = slice(i * STRETCH, (i + 1) * STRETCH)
            mixed = u_vm[c, rows, :]
            high, low = split(mixed)
            parts = jnp.dot(
                local_ref[...], jnp.concatenate([high, low, high], axis=0), preferred_element_type=F32
            )
            total = skip_ref[:, cols] * mixed
            for p in range(RANK):
                total = total + weights[p] * parts[p * STRETCH : (p + 1) * STRETCH, :]
            y_ref[c, rows, :] = total


def middle_kernel(
    perm_ref, x_ref, taps_ref, rates_ref, res_ref, skip_ref, out_ref,
    raw, ext, moments, past, heads, first, second, states, mids, coefs, fades, result, slab, packed, out_sems,
):
    slots = perm_ref.shape[0]
    groups = x_ref.shape[2] // LANES
    order = rates_ref.shape[0]
    span = 2 * PIECE
    row = lax.broadcasted_iota(jnp.int32, (8, LANES), 0)
    ext[:, :, 0, 0:8, :] = jnp.zeros((3, groups, 8, LANES), F32)
    past[:, :, 0:8, :] = jnp.zeros((groups, slots, 8, LANES), F32)

    def unpack(src, carry):
        for g in range(groups):
            raw[src, g, 8 : 8 + span, :] = x_ref[src, :, g * LANES : (g + 1) * LANES].astype(F32)
        for i in range(2):
            n = perm_ref[2 * src + i]
            for g in range(groups):
                for a in range(3):
                    at = 8 + i * PIECE + a * REACH
                    ext[a, g, n + 1, 0:8, :] = raw[src, g, at + REACH - 8 : at + REACH, :]
                    at = at + 3 * REACH
                    ext[a, g, n, 8:16, :] = raw[src, g, at : at + 8, :]
                at = 8 + i * PIECE + RAW
                fine = jnp.where(row < FINE, raw[src, g, at + RANK : at + RANK + 8, :], 0.0)
                moments[g, n] = raw[src, g, at : at + 8, :] + fine
        return carry

    lax.fori_loop(0, slots // 2, unpack, 0, unroll=2)

    def group_pass(g, carry):
        cols = pl.ds(pl.multiple_of(g * LANES, LANES), LANES)
        rate = rates_ref[:, cols]
        amount = amplitude(rate, res_ref[:, cols])
        basis = strengths(rate)
        powers = [jnp.ones_like(rate), jnp.exp(-rate)]
        for d in range(2, REACH + 1):
            powers.append(powers[-1] * powers[1])
        for t in range(REACH):
            coefs[g, 0, t * order : (t + 1) * order, :] = amount * powers[t + 1]
        for p in range(RANK):
            coefs[g, 1, p * order : (p + 1) * order, :] = amount * powers[1] * basis[p]
        fade_rest = jnp.exp(-rate * float(INNER))
        fades[g, 0] = powers[REACH]
        fades[g, 1] = fade_rest * powers[REACH]
        taps = [[taps_ref[a, j : j + 1, cols] for j in range(REACH + 1)] for a in range(3)]
        near = [jnp.sum(amount * powers[d], axis=0, keepdims=True) for d in range(REACH)]
        near[0] = near[0] + skip_ref[:, cols]

        def head_pass(n, carry):
            feats = []
            for a in range(3):
                total = taps[a][0] * ext[a, g, n, 8:16, :]
                for j in range(1, REACH + 1):
                    total = total + taps[a][j] * ext[a, g, n, 8 - j : 16 - j, :]
                feats.append(jnp.where(row < REACH, total, 0.0))
            mixed = feats[1] * feats[2]
            past[g, n, 8:16, :] = mixed
            total = near[0] * mixed
            for d in range(1, REACH):
                total = total + near[d] * past[g, n, 8 - d : 16 - d, :]
            at = pl.multiple_of(n * 16, 16)
            heads[g, pl.ds(at, 8), :] = feats[0]
            heads[g, pl.ds(at + 8, 8), :] = total
            value = powers[REACH - 1] * past[g, n, 8:9, :]
            for s in range(1, REACH):
                value = value + powers[REACH - 1 - s] * past[g, n, 8 + s : 9 + s, :]
            first[g, n] = value
            return carry

        lax.fori_loop(0, slots, head_pass, 0, unroll=4)

        def rest_pass(n, carry):
            value = fade_rest * first[g, n]
            for p in range(RANK):
                value = value + basis[p] * moments[g, n, p : p + 1, :]
            second[g, n] = value
            return carry

        lax.fori_loop(0, slots, rest_pass, 0, unroll=4)
        return carry

    lax.fori_loop(0, groups, group_pass, 0)

    def scan_pass(n, state):
        after = []
        at = pl.multiple_of(n * order, order)
        for g in range(groups):
            states[g, pl.ds(at, order), :] = state[g]
            mids[g, pl.ds(at, order), :] = fades[g, 0] * state[g] + first[g, n]
            after.append(fades[g, 1] * state[g] + second[g, n])
        return tuple(after)

    lax.fori_loop(0, slots, scan_pass, tuple(jnp.zeros((order, LANES), F32) for _ in range(groups)), unroll=4)

    quad = 4

    def sums(g, kind, held, first_tile):
        totals = [[None] * quad for _ in range(RANK)]
        for r in range(order):
            values = [held[g, pl.ds((first_tile + k) * 8 * order + r, 8, stride=order), :] for k in range(quad)]
            for p in range(RANK):
                weight = coefs[g, kind, p * order + r : p * order + r + 1, :]
                for k in range(quad):
                    term = weight * values[k]
                    totals[p][k] = term if r == 0 else totals[p][k] + term
        return totals

    quads = slots // (8 * quad)

    def out_pass(step, carry):
        g, q = step // quads, lax.rem(step, quads)
        totals = sums(g, 0, states, q * quad)
        for t in range(REACH):
            for k in range(quad):
                tile = q * quad + k
                query = heads[g, pl.ds(tile * 128 + t, 8, stride=16), :]
                local = heads[g, pl.ds(tile * 128 + 8 + t, 8, stride=16), :]
                z = query * (local + totals[t][k])
                result[g, pl.ds(tile * 192 + t, 8, stride=24), :] = z
                result[g, pl.ds(tile * 192 + REACH + t, 8, stride=24), :] = z - z.astype(BF16).astype(F32)
        totals = sums(g, 1, mids, q * quad)
        for p in range(RANK):
            for k in range(quad):
                tile = q * quad + k
                value = totals[p][k]
                result[g, pl.ds(tile * 192 + 2 * REACH + p, 8, stride=24), :] = value
                if p < FINE:
                    rest = value - value.astype(BF16).astype(F32)
                    result[g, pl.ds(tile * 192 + 2 * REACH + RANK + p, 8, stride=24), :] = rest
        return carry

    lax.fori_loop(0, groups * quads, out_pass, 0)

    def store(src):
        return pltpu.make_async_copy(packed.at[src], out_ref.at[src], out_sems.at[src])

    def pack(src, carry):
        for g in range(groups):
            for i in range(2):
                at = pl.multiple_of(perm_ref[2 * src + i] * 24, 8)
                slab[src, g, i * BACK : i * BACK + 24, :] = result[g, pl.ds(at, 24), :]
            packed[src, :, g * LANES : (g + 1) * LANES] = slab[src, g, 0 : 2 * BACK, :].astype(BF16)
        return carry

    lax.fori_loop(0, slots // 2, pack, 0, unroll=2)

    def send(src, carry):
        store(src).start()
        return carry

    def end(src, carry):
        store(src).wait()
        return carry

    lax.fori_loop(0, slots // 2, send, 0)
    lax.fori_loop(0, slots // 2, end, 0)


def join_kernel(back_ref, lift_ref, qc_ref, y_ref, z_ref, sq_ref, qc_vm, carry, total, sems):
    blocks, tokens, _ = qc_vm.shape
    by_dest = len(back_ref.shape) == 3
    chunk = 4

    def load(c):
        rows = pl.ds(c * chunk, chunk)
        return pltpu.make_async_copy(qc_ref.at[rows], qc_vm.at[rows], sems.at[c])

    def lanes(b):
        return pl.ds(pl.multiple_of(b * SPAN, SPAN), SPAN)

    for c in range(blocks // chunk):
        load(c).start()

    def products(c, unused):
        for k in range(chunk):
            b = c * chunk + k
            back = back_ref[b] if by_dest else back_ref[:, lanes(b)]
            product = jnp.dot(lift_ref[0], back, preferred_element_type=F32)
            carry[b] = y_ref[b] + product + jnp.dot(lift_ref[1], back, preferred_element_type=F32)
        return unused

    lax.fori_loop(0, blocks // chunk, products, 0)
    total[...] = jnp.zeros((tokens, LANES), F32)

    def square(c, unused):
        load(c).wait()
        part = total[...]
        for k in range(chunk):
            b = c * chunk + k
            z = qc_vm[b] * carry[b]
            z_ref[:, lanes(b)] = z
            squares = z * z
            for h in range(SPAN // LANES):
                part = part + squares[:, h * LANES : (h + 1) * LANES]
        total[...] = part
        return unused

    lax.fori_loop(0, blocks // chunk, square, 0)
    sq_ref[...] = jnp.sum(total[...].T, axis=0, keepdims=True)


def scale_kernel(*refs, channels):
    z_ref, gain_ref, refs, (out_ref, held, sems) = refs[0], refs[1], refs[2:-3], refs[-3:]
    tokens, width = z_ref.shape
    chunks = sems.shape[0]
    wide = width // chunks
    total = refs[0][...]
    for ref in refs[1:]:
        total = total + ref[...]
    scale = lax.rsqrt(total / channels + 1e-05)
    scale = jnp.broadcast_to(scale, (LANES, tokens)).T
    copies = []
    for c in range(chunks):
        for g in range(c * wide // LANES, (c + 1) * wide // LANES):
            cols = slice(g * LANES, (g + 1) * LANES)
            held[:, cols] = (z_ref[:, cols] * scale * gain_ref[:, cols]).astype(BF16)
        cols = pl.ds(c * wide, wide)
        copy = pltpu.make_async_copy(held.at[:, cols], out_ref.at[:, cols], sems.at[c])
        copy.start()
        copies.append(copy)
    for copy in copies:
        copy.wait()


def limit(mib):
    return pltpu.CompilerParams(vmem_limit_bytes=mib * 1024 * 1024)


def on_device(sizes, q_in, k_in, v_in, stretch_of_slot, short_weight, rates, residues, skip, gain):
    n_ctx, n_ch = sizes
    tokens, width = q_in.shape
    slots = stretch_of_slot.shape[0]
    order = rates.shape[0]
    share = width // n_ctx
    direct = share == SPAN
    tile = min(width, 1024)
    steps = width // tile
    groups = tile // LANES
    ends_np, local_np, lift_np = constant_matrices()
    ends, local, lift = jnp.asarray(ends_np), jnp.asarray(local_np), jnp.asarray(lift_np)
    skip, gain = skip.reshape(1, width), gain.reshape(1, width)
    me = lax.axis_index("ctx").astype(jnp.int32).reshape(1)

    def whole(array):
        return pl.BlockSpec(array.shape, lambda c: (0,) * array.ndim)

    def columns(*lead):
        return pl.BlockSpec((*lead, tile), lambda c: (0,) * len(lead) + (c,))

    def exchange(array):
        if direct:
            return lax.all_to_all(array, "ctx", 0, 0, tiled=True)
        array = array.reshape(array.shape[0], n_ctx, share).transpose(1, 0, 2)
        return widen(lax.all_to_all(array, "ctx", 0, 0, tiled=True))

    lanes = -(-share // LANES) * LANES

    def widen(array, fill=0.0):
        pad = [(0, 0)] * (array.ndim - 1) + [(0, lanes - share)]
        return jnp.pad(array, pad, constant_values=fill)

    def cut(array, fill=0.0):
        return widen(lax.dynamic_slice_in_dim(array, lax.axis_index("ctx") * share, share, array.ndim - 1), fill)

    smem = pl.BlockSpec(memory_space=pltpu.SMEM)
    vmem = pl.BlockSpec(memory_space=pltpu.VMEM)
    hbm = pl.BlockSpec(memory_space=pltpu.HBM)
    f32 = lambda *shape: jax.ShapeDtypeStruct(shape, F32)
    pin = lambda array: pltpu.with_memory_space_constraint(array, pltpu.HBM)

    weights = (short_weight, rates, residues, skip)
    own = [f32(*w.shape[:-1], share) for w in weights] if direct else []
    blocks = width // SPAN
    pay, *mine = pl.pallas_call(
        functools.partial(front_kernel, direct=direct),
        in_specs=[smem] + [hbm] * (5 + len(own)),
        out_specs=[hbm] + [vmem] * len(own),
        out_shape=[
            pltpu.HBM((n_ctx, 2 * PIECE, share) if direct else (2 * PIECE, width), BF16),
        ]
        + own,
        scratch_shapes=[
            pltpu.VMEM((2, tokens, width), BF16),
            pltpu.VMEM((4, 16, width), BF16),
            pltpu.VMEM((2, REACH + 1, width), F32),
            pltpu.VMEM(ends.shape, BF16),
            pltpu.VMEM((2, 2, 2, 2 * (STRETCH + 8), LANES), F32),
            pltpu.VMEM((2, 2, 2, 32, LANES), F32),
            pltpu.VMEM((blocks, 2, 2 * PIECE, LANES), F32),
            pltpu.VMEM((blocks, 2 * PIECE, SPAN), BF16),
            pltpu.VMEM((blocks, 2, tokens, SPAN), BF16),
            pltpu.SemaphoreType.DMA((3, blocks // WIDE)),
            pltpu.SemaphoreType.DMA((4,)),
            pltpu.SemaphoreType.DMA((1,)),
            pltpu.SemaphoreType.DMA((4,)),
            pltpu.SemaphoreType.DMA((blocks,)),
        ],
        compiler_params=limit(24),
        name="front_pieces",
    )(me, *map(pin, (q_in, k_in, v_in, short_weight, ends)), *(map(pin, weights) if direct else ()))
    arrived = exchange(pay)
    if not direct:
        mine = (cut(short_weight), cut(rates, 0.01), cut(residues), cut(skip))

    query, inner = pl.pallas_call(
        local_kernel,
        grid=(steps,),
        in_specs=[columns(tokens)] * 3
        + [columns(3, REACH + 1), columns(order), columns(order), columns(1), whole(local)],
        out_specs=[pl.BlockSpec((tile // SPAN, tokens, SPAN), lambda c: (c, 0, 0))] * 2,
        out_shape=[pltpu.HBM((blocks, tokens, SPAN), F32), pltpu.VMEM((blocks, tokens, SPAN), F32)],
        scratch_shapes=[
            pltpu.VMEM((3, groups, 2 * (STRETCH + 8), LANES), F32),
            pltpu.VMEM((tile // SPAN, tokens, SPAN), F32),
        ],
        compiler_params=limit(24),
        name="local_filter",
        cost_estimate=pl.CostEstimate(flops=10**9, bytes_accessed=20 * 10**6, transcendentals=0),
    )(*map(pin, (q_in, k_in, v_in, short_weight, rates, residues)), skip, local)
    arrived, query, inner = lax.optimization_barrier((arrived, query, inner))

    groups = lanes // LANES
    back = pl.pallas_call(
        middle_kernel,
        in_specs=[smem] + [vmem] * 5,
        out_specs=hbm,
        scratch_shapes=[
            pltpu.VMEM((n_ctx, groups, 8 + 2 * PIECE + 8, LANES), F32),
            pltpu.VMEM((3, groups, slots + 1, 16, LANES), F32),
            pltpu.VMEM((groups, slots, 8, LANES), F32),
            pltpu.VMEM((groups, slots, 16, LANES), F32),
            pltpu.VMEM((groups, slots * 16, LANES), F32),
            pltpu.VMEM((groups, slots, order, LANES), F32),
            pltpu.VMEM((groups, slots, order, LANES), F32),
            pltpu.VMEM((groups, slots * order, LANES), F32),
            pltpu.VMEM((groups, slots * order, LANES), F32),
            pltpu.VMEM((groups, 2, RANK * order, LANES), F32),
            pltpu.VMEM((groups, 2, order, LANES), F32),
            pltpu.VMEM((groups, slots * 24, LANES), F32),
            pltpu.VMEM((n_ctx, groups, BACK + 28, LANES), F32),
            pltpu.VMEM((n_ctx, 2 * BACK, lanes), BF16),
            pltpu.SemaphoreType.DMA((n_ctx,)),
        ],
        out_shape=pltpu.HBM((n_ctx, 2 * BACK, lanes), BF16),
        compiler_params=limit(24),
        name="middle_states",
    )(stretch_of_slot, arrived, *mine)
    if not direct:
        back = back[:, :, :share]
    back = lax.all_to_all(back, "ctx", 0, 0, tiled=True)
    if not direct:
        back = back.transpose(1, 0, 2).reshape(2 * BACK, width)

    keep = lambda array: pltpu.with_memory_space_constraint(array, pltpu.VMEM)
    zvalues, squares = pl.pallas_call(
        join_kernel,
        in_specs=[vmem] * 2 + [hbm, vmem],
        out_specs=[vmem] * 2,
        out_shape=[f32(tokens, width), f32(1, tokens)],
        scratch_shapes=[pltpu.VMEM((blocks, tokens, SPAN), F32)] * 2
        + [pltpu.VMEM((tokens, LANES), F32), pltpu.SemaphoreType.DMA((blocks // 4,))],
        compiler_params=limit(24),
        name="join_carry",
    )(back, lift, pin(query), keep(inner))
    sums = [squares]
    for shift in range(1, n_ch):
        sums.append(lax.ppermute(squares, "ch", [(i, (i + shift) % n_ch) for i in range(n_ch)]))
    return pl.pallas_call(
        functools.partial(scale_kernel, channels=width * n_ch),
        in_specs=[vmem] * (2 + n_ch),
        out_specs=hbm,
        out_shape=pltpu.HBM((tokens, width), BF16),
        scratch_shapes=[pltpu.VMEM((tokens, width), BF16), pltpu.SemaphoreType.DMA((8 if width % 1024 == 0 else 1,))],
        compiler_params=limit(24),
        name="scale_rows",
    )(zvalues, gain, *sums)


def solution(mesh):
    sizes = (mesh.shape["ctx"], mesh.shape["ch"])
    in_specs = (
        P("ctx", "ch"),
        P("ctx", "ch"),
        P("ctx", "ch"),
        P(),
        P(None, None, "ch"),
        P(None, "ch"),
        P(None, "ch"),
        P("ch"),
        P("ch"),
    )

    def run(*arrays):
        return on_device(sizes, *arrays)

    return jax.shard_map(run, mesh=mesh, in_specs=in_specs, out_specs=P("ctx", "ch"), check_vma=False)
```

```python
import functools
from decimal import Decimal, getcontext

import jax
import jax.numpy as jnp
import ml_dtypes
import numpy as np
from jax import lax
from jax.experimental import pallas as pl
from jax.experimental.pallas import tpu as pltpu
from jax.sharding import PartitionSpec as P

F32, BF16 = jnp.float32, jnp.bfloat16
LANES = 128
SPAN = 256
WIDE = 4
STRETCH = 64
REACH = 6
INNER = STRETCH - REACH
PIVOTS = (8, 49, 21, 56, 36, 1)
ANCHORS = ("0.0020", "0.0235", "0.0110", "0.0295", "0.0185", "0.0004")
RANK = len(PIVOTS)
FINE = 2
COEFS = RANK + FINE
RAW = 6 * REACH
PIECE = RAW + COEFS
BACK = 2 * REACH + COEFS


def shape_table():
    getcontext().prec = 50
    rest = [[(-Decimal(a) * d).exp() for d in range(INNER)] for a in ANCHORS]
    table = []
    for p in range(RANK):
        shape = [x / rest[p][PIVOTS[p]] for x in rest[p]]
        rest = [[x - row[PIVOTS[p]] * y for x, y in zip(row, shape)] for row in rest]
        table.append([float(x) for x in shape])
    return table


SHAPE = shape_table()


def halves(values):
    high = values.astype(ml_dtypes.bfloat16)
    low = (values - high.astype(np.float32)).astype(ml_dtypes.bfloat16)
    return high, low


def constant_matrices():
    shape = np.array(SHAPE, np.float32)
    ends = np.zeros((16, STRETCH), np.float32)
    local = np.zeros((RANK, STRETCH, STRETCH), np.float32)
    lift = np.zeros((2, 2 * STRETCH, 2 * BACK), np.float32)
    parts = [h.astype(np.float32) for h in halves(shape)]
    for p in range(RANK):
        for s in range(REACH, STRETCH):
            ends[p, s] = shape[p, STRETCH - 1 - s]
            local[p, s:, s] = shape[p, : STRETCH - s]
        for half in range(2):
            rows = slice(half * STRETCH + REACH, (half + 1) * STRETCH)
            at = half * BACK + 2 * REACH
            for k in range(2):
                lift[k, rows, at + p] = parts[k][p]
                if p < FINE:
                    lift[k, rows, at + RANK + p] = parts[k][p]
    for half in range(2):
        for t in range(REACH):
            lift[0, half * STRETCH + t, half * BACK + t] = 1.0
            lift[0, half * STRETCH + t, half * BACK + REACH + t] = 1.0
    local = local.reshape(RANK * STRETCH, STRETCH)
    ends = ends.reshape(16, 8, STRETCH // 8).transpose(0, 2, 1).reshape(16, STRETCH)

    def triple(m):
        h, l = halves(m)
        return np.concatenate([h, h, l], axis=1)

    return triple(ends), triple(local), lift.astype(ml_dtypes.bfloat16)


def strengths(rate):
    found = []
    for p in range(RANK):
        value = jnp.exp(-rate * float(PIVOTS[p]))
        for q in range(p):
            value = value - found[q] * SHAPE[q][PIVOTS[p]]
        found.append(value)
    return found


def split(values):
    high = values.astype(BF16)
    return high, (values - high.astype(F32)).astype(BF16)


def amplitude(rate, residue):
    x = 2.0 * rate
    series = 1.0 - x * (0.5 - x * (1 / 6 - x * (1 / 24 - x * (1 / 120 - x * (1 / 720)))))
    return residue * jnp.sqrt(x * series)


EDGES = (0, STRETCH - 16, STRETCH, 2 * STRETCH - 16)


def front_kernel(*refs, direct):
    me_ref, q_ref, k_ref, v_ref, taps_ref, ends_ref = refs[:6]
    refs = refs[6:]
    weights, refs = (refs[:4], refs[4:]) if direct else ((), refs)
    pay_ref, refs = refs[0], refs[1:]
    kept, refs = (refs[:4], refs[4:]) if direct else ((), refs)
    held, edge, taps_vm, ends_vm, xs, qs, pay, packed, u_vm, in_sems, edge_sems, tap_sem, own_sems, out_sems = refs
    blocks = k_ref.shape[1] // SPAN

    def lanes(c):
        return pl.ds(pl.multiple_of(c * SPAN, SPAN), SPAN)

    def loads(w):
        cols = pl.ds(pl.multiple_of(w * WIDE * SPAN, SPAN), WIDE * SPAN)
        return [
            pltpu.make_async_copy(ref.at[:, cols], held.at[a, :, cols], in_sems.at[a, w])
            for a, ref in enumerate((k_ref, v_ref))
        ] + [pltpu.make_async_copy(taps_ref.at[pl.ds(1, 2), :, cols], taps_vm.at[:, :, cols], in_sems.at[2, w])]

    def edge_loads():
        return [
            pltpu.make_async_copy(q_ref.at[pl.ds(at, 16), :], edge.at[e], edge_sems.at[e])
            for e, at in enumerate(EDGES)
        ]

    def stores(c):
        target = pay_ref.at[c] if direct else pay_ref.at[:, lanes(c)]
        return [pltpu.make_async_copy(packed.at[c], target, out_sems.at[c])]

    def own_loads():
        share = kept[0].shape[-1]
        cols = pl.ds(pl.multiple_of(me_ref[0] * share, share), share)
        views = (weights[0].at[:, :, cols], weights[1].at[:, cols], weights[2].at[:, cols], weights[3].at[:, cols])
        return [pltpu.make_async_copy(view, ref, own_sems.at[n]) for n, (view, ref) in enumerate(zip(views, kept))]

    ends_copy = pltpu.make_async_copy(ends_ref, ends_vm, tap_sem.at[0])
    for copy in loads(0) + edge_loads():
        copy.start()
    ends_copy.start()
    waves = blocks // WIDE

    def begin(c, carry):
        for copy in loads(c):
            copy.start()
        return carry

    lax.fori_loop(1, waves, begin, 0)
    if direct:
        for copy in own_loads():
            copy.start()
    for parity in range(2):
        for a in range(2):
            for h in range(2):
                for i in range(2):
                    at = i * (STRETCH + 8)
                    xs[parity, a, h, at : at + 8, :] = jnp.zeros((8, LANES), F32)
    for copy in edge_loads():
        copy.wait()
    ends_copy.wait()

    def features(c, carry):
        @pl.when(lax.rem(c, WIDE) == 0)
        def _():
            for copy in loads(c // WIDE):
                copy.wait()

        parity = lax.rem(c, 2)
        for h in range(2):
            part = slice(h * LANES, (h + 1) * LANES)
            cols = pl.ds(pl.multiple_of(c * SPAN + h * LANES, LANES), LANES)
            for i in range(2):
                base = i * (STRETCH + 8) + 8
                for a in range(2):
                    xs[parity, a, h, base : base + STRETCH, :] = held[
                        a, i * STRETCH : (i + 1) * STRETCH, cols
                    ].astype(F32)
                    at = i * PIECE + (1 + a) * REACH
                    pay[c, h, at : at + REACH, :] = xs[parity, a, h, base + STRETCH - REACH : base + STRETCH, :]
                    at = at + 3 * REACH
                    pay[c, h, at : at + REACH, :] = xs[parity, a, h, base : base + REACH, :]
                qs[parity, h, i, 0:16, :] = edge[2 * i, :, cols].astype(F32)
                qs[parity, h, i, 16:32, :] = edge[2 * i + 1, :, cols].astype(F32)
                at = i * PIECE
                pay[c, h, at : at + REACH, :] = qs[parity, h, i, 32 - REACH : 32, :]
                pay[c, h, at + 3 * REACH : at + 4 * REACH, :] = qs[parity, h, i, 0:REACH, :]
            taps = [[taps_vm[a, j : j + 1, cols] for j in range(REACH + 1)] for a in range(2)]
            for i in range(2):
                base = i * (STRETCH + 8) + 8
                both = []
                for a in range(2):
                    strided = {
                        m: xs[parity, a, h, pl.ds(base + m, 8, stride=8), :] for m in range(-REACH, STRETCH // 8)
                    }
                    found = []
                    for m in range(STRETCH // 8):
                        total = taps[a][0] * strided[m]
                        for j in range(1, REACH + 1):
                            total = total + taps[a][j] * strided[m - j]
                        found.append(total)
                    both.append(found)
                mixed = [k * v for k, v in zip(*both)]
                for m in range(0, STRETCH // 8, 2):
                    high, low = split(jnp.concatenate(mixed[m : m + 2], axis=0))
                    rows = slice(i * STRETCH + 8 * m, i * STRETCH + 8 * m + 16)
                    u_vm[c, 0, rows, part] = high
                    u_vm[c, 1, rows, part] = low
        return carry

    lax.fori_loop(0, blocks, features, 0)
    chunk = 4

    def finish(step, carry):
        for k in range(chunk):
            c = step * chunk + k
            for i in range(2):
                rows = slice(i * STRETCH, (i + 1) * STRETCH)
                high, low = u_vm[c, 0, rows, :], u_vm[c, 1, rows, :]
                stacked = jnp.concatenate([high, low, high], axis=0)
                moments = jnp.dot(ends_vm[...], stacked, preferred_element_type=F32)[:8]
                rest = (moments - moments.astype(BF16).astype(F32))[:FINE]
                at = PIECE * i + RAW
                for h in range(2):
                    part = slice(h * LANES, (h + 1) * LANES)
                    pay[c, h, at : at + RANK, :] = moments[:RANK, part]
                    pay[c, h, at + RANK : at + COEFS, :] = rest[:, part]
            for h in range(2):
                packed[c, :, h * LANES : (h + 1) * LANES] = pay[c, h].astype(BF16)
        for k in range(chunk):
            for copy in stores(step * chunk + k):
                copy.start()
        return carry

    lax.fori_loop(0, blocks // chunk, finish, 0)

    def end(c, carry):
        for copy in stores(c):
            copy.wait()
        return carry

    lax.fori_loop(0, blocks, end, 0)
    if direct:
        for copy in own_loads():
            copy.wait()


def local_kernel(
    q_ref, k_ref, v_ref, taps_ref, rates_ref, res_ref, skip_ref, local_ref, qc_ref, y_ref, xs, u_vm
):
    tile = q_ref.shape[1]
    per = SPAN // LANES
    first_row = lax.broadcasted_iota(jnp.int32, (8, LANES), 0)
    for g in range(tile // LANES):
        cols = slice(g * LANES, (g + 1) * LANES)
        part = slice(g % per * LANES, (g % per + 1) * LANES)
        taps = [[taps_ref[a, j : j + 1, cols] for j in range(REACH + 1)] for a in range(3)]
        for i in range(2):
            base = i * (STRETCH + 8) + 8
            for a, ref in enumerate((q_ref, k_ref, v_ref)):
                xs[a, g, base - 8 : base, :] = jnp.zeros((8, LANES), F32)
                xs[a, g, base : base + STRETCH, :] = ref[i * STRETCH : (i + 1) * STRETCH, cols].astype(F32)
            for b in range(STRETCH // 8):
                at = base + 8 * b
                totals = []
                for a in range(3):
                    total = taps[a][0] * xs[a, g, at : at + 8, :]
                    for j in range(1, REACH + 1):
                        total = total + taps[a][j] * xs[a, g, at - j : at - j + 8, :]
                    totals.append(total)
                query, mixed = totals[0], totals[1] * totals[2]
                if b == 0:
                    query = jnp.where(first_row >= REACH, query, 1.0)
                    mixed = jnp.where(first_row >= REACH, mixed, 0.0)
                rows = slice(i * STRETCH + 8 * b, i * STRETCH + 8 * b + 8)
                qc_ref[g // per, rows, part] = query
                u_vm[g // per, rows, part] = mixed
    for c in range(tile // SPAN):
        cols = slice(c * SPAN, (c + 1) * SPAN)
        rate = rates_ref[:, cols]
        amount = amplitude(rate, res_ref[:, cols])
        weights = [jnp.sum(amount * value, axis=0, keepdims=True) for value in strengths(rate)]
        for i in range(2):
            rows = slice(i * STRETCH, (i + 1) * STRETCH)
            mixed = u_vm[c, rows, :]
            high, low = split(mixed)
            parts = jnp.dot(
                local_ref[...], jnp.concatenate([high, low, high], axis=0), preferred_element_type=F32
            )
            total = skip_ref[:, cols] * mixed
            for p in range(RANK):
                total = total + weights[p] * parts[p * STRETCH : (p + 1) * STRETCH, :]
            y_ref[c, rows, :] = total


def middle_kernel(
    perm_ref, x_ref, taps_ref, rates_ref, res_ref, skip_ref, out_ref,
    raw, ext, moments, past, heads, first, second, states, mids, coefs, fades, result, slab, packed, out_sems,
):
    slots = perm_ref.shape[0]
    groups = x_ref.shape[2] // LANES
    order = rates_ref.shape[0]
    span = 2 * PIECE
    row = lax.broadcasted_iota(jnp.int32, (8, LANES), 0)
    ext[:, :, 0, 0:8, :] = jnp.zeros((3, groups, 8, LANES), F32)
    past[:, :, 0:8, :] = jnp.zeros((groups, slots, 8, LANES), F32)

    def unpack(src, carry):
        for g in range(groups):
            raw[src, g, 8 : 8 + span, :] = x_ref[src, :, g * LANES : (g + 1) * LANES].astype(F32)
        for i in range(2):
            n = perm_ref[2 * src + i]
            for g in range(groups):
                for a in range(3):
                    at = 8 + i * PIECE + a * REACH
                    ext[a, g, n + 1, 0:8, :] = raw[src, g, at + REACH - 8 : at + REACH, :]
                    at = at + 3 * REACH
                    ext[a, g, n, 8:16, :] = raw[src, g, at : at + 8, :]
                at = 8 + i * PIECE + RAW
                fine = jnp.where(row < FINE, raw[src, g, at + RANK : at + RANK + 8, :], 0.0)
                moments[g, n] = raw[src, g, at : at + 8, :] + fine
        return carry

    lax.fori_loop(0, slots // 2, unpack, 0, unroll=2)

    def group_pass(g, carry):
        cols = pl.ds(pl.multiple_of(g * LANES, LANES), LANES)
        rate = rates_ref[:, cols]
        amount = amplitude(rate, res_ref[:, cols])
        basis = strengths(rate)
        powers = [jnp.ones_like(rate), jnp.exp(-rate)]
        for d in range(2, REACH + 1):
            powers.append(powers[-1] * powers[1])
        for t in range(REACH):
            coefs[g, 0, t * order : (t + 1) * order, :] = amount * powers[t + 1]
        for p in range(RANK):
            coefs[g, 1, p * order : (p + 1) * order, :] = amount * powers[1] * basis[p]
        fade_rest = jnp.exp(-rate * float(INNER))
        fades[g, 0] = powers[REACH]
        fades[g, 1] = fade_rest * powers[REACH]
        taps = [[taps_ref[a, j : j + 1, cols] for j in range(REACH + 1)] for a in range(3)]
        near = [jnp.sum(amount * powers[d], axis=0, keepdims=True) for d in range(REACH)]
        near[0] = near[0] + skip_ref[:, cols]

        def head_pass(n, carry):
            feats = []
            for a in range(3):
                total = taps[a][0] * ext[a, g, n, 8:16, :]
                for j in range(1, REACH + 1):
                    total = total + taps[a][j] * ext[a, g, n, 8 - j : 16 - j, :]
                feats.append(jnp.where(row < REACH, total, 0.0))
            mixed = feats[1] * feats[2]
            past[g, n, 8:16, :] = mixed
            total = near[0] * mixed
            for d in range(1, REACH):
                total = total + near[d] * past[g, n, 8 - d : 16 - d, :]
            at = pl.multiple_of(n * 16, 16)
            heads[g, pl.ds(at, 8), :] = feats[0]
            heads[g, pl.ds(at + 8, 8), :] = total
            value = powers[REACH - 1] * past[g, n, 8:9, :]
            for s in range(1, REACH):
                value = value + powers[REACH - 1 - s] * past[g, n, 8 + s : 9 + s, :]
            first[g, n] = value
            return carry

        lax.fori_loop(0, slots, head_pass, 0, unroll=4)

        def rest_pass(n, carry):
            value = fade_rest * first[g, n]
            for p in range(RANK):
                value = value + basis[p] * moments[g, n, p : p + 1, :]
            second[g, n] = value
            return carry

        lax.fori_loop(0, slots, rest_pass, 0, unroll=4)
        return carry

    lax.fori_loop(0, groups, group_pass, 0)

    def scan_pass(n, state):
        after = []
        at = pl.multiple_of(n * order, order)
        for g in range(groups):
            states[g, pl.ds(at, order), :] = state[g]
            mids[g, pl.ds(at, order), :] = fades[g, 0] * state[g] + first[g, n]
            after.append(fades[g, 1] * state[g] + second[g, n])
        return tuple(after)

    lax.fori_loop(0, slots, scan_pass, tuple(jnp.zeros((order, LANES), F32) for _ in range(groups)), unroll=4)

    quad = 4

    def sums(g, kind, held, first_tile):
        totals = [[None] * quad for _ in range(RANK)]
        for r in range(order):
            values = [held[g, pl.ds((first_tile + k) * 8 * order + r, 8, stride=order), :] for k in range(quad)]
            for p in range(RANK):
                weight = coefs[g, kind, p * order + r : p * order + r + 1, :]
                for k in range(quad):
                    term = weight * values[k]
                    totals[p][k] = term if r == 0 else totals[p][k] + term
        return totals

    quads = slots // (8 * quad)

    def out_pass(step, carry):
        g, q = step // quads, lax.rem(step, quads)
        totals = sums(g, 0, states, q * quad)
        for t in range(REACH):
            for k in range(quad):
                tile = q * quad + k
                query = heads[g, pl.ds(tile * 128 + t, 8, stride=16), :]
                local = heads[g, pl.ds(tile * 128 + 8 + t, 8, stride=16), :]
                z = query * (local + totals[t][k])
                result[g, pl.ds(tile * 192 + t, 8, stride=24), :] = z
                result[g, pl.ds(tile * 192 + REACH + t, 8, stride=24), :] = z - z.astype(BF16).astype(F32)
        totals = sums(g, 1, mids, q * quad)
        for p in range(RANK):
            for k in range(quad):
                tile = q * quad + k
                value = totals[p][k]
                result[g, pl.ds(tile * 192 + 2 * REACH + p, 8, stride=24), :] = value
                if p < FINE:
                    rest = value - value.astype(BF16).astype(F32)
                    result[g, pl.ds(tile * 192 + 2 * REACH + RANK + p, 8, stride=24), :] = rest
        return carry

    lax.fori_loop(0, groups * quads, out_pass, 0)

    def store(src):
        return pltpu.make_async_copy(packed.at[src], out_ref.at[src], out_sems.at[src])

    def pack(src, carry):
        for g in range(groups):
            for i in range(2):
                at = pl.multiple_of(perm_ref[2 * src + i] * 24, 8)
                slab[src, g, i * BACK : i * BACK + 24, :] = result[g, pl.ds(at, 24), :]
            packed[src, :, g * LANES : (g + 1) * LANES] = slab[src, g, 0 : 2 * BACK, :].astype(BF16)
        return carry

    lax.fori_loop(0, slots // 2, pack, 0, unroll=2)

    def send(src, carry):
        store(src).start()
        return carry

    def end(src, carry):
        store(src).wait()
        return carry

    lax.fori_loop(0, slots // 2, send, 0)
    lax.fori_loop(0, slots // 2, end, 0)


def join_kernel(back_ref, lift_ref, qc_ref, y_ref, z_ref, sq_ref, qc_vm, carry, total, sems):
    blocks, tokens, _ = qc_vm.shape
    by_dest = len(back_ref.shape) == 3
    chunk = 4

    def load(c):
        rows = pl.ds(c * chunk, chunk)
        return pltpu.make_async_copy(qc_ref.at[rows], qc_vm.at[rows], sems.at[c])

    def lanes(b):
        return pl.ds(pl.multiple_of(b * SPAN, SPAN), SPAN)

    for c in range(blocks // chunk):
        load(c).start()

    def products(c, unused):
        for k in range(chunk):
            b = c * chunk + k
            back = back_ref[b] if by_dest else back_ref[:, lanes(b)]
            product = jnp.dot(lift_ref[0], back, preferred_element_type=F32)
            carry[b] = y_ref[b] + product + jnp.dot(lift_ref[1], back, preferred_element_type=F32)
        return unused

    lax.fori_loop(0, blocks // chunk, products, 0)
    total[...] = jnp.zeros((tokens, LANES), F32)

    def square(c, unused):
        load(c).wait()
        part = total[...]
        for k in range(chunk):
            b = c * chunk + k
            z = qc_vm[b] * carry[b]
            z_ref[:, lanes(b)] = z
            squares = z * z
            for h in range(SPAN // LANES):
                part = part + squares[:, h * LANES : (h + 1) * LANES]
        total[...] = part
        return unused

    lax.fori_loop(0, blocks // chunk, square, 0)
    sq_ref[...] = jnp.sum(total[...].T, axis=0, keepdims=True)


def scale_kernel(*refs, channels):
    z_ref, gain_ref, refs, (out_ref, held, sems) = refs[0], refs[1], refs[2:-3], refs[-3:]
    tokens, width = z_ref.shape
    chunks = sems.shape[0]
    wide = width // chunks
    total = refs[0][...]
    for ref in refs[1:]:
        total = total + ref[...]
    scale = lax.rsqrt(total / channels + 1e-05)
    scale = jnp.broadcast_to(scale, (LANES, tokens)).T
    copies = []
    for c in range(chunks):
        for g in range(c * wide // LANES, (c + 1) * wide // LANES):
            cols = slice(g * LANES, (g + 1) * LANES)
            held[:, cols] = (z_ref[:, cols] * scale * gain_ref[:, cols]).astype(BF16)
        cols = pl.ds(c * wide, wide)
        copy = pltpu.make_async_copy(held.at[:, cols], out_ref.at[:, cols], sems.at[c])
        copy.start()
        copies.append(copy)
    for copy in copies:
        copy.wait()


def limit(mib):
    return pltpu.CompilerParams(vmem_limit_bytes=mib * 1024 * 1024)


def on_device(sizes, q_in, k_in, v_in, stretch_of_slot, short_weight, rates, residues, skip, gain):
    n_ctx, n_ch = sizes
    tokens, width = q_in.shape
    slots = stretch_of_slot.shape[0]
    order = rates.shape[0]
    share = width // n_ctx
    direct = share == SPAN
    tile = min(width, 1024)
    steps = width // tile
    groups = tile // LANES
    ends_np, local_np, lift_np = constant_matrices()
    ends, local, lift = jnp.asarray(ends_np), jnp.asarray(local_np), jnp.asarray(lift_np)
    skip, gain = skip.reshape(1, width), gain.reshape(1, width)
    me = lax.axis_index("ctx").astype(jnp.int32).reshape(1)

    def whole(array):
        return pl.BlockSpec(array.shape, lambda c: (0,) * array.ndim)

    def columns(*lead):
        return pl.BlockSpec((*lead, tile), lambda c: (0,) * len(lead) + (c,))

    def exchange(array):
        if direct:
            return lax.all_to_all(array, "ctx", 0, 0, tiled=True)
        array = array.reshape(array.shape[0], n_ctx, share).transpose(1, 0, 2)
        return widen(lax.all_to_all(array, "ctx", 0, 0, tiled=True))

    lanes = -(-share // LANES) * LANES

    def widen(array, fill=0.0):
        pad = [(0, 0)] * (array.ndim - 1) + [(0, lanes - share)]
        return jnp.pad(array, pad, constant_values=fill)

    def cut(array, fill=0.0):
        return widen(lax.dynamic_slice_in_dim(array, lax.axis_index("ctx") * share, share, array.ndim - 1), fill)

    smem = pl.BlockSpec(memory_space=pltpu.SMEM)
    vmem = pl.BlockSpec(memory_space=pltpu.VMEM)
    hbm = pl.BlockSpec(memory_space=pltpu.HBM)
    f32 = lambda *shape: jax.ShapeDtypeStruct(shape, F32)
    pin = lambda array: pltpu.with_memory_space_constraint(array, pltpu.HBM)

    weights = (short_weight, rates, residues, skip)
    own = [f32(*w.shape[:-1], share) for w in weights] if direct else []
    blocks = width // SPAN
    pay, *mine = pl.pallas_call(
        functools.partial(front_kernel, direct=direct),
        in_specs=[smem] + [hbm] * (5 + len(own)),
        out_specs=[hbm] + [vmem] * len(own),
        out_shape=[
            pltpu.HBM((n_ctx, 2 * PIECE, share) if direct else (2 * PIECE, width), BF16),
        ]
        + own,
        scratch_shapes=[
            pltpu.VMEM((2, tokens, width), BF16),
            pltpu.VMEM((4, 16, width), BF16),
            pltpu.VMEM((2, REACH + 1, width), F32),
            pltpu.VMEM(ends.shape, BF16),
            pltpu.VMEM((2, 2, 2, 2 * (STRETCH + 8), LANES), F32),
            pltpu.VMEM((2, 2, 2, 32, LANES), F32),
            pltpu.VMEM((blocks, 2, 2 * PIECE, LANES), F32),
            pltpu.VMEM((blocks, 2 * PIECE, SPAN), BF16),
            pltpu.VMEM((blocks, 2, tokens, SPAN), BF16),
            pltpu.SemaphoreType.DMA((3, blocks // WIDE)),
            pltpu.SemaphoreType.DMA((4,)),
            pltpu.SemaphoreType.DMA((1,)),
            pltpu.SemaphoreType.DMA((4,)),
            pltpu.SemaphoreType.DMA((blocks,)),
        ],
        compiler_params=limit(24),
        name="front_pieces",
    )(me, *map(pin, (q_in, k_in, v_in, short_weight, ends)), *(map(pin, weights) if direct else ()))
    arrived = exchange(pay)
    if not direct:
        mine = (cut(short_weight), cut(rates, 0.01), cut(residues), cut(skip))

    query, inner = pl.pallas_call(
        local_kernel,
        grid=(steps,),
        in_specs=[columns(tokens)] * 3
        + [columns(3, REACH + 1), columns(order), columns(order), columns(1), whole(local)],
        out_specs=[pl.BlockSpec((tile // SPAN, tokens, SPAN), lambda c: (c, 0, 0))] * 2,
        out_shape=[pltpu.HBM((blocks, tokens, SPAN), F32), pltpu.VMEM((blocks, tokens, SPAN), F32)],
        scratch_shapes=[
            pltpu.VMEM((3, groups, 2 * (STRETCH + 8), LANES), F32),
            pltpu.VMEM((tile // SPAN, tokens, SPAN), F32),
        ],
        compiler_params=limit(24),
        name="local_filter",
        cost_estimate=pl.CostEstimate(flops=10**9, bytes_accessed=20 * 10**6, transcendentals=0),
    )(*map(pin, (q_in, k_in, v_in, short_weight, rates, residues)), skip, local)
    arrived, query, inner = lax.optimization_barrier((arrived, query, inner))

    groups = lanes // LANES
    back = pl.pallas_call(
        middle_kernel,
        in_specs=[smem] + [vmem] * 5,
        out_specs=hbm,
        scratch_shapes=[
            pltpu.VMEM((n_ctx, groups, 8 + 2 * PIECE + 8, LANES), F32),
            pltpu.VMEM((3, groups, slots + 1, 16, LANES), F32),
            pltpu.VMEM((groups, slots, 8, LANES), F32),
            pltpu.VMEM((groups, slots, 16, LANES), F32),
            pltpu.VMEM((groups, slots * 16, LANES), F32),
            pltpu.VMEM((groups, slots, order, LANES), F32),
            pltpu.VMEM((groups, slots, order, LANES), F32),
            pltpu.VMEM((groups, slots * order, LANES), F32),
            pltpu.VMEM((groups, slots * order, LANES), F32),
            pltpu.VMEM((groups, 2, RANK * order, LANES), F32),
            pltpu.VMEM((groups, 2, order, LANES), F32),
            pltpu.VMEM((groups, slots * 24, LANES), F32),
            pltpu.VMEM((n_ctx, groups, BACK + 28, LANES), F32),
            pltpu.VMEM((n_ctx, 2 * BACK, lanes), BF16),
            pltpu.SemaphoreType.DMA((n_ctx,)),
        ],
        out_shape=pltpu.HBM((n_ctx, 2 * BACK, lanes), BF16),
        compiler_params=limit(24),
        name="middle_states",
    )(stretch_of_slot, arrived, *mine)
    if not direct:
        back = back[:, :, :share]
    back = lax.all_to_all(back, "ctx", 0, 0, tiled=True)
    if not direct:
        back = back.transpose(1, 0, 2).reshape(2 * BACK, width)

    keep = lambda array: pltpu.with_memory_space_constraint(array, pltpu.VMEM)
    zvalues, squares = pl.pallas_call(
        join_kernel,
        in_specs=[vmem] * 2 + [hbm, vmem],
        out_specs=[vmem] * 2,
        out_shape=[f32(tokens, width), f32(1, tokens)],
        scratch_shapes=[pltpu.VMEM((blocks, tokens, SPAN), F32)] * 2
        + [pltpu.VMEM((tokens, LANES), F32), pltpu.SemaphoreType.DMA((blocks // 4,))],
        compiler_params=limit(24),
        name="join_carry",
    )(back, lift, pin(query), keep(inner))
    sums = [squares]
    for shift in range(1, n_ch):
        sums.append(lax.ppermute(squares, "ch", [(i, (i + shift) % n_ch) for i in range(n_ch)]))
    return pl.pallas_call(
        functools.partial(scale_kernel, channels=width * n_ch),
        in_specs=[vmem] * (2 + n_ch),
        out_specs=hbm,
        out_shape=pltpu.HBM((tokens, width), BF16),
        scratch_shapes=[pltpu.VMEM((tokens, width), BF16), pltpu.SemaphoreType.DMA((8 if width % 1024 == 0 else 1,))],
        compiler_params=limit(24),
        name="scale_rows",
    )(zvalues, gain, *sums)


def solution(mesh):
    sizes = (mesh.shape["ctx"], mesh.shape["ch"])
    in_specs = (
        P("ctx", "ch"),
        P("ctx", "ch"),
        P("ctx", "ch"),
        P(),
        P(None, None, "ch"),
        P(None, "ch"),
        P(None, "ch"),
        P("ch"),
        P("ch"),
    )

    def run(*arrays):
        return on_device(sizes, *arrays)

    return jax.shard_map(run, mesh=mesh, in_specs=in_specs, out_specs=P("ctx", "ch"), check_vma=False)
```

```python
import functools
from decimal import Decimal, getcontext

import jax
import jax.numpy as jnp
import ml_dtypes
import numpy as np
from jax import lax
from jax.experimental import pallas as pl
from jax.experimental.pallas import tpu as pltpu
from jax.sharding import PartitionSpec as P

F32, BF16 = jnp.float32, jnp.bfloat16
LANES = 128
SPAN = 256
WIDE = 2
STRETCH = 64
REACH = 6
INNER = STRETCH - REACH
PIVOTS = (8, 49, 21, 56, 36, 1)
ANCHORS = ("0.0020", "0.0235", "0.0110", "0.0295", "0.0185", "0.0004")
RANK = len(PIVOTS)
FINE = 2
COEFS = RANK + FINE
RAW = 6 * REACH
PIECE = RAW + COEFS
BACK = 2 * REACH + COEFS


def shape_table():
    getcontext().prec = 50
    rest = [[(-Decimal(a) * d).exp() for d in range(INNER)] for a in ANCHORS]
    table = []
    for p in range(RANK):
        shape = [x / rest[p][PIVOTS[p]] for x in rest[p]]
        rest = [[x - row[PIVOTS[p]] * y for x, y in zip(row, shape)] for row in rest]
        table.append([float(x) for x in shape])
    return table


SHAPE = shape_table()


def halves(values):
    high = values.astype(ml_dtypes.bfloat16)
    low = (values - high.astype(np.float32)).astype(ml_dtypes.bfloat16)
    return high, low


def constant_matrices():
    shape = np.array(SHAPE, np.float32)
    ends = np.zeros((16, STRETCH), np.float32)
    local = np.zeros((RANK, STRETCH, STRETCH), np.float32)
    lift = np.zeros((2, 2 * STRETCH, 2 * BACK), np.float32)
    parts = [h.astype(np.float32) for h in halves(shape)]
    for p in range(RANK):
        for s in range(REACH, STRETCH):
            ends[p, s] = shape[p, STRETCH - 1 - s]
            local[p, s:, s] = shape[p, : STRETCH - s]
        for half in range(2):
            rows = slice(half * STRETCH + REACH, (half + 1) * STRETCH)
            at = half * BACK + 2 * REACH
            for k in range(2):
                lift[k, rows, at + p] = parts[k][p]
                if p < FINE:
                    lift[k, rows, at + RANK + p] = parts[k][p]
    for half in range(2):
        for t in range(REACH):
            lift[0, half * STRETCH + t, half * BACK + t] = 1.0
            lift[0, half * STRETCH + t, half * BACK + REACH + t] = 1.0
    local = local.reshape(RANK * STRETCH, STRETCH)
    ends = ends.reshape(16, 8, STRETCH // 8).transpose(0, 2, 1).reshape(16, STRETCH)

    def triple(m):
        h, l = halves(m)
        return np.concatenate([h, h, l], axis=1)

    return triple(ends), triple(local), lift.astype(ml_dtypes.bfloat16)


def strengths(rate):
    found = []
    for p in range(RANK):
        value = jnp.exp(-rate * float(PIVOTS[p]))
        for q in range(p):
            value = value - found[q] * SHAPE[q][PIVOTS[p]]
        found.append(value)
    return found


def split(values):
    high = values.astype(BF16)
    return high, (values - high.astype(F32)).astype(BF16)


def amplitude(rate, residue):
    x = 2.0 * rate
    series = 1.0 - x * (0.5 - x * (1 / 6 - x * (1 / 24 - x * (1 / 120 - x * (1 / 720)))))
    return residue * jnp.sqrt(x * series)


EDGES = (0, STRETCH - 16, STRETCH, 2 * STRETCH - 16)


def front_kernel(*refs, direct):
    me_ref, q_ref, k_ref, v_ref, taps_ref, ends_ref = refs[:6]
    refs = refs[6:]
    weights, refs = (refs[:4], refs[4:]) if direct else ((), refs)
    pay_ref, refs = refs[0], refs[1:]
    kept, refs = (refs[:4], refs[4:]) if direct else ((), refs)
    held, edge, taps_vm, ends_vm, xs, qs, pay, packed, u_vm, in_sems, edge_sems, tap_sem, own_sems, out_sems = refs
    blocks = k_ref.shape[1] // SPAN

    def lanes(c):
        return pl.ds(pl.multiple_of(c * SPAN, SPAN), SPAN)

    def loads(w):
        cols = pl.ds(pl.multiple_of(w * WIDE * SPAN, SPAN), WIDE * SPAN)
        return [
            pltpu.make_async_copy(ref.at[:, cols], held.at[a, :, cols], in_sems.at[a, w])
            for a, ref in enumerate((k_ref, v_ref))
        ] + [pltpu.make_async_copy(taps_ref.at[pl.ds(1, 2), :, cols], taps_vm.at[:, :, cols], in_sems.at[2, w])]

    def edge_loads():
        return [
            pltpu.make_async_copy(q_ref.at[pl.ds(at, 16), :], edge.at[e], edge_sems.at[e])
            for e, at in enumerate(EDGES)
        ]

    def stores(c):
        target = pay_ref.at[c] if direct else pay_ref.at[:, lanes(c)]
        return [pltpu.make_async_copy(packed.at[c], target, out_sems.at[c])]

    def own_loads():
        share = kept[0].shape[-1]
        cols = pl.ds(pl.multiple_of(me_ref[0] * share, share), share)
        views = (weights[0].at[:, :, cols], weights[1].at[:, cols], weights[2].at[:, cols], weights[3].at[:, cols])
        return [pltpu.make_async_copy(view, ref, own_sems.at[n]) for n, (view, ref) in enumerate(zip(views, kept))]

    ends_copy = pltpu.make_async_copy(ends_ref, ends_vm, tap_sem.at[0])
    for copy in loads(0) + edge_loads():
        copy.start()
    ends_copy.start()
    waves = blocks // WIDE

    def begin(c, carry):
        for copy in loads(c):
            copy.start()
        return carry

    lax.fori_loop(1, waves, begin, 0)
    if direct:
        for copy in own_loads():
            copy.start()
    for parity in range(2):
        for a in range(2):
            for h in range(2):
                for i in range(2):
                    at = i * (STRETCH + 8)
                    xs[parity, a, h, at : at + 8, :] = jnp.zeros((8, LANES), F32)
    for copy in edge_loads():
        copy.wait()
    ends_copy.wait()

    def features(c):
        parity = lax.rem(c, 2)
        for h in range(2):
            part = slice(h * LANES, (h + 1) * LANES)
            cols = pl.ds(pl.multiple_of(c * SPAN + h * LANES, LANES), LANES)
            for i in range(2):
                base = i * (STRETCH + 8) + 8
                for a in range(2):
                    xs[parity, a, h, base : base + STRETCH, :] = held[
                        a, i * STRETCH : (i + 1) * STRETCH, cols
                    ].astype(F32)
                    at = i * PIECE + (1 + a) * REACH
                    pay[c, h, at : at + REACH, :] = xs[parity, a, h, base + STRETCH - REACH : base + STRETCH, :]
                    at = at + 3 * REACH
                    pay[c, h, at : at + REACH, :] = xs[parity, a, h, base : base + REACH, :]
                qs[parity, h, i, 0:16, :] = edge[2 * i, :, cols].astype(F32)
                qs[parity, h, i, 16:32, :] = edge[2 * i + 1, :, cols].astype(F32)
                at = i * PIECE
                pay[c, h, at : at + REACH, :] = qs[parity, h, i, 32 - REACH : 32, :]
                pay[c, h, at + 3 * REACH : at + 4 * REACH, :] = qs[parity, h, i, 0:REACH, :]
            taps = [[taps_vm[a, j : j + 1, cols] for j in range(REACH + 1)] for a in range(2)]
            for i in range(2):
                base = i * (STRETCH + 8) + 8
                both = []
                for a in range(2):
                    strided = {
                        m: xs[parity, a, h, pl.ds(base + m, 8, stride=8), :] for m in range(-REACH, STRETCH // 8)
                    }
                    found = []
                    for m in range(STRETCH // 8):
                        total = taps[a][0] * strided[m]
                        for j in range(1, REACH + 1):
                            total = total + taps[a][j] * strided[m - j]
                        found.append(total)
                    both.append(found)
                mixed = [k * v for k, v in zip(*both)]
                for m in range(0, STRETCH // 8, 2):
                    high, low = split(jnp.concatenate(mixed[m : m + 2], axis=0))
                    rows = slice(i * STRETCH + 8 * m, i * STRETCH + 8 * m + 16)
                    u_vm[c, 0, rows, part] = high
                    u_vm[c, 1, rows, part] = low

    def products(c):
        found = []
        for i in range(2):
            rows = slice(i * STRETCH, (i + 1) * STRETCH)
            high, low = u_vm[c, 0, rows, :], u_vm[c, 1, rows, :]
            stacked = jnp.concatenate([high, low, high], axis=0)
            found.append(jnp.dot(ends_vm[...], stacked, preferred_element_type=F32)[:8])
        return found

    def finish(c, found):
        for i in range(2):
            moments = found[i]
            rest = (moments - moments.astype(BF16).astype(F32))[:FINE]
            at = PIECE * i + RAW
            for h in range(2):
                part = slice(h * LANES, (h + 1) * LANES)
                pay[c, h, at : at + RANK, :] = moments[:RANK, part]
                pay[c, h, at + RANK : at + COEFS, :] = rest[:, part]
        for h in range(2):
            packed[c, :, h * LANES : (h + 1) * LANES] = pay[c, h].astype(BF16)

    def step(c, carry):
        @pl.when(lax.rem(c, WIDE) == 0)
        def _():
            for copy in loads(c // WIDE):
                copy.wait()

        before = jnp.maximum(c - 1, 0)
        found = products(before)
        features(c)

        @pl.when(c > 0)
        def _():
            finish(before, found)
            for copy in stores(before):
                copy.start()

        return carry

    lax.fori_loop(0, blocks, step, 0)
    finish(blocks - 1, products(blocks - 1))
    for copy in stores(blocks - 1):
        copy.start()

    def end(c, carry):
        for copy in stores(c):
            copy.wait()
        return carry

    lax.fori_loop(0, blocks, end, 0)
    if direct:
        for copy in own_loads():
            copy.wait()


def local_kernel(
    q_ref, k_ref, v_ref, taps_ref, rates_ref, res_ref, skip_ref, local_ref, qc_ref, y_ref, xs, u_vm
):
    tile = q_ref.shape[1]
    per = SPAN // LANES
    first_row = lax.broadcasted_iota(jnp.int32, (8, LANES), 0)
    for g in range(tile // LANES):
        cols = slice(g * LANES, (g + 1) * LANES)
        part = slice(g % per * LANES, (g % per + 1) * LANES)
        taps = [[taps_ref[a, j : j + 1, cols] for j in range(REACH + 1)] for a in range(3)]
        for i in range(2):
            base = i * (STRETCH + 8) + 8
            for a, ref in enumerate((q_ref, k_ref, v_ref)):
                xs[a, g, base - 8 : base, :] = jnp.zeros((8, LANES), F32)
                xs[a, g, base : base + STRETCH, :] = ref[i * STRETCH : (i + 1) * STRETCH, cols].astype(F32)
            for b in range(STRETCH // 8):
                at = base + 8 * b
                totals = []
                for a in range(3):
                    total = taps[a][0] * xs[a, g, at : at + 8, :]
                    for j in range(1, REACH + 1):
                        total = total + taps[a][j] * xs[a, g, at - j : at - j + 8, :]
                    totals.append(total)
                query, mixed = totals[0], totals[1] * totals[2]
                if b == 0:
                    query = jnp.where(first_row >= REACH, query, 1.0)
                    mixed = jnp.where(first_row >= REACH, mixed, 0.0)
                rows = slice(i * STRETCH + 8 * b, i * STRETCH + 8 * b + 8)
                qc_ref[g // per, rows, part] = query
                u_vm[g // per, rows, part] = mixed
    for c in range(tile // SPAN):
        cols = slice(c * SPAN, (c + 1) * SPAN)
        rate = rates_ref[:, cols]
        amount = amplitude(rate, res_ref[:, cols])
        weights = [jnp.sum(amount * value, axis=0, keepdims=True) for value in strengths(rate)]
        for i in range(2):
            rows = slice(i * STRETCH, (i + 1) * STRETCH)
            mixed = u_vm[c, rows, :]
            high, low = split(mixed)
            parts = jnp.dot(
                local_ref[...], jnp.concatenate([high, low, high], axis=0), preferred_element_type=F32
            )
            total = skip_ref[:, cols] * mixed
            for p in range(RANK):
                total = total + weights[p] * parts[p * STRETCH : (p + 1) * STRETCH, :]
            y_ref[c, rows, :] = total


def middle_kernel(
    perm_ref, x_ref, taps_ref, rates_ref, res_ref, skip_ref, out_ref,
    raw, ext, moments, past, heads, first, second, states, mids, coefs, fades, result, slab, packed, out_sems,
):
    slots = perm_ref.shape[0]
    groups = x_ref.shape[2] // LANES
    order = rates_ref.shape[0]
    span = 2 * PIECE
    row = lax.broadcasted_iota(jnp.int32, (8, LANES), 0)
    ext[:, :, 0, 0:8, :] = jnp.zeros((3, groups, 8, LANES), F32)
    past[:, :, 0:8, :] = jnp.zeros((groups, slots, 8, LANES), F32)

    def unpack(src, carry):
        for g in range(groups):
            raw[src, g, 8 : 8 + span, :] = x_ref[src, :, g * LANES : (g + 1) * LANES].astype(F32)
        for i in range(2):
            n = perm_ref[2 * src + i]
            for g in range(groups):
                for a in range(3):
                    at = 8 + i * PIECE + a * REACH
                    ext[a, g, n + 1, 0:8, :] = raw[src, g, at + REACH - 8 : at + REACH, :]
                    at = at + 3 * REACH
                    ext[a, g, n, 8:16, :] = raw[src, g, at : at + 8, :]
                at = 8 + i * PIECE + RAW
                fine = jnp.where(row < FINE, raw[src, g, at + RANK : at + RANK + 8, :], 0.0)
                moments[g, n] = raw[src, g, at : at + 8, :] + fine
        return carry

    lax.fori_loop(0, slots // 2, unpack, 0, unroll=2)

    def group_pass(g, carry):
        cols = pl.ds(pl.multiple_of(g * LANES, LANES), LANES)
        rate = rates_ref[:, cols]
        amount = amplitude(rate, res_ref[:, cols])
        basis = strengths(rate)
        powers = [jnp.ones_like(rate), jnp.exp(-rate)]
        for d in range(2, REACH + 1):
            powers.append(powers[-1] * powers[1])
        for t in range(REACH):
            coefs[g, 0, t * order : (t + 1) * order, :] = amount * powers[t + 1]
        for p in range(RANK):
            coefs[g, 1, p * order : (p + 1) * order, :] = amount * powers[1] * basis[p]
        fade_rest = jnp.exp(-rate * float(INNER))
        fades[g, 0] = powers[REACH]
        fades[g, 1] = fade_rest * powers[REACH]
        taps = [[taps_ref[a, j : j + 1, cols] for j in range(REACH + 1)] for a in range(3)]
        near = [jnp.sum(amount * powers[d], axis=0, keepdims=True) for d in range(REACH)]
        near[0] = near[0] + skip_ref[:, cols]

        def head_pass(n, carry):
            feats = []
            for a in range(3):
                total = taps[a][0] * ext[a, g, n, 8:16, :]
                for j in range(1, REACH + 1):
                    total = total + taps[a][j] * ext[a, g, n, 8 - j : 16 - j, :]
                feats.append(jnp.where(row < REACH, total, 0.0))
            mixed = feats[1] * feats[2]
            past[g, n, 8:16, :] = mixed
            total = near[0] * mixed
            for d in range(1, REACH):
                total = total + near[d] * past[g, n, 8 - d : 16 - d, :]
            at = pl.multiple_of(n * 16, 16)
            heads[g, pl.ds(at, 8), :] = feats[0]
            heads[g, pl.ds(at + 8, 8), :] = total
            value = powers[REACH - 1] * past[g, n, 8:9, :]
            for s in range(1, REACH):
                value = value + powers[REACH - 1 - s] * past[g, n, 8 + s : 9 + s, :]
            first[g, n] = value
            return carry

        lax.fori_loop(0, slots, head_pass, 0, unroll=4)

        def rest_pass(n, carry):
            value = fade_rest * first[g, n]
            for p in range(RANK):
                value = value + basis[p] * moments[g, n, p : p + 1, :]
            second[g, n] = value
            return carry

        lax.fori_loop(0, slots, rest_pass, 0, unroll=4)
        return carry

    lax.fori_loop(0, groups, group_pass, 0)

    def scan_pass(n, state):
        after = []
        at = pl.multiple_of(n * order, order)
        for g in range(groups):
            states[g, pl.ds(at, order), :] = state[g]
            mids[g, pl.ds(at, order), :] = fades[g, 0] * state[g] + first[g, n]
            after.append(fades[g, 1] * state[g] + second[g, n])
        return tuple(after)

    lax.fori_loop(0, slots, scan_pass, tuple(jnp.zeros((order, LANES), F32) for _ in range(groups)), unroll=4)

    quad = 4

    def sums(g, kind, held, first_tile):
        totals = [[None] * quad for _ in range(RANK)]
        for r in range(order):
            values = [held[g, pl.ds((first_tile + k) * 8 * order + r, 8, stride=order), :] for k in range(quad)]
            for p in range(RANK):
                weight = coefs[g, kind, p * order + r : p * order + r + 1, :]
                for k in range(quad):
                    term = weight * values[k]
                    totals[p][k] = term if r == 0 else totals[p][k] + term
        return totals

    quads = slots // (8 * quad)

    def out_pass(step, carry):
        g, q = step // quads, lax.rem(step, quads)
        totals = sums(g, 0, states, q * quad)
        for t in range(REACH):
            for k in range(quad):
                tile = q * quad + k
                query = heads[g, pl.ds(tile * 128 + t, 8, stride=16), :]
                local = heads[g, pl.ds(tile * 128 + 8 + t, 8, stride=16), :]
                z = query * (local + totals[t][k])
                result[g, pl.ds(tile * 192 + t, 8, stride=24), :] = z
                result[g, pl.ds(tile * 192 + REACH + t, 8, stride=24), :] = z - z.astype(BF16).astype(F32)
        totals = sums(g, 1, mids, q * quad)
        for p in range(RANK):
            for k in range(quad):
                tile = q * quad + k
                value = totals[p][k]
                result[g, pl.ds(tile * 192 + 2 * REACH + p, 8, stride=24), :] = value
                if p < FINE:
                    rest = value - value.astype(BF16).astype(F32)
                    result[g, pl.ds(tile * 192 + 2 * REACH + RANK + p, 8, stride=24), :] = rest
        return carry

    lax.fori_loop(0, groups * quads, out_pass, 0)

    def store(src):
        return pltpu.make_async_copy(packed.at[src], out_ref.at[src], out_sems.at[src])

    def pack(src, carry):
        for g in range(groups):
            for i in range(2):
                at = pl.multiple_of(perm_ref[2 * src + i] * 24, 8)
                slab[src, g, i * BACK : i * BACK + 24, :] = result[g, pl.ds(at, 24), :]
            packed[src, :, g * LANES : (g + 1) * LANES] = slab[src, g, 0 : 2 * BACK, :].astype(BF16)
        return carry

    lax.fori_loop(0, slots // 2, pack, 0, unroll=2)

    def send(src, carry):
        store(src).start()
        return carry

    def end(src, carry):
        store(src).wait()
        return carry

    lax.fori_loop(0, slots // 2, send, 0)
    lax.fori_loop(0, slots // 2, end, 0)


def join_kernel(back_ref, lift_ref, qc_ref, y_ref, z_ref, sq_ref, qc_vm, carry, total, sems):
    blocks, tokens, _ = qc_vm.shape
    by_dest = len(back_ref.shape) == 3
    chunk = 4

    def load(c):
        rows = pl.ds(c * chunk, chunk)
        return pltpu.make_async_copy(qc_ref.at[rows], qc_vm.at[rows], sems.at[c])

    def lanes(b):
        return pl.ds(pl.multiple_of(b * SPAN, SPAN), SPAN)

    for c in range(blocks // chunk):
        load(c).start()

    def products(c, unused):
        for k in range(chunk):
            b = c * chunk + k
            back = back_ref[b] if by_dest else back_ref[:, lanes(b)]
            product = jnp.dot(lift_ref[0], back, preferred_element_type=F32)
            carry[b] = y_ref[b] + product + jnp.dot(lift_ref[1], back, preferred_element_type=F32)
        return unused

    lax.fori_loop(0, blocks // chunk, products, 0)
    total[...] = jnp.zeros((tokens, LANES), F32)

    def square(c, unused):
        load(c).wait()
        part = total[...]
        for k in range(chunk):
            b = c * chunk + k
            z = qc_vm[b] * carry[b]
            z_ref[:, lanes(b)] = z
            squares = z * z
            for h in range(SPAN // LANES):
                part = part + squares[:, h * LANES : (h + 1) * LANES]
        total[...] = part
        return unused

    lax.fori_loop(0, blocks // chunk, square, 0)
    sq_ref[...] = jnp.sum(total[...].T, axis=0, keepdims=True)


def scale_kernel(*refs, channels):
    z_ref, gain_ref, refs, (out_ref, held, sems) = refs[0], refs[1], refs[2:-3], refs[-3:]
    tokens, width = z_ref.shape
    chunks = sems.shape[0]
    wide = width // chunks
    total = refs[0][...]
    for ref in refs[1:]:
        total = total + ref[...]
    scale = lax.rsqrt(total / channels + 1e-05)
    scale = jnp.broadcast_to(scale, (LANES, tokens)).T
    copies = []
    for c in range(chunks):
        for g in range(c * wide // LANES, (c + 1) * wide // LANES):
            cols = slice(g * LANES, (g + 1) * LANES)
            held[:, cols] = (z_ref[:, cols] * scale * gain_ref[:, cols]).astype(BF16)
        cols = pl.ds(c * wide, wide)
        copy = pltpu.make_async_copy(held.at[:, cols], out_ref.at[:, cols], sems.at[c])
        copy.start()
        copies.append(copy)
    for copy in copies:
        copy.wait()


def limit(mib):
    return pltpu.CompilerParams(vmem_limit_bytes=mib * 1024 * 1024)


def on_device(sizes, q_in, k_in, v_in, stretch_of_slot, short_weight, rates, residues, skip, gain):
    n_ctx, n_ch = sizes
    tokens, width = q_in.shape
    slots = stretch_of_slot.shape[0]
    order = rates.shape[0]
    share = width // n_ctx
    direct = share == SPAN
    tile = min(width, 1024)
    steps = width // tile
    groups = tile // LANES
    ends_np, local_np, lift_np = constant_matrices()
    ends, local, lift = jnp.asarray(ends_np), jnp.asarray(local_np), jnp.asarray(lift_np)
    skip, gain = skip.reshape(1, width), gain.reshape(1, width)
    me = lax.axis_index("ctx").astype(jnp.int32).reshape(1)

    def whole(array):
        return pl.BlockSpec(array.shape, lambda c: (0,) * array.ndim)

    def columns(*lead):
        return pl.BlockSpec((*lead, tile), lambda c: (0,) * len(lead) + (c,))

    def exchange(array):
        if direct:
            return lax.all_to_all(array, "ctx", 0, 0, tiled=True)
        array = array.reshape(array.shape[0], n_ctx, share).transpose(1, 0, 2)
        return widen(lax.all_to_all(array, "ctx", 0, 0, tiled=True))

    lanes = -(-share // LANES) * LANES

    def widen(array, fill=0.0):
        pad = [(0, 0)] * (array.ndim - 1) + [(0, lanes - share)]
        return jnp.pad(array, pad, constant_values=fill)

    def cut(array, fill=0.0):
        return widen(lax.dynamic_slice_in_dim(array, lax.axis_index("ctx") * share, share, array.ndim - 1), fill)

    smem = pl.BlockSpec(memory_space=pltpu.SMEM)
    vmem = pl.BlockSpec(memory_space=pltpu.VMEM)
    hbm = pl.BlockSpec(memory_space=pltpu.HBM)
    f32 = lambda *shape: jax.ShapeDtypeStruct(shape, F32)
    pin = lambda array: pltpu.with_memory_space_constraint(array, pltpu.HBM)

    weights = (short_weight, rates, residues, skip)
    own = [f32(*w.shape[:-1], share) for w in weights] if direct else []
    blocks = width // SPAN
    pay, *mine = pl.pallas_call(
        functools.partial(front_kernel, direct=direct),
        in_specs=[smem] + [hbm] * (5 + len(own)),
        out_specs=[hbm] + [vmem] * len(own),
        out_shape=[
            pltpu.HBM((n_ctx, 2 * PIECE, share) if direct else (2 * PIECE, width), BF16),
        ]
        + own,
        scratch_shapes=[
            pltpu.VMEM((2, tokens, width), BF16),
            pltpu.VMEM((4, 16, width), BF16),
            pltpu.VMEM((2, REACH + 1, width), F32),
            pltpu.VMEM(ends.shape, BF16),
            pltpu.VMEM((2, 2, 2, 2 * (STRETCH + 8), LANES), F32),
            pltpu.VMEM((2, 2, 2, 32, LANES), F32),
            pltpu.VMEM((blocks, 2, 2 * PIECE, LANES), F32),
            pltpu.VMEM((blocks, 2 * PIECE, SPAN), BF16),
            pltpu.VMEM((blocks, 2, tokens, SPAN), BF16),
            pltpu.SemaphoreType.DMA((3, blocks // WIDE)),
            pltpu.SemaphoreType.DMA((4,)),
            pltpu.SemaphoreType.DMA((1,)),
            pltpu.SemaphoreType.DMA((4,)),
            pltpu.SemaphoreType.DMA((blocks,)),
        ],
        compiler_params=limit(24),
        name="front_pieces",
    )(me, *map(pin, (q_in, k_in, v_in, short_weight, ends)), *(map(pin, weights) if direct else ()))
    arrived = exchange(pay)
    if not direct:
        mine = (cut(short_weight), cut(rates, 0.01), cut(residues), cut(skip))

    query, inner = pl.pallas_call(
        local_kernel,
        grid=(steps,),
        in_specs=[columns(tokens)] * 3
        + [columns(3, REACH + 1), columns(order), columns(order), columns(1), whole(local)],
        out_specs=[pl.BlockSpec((tile // SPAN, tokens, SPAN), lambda c: (c, 0, 0))] * 2,
        out_shape=[pltpu.HBM((blocks, tokens, SPAN), F32), pltpu.VMEM((blocks, tokens, SPAN), F32)],
        scratch_shapes=[
            pltpu.VMEM((3, groups, 2 * (STRETCH + 8), LANES), F32),
            pltpu.VMEM((tile // SPAN, tokens, SPAN), F32),
        ],
        compiler_params=limit(24),
        name="local_filter",
        cost_estimate=pl.CostEstimate(flops=10**9, bytes_accessed=20 * 10**6, transcendentals=0),
    )(*map(pin, (q_in, k_in, v_in, short_weight, rates, residues)), skip, local)
    arrived, query, inner = lax.optimization_barrier((arrived, query, inner))

    groups = lanes // LANES
    back = pl.pallas_call(
        middle_kernel,
        in_specs=[smem] + [vmem] * 5,
        out_specs=hbm,
        scratch_shapes=[
            pltpu.VMEM((n_ctx, groups, 8 + 2 * PIECE + 8, LANES), F32),
            pltpu.VMEM((3, groups, slots + 1, 16, LANES), F32),
            pltpu.VMEM((groups, slots, 8, LANES), F32),
            pltpu.VMEM((groups, slots, 16, LANES), F32),
            pltpu.VMEM((groups, slots * 16, LANES), F32),
            pltpu.VMEM((groups, slots, order, LANES), F32),
            pltpu.VMEM((groups, slots, order, LANES), F32),
            pltpu.VMEM((groups, slots * order, LANES), F32),
            pltpu.VMEM((groups, slots * order, LANES), F32),
            pltpu.VMEM((groups, 2, RANK * order, LANES), F32),
            pltpu.VMEM((groups, 2, order, LANES), F32),
            pltpu.VMEM((groups, slots * 24, LANES), F32),
            pltpu.VMEM((n_ctx, groups, BACK + 28, LANES), F32),
            pltpu.VMEM((n_ctx, 2 * BACK, lanes), BF16),
            pltpu.SemaphoreType.DMA((n_ctx,)),
        ],
        out_shape=pltpu.HBM((n_ctx, 2 * BACK, lanes), BF16),
        compiler_params=limit(24),
        name="middle_states",
    )(stretch_of_slot, arrived, *mine)
    if not direct:
        back = back[:, :, :share]
    back = lax.all_to_all(back, "ctx", 0, 0, tiled=True)
    if not direct:
        back = back.transpose(1, 0, 2).reshape(2 * BACK, width)

    keep = lambda array: pltpu.with_memory_space_constraint(array, pltpu.VMEM)
    zvalues, squares = pl.pallas_call(
        join_kernel,
        in_specs=[vmem] * 2 + [hbm, vmem],
        out_specs=[vmem] * 2,
        out_shape=[f32(tokens, width), f32(1, tokens)],
        scratch_shapes=[pltpu.VMEM((blocks, tokens, SPAN), F32)] * 2
        + [pltpu.VMEM((tokens, LANES), F32), pltpu.SemaphoreType.DMA((blocks // 4,))],
        compiler_params=limit(24),
        name="join_carry",
    )(back, lift, pin(query), keep(inner))
    sums = [squares]
    for shift in range(1, n_ch):
        sums.append(lax.ppermute(squares, "ch", [(i, (i + shift) % n_ch) for i in range(n_ch)]))
    return pl.pallas_call(
        functools.partial(scale_kernel, channels=width * n_ch),
        in_specs=[vmem] * (2 + n_ch),
        out_specs=hbm,
        out_shape=pltpu.HBM((tokens, width), BF16),
        scratch_shapes=[pltpu.VMEM((tokens, width), BF16), pltpu.SemaphoreType.DMA((8 if width % 1024 == 0 else 1,))],
        compiler_params=limit(24),
        name="scale_rows",
    )(zvalues, gain, *sums)


def solution(mesh):
    sizes = (mesh.shape["ctx"], mesh.shape["ch"])
    in_specs = (
        P("ctx", "ch"),
        P("ctx", "ch"),
        P("ctx", "ch"),
        P(),
        P(None, None, "ch"),
        P(None, "ch"),
        P(None, "ch"),
        P("ch"),
        P("ch"),
    )

    def run(*arrays):
        return on_device(sizes, *arrays)

    return jax.shard_map(run, mesh=mesh, in_specs=in_specs, out_specs=P("ctx", "ch"), check_vma=False)
```

```python
import functools
from decimal import Decimal, getcontext

import jax
import jax.numpy as jnp
import ml_dtypes
import numpy as np
from jax import lax
from jax.experimental import pallas as pl
from jax.experimental.pallas import tpu as pltpu
from jax.sharding import PartitionSpec as P

F32, BF16 = jnp.float32, jnp.bfloat16
LANES = 128
SPAN = 256
WIDE = 2
STRETCH = 64
REACH = 6
INNER = STRETCH - REACH
PIVOTS = (8, 49, 21, 56, 36, 1)
ANCHORS = ("0.0020", "0.0235", "0.0110", "0.0295", "0.0185", "0.0004")
RANK = len(PIVOTS)
FINE = 2
COEFS = RANK + FINE
RAW = 6 * REACH
PIECE = RAW + COEFS
BACK = 2 * REACH + COEFS


def shape_table():
    getcontext().prec = 50
    rest = [[(-Decimal(a) * d).exp() for d in range(INNER)] for a in ANCHORS]
    table = []
    for p in range(RANK):
        shape = [x / rest[p][PIVOTS[p]] for x in rest[p]]
        rest = [[x - row[PIVOTS[p]] * y for x, y in zip(row, shape)] for row in rest]
        table.append([float(x) for x in shape])
    return table


SHAPE = shape_table()


def halves(values):
    high = values.astype(ml_dtypes.bfloat16)
    low = (values - high.astype(np.float32)).astype(ml_dtypes.bfloat16)
    return high, low


def constant_matrices():
    shape = np.array(SHAPE, np.float32)
    ends = np.zeros((16, STRETCH), np.float32)
    local = np.zeros((RANK, STRETCH, STRETCH), np.float32)
    lift = np.zeros((2, 2 * STRETCH, 2 * BACK), np.float32)
    parts = [h.astype(np.float32) for h in halves(shape)]
    for p in range(RANK):
        for s in range(REACH, STRETCH):
            ends[p, s] = shape[p, STRETCH - 1 - s]
            local[p, s:, s] = shape[p, : STRETCH - s]
        for half in range(2):
            rows = slice(half * STRETCH + REACH, (half + 1) * STRETCH)
            at = half * BACK + 2 * REACH
            for k in range(2):
                lift[k, rows, at + p] = parts[k][p]
                if p < FINE:
                    lift[k, rows, at + RANK + p] = parts[k][p]
    for half in range(2):
        for t in range(REACH):
            lift[0, half * STRETCH + t, half * BACK + t] = 1.0
            lift[0, half * STRETCH + t, half * BACK + REACH + t] = 1.0
    local = local.reshape(RANK * STRETCH, STRETCH)
    ends = ends.reshape(16, 8, STRETCH // 8).transpose(0, 2, 1).reshape(16, STRETCH)

    def triple(m):
        h, l = halves(m)
        return np.concatenate([h, h, l], axis=1)

    return triple(ends), triple(local), lift.astype(ml_dtypes.bfloat16)


def strengths(rate):
    found = []
    for p in range(RANK):
        value = jnp.exp(-rate * float(PIVOTS[p]))
        for q in range(p):
            value = value - found[q] * SHAPE[q][PIVOTS[p]]
        found.append(value)
    return found


def split(values):
    high = values.astype(BF16)
    return high, (values - high.astype(F32)).astype(BF16)


def amplitude(rate, residue):
    x = 2.0 * rate
    series = 1.0 - x * (0.5 - x * (1 / 6 - x * (1 / 24 - x * (1 / 120 - x * (1 / 720)))))
    return residue * jnp.sqrt(x * series)


EDGES = (0, STRETCH - 16, STRETCH, 2 * STRETCH - 16)


def front_kernel(*refs, direct):
    me_ref, q_ref, k_ref, v_ref, taps_ref, ends_ref = refs[:6]
    refs = refs[6:]
    weights, refs = (refs[:4], refs[4:]) if direct else ((), refs)
    pay_ref, refs = refs[0], refs[1:]
    kept, refs = (refs[:4], refs[4:]) if direct else ((), refs)
    held, edge, taps_vm, ends_vm, xs, qs, pay, packed, u_vm, in_sems, edge_sems, tap_sem, own_sems, out_sems = refs
    blocks = k_ref.shape[1] // SPAN

    def lanes(c):
        return pl.ds(pl.multiple_of(c * SPAN, SPAN), SPAN)

    def loads(w):
        cols = pl.ds(pl.multiple_of(w * WIDE * SPAN, SPAN), WIDE * SPAN)
        return [
            pltpu.make_async_copy(ref.at[:, cols], held.at[a, :, cols], in_sems.at[a, w])
            for a, ref in enumerate((k_ref, v_ref))
        ] + [pltpu.make_async_copy(taps_ref.at[pl.ds(1, 2), :, cols], taps_vm.at[:, :, cols], in_sems.at[2, w])]

    def edge_loads():
        return [
            pltpu.make_async_copy(q_ref.at[pl.ds(at, 16), :], edge.at[e], edge_sems.at[e])
            for e, at in enumerate(EDGES)
        ]

    def stores(c):
        target = pay_ref.at[c] if direct else pay_ref.at[:, lanes(c)]
        return [pltpu.make_async_copy(packed.at[c], target, out_sems.at[c])]

    def own_loads():
        share = kept[0].shape[-1]
        cols = pl.ds(pl.multiple_of(me_ref[0] * share, share), share)
        views = (weights[0].at[:, :, cols], weights[1].at[:, cols], weights[2].at[:, cols], weights[3].at[:, cols])
        return [pltpu.make_async_copy(view, ref, own_sems.at[n]) for n, (view, ref) in enumerate(zip(views, kept))]

    ends_copy = pltpu.make_async_copy(ends_ref, ends_vm, tap_sem.at[0])
    for copy in loads(0) + edge_loads():
        copy.start()
    ends_copy.start()
    waves = blocks // WIDE

    def begin(c, carry):
        for copy in loads(c):
            copy.start()
        return carry

    lax.fori_loop(1, waves, begin, 0)
    if direct:
        for copy in own_loads():
            copy.start()
    for parity in range(2):
        for a in range(2):
            for h in range(2):
                for i in range(2):
                    at = i * (STRETCH + 8)
                    xs[parity, a, h, at : at + 8, :] = jnp.zeros((8, LANES), F32)
    for copy in edge_loads():
        copy.wait()
    ends_copy.wait()

    def features(c):
        parity = lax.rem(c, 2)
        for h in range(2):
            part = slice(h * LANES, (h + 1) * LANES)
            cols = pl.ds(pl.multiple_of(c * SPAN + h * LANES, LANES), LANES)
            for i in range(2):
                base = i * (STRETCH + 8) + 8
                for a in range(2):
                    xs[parity, a, h, base : base + STRETCH, :] = held[
                        a, i * STRETCH : (i + 1) * STRETCH, cols
                    ].astype(F32)
                    at = i * PIECE + (1 + a) * REACH
                    pay[c, h, at : at + REACH, :] = xs[parity, a, h, base + STRETCH - REACH : base + STRETCH, :]
                    at = at + 3 * REACH
                    pay[c, h, at : at + REACH, :] = xs[parity, a, h, base : base + REACH, :]
                qs[parity, h, i, 0:16, :] = edge[2 * i, :, cols].astype(F32)
                qs[parity, h, i, 16:32, :] = edge[2 * i + 1, :, cols].astype(F32)
                at = i * PIECE
                pay[c, h, at : at + REACH, :] = qs[parity, h, i, 32 - REACH : 32, :]
                pay[c, h, at + 3 * REACH : at + 4 * REACH, :] = qs[parity, h, i, 0:REACH, :]
            taps = [[taps_vm[a, j : j + 1, cols] for j in range(REACH + 1)] for a in range(2)]
            for i in range(2):
                base = i * (STRETCH + 8) + 8
                both = []
                for a in range(2):
                    strided = {
                        m: xs[parity, a, h, pl.ds(base + m, 8, stride=8), :] for m in range(-REACH, STRETCH // 8)
                    }
                    found = []
                    for m in range(STRETCH // 8):
                        total = taps[a][0] * strided[m]
                        for j in range(1, REACH + 1):
                            total = total + taps[a][j] * strided[m - j]
                        found.append(total)
                    both.append(found)
                mixed = [k * v for k, v in zip(*both)]
                for m in range(0, STRETCH // 8, 2):
                    high, low = split(jnp.concatenate(mixed[m : m + 2], axis=0))
                    rows = slice(i * STRETCH + 8 * m, i * STRETCH + 8 * m + 16)
                    u_vm[c, 0, rows, part] = high
                    u_vm[c, 1, rows, part] = low

    def products(c):
        found = []
        for i in range(2):
            rows = slice(i * STRETCH, (i + 1) * STRETCH)
            high, low = u_vm[c, 0, rows, :], u_vm[c, 1, rows, :]
            stacked = jnp.concatenate([high, low, high], axis=0)
            found.append(jnp.dot(ends_vm[...], stacked, preferred_element_type=F32)[:8])
        return found

    def finish(c, found):
        for i in range(2):
            moments = found[i]
            rest = (moments - moments.astype(BF16).astype(F32))[:FINE]
            at = PIECE * i + RAW
            for h in range(2):
                part = slice(h * LANES, (h + 1) * LANES)
                pay[c, h, at : at + RANK, :] = moments[:RANK, part]
                pay[c, h, at + RANK : at + COEFS, :] = rest[:, part]
        for h in range(2):
            packed[c, :, h * LANES : (h + 1) * LANES] = pay[c, h].astype(BF16)

    def step(c, carry):
        @pl.when(lax.rem(c, WIDE) == 0)
        def _():
            for copy in loads(c // WIDE):
                copy.wait()

        before = jnp.maximum(c - 1, 0)
        found = products(before)
        features(c)

        @pl.when(c > 0)
        def _():
            finish(before, found)
            for copy in stores(before):
                copy.start()

        return carry

    lax.fori_loop(0, blocks, step, 0)
    finish(blocks - 1, products(blocks - 1))
    for copy in stores(blocks - 1):
        copy.start()

    def end(c, carry):
        for copy in stores(c):
            copy.wait()
        return carry

    lax.fori_loop(0, blocks, end, 0)
    if direct:
        for copy in own_loads():
            copy.wait()


def local_kernel(q_ref, k_ref, v_ref, taps_ref, rates_ref, res_ref, skip_ref, local_ref, *refs):
    *kept, rest_ref, y_ref, xs, u_vm, qc_ref = refs
    tile = q_ref.shape[1]
    per = SPAN // LANES
    first_row = lax.broadcasted_iota(jnp.int32, (8, LANES), 0)
    for g in range(tile // LANES):
        cols = slice(g * LANES, (g + 1) * LANES)
        part = slice(g % per * LANES, (g % per + 1) * LANES)
        taps = [[taps_ref[a, j : j + 1, cols] for j in range(REACH + 1)] for a in range(3)]
        for i in range(2):
            base = i * (STRETCH + 8) + 8
            for a, ref in enumerate((q_ref, k_ref, v_ref)):
                xs[a, g, base - 8 : base, :] = jnp.zeros((8, LANES), F32)
                xs[a, g, base : base + STRETCH, :] = ref[i * STRETCH : (i + 1) * STRETCH, cols].astype(F32)
            for b in range(STRETCH // 8):
                at = base + 8 * b
                totals = []
                for a in range(3):
                    total = taps[a][0] * xs[a, g, at : at + 8, :]
                    for j in range(1, REACH + 1):
                        total = total + taps[a][j] * xs[a, g, at - j : at - j + 8, :]
                    totals.append(total)
                query, mixed = totals[0], totals[1] * totals[2]
                if b == 0:
                    query = jnp.where(first_row >= REACH, query, 1.0)
                    mixed = jnp.where(first_row >= REACH, mixed, 0.0)
                rows = slice(i * STRETCH + 8 * b, i * STRETCH + 8 * b + 8)
                qc_ref[g // per, rows, part] = query
                u_vm[g // per, rows, part] = mixed
    for c in range(tile // SPAN):
        cols = slice(c * SPAN, (c + 1) * SPAN)
        rate = rates_ref[:, cols]
        amount = amplitude(rate, res_ref[:, cols])
        weights = [jnp.sum(amount * value, axis=0, keepdims=True) for value in strengths(rate)]
        for i in range(2):
            rows = slice(i * STRETCH, (i + 1) * STRETCH)
            mixed = u_vm[c, rows, :]
            high, low = split(mixed)
            parts = jnp.dot(
                local_ref[...], jnp.concatenate([high, low, high], axis=0), preferred_element_type=F32
            )
            total = skip_ref[:, cols] * mixed
            for p in range(RANK):
                total = total + weights[p] * parts[p * STRETCH : (p + 1) * STRETCH, :]
            y_ref[c, rows, :] = total
    if not kept:
        rest_ref[...] = qc_ref[...]
        return
    half = pl.num_programs(0) // 2

    @pl.when(pl.program_id(0) < half)
    def _():
        kept[0][...] = qc_ref[...]

    @pl.when(pl.program_id(0) >= half)
    def _():
        rest_ref[...] = qc_ref[...]


def middle_kernel(
    perm_ref, x_ref, taps_ref, rates_ref, res_ref, skip_ref, out_ref,
    raw, ext, moments, past, heads, first, second, states, mids, coefs, fades, result, slab, packed, out_sems,
):
    slots = perm_ref.shape[0]
    groups = x_ref.shape[2] // LANES
    order = rates_ref.shape[0]
    span = 2 * PIECE
    row = lax.broadcasted_iota(jnp.int32, (8, LANES), 0)
    ext[:, :, 0, 0:8, :] = jnp.zeros((3, groups, 8, LANES), F32)
    past[:, :, 0:8, :] = jnp.zeros((groups, slots, 8, LANES), F32)

    def unpack(src, carry):
        for g in range(groups):
            raw[src, g, 8 : 8 + span, :] = x_ref[src, :, g * LANES : (g + 1) * LANES].astype(F32)
        for i in range(2):
            n = perm_ref[2 * src + i]
            for g in range(groups):
                for a in range(3):
                    at = 8 + i * PIECE + a * REACH
                    ext[a, g, n + 1, 0:8, :] = raw[src, g, at + REACH - 8 : at + REACH, :]
                    at = at + 3 * REACH
                    ext[a, g, n, 8:16, :] = raw[src, g, at : at + 8, :]
                at = 8 + i * PIECE + RAW
                fine = jnp.where(row < FINE, raw[src, g, at + RANK : at + RANK + 8, :], 0.0)
                moments[g, n] = raw[src, g, at : at + 8, :] + fine
        return carry

    lax.fori_loop(0, slots // 2, unpack, 0, unroll=2)

    def group_pass(g, carry):
        cols = pl.ds(pl.multiple_of(g * LANES, LANES), LANES)
        rate = rates_ref[:, cols]
        amount = amplitude(rate, res_ref[:, cols])
        basis = strengths(rate)
        powers = [jnp.ones_like(rate), jnp.exp(-rate)]
        for d in range(2, REACH + 1):
            powers.append(powers[-1] * powers[1])
        for t in range(REACH):
            coefs[g, 0, t * order : (t + 1) * order, :] = amount * powers[t + 1]
        for p in range(RANK):
            coefs[g, 1, p * order : (p + 1) * order, :] = amount * powers[1] * basis[p]
        fade_rest = jnp.exp(-rate * float(INNER))
        fades[g, 0] = powers[REACH]
        fades[g, 1] = fade_rest * powers[REACH]
        taps = [[taps_ref[a, j : j + 1, cols] for j in range(REACH + 1)] for a in range(3)]
        near = [jnp.sum(amount * powers[d], axis=0, keepdims=True) for d in range(REACH)]
        near[0] = near[0] + skip_ref[:, cols]

        def head_pass(n, carry):
            feats = []
            for a in range(3):
                total = taps[a][0] * ext[a, g, n, 8:16, :]
                for j in range(1, REACH + 1):
                    total = total + taps[a][j] * ext[a, g, n, 8 - j : 16 - j, :]
                feats.append(jnp.where(row < REACH, total, 0.0))
            mixed = feats[1] * feats[2]
            past[g, n, 8:16, :] = mixed
            total = near[0] * mixed
            for d in range(1, REACH):
                total = total + near[d] * past[g, n, 8 - d : 16 - d, :]
            at = pl.multiple_of(n * 16, 16)
            heads[g, pl.ds(at, 8), :] = feats[0]
            heads[g, pl.ds(at + 8, 8), :] = total
            value = powers[REACH - 1] * past[g, n, 8:9, :]
            for s in range(1, REACH):
                value = value + powers[REACH - 1 - s] * past[g, n, 8 + s : 9 + s, :]
            first[g, n] = value
            return carry

        lax.fori_loop(0, slots, head_pass, 0, unroll=4)

        def rest_pass(n, carry):
            value = fade_rest * first[g, n]
            for p in range(RANK):
                value = value + basis[p] * moments[g, n, p : p + 1, :]
            second[g, n] = value
            return carry

        lax.fori_loop(0, slots, rest_pass, 0, unroll=4)
        return carry

    lax.fori_loop(0, groups, group_pass, 0)

    def scan_pass(n, state):
        after = []
        at = pl.multiple_of(n * order, order)
        for g in range(groups):
            states[g, pl.ds(at, order), :] = state[g]
            mids[g, pl.ds(at, order), :] = fades[g, 0] * state[g] + first[g, n]
            after.append(fades[g, 1] * state[g] + second[g, n])
        return tuple(after)

    lax.fori_loop(0, slots, scan_pass, tuple(jnp.zeros((order, LANES), F32) for _ in range(groups)), unroll=4)

    quad = 4

    def sums(g, kind, held, first_tile):
        totals = [[None] * quad for _ in range(RANK)]
        for r in range(order):
            values = [held[g, pl.ds((first_tile + k) * 8 * order + r, 8, stride=order), :] for k in range(quad)]
            for p in range(RANK):
                weight = coefs[g, kind, p * order + r : p * order + r + 1, :]
                for k in range(quad):
                    term = weight * values[k]
                    totals[p][k] = term if r == 0 else totals[p][k] + term
        return totals

    quads = slots // (8 * quad)

    def out_pass(step, carry):
        g, q = step // quads, lax.rem(step, quads)
        totals = sums(g, 0, states, q * quad)
        for t in range(REACH):
            for k in range(quad):
                tile = q * quad + k
                query = heads[g, pl.ds(tile * 128 + t, 8, stride=16), :]
                local = heads[g, pl.ds(tile * 128 + 8 + t, 8, stride=16), :]
                z = query * (local + totals[t][k])
                result[g, pl.ds(tile * 192 + t, 8, stride=24), :] = z
                result[g, pl.ds(tile * 192 + REACH + t, 8, stride=24), :] = z - z.astype(BF16).astype(F32)
        totals = sums(g, 1, mids, q * quad)
        for p in range(RANK):
            for k in range(quad):
                tile = q * quad + k
                value = totals[p][k]
                result[g, pl.ds(tile * 192 + 2 * REACH + p, 8, stride=24), :] = value
                if p < FINE:
                    rest = value - value.astype(BF16).astype(F32)
                    result[g, pl.ds(tile * 192 + 2 * REACH + RANK + p, 8, stride=24), :] = rest
        return carry

    lax.fori_loop(0, groups * quads, out_pass, 0)

    def store(src):
        return pltpu.make_async_copy(packed.at[src], out_ref.at[src], out_sems.at[src])

    def pack(src, carry):
        for g in range(groups):
            for i in range(2):
                at = pl.multiple_of(perm_ref[2 * src + i] * 24, 8)
                slab[src, g, i * BACK : i * BACK + 24, :] = result[g, pl.ds(at, 24), :]
            packed[src, :, g * LANES : (g + 1) * LANES] = slab[src, g, 0 : 2 * BACK, :].astype(BF16)
        return carry

    lax.fori_loop(0, slots // 2, pack, 0, unroll=2)

    def send(src, carry):
        store(src).start()
        return carry

    def end(src, carry):
        store(src).wait()
        return carry

    lax.fori_loop(0, slots // 2, send, 0)
    lax.fori_loop(0, slots // 2, end, 0)


def join_kernel(back_ref, lift_ref, *refs):
    *kept, rest_ref, y_ref, z_ref, sq_ref, rest_vm, carry, total, sems = refs
    blocks, tokens, _ = y_ref.shape
    by_dest = len(back_ref.shape) == 3
    chunk = 4
    first = blocks - rest_vm.shape[0]

    def load(c):
        rows = pl.ds(c * chunk, chunk)
        return pltpu.make_async_copy(rest_ref.at[rows], rest_vm.at[rows], sems.at[c])

    def lanes(b):
        return pl.ds(pl.multiple_of(b * SPAN, SPAN), SPAN)

    for c in range((blocks - first) // chunk):
        load(c).start()

    def products(c, unused):
        for k in range(chunk):
            b = c * chunk + k
            back = back_ref[b] if by_dest else back_ref[:, lanes(b)]
            product = jnp.dot(lift_ref[0], back, preferred_element_type=F32)
            carry[b] = y_ref[b] + product + jnp.dot(lift_ref[1], back, preferred_element_type=F32)
        return unused

    lax.fori_loop(0, blocks // chunk, products, 0)
    total[...] = jnp.zeros((tokens, LANES), F32)

    def square(held, offset, c):
        part = total[...]
        for k in range(chunk):
            b = c * chunk + k
            z = held[b] * carry[offset + b]
            z_ref[:, lanes(offset + b)] = z
            squares = z * z
            for h in range(SPAN // LANES):
                part = part + squares[:, h * LANES : (h + 1) * LANES]
        total[...] = part

    def from_kept(c, unused):
        square(kept[0], 0, c)
        return unused

    def from_rest(c, unused):
        load(c).wait()
        square(rest_vm, first, c)
        return unused

    if kept:
        lax.fori_loop(0, first // chunk, from_kept, 0)
    lax.fori_loop(0, (blocks - first) // chunk, from_rest, 0)
    sq_ref[...] = jnp.sum(total[...].T, axis=0, keepdims=True)


def scale_kernel(*refs, channels):
    z_ref, gain_ref, refs, (out_ref, held, sems) = refs[0], refs[1], refs[2:-3], refs[-3:]
    tokens, width = z_ref.shape
    chunks = sems.shape[0]
    wide = width // chunks
    total = refs[0][...]
    for ref in refs[1:]:
        total = total + ref[...]
    scale = lax.rsqrt(total / channels + 1e-05)
    scale = jnp.broadcast_to(scale, (LANES, tokens)).T
    copies = []
    for c in range(chunks):
        for g in range(c * wide // LANES, (c + 1) * wide // LANES):
            cols = slice(g * LANES, (g + 1) * LANES)
            held[:, cols] = (z_ref[:, cols] * scale * gain_ref[:, cols]).astype(BF16)
        cols = pl.ds(c * wide, wide)
        copy = pltpu.make_async_copy(held.at[:, cols], out_ref.at[:, cols], sems.at[c])
        copy.start()
        copies.append(copy)
    for copy in copies:
        copy.wait()


def limit(mib):
    return pltpu.CompilerParams(vmem_limit_bytes=mib * 1024 * 1024)


def on_device(sizes, q_in, k_in, v_in, stretch_of_slot, short_weight, rates, residues, skip, gain):
    n_ctx, n_ch = sizes
    tokens, width = q_in.shape
    slots = stretch_of_slot.shape[0]
    order = rates.shape[0]
    share = width // n_ctx
    direct = share == SPAN
    tile = min(width, 1024)
    steps = width // tile
    groups = tile // LANES
    ends_np, local_np, lift_np = constant_matrices()
    ends, local, lift = jnp.asarray(ends_np), jnp.asarray(local_np), jnp.asarray(lift_np)
    skip, gain = skip.reshape(1, width), gain.reshape(1, width)
    me = lax.axis_index("ctx").astype(jnp.int32).reshape(1)

    def whole(array):
        return pl.BlockSpec(array.shape, lambda c: (0,) * array.ndim)

    def columns(*lead):
        return pl.BlockSpec((*lead, tile), lambda c: (0,) * len(lead) + (c,))

    def exchange(array):
        if direct:
            return lax.all_to_all(array, "ctx", 0, 0, tiled=True)
        array = array.reshape(array.shape[0], n_ctx, share).transpose(1, 0, 2)
        return widen(lax.all_to_all(array, "ctx", 0, 0, tiled=True))

    lanes = -(-share // LANES) * LANES

    def widen(array, fill=0.0):
        pad = [(0, 0)] * (array.ndim - 1) + [(0, lanes - share)]
        return jnp.pad(array, pad, constant_values=fill)

    def cut(array, fill=0.0):
        return widen(lax.dynamic_slice_in_dim(array, lax.axis_index("ctx") * share, share, array.ndim - 1), fill)

    smem = pl.BlockSpec(memory_space=pltpu.SMEM)
    vmem = pl.BlockSpec(memory_space=pltpu.VMEM)
    hbm = pl.BlockSpec(memory_space=pltpu.HBM)
    f32 = lambda *shape: jax.ShapeDtypeStruct(shape, F32)
    pin = lambda array: pltpu.with_memory_space_constraint(array, pltpu.HBM)

    weights = (short_weight, rates, residues, skip)
    own = [f32(*w.shape[:-1], share) for w in weights] if direct else []
    blocks = width // SPAN
    pay, *mine = pl.pallas_call(
        functools.partial(front_kernel, direct=direct),
        in_specs=[smem] + [hbm] * (5 + len(own)),
        out_specs=[hbm] + [vmem] * len(own),
        out_shape=[
            pltpu.HBM((n_ctx, 2 * PIECE, share) if direct else (2 * PIECE, width), BF16),
        ]
        + own,
        scratch_shapes=[
            pltpu.VMEM((2, tokens, width), BF16),
            pltpu.VMEM((4, 16, width), BF16),
            pltpu.VMEM((2, REACH + 1, width), F32),
            pltpu.VMEM(ends.shape, BF16),
            pltpu.VMEM((2, 2, 2, 2 * (STRETCH + 8), LANES), F32),
            pltpu.VMEM((2, 2, 2, 32, LANES), F32),
            pltpu.VMEM((blocks, 2, 2 * PIECE, LANES), F32),
            pltpu.VMEM((blocks, 2 * PIECE, SPAN), BF16),
            pltpu.VMEM((blocks, 2, tokens, SPAN), BF16),
            pltpu.SemaphoreType.DMA((3, blocks // WIDE)),
            pltpu.SemaphoreType.DMA((4,)),
            pltpu.SemaphoreType.DMA((1,)),
            pltpu.SemaphoreType.DMA((4,)),
            pltpu.SemaphoreType.DMA((blocks,)),
        ],
        compiler_params=limit(24),
        name="front_pieces",
    )(me, *map(pin, (q_in, k_in, v_in, short_weight, ends)), *(map(pin, weights) if direct else ()))
    arrived = exchange(pay)
    if not direct:
        mine = (cut(short_weight), cut(rates, 0.01), cut(residues), cut(skip))

    half = steps // 2 if steps % 2 == 0 else 0
    kept = half * (tile // SPAN)
    places = [lambda c: (jnp.minimum(c, half - 1), 0, 0)] * (kept > 0)
    places += [lambda c: (jnp.maximum(c - half, 0), 0, 0), lambda c: (c, 0, 0)]
    *query, inner = pl.pallas_call(
        local_kernel,
        grid=(steps,),
        in_specs=[columns(tokens)] * 3
        + [columns(3, REACH + 1), columns(order), columns(order), columns(1), whole(local)],
        out_specs=[pl.BlockSpec((tile // SPAN, tokens, SPAN), at) for at in places],
        out_shape=[pltpu.VMEM((kept, tokens, SPAN), F32)] * (kept > 0)
        + [pltpu.HBM((blocks - kept, tokens, SPAN), F32), pltpu.VMEM((blocks, tokens, SPAN), F32)],
        scratch_shapes=[
            pltpu.VMEM((3, groups, 2 * (STRETCH + 8), LANES), F32),
            pltpu.VMEM((tile // SPAN, tokens, SPAN), F32),
            pltpu.VMEM((tile // SPAN, tokens, SPAN), F32),
        ],
        compiler_params=limit(24),
        name="local_filter",
        cost_estimate=pl.CostEstimate(flops=10**9, bytes_accessed=20 * 10**6, transcendentals=0),
    )(*map(pin, (q_in, k_in, v_in, short_weight, rates, residues)), skip, local)
    arrived, query, inner = lax.optimization_barrier((arrived, query, inner))

    groups = lanes // LANES
    back = pl.pallas_call(
        middle_kernel,
        in_specs=[smem] + [vmem] * 5,
        out_specs=hbm,
        scratch_shapes=[
            pltpu.VMEM((n_ctx, groups, 8 + 2 * PIECE + 8, LANES), F32),
            pltpu.VMEM((3, groups, slots + 1, 16, LANES), F32),
            pltpu.VMEM((groups, slots, 8, LANES), F32),
            pltpu.VMEM((groups, slots, 16, LANES), F32),
            pltpu.VMEM((groups, slots * 16, LANES), F32),
            pltpu.VMEM((groups, slots, order, LANES), F32),
            pltpu.VMEM((groups, slots, order, LANES), F32),
            pltpu.VMEM((groups, slots * order, LANES), F32),
            pltpu.VMEM((groups, slots * order, LANES), F32),
            pltpu.VMEM((groups, 2, RANK * order, LANES), F32),
            pltpu.VMEM((groups, 2, order, LANES), F32),
            pltpu.VMEM((groups, slots * 24, LANES), F32),
            pltpu.VMEM((n_ctx, groups, BACK + 28, LANES), F32),
            pltpu.VMEM((n_ctx, 2 * BACK, lanes), BF16),
            pltpu.SemaphoreType.DMA((n_ctx,)),
        ],
        out_shape=pltpu.HBM((n_ctx, 2 * BACK, lanes), BF16),
        compiler_params=limit(24),
        name="middle_states",
    )(stretch_of_slot, arrived, *mine)
    if not direct:
        back = back[:, :, :share]
    back = lax.all_to_all(back, "ctx", 0, 0, tiled=True)
    if not direct:
        back = back.transpose(1, 0, 2).reshape(2 * BACK, width)

    keep = lambda array: pltpu.with_memory_space_constraint(array, pltpu.VMEM)
    zvalues, squares = pl.pallas_call(
        join_kernel,
        in_specs=[vmem] * (1 + len(query)) + [hbm, vmem],
        out_specs=[vmem] * 2,
        out_shape=[f32(tokens, width), f32(1, tokens)],
        scratch_shapes=[
            pltpu.VMEM((blocks - kept, tokens, SPAN), F32),
            pltpu.VMEM((blocks, tokens, SPAN), F32),
            pltpu.VMEM((tokens, LANES), F32),
            pltpu.SemaphoreType.DMA(((blocks - kept) // 4,)),
        ],
        compiler_params=limit(24),
        name="join_carry",
    )(back, lift, *map(keep, query[:-1]), pin(query[-1]), keep(inner))
    sums = [squares]
    for shift in range(1, n_ch):
        sums.append(lax.ppermute(squares, "ch", [(i, (i + shift) % n_ch) for i in range(n_ch)]))
    return pl.pallas_call(
        functools.partial(scale_kernel, channels=width * n_ch),
        in_specs=[vmem] * (2 + n_ch),
        out_specs=hbm,
        out_shape=pltpu.HBM((tokens, width), BF16),
        scratch_shapes=[pltpu.VMEM((tokens, width), BF16), pltpu.SemaphoreType.DMA((8 if width % 1024 == 0 else 1,))],
        compiler_params=limit(24),
        name="scale_rows",
    )(zvalues, gain, *sums)


def solution(mesh):
    sizes = (mesh.shape["ctx"], mesh.shape["ch"])
    in_specs = (
        P("ctx", "ch"),
        P("ctx", "ch"),
        P("ctx", "ch"),
        P(),
        P(None, None, "ch"),
        P(None, "ch"),
        P(None, "ch"),
        P("ch"),
        P("ch"),
    )

    def run(*arrays):
        return on_device(sizes, *arrays)

    return jax.shard_map(run, mesh=mesh, in_specs=in_specs, out_specs=P("ctx", "ch"), check_vma=False)
```

```python
import functools
from decimal import Decimal, getcontext

import jax
import jax.numpy as jnp
import ml_dtypes
import numpy as np
from jax import lax
from jax.experimental import pallas as pl
from jax.experimental.pallas import tpu as pltpu
from jax.sharding import PartitionSpec as P

F32, BF16 = jnp.float32, jnp.bfloat16
LANES = 128
SPAN = 256
WIDE = 2
STRETCH = 64
REACH = 6
INNER = STRETCH - REACH
PIVOTS = (8, 49, 21, 56, 36, 1)
ANCHORS = ("0.0020", "0.0235", "0.0110", "0.0295", "0.0185", "0.0004")
RANK = len(PIVOTS)
FINE = 2
COEFS = RANK + FINE
RAW = 6 * REACH
PIECE = RAW + COEFS
BACK = 2 * REACH + COEFS


def shape_table():
    getcontext().prec = 50
    rest = [[(-Decimal(a) * d).exp() for d in range(INNER)] for a in ANCHORS]
    table = []
    for p in range(RANK):
        shape = [x / rest[p][PIVOTS[p]] for x in rest[p]]
        rest = [[x - row[PIVOTS[p]] * y for x, y in zip(row, shape)] for row in rest]
        table.append([float(x) for x in shape])
    return table


SHAPE = shape_table()


def halves(values):
    high = values.astype(ml_dtypes.bfloat16)
    low = (values - high.astype(np.float32)).astype(ml_dtypes.bfloat16)
    return high, low


def constant_matrices():
    shape = np.array(SHAPE, np.float32)
    ends = np.zeros((16, STRETCH), np.float32)
    local = np.zeros((RANK, STRETCH, STRETCH), np.float32)
    lift = np.zeros((2, 2 * STRETCH, 2 * BACK), np.float32)
    parts = [h.astype(np.float32) for h in halves(shape)]
    for p in range(RANK):
        for s in range(REACH, STRETCH):
            ends[p, s] = shape[p, STRETCH - 1 - s]
            local[p, s:, s] = shape[p, : STRETCH - s]
        for half in range(2):
            rows = slice(half * STRETCH + REACH, (half + 1) * STRETCH)
            at = half * BACK + 2 * REACH
            for k in range(2):
                lift[k, rows, at + p] = parts[k][p]
                if p < FINE:
                    lift[k, rows, at + RANK + p] = parts[k][p]
    for half in range(2):
        for t in range(REACH):
            lift[0, half * STRETCH + t, half * BACK + t] = 1.0
            lift[0, half * STRETCH + t, half * BACK + REACH + t] = 1.0
    local = local.reshape(RANK * STRETCH, STRETCH)
    ends = ends.reshape(16, 8, STRETCH // 8).transpose(0, 2, 1).reshape(16, STRETCH)

    def triple(m):
        h, l = halves(m)
        return np.concatenate([h, h, l], axis=1)

    return triple(ends), triple(local), lift.astype(ml_dtypes.bfloat16)


def strengths(rate):
    found = []
    for p in range(RANK):
        value = jnp.exp(-rate * float(PIVOTS[p]))
        for q in range(p):
            value = value - found[q] * SHAPE[q][PIVOTS[p]]
        found.append(value)
    return found


def split(values):
    high = values.astype(BF16)
    return high, (values - high.astype(F32)).astype(BF16)


def amplitude(rate, residue):
    x = 2.0 * rate
    series = 1.0 - x * (0.5 - x * (1 / 6 - x * (1 / 24 - x * (1 / 120 - x * (1 / 720)))))
    return residue * jnp.sqrt(x * series)


EDGES = (0, STRETCH - 16, STRETCH, 2 * STRETCH - 16)


def front_kernel(*refs, direct):
    me_ref, q_ref, k_ref, v_ref, taps_ref, ends_ref = refs[:6]
    refs = refs[6:]
    weights, refs = (refs[:4], refs[4:]) if direct else ((), refs)
    pay_ref, refs = refs[0], refs[1:]
    kept, refs = (refs[:4], refs[4:]) if direct else ((), refs)
    held, edge, taps_vm, ends_vm, xs, qs, pay, packed, u_vm, in_sems, edge_sems, tap_sem, own_sems, out_sems = refs
    blocks = k_ref.shape[1] // SPAN

    def lanes(c):
        return pl.ds(pl.multiple_of(c * SPAN, SPAN), SPAN)

    def loads(w):
        cols = pl.ds(pl.multiple_of(w * WIDE * SPAN, SPAN), WIDE * SPAN)
        return [
            pltpu.make_async_copy(ref.at[:, cols], held.at[a, :, cols], in_sems.at[a, w])
            for a, ref in enumerate((k_ref, v_ref))
        ] + [pltpu.make_async_copy(taps_ref.at[pl.ds(1, 2), :, cols], taps_vm.at[:, :, cols], in_sems.at[2, w])]

    def edge_loads():
        return [
            pltpu.make_async_copy(q_ref.at[pl.ds(at, 16), :], edge.at[e], edge_sems.at[e])
            for e, at in enumerate(EDGES)
        ]

    def stores(c):
        target = pay_ref.at[c] if direct else pay_ref.at[:, lanes(c)]
        return [pltpu.make_async_copy(packed.at[c], target, out_sems.at[c])]

    def own_loads():
        share = kept[0].shape[-1]
        cols = pl.ds(pl.multiple_of(me_ref[0] * share, share), share)
        views = (weights[0].at[:, :, cols], weights[1].at[:, cols], weights[2].at[:, cols], weights[3].at[:, cols])
        return [pltpu.make_async_copy(view, ref, own_sems.at[n]) for n, (view, ref) in enumerate(zip(views, kept))]

    ends_copy = pltpu.make_async_copy(ends_ref, ends_vm, tap_sem.at[0])
    for copy in loads(0) + edge_loads():
        copy.start()
    ends_copy.start()
    waves = blocks // WIDE

    def begin(c, carry):
        for copy in loads(c):
            copy.start()
        return carry

    lax.fori_loop(1, waves, begin, 0)
    if direct:
        for copy in own_loads():
            copy.start()
    for parity in range(2):
        for a in range(2):
            for h in range(2):
                for i in range(2):
                    at = i * (STRETCH + 8)
                    xs[parity, a, h, at : at + 8, :] = jnp.zeros((8, LANES), F32)
    for copy in edge_loads():
        copy.wait()
    ends_copy.wait()

    def features(c):
        parity = lax.rem(c, 2)
        for h in range(2):
            part = slice(h * LANES, (h + 1) * LANES)
            cols = pl.ds(pl.multiple_of(c * SPAN + h * LANES, LANES), LANES)
            for i in range(2):
                base = i * (STRETCH + 8) + 8
                for a in range(2):
                    xs[parity, a, h, base : base + STRETCH, :] = held[
                        a, i * STRETCH : (i + 1) * STRETCH, cols
                    ].astype(F32)
                    at = i * PIECE + (1 + a) * REACH
                    pay[c, h, at : at + REACH, :] = xs[parity, a, h, base + STRETCH - REACH : base + STRETCH, :]
                    at = at + 3 * REACH
                    pay[c, h, at : at + REACH, :] = xs[parity, a, h, base : base + REACH, :]
                qs[parity, h, i, 0:16, :] = edge[2 * i, :, cols].astype(F32)
                qs[parity, h, i, 16:32, :] = edge[2 * i + 1, :, cols].astype(F32)
                at = i * PIECE
                pay[c, h, at : at + REACH, :] = qs[parity, h, i, 32 - REACH : 32, :]
                pay[c, h, at + 3 * REACH : at + 4 * REACH, :] = qs[parity, h, i, 0:REACH, :]
            taps = [[taps_vm[a, j : j + 1, cols] for j in range(REACH + 1)] for a in range(2)]
            for i in range(2):
                base = i * (STRETCH + 8) + 8
                both = []
                for a in range(2):
                    strided = {
                        m: xs[parity, a, h, pl.ds(base + m, 8, stride=8), :] for m in range(-REACH, STRETCH // 8)
                    }
                    found = []
                    for m in range(STRETCH // 8):
                        total = taps[a][0] * strided[m]
                        for j in range(1, REACH + 1):
                            total = total + taps[a][j] * strided[m - j]
                        found.append(total)
                    both.append(found)
                mixed = [k * v for k, v in zip(*both)]
                for m in range(0, STRETCH // 8, 2):
                    high, low = split(jnp.concatenate(mixed[m : m + 2], axis=0))
                    rows = slice(i * STRETCH + 8 * m, i * STRETCH + 8 * m + 16)
                    u_vm[c, 0, rows, part] = high
                    u_vm[c, 1, rows, part] = low

    def products(c):
        found = []
        for i in range(2):
            rows = slice(i * STRETCH, (i + 1) * STRETCH)
            high, low = u_vm[c, 0, rows, :], u_vm[c, 1, rows, :]
            stacked = jnp.concatenate([high, low, high], axis=0)
            found.append(jnp.dot(ends_vm[...], stacked, preferred_element_type=F32)[:8])
        return found

    def finish(c, found):
        for i in range(2):
            moments = found[i]
            rest = (moments - moments.astype(BF16).astype(F32))[:FINE]
            at = PIECE * i + RAW
            for h in range(2):
                part = slice(h * LANES, (h + 1) * LANES)
                pay[c, h, at : at + RANK, :] = moments[:RANK, part]
                pay[c, h, at + RANK : at + COEFS, :] = rest[:, part]
        for h in range(2):
            packed[c, :, h * LANES : (h + 1) * LANES] = pay[c, h].astype(BF16)

    def step(c, carry):
        @pl.when(lax.rem(c, WIDE) == 0)
        def _():
            for copy in loads(c // WIDE):
                copy.wait()

        before = jnp.maximum(c - 1, 0)
        found = products(before)
        features(c)

        @pl.when(c > 0)
        def _():
            finish(before, found)
            for copy in stores(before):
                copy.start()

        return carry

    lax.fori_loop(0, blocks, step, 0)
    finish(blocks - 1, products(blocks - 1))
    for copy in stores(blocks - 1):
        copy.start()

    def end(c, carry):
        for copy in stores(c):
            copy.wait()
        return carry

    lax.fori_loop(0, blocks, end, 0)
    if direct:
        for copy in own_loads():
            copy.wait()


def local_kernel(q_ref, k_ref, v_ref, taps_ref, rates_ref, res_ref, skip_ref, local_ref, *refs):
    *kept, rest_ref, y_ref, xs, u_vm, qc_ref = refs
    tile = q_ref.shape[1]
    per = SPAN // LANES
    first_row = lax.broadcasted_iota(jnp.int32, (8, LANES), 0)
    for g in range(tile // LANES):
        cols = slice(g * LANES, (g + 1) * LANES)
        part = slice(g % per * LANES, (g % per + 1) * LANES)
        taps = [[taps_ref[a, j : j + 1, cols] for j in range(REACH + 1)] for a in range(3)]
        for i in range(2):
            base = i * (STRETCH + 8) + 8
            for a, ref in enumerate((q_ref, k_ref, v_ref)):
                xs[a, g, base - 8 : base, :] = jnp.zeros((8, LANES), F32)
                xs[a, g, base : base + STRETCH, :] = ref[i * STRETCH : (i + 1) * STRETCH, cols].astype(F32)
            for b in range(STRETCH // 8):
                at = base + 8 * b
                totals = []
                for a in range(3):
                    total = taps[a][0] * xs[a, g, at : at + 8, :]
                    for j in range(1, REACH + 1):
                        total = total + taps[a][j] * xs[a, g, at - j : at - j + 8, :]
                    totals.append(total)
                query, mixed = totals[0], totals[1] * totals[2]
                if b == 0:
                    query = jnp.where(first_row >= REACH, query, 1.0)
                    mixed = jnp.where(first_row >= REACH, mixed, 0.0)
                rows = slice(i * STRETCH + 8 * b, i * STRETCH + 8 * b + 8)
                qc_ref[g // per, rows, part] = query
                u_vm[g // per, rows, part] = mixed
    for c in range(tile // SPAN):
        cols = slice(c * SPAN, (c + 1) * SPAN)
        rate = rates_ref[:, cols]
        amount = amplitude(rate, res_ref[:, cols])
        weights = [jnp.sum(amount * value, axis=0, keepdims=True) for value in strengths(rate)]
        for i in range(2):
            rows = slice(i * STRETCH, (i + 1) * STRETCH)
            mixed = u_vm[c, rows, :]
            high, low = split(mixed)
            parts = jnp.dot(
                local_ref[...], jnp.concatenate([high, low, high], axis=0), preferred_element_type=F32
            )
            total = skip_ref[:, cols] * mixed
            for p in range(RANK):
                total = total + weights[p] * parts[p * STRETCH : (p + 1) * STRETCH, :]
            y_ref[c, rows, :] = total
    if not kept:
        rest_ref[...] = qc_ref[...]
        return
    half = pl.num_programs(0) // 2

    @pl.when(pl.program_id(0) < half)
    def _():
        kept[0][...] = qc_ref[...]

    @pl.when(pl.program_id(0) >= half)
    def _():
        rest_ref[...] = qc_ref[...]


def middle_kernel(
    perm_ref, x_ref, taps_ref, rates_ref, res_ref, skip_ref, out_ref,
    raw, ext, moments, past, heads, first, second, states, mids, coefs, fades, result, slab, packed, out_sems,
):
    slots = perm_ref.shape[0]
    groups = x_ref.shape[2] // LANES
    order = rates_ref.shape[0]
    span = 2 * PIECE
    row = lax.broadcasted_iota(jnp.int32, (8, LANES), 0)
    ext[:, :, 0, 0:8, :] = jnp.zeros((3, groups, 8, LANES), F32)
    past[:, :, 0:8, :] = jnp.zeros((groups, slots, 8, LANES), F32)

    def unpack(src, carry):
        for g in range(groups):
            raw[src, g, 8 : 8 + span, :] = x_ref[src, :, g * LANES : (g + 1) * LANES].astype(F32)
        for i in range(2):
            n = perm_ref[2 * src + i]
            for g in range(groups):
                for a in range(3):
                    at = 8 + i * PIECE + a * REACH
                    ext[a, g, n + 1, 0:8, :] = raw[src, g, at + REACH - 8 : at + REACH, :]
                    at = at + 3 * REACH
                    ext[a, g, n, 8:16, :] = raw[src, g, at : at + 8, :]
                at = 8 + i * PIECE + RAW
                fine = jnp.where(row < FINE, raw[src, g, at + RANK : at + RANK + 8, :], 0.0)
                moments[g, n] = raw[src, g, at : at + 8, :] + fine
        return carry

    lax.fori_loop(0, slots // 2, unpack, 0, unroll=2)

    def group_pass(g, carry):
        cols = pl.ds(pl.multiple_of(g * LANES, LANES), LANES)
        rate = rates_ref[:, cols]
        amount = amplitude(rate, res_ref[:, cols])
        basis = strengths(rate)
        powers = [jnp.ones_like(rate), jnp.exp(-rate)]
        for d in range(2, REACH + 1):
            powers.append(powers[-1] * powers[1])
        for t in range(REACH):
            coefs[g, 0, t * order : (t + 1) * order, :] = amount * powers[t + 1]
        for p in range(RANK):
            coefs[g, 1, p * order : (p + 1) * order, :] = amount * powers[1] * basis[p]
        fade_rest = jnp.exp(-rate * float(INNER))
        fades[g, 0] = powers[REACH]
        fades[g, 1] = fade_rest * powers[REACH]
        taps = [[taps_ref[a, j : j + 1, cols] for j in range(REACH + 1)] for a in range(3)]
        near = [jnp.sum(amount * powers[d], axis=0, keepdims=True) for d in range(REACH)]
        near[0] = near[0] + skip_ref[:, cols]

        def head_pass(n, carry):
            feats = []
            for a in range(3):
                total = taps[a][0] * ext[a, g, n, 8:16, :]
                for j in range(1, REACH + 1):
                    total = total + taps[a][j] * ext[a, g, n, 8 - j : 16 - j, :]
                feats.append(jnp.where(row < REACH, total, 0.0))
            mixed = feats[1] * feats[2]
            past[g, n, 8:16, :] = mixed
            total = near[0] * mixed
            for d in range(1, REACH):
                total = total + near[d] * past[g, n, 8 - d : 16 - d, :]
            at = pl.multiple_of(n * 16, 16)
            heads[g, pl.ds(at, 8), :] = feats[0]
            heads[g, pl.ds(at + 8, 8), :] = total
            value = powers[REACH - 1] * past[g, n, 8:9, :]
            for s in range(1, REACH):
                value = value + powers[REACH - 1 - s] * past[g, n, 8 + s : 9 + s, :]
            first[g, n] = value
            return carry

        lax.fori_loop(0, slots, head_pass, 0, unroll=4)

        def rest_pass(n, carry):
            value = fade_rest * first[g, n]
            for p in range(RANK):
                value = value + basis[p] * moments[g, n, p : p + 1, :]
            second[g, n] = value
            return carry

        lax.fori_loop(0, slots, rest_pass, 0, unroll=4)
        return carry

    lax.fori_loop(0, groups, group_pass, 0)

    def scan_pass(n, state):
        after = []
        at = pl.multiple_of(n * order, order)
        for g in range(groups):
            states[g, pl.ds(at, order), :] = state[g]
            mids[g, pl.ds(at, order), :] = fades[g, 0] * state[g] + first[g, n]
            after.append(fades[g, 1] * state[g] + second[g, n])
        return tuple(after)

    lax.fori_loop(0, slots, scan_pass, tuple(jnp.zeros((order, LANES), F32) for _ in range(groups)), unroll=4)

    quad = 4

    def sums(g, kind, held, first_tile):
        totals = [[None] * quad for _ in range(RANK)]
        for r in range(order):
            values = [held[g, pl.ds((first_tile + k) * 8 * order + r, 8, stride=order), :] for k in range(quad)]
            for p in range(RANK):
                weight = coefs[g, kind, p * order + r : p * order + r + 1, :]
                for k in range(quad):
                    term = weight * values[k]
                    totals[p][k] = term if r == 0 else totals[p][k] + term
        return totals

    quads = slots // (8 * quad)

    def out_pass(step, carry):
        g, q = step // quads, lax.rem(step, quads)
        totals = sums(g, 0, states, q * quad)
        for t in range(REACH):
            for k in range(quad):
                tile = q * quad + k
                query = heads[g, pl.ds(tile * 128 + t, 8, stride=16), :]
                local = heads[g, pl.ds(tile * 128 + 8 + t, 8, stride=16), :]
                z = query * (local + totals[t][k])
                result[g, pl.ds(tile * 192 + t, 8, stride=24), :] = z
                result[g, pl.ds(tile * 192 + REACH + t, 8, stride=24), :] = z - z.astype(BF16).astype(F32)
        totals = sums(g, 1, mids, q * quad)
        for p in range(RANK):
            for k in range(quad):
                tile = q * quad + k
                value = totals[p][k]
                result[g, pl.ds(tile * 192 + 2 * REACH + p, 8, stride=24), :] = value
                if p < FINE:
                    rest = value - value.astype(BF16).astype(F32)
                    result[g, pl.ds(tile * 192 + 2 * REACH + RANK + p, 8, stride=24), :] = rest
        return carry

    lax.fori_loop(0, groups * quads, out_pass, 0)

    def store(src):
        return pltpu.make_async_copy(packed.at[src], out_ref.at[src], out_sems.at[src])

    def pack(src, carry):
        for g in range(groups):
            for i in range(2):
                at = pl.multiple_of(perm_ref[2 * src + i] * 24, 8)
                slab[src, g, i * BACK : i * BACK + 24, :] = result[g, pl.ds(at, 24), :]
            packed[src, :, g * LANES : (g + 1) * LANES] = slab[src, g, 0 : 2 * BACK, :].astype(BF16)
        return carry

    def send(src, carry):
        store(src).start()
        return carry

    def end(src, carry):
        store(src).wait()
        return carry

    middle = slots // 4
    for low, high in ((0, middle), (middle, slots // 2)):
        lax.fori_loop(low, high, pack, 0, unroll=4)
        lax.fori_loop(low, high, send, 0)
    lax.fori_loop(0, slots // 2, end, 0)


def join_kernel(back_ref, lift_ref, *refs):
    *kept, rest_ref, y_ref, z_ref, sq_ref, rest_vm, carry, total, sems = refs
    blocks, tokens, _ = y_ref.shape
    by_dest = len(back_ref.shape) == 3
    chunk = 4
    first = blocks - rest_vm.shape[0]

    def load(c):
        rows = pl.ds(c * chunk, chunk)
        return pltpu.make_async_copy(rest_ref.at[rows], rest_vm.at[rows], sems.at[c])

    def lanes(b):
        return pl.ds(pl.multiple_of(b * SPAN, SPAN), SPAN)

    for c in range((blocks - first) // chunk):
        load(c).start()

    def products(c, unused):
        for k in range(chunk):
            b = c * chunk + k
            back = back_ref[b] if by_dest else back_ref[:, lanes(b)]
            product = jnp.dot(lift_ref[0], back, preferred_element_type=F32)
            carry[b] = y_ref[b] + product + jnp.dot(lift_ref[1], back, preferred_element_type=F32)
        return unused

    lax.fori_loop(0, blocks // chunk, products, 0)
    total[...] = jnp.zeros((tokens, LANES), F32)

    def square(held, offset, c):
        part = total[...]
        for k in range(chunk):
            b = c * chunk + k
            z = held[b] * carry[offset + b]
            z_ref[:, lanes(offset + b)] = z
            squares = z * z
            for h in range(SPAN // LANES):
                part = part + squares[:, h * LANES : (h + 1) * LANES]
        total[...] = part

    def from_kept(c, unused):
        square(kept[0], 0, c)
        return unused

    def from_rest(c, unused):
        load(c).wait()
        square(rest_vm, first, c)
        return unused

    if kept:
        lax.fori_loop(0, first // chunk, from_kept, 0)
    lax.fori_loop(0, (blocks - first) // chunk, from_rest, 0)
    sq_ref[...] = jnp.sum(total[...].T, axis=0, keepdims=True)


def scale_kernel(*refs, channels):
    z_ref, gain_ref, refs, (out_ref, held, sems) = refs[0], refs[1], refs[2:-3], refs[-3:]
    tokens, width = z_ref.shape
    chunks = sems.shape[0]
    wide = width // chunks
    total = refs[0][...]
    for ref in refs[1:]:
        total = total + ref[...]
    scale = lax.rsqrt(total / channels + 1e-05)
    scale = jnp.broadcast_to(scale, (LANES, tokens)).T
    copies = []
    for c in range(chunks):
        for g in range(c * wide // LANES, (c + 1) * wide // LANES):
            cols = slice(g * LANES, (g + 1) * LANES)
            held[:, cols] = (z_ref[:, cols] * scale * gain_ref[:, cols]).astype(BF16)
        cols = pl.ds(c * wide, wide)
        copy = pltpu.make_async_copy(held.at[:, cols], out_ref.at[:, cols], sems.at[c])
        copy.start()
        copies.append(copy)
    for copy in copies:
        copy.wait()


def limit(mib):
    return pltpu.CompilerParams(vmem_limit_bytes=mib * 1024 * 1024)


def on_device(sizes, q_in, k_in, v_in, stretch_of_slot, short_weight, rates, residues, skip, gain):
    n_ctx, n_ch = sizes
    tokens, width = q_in.shape
    slots = stretch_of_slot.shape[0]
    order = rates.shape[0]
    share = width // n_ctx
    direct = share == SPAN
    tile = min(width, 1024)
    steps = width // tile
    groups = tile // LANES
    ends_np, local_np, lift_np = constant_matrices()
    ends, local, lift = jnp.asarray(ends_np), jnp.asarray(local_np), jnp.asarray(lift_np)
    skip, gain = skip.reshape(1, width), gain.reshape(1, width)
    me = lax.axis_index("ctx").astype(jnp.int32).reshape(1)

    def whole(array):
        return pl.BlockSpec(array.shape, lambda c: (0,) * array.ndim)

    def columns(*lead):
        return pl.BlockSpec((*lead, tile), lambda c: (0,) * len(lead) + (c,))

    def exchange(array):
        if direct:
            return lax.all_to_all(array, "ctx", 0, 0, tiled=True)
        array = array.reshape(array.shape[0], n_ctx, share).transpose(1, 0, 2)
        return widen(lax.all_to_all(array, "ctx", 0, 0, tiled=True))

    lanes = -(-share // LANES) * LANES

    def widen(array, fill=0.0):
        pad = [(0, 0)] * (array.ndim - 1) + [(0, lanes - share)]
        return jnp.pad(array, pad, constant_values=fill)

    def cut(array, fill=0.0):
        return widen(lax.dynamic_slice_in_dim(array, lax.axis_index("ctx") * share, share, array.ndim - 1), fill)

    smem = pl.BlockSpec(memory_space=pltpu.SMEM)
    vmem = pl.BlockSpec(memory_space=pltpu.VMEM)
    hbm = pl.BlockSpec(memory_space=pltpu.HBM)
    f32 = lambda *shape: jax.ShapeDtypeStruct(shape, F32)
    pin = lambda array: pltpu.with_memory_space_constraint(array, pltpu.HBM)

    weights = (short_weight, rates, residues, skip)
    own = [f32(*w.shape[:-1], share) for w in weights] if direct else []
    blocks = width // SPAN
    pay, *mine = pl.pallas_call(
        functools.partial(front_kernel, direct=direct),
        in_specs=[smem] + [hbm] * (5 + len(own)),
        out_specs=[hbm] + [vmem] * len(own),
        out_shape=[
            pltpu.HBM((n_ctx, 2 * PIECE, share) if direct else (2 * PIECE, width), BF16),
        ]
        + own,
        scratch_shapes=[
            pltpu.VMEM((2, tokens, width), BF16),
            pltpu.VMEM((4, 16, width), BF16),
            pltpu.VMEM((2, REACH + 1, width), F32),
            pltpu.VMEM(ends.shape, BF16),
            pltpu.VMEM((2, 2, 2, 2 * (STRETCH + 8), LANES), F32),
            pltpu.VMEM((2, 2, 2, 32, LANES), F32),
            pltpu.VMEM((blocks, 2, 2 * PIECE, LANES), F32),
            pltpu.VMEM((blocks, 2 * PIECE, SPAN), BF16),
            pltpu.VMEM((blocks, 2, tokens, SPAN), BF16),
            pltpu.SemaphoreType.DMA((3, blocks // WIDE)),
            pltpu.SemaphoreType.DMA((4,)),
            pltpu.SemaphoreType.DMA((1,)),
            pltpu.SemaphoreType.DMA((4,)),
            pltpu.SemaphoreType.DMA((blocks,)),
        ],
        compiler_params=limit(24),
        name="front_pieces",
    )(me, *map(pin, (q_in, k_in, v_in, short_weight, ends)), *(map(pin, weights) if direct else ()))
    arrived = exchange(pay)
    if not direct:
        mine = (cut(short_weight), cut(rates, 0.01), cut(residues), cut(skip))

    half = steps // 2 if steps % 2 == 0 else 0
    kept = half * (tile // SPAN)
    places = [lambda c: (jnp.minimum(c, half - 1), 0, 0)] * (kept > 0)
    places += [lambda c: (jnp.maximum(c - half, 0), 0, 0), lambda c: (c, 0, 0)]
    *query, inner = pl.pallas_call(
        local_kernel,
        grid=(steps,),
        in_specs=[columns(tokens)] * 3
        + [columns(3, REACH + 1), columns(order), columns(order), columns(1), whole(local)],
        out_specs=[pl.BlockSpec((tile // SPAN, tokens, SPAN), at) for at in places],
        out_shape=[pltpu.VMEM((kept, tokens, SPAN), F32)] * (kept > 0)
        + [pltpu.HBM((blocks - kept, tokens, SPAN), F32), pltpu.VMEM((blocks, tokens, SPAN), F32)],
        scratch_shapes=[
            pltpu.VMEM((3, groups, 2 * (STRETCH + 8), LANES), F32),
            pltpu.VMEM((tile // SPAN, tokens, SPAN), F32),
            pltpu.VMEM((tile // SPAN, tokens, SPAN), F32),
        ],
        compiler_params=limit(24),
        name="local_filter",
        cost_estimate=pl.CostEstimate(flops=10**9, bytes_accessed=20 * 10**6, transcendentals=0),
    )(*map(pin, (q_in, k_in, v_in, short_weight, rates, residues)), skip, local)
    arrived, query, inner = lax.optimization_barrier((arrived, query, inner))

    groups = lanes // LANES
    back = pl.pallas_call(
        middle_kernel,
        in_specs=[smem] + [vmem] * 5,
        out_specs=hbm,
        scratch_shapes=[
            pltpu.VMEM((n_ctx, groups, 8 + 2 * PIECE + 8, LANES), F32),
            pltpu.VMEM((3, groups, slots + 1, 16, LANES), F32),
            pltpu.VMEM((groups, slots, 8, LANES), F32),
            pltpu.VMEM((groups, slots, 16, LANES), F32),
            pltpu.VMEM((groups, slots * 16, LANES), F32),
            pltpu.VMEM((groups, slots, order, LANES), F32),
            pltpu.VMEM((groups, slots, order, LANES), F32),
            pltpu.VMEM((groups, slots * order, LANES), F32),
            pltpu.VMEM((groups, slots * order, LANES), F32),
            pltpu.VMEM((groups, 2, RANK * order, LANES), F32),
            pltpu.VMEM((groups, 2, order, LANES), F32),
            pltpu.VMEM((groups, slots * 24, LANES), F32),
            pltpu.VMEM((n_ctx, groups, BACK + 28, LANES), F32),
            pltpu.VMEM((n_ctx, 2 * BACK, lanes), BF16),
            pltpu.SemaphoreType.DMA((n_ctx,)),
        ],
        out_shape=pltpu.HBM((n_ctx, 2 * BACK, lanes), BF16),
        compiler_params=limit(24),
        name="middle_states",
    )(stretch_of_slot, arrived, *mine)
    if not direct:
        back = back[:, :, :share]
    back = lax.all_to_all(back, "ctx", 0, 0, tiled=True)
    if not direct:
        back = back.transpose(1, 0, 2).reshape(2 * BACK, width)

    keep = lambda array: pltpu.with_memory_space_constraint(array, pltpu.VMEM)
    zvalues, squares = pl.pallas_call(
        join_kernel,
        in_specs=[vmem] * (1 + len(query)) + [hbm, vmem],
        out_specs=[vmem] * 2,
        out_shape=[f32(tokens, width), f32(1, tokens)],
        scratch_shapes=[
            pltpu.VMEM((blocks - kept, tokens, SPAN), F32),
            pltpu.VMEM((blocks, tokens, SPAN), F32),
            pltpu.VMEM((tokens, LANES), F32),
            pltpu.SemaphoreType.DMA(((blocks - kept) // 4,)),
        ],
        compiler_params=limit(24),
        name="join_carry",
    )(back, lift, *map(keep, query[:-1]), pin(query[-1]), keep(inner))
    sums = [squares]
    for shift in range(1, n_ch):
        sums.append(lax.ppermute(squares, "ch", [(i, (i + shift) % n_ch) for i in range(n_ch)]))
    return pl.pallas_call(
        functools.partial(scale_kernel, channels=width * n_ch),
        in_specs=[vmem] * (2 + n_ch),
        out_specs=hbm,
        out_shape=pltpu.HBM((tokens, width), BF16),
        scratch_shapes=[pltpu.VMEM((tokens, width), BF16), pltpu.SemaphoreType.DMA((8 if width % 1024 == 0 else 1,))],
        compiler_params=limit(24),
        name="scale_rows",
    )(zvalues, gain, *sums)


def solution(mesh):
    sizes = (mesh.shape["ctx"], mesh.shape["ch"])
    in_specs = (
        P("ctx", "ch"),
        P("ctx", "ch"),
        P("ctx", "ch"),
        P(),
        P(None, None, "ch"),
        P(None, "ch"),
        P(None, "ch"),
        P("ch"),
        P("ch"),
    )

    def run(*arrays):
        return on_device(sizes, *arrays)

    return jax.shard_map(run, mesh=mesh, in_specs=in_specs, out_specs=P("ctx", "ch"), check_vma=False)
```
